32 devices in a mesh: groups: 2 (over x), store: 8 (over z, y), tensor: 2 (over core).
Axes of the slice: x: 2, y: 2, z: 4, core: 2. Of those that a mesh axis runs over, the one named last changes fastest.
Arguments:
- queries: bfloat16 [16, 64, 8192], P(('groups', 'store'), None, 'tensor'), parts along dimension 0, may hold values from -9 to 9
- suffix_key_value: bfloat16 [16, 2, 64, 1024], P(('groups', 'store'), None, None, 'tensor'), parts along dimension 0, may hold values from -6 to 6
- kv_pages: bfloat16 [512, 2, 64, 1024], P(('groups', 'store'), None, None, 'tensor'), parts along dimension 0, may hold values from -6 to 6
- page_table: int32 [16, 64], P(('groups', 'store')), parts along dimension 0, may hold values from 0 to 255, as said below
- prefix_pages: int32 [16], P(('groups', 'store')), parts along dimension 0, may hold values from 1 to 64, as said below
- new_slots: int32 [16], P(('groups', 'store')), parts along dimension 0, may hold values from 0 to 31
Outputs:
- attended: bfloat16 [16, 64, 8192], P(('groups', 'store'), None, 'tensor'), parts along dimension 0
- new_store: bfloat16 [512, 2, 64, 1024], P(('groups', 'store'), None, None, 'tensor'), parts along dimension 0
The draws below stay inside these ranges and needn't reach their ends.
There are 2 independent parts, one for each index of `groups`. The reference program is written for one: setup_inputs(seed, part) draws one part's arguments, and reference() takes and returns one part's arrays. A program takes and returns all parts, laid end to end along the dimension named above; each array names one. Nothing has to cross between parts.
Inputs may be any that keep to these rules, and one draw needn't show every extreme that they name: `page_table`: A page id p lives on store device p // 32. In every row each store device owns exactly 8 of the 64 entries; entries past the prefix length are valid ids that are not read; ids may repeat across requests. `prefix_pages`: some request has exactly 64 prefix pages.
All inputs are finite; a program needn't handle non-finite values.
Results may differ from the reference program's by a relative error of at most 0.0075.
Values may be sent and summed in bfloat16 or wider, within the bound.
No kernel may reach another device: no remote copies, remote signals or barrier semaphores. Data moves between devices by JAX's collectives and lax.ppermute only.
A program may use at most 64 MiB of HBM per device.

```python
import jax
import jax.numpy as jnp
from jax import lax

QUERY_HEADS = 64
KEY_VALUE_HEADS = 8
HEAD_SIZE = 128
PAGE_TOKENS = 64
MAXP = 64
PAGES_DEV = 32
SUFFIX_TOKENS = 64
REQUEST_COUNT = 8
STORED_PAGES = 256
CAP = 8
N_STORE = 8


def draw_queries(key, part):
    key = jax.random.fold_in(key, 7)
    first = jax.random.fold_in(key, 0)
    array_shape = (REQUEST_COUNT, SUFFIX_TOKENS, QUERY_HEADS, HEAD_SIZE)
    base_offset = jnp.clip(jax.random.normal(first, array_shape, jnp.float32), -6.0, 6.0)
    return base_offset.reshape(REQUEST_COUNT, SUFFIX_TOKENS, QUERY_HEADS * HEAD_SIZE).astype(jnp.bfloat16)


def draw_kv_pages(key, part):
    key = jax.random.fold_in(key, 11)
    first = jax.random.fold_in(key, 0)
    array_shape = (STORED_PAGES, 2, PAGE_TOKENS, KEY_VALUE_HEADS, HEAD_SIZE)
    base_offset = jnp.clip(jax.random.normal(first, array_shape, jnp.float32), -6.0, 6.0)
    return base_offset.reshape(STORED_PAGES, 2, PAGE_TOKENS, KEY_VALUE_HEADS * HEAD_SIZE).astype(jnp.bfloat16)


def draw_page_table(key, part):
    key = jax.random.fold_in(key, 3)
    first, second_part = jax.random.split(key)
    row_keys = jax.random.split(first, REQUEST_COUNT)
    orders = jax.vmap(lambda row_key: jax.random.permutation(row_key, MAXP))(row_keys)
    owners = orders // CAP
    local_ids = jax.random.randint(second_part, (REQUEST_COUNT, MAXP), 0, PAGES_DEV)
    return (owners * PAGES_DEV + local_ids).astype(jnp.int32)


def draw_prefix_pages(key, part):
    key = jax.random.fold_in(key, 5)
    first, second_part = jax.random.split(key)
    lengths = jax.random.randint(first, (REQUEST_COUNT,), 1, MAXP + 1)
    longest = jax.random.randint(second_part, (), 0, REQUEST_COUNT)
    return jnp.where(jnp.arange(REQUEST_COUNT) == longest, MAXP, lengths).astype(jnp.int32)


def plant(result, key, smallest, largest):
    dims = result.shape
    spot = [jax.random.randint(jax.random.fold_in(key, axis), (), 0, dims[axis]) for axis in range(len(dims))]
    result = result.at[tuple(spot)].set(smallest)
    longest = dims.index(max(dims))
    spot[longest] = (spot[longest] + 1) % dims[longest]
    return result.at[tuple(spot)].set(largest)


def shard_levels(own_key, dims, cuts, low, largest):
    level = 1.0
    for position, blocks in cuts:
        draws = jax.random.uniform(jax.random.fold_in(jax.random.fold_in(own_key, 6), position), (blocks,), jnp.float32, low / len(cuts), largest / len(cuts))
        level = level * jnp.repeat(jnp.exp(draws), dims[position] // blocks).reshape((-1,) + (1,) * (len(dims) - 1 - position))
    return level


def centred(stream_key, dims, scale, limit, cuts=(), held_as=jnp.bfloat16):
    result = scale * jax.random.normal(stream_key, dims, jnp.float32)
    if cuts:
        result = result * shard_levels(stream_key, dims, cuts, -0.22, 0.18)
    return jnp.clip(result, -limit, limit).astype(held_as)


def setup_inputs(seed: int = 0, part: int = 0) -> dict:
    seeds = jax.random.split(jax.random.key(seed), 7)
    own_keys = jax.random.split(jax.random.fold_in(seeds[6], part), 7)
    queries = draw_queries(jax.random.fold_in(jax.random.fold_in(seeds[6], part), 71), part)
    suffix_key_value = centred(own_keys[1], (REQUEST_COUNT, 2, SUFFIX_TOKENS, KEY_VALUE_HEADS * HEAD_SIZE), 1.0, 6.0, ((0, 8), (3, 2)))
    kv_pages = draw_kv_pages(jax.random.fold_in(jax.random.fold_in(seeds[6], part), 71), part)
    page_table = draw_page_table(jax.random.fold_in(jax.random.fold_in(seeds[6], part), 71), part)
    prefix_pages = draw_prefix_pages(jax.random.fold_in(jax.random.fold_in(seeds[6], part), 71), part)
    new_slots = plant(jax.random.randint(own_keys[5], (REQUEST_COUNT,), 0, PAGES_DEV), jax.random.fold_in(own_keys[5], 1), 0, PAGES_DEV - 1).astype(jnp.int32)
    return {"queries": queries, "suffix_key_value": suffix_key_value, "kv_pages": kv_pages, "page_table": page_table, "prefix_pages": prefix_pages, "new_slots": new_slots}


def reference(queries, suffix_key_value, kv_pages, page_table, prefix_pages, new_slots):
    groups_per_head = QUERY_HEADS // KEY_VALUE_HEADS
    scale = HEAD_SIZE ** -0.5
    prefix_length = MAXP * PAGE_TOKENS

    def one_request(items):
        query_matrix, suffix_key_value_pair, table, length = items
        page_list = kv_pages[table]
        key_rows = jnp.concatenate([page_list[:, 0].reshape(prefix_length, KEY_VALUE_HEADS, HEAD_SIZE), suffix_key_value_pair[0].reshape(SUFFIX_TOKENS, KEY_VALUE_HEADS, HEAD_SIZE)], axis=0)
        value_rows = jnp.concatenate([page_list[:, 1].reshape(prefix_length, KEY_VALUE_HEADS, HEAD_SIZE), suffix_key_value_pair[1].reshape(SUFFIX_TOKENS, KEY_VALUE_HEADS, HEAD_SIZE)], axis=0)
        positions = jnp.arange(prefix_length, dtype=jnp.int32)
        live_prefix = jnp.broadcast_to((positions < length * PAGE_TOKENS)[None, :], (SUFFIX_TOKENS, prefix_length)).astype(jnp.int32)
        rows = jnp.arange(SUFFIX_TOKENS, dtype=jnp.int32)
        causal = (rows[None, :] <= rows[:, None]).astype(jnp.int32)
        live = jnp.concatenate([live_prefix, causal], axis=1) == 1
        head_count = query_matrix.reshape(SUFFIX_TOKENS, KEY_VALUE_HEADS, groups_per_head, HEAD_SIZE)
        scores = jnp.einsum("qhgd,khd->hgqk", head_count.astype(jnp.float32), key_rows.astype(jnp.float32)) * scale
        scores = jnp.where(live, scores, -1e30)
        top = jnp.max(scores, axis=-1, keepdims=True)
        weights = jnp.where(live, jnp.exp(scores - top), 0.0)
        total = jnp.sum(weights, axis=-1)
        rounded = weights.astype(jnp.bfloat16).astype(jnp.float32)
        output = jnp.einsum("hgqk,khd->hgqd", rounded, value_rows.astype(jnp.float32)) / total[..., None]
        return output.transpose(2, 0, 1, 3).reshape(SUFFIX_TOKENS, QUERY_HEADS * HEAD_SIZE).astype(jnp.bfloat16)

    attended = lax.map(one_request, (queries, suffix_key_value, page_table, prefix_pages))
    requests = jnp.arange(REQUEST_COUNT, dtype=jnp.int32)
    targets = ((requests + N_STORE // 2) % N_STORE) * PAGES_DEV + new_slots
    new_store = kv_pages.at[targets].set(suffix_key_value)
    return attended, new_store
```

```python
import functools

import jax
import jax.numpy as jnp
from jax import lax
from jax.experimental import pallas as pl
from jax.experimental.pallas import tpu as pltpu
from jax.sharding import PartitionSpec as P

HEAD_SIZE = 128
LOG2E = 1.4426950408889634
DEAD = -1e30
FLOOR = -1e29
STAT_ROWS = 16
VMEM = pl.BlockSpec(memory_space=pltpu.VMEM)
SMEM = pl.BlockSpec(memory_space=pltpu.SMEM)
HBM = pl.BlockSpec(memory_space=pl.ANY)


def shifted(block, axis, distance):
    devices = range(lax.axis_size(axis))
    route = [((i - distance) % len(devices), i) for i in devices]
    return lax.ppermute(block, axis, route)


def block_update(state, head_count, key_rows, value_rows, live, scale):
    top_old, total_old, acc_old = state
    scores = (
        jnp.einsum("qhgd,khd->hgqk", head_count, key_rows, preferred_element_type=jnp.float32)
        * scale
    )
    scores = jnp.where(live, scores, -1e30)
    top_new = jnp.maximum(top_old, jnp.max(scores, axis=-1))
    weights = jnp.where(live, jnp.exp(scores - top_new[..., None]), 0.0)
    factor = jnp.exp(top_old - top_new)
    total_new = total_old * factor + jnp.sum(weights, axis=-1)
    product = jnp.einsum(
        "hgqk,khd->hgqd",
        weights.astype(jnp.bfloat16),
        value_rows,
        preferred_element_type=jnp.float32,
    )
    return (top_new, total_new, acc_old * factor[..., None] + product)


def pages_travel(queries, suffix_key_value, kv_pages, page_table, prefix_pages, new_slots):
    stores = lax.axis_size("store")
    pages_dev = kv_pages.shape[0]
    maxp = page_table.shape[1]
    cap = maxp // stores
    page_len = kv_pages.shape[2]
    width = kv_pages.shape[3]
    kv_heads = width // HEAD_SIZE
    suffix = queries.shape[1]
    groups_per_head = queries.shape[2] // width
    scale = HEAD_SIZE ** (-0.5)
    length = prefix_pages[0]
    table = page_table[0]
    owners = table // pages_dev
    local_ids = table % pages_dev
    entries = jnp.arange(maxp, dtype=jnp.int32)
    same_owner = (owners[:, None] == owners[None, :]) & (entries[:, None] < entries[None, :])
    ranks = jnp.sum(same_owner.astype(jnp.int32), axis=0)
    slots = owners * cap + ranks
    placed = slots[:, None] == entries[None, :]
    slot_entry = jnp.sum(jnp.where(placed, entries[:, None], 0), axis=0)
    wanted = jnp.sum(jnp.where(placed, local_ids[:, None], 0), axis=0)
    asked = lax.all_to_all(
        wanted.reshape(stores, cap), "store", split_axis=0, concat_axis=0, tiled=True
    )
    served = kv_pages[asked.reshape(-1)].reshape(stores, cap, 2, page_len, width)
    received = lax.all_to_all(served, "store", split_axis=0, concat_axis=0, tiled=True).reshape(
        maxp, 2, page_len, width
    )
    head_count = queries[0].reshape(suffix, kv_heads, groups_per_head, HEAD_SIZE)
    own_keys = suffix_key_value[0, 0].reshape(suffix, kv_heads, HEAD_SIZE)
    own_values = suffix_key_value[0, 1].reshape(suffix, kv_heads, HEAD_SIZE)
    rows = jnp.arange(suffix, dtype=jnp.int32)
    causal = rows[None, :] <= rows[:, None]
    start_state = (
        jnp.full((kv_heads, groups_per_head, suffix), -1e30, jnp.float32),
        jnp.zeros((kv_heads, groups_per_head, suffix), jnp.float32),
        jnp.zeros((kv_heads, groups_per_head, suffix, HEAD_SIZE), jnp.float32),
    )
    state = block_update(start_state, head_count, own_keys, own_values, causal, scale)
    block_pages = min(8, maxp)
    live_pages = slot_entry < length
    trips = maxp // block_pages

    def step_block(index, carry):
        first = index * block_pages
        block = lax.dynamic_slice_in_dim(received, first, block_pages, 0)
        alive = lax.dynamic_slice_in_dim(live_pages, first, block_pages, 0)
        alive = jnp.broadcast_to(alive[:, None], (block_pages, page_len)).reshape(
            1, block_pages * page_len
        )
        block_keys = block[:, 0].reshape(block_pages * page_len, kv_heads, HEAD_SIZE)
        block_values = block[:, 1].reshape(block_pages * page_len, kv_heads, HEAD_SIZE)
        return block_update(carry, head_count, block_keys, block_values, alive, scale)

    top_final, total_final, acc_final = lax.fori_loop(0, trips, step_block, state)
    output = acc_final / total_final[..., None]
    attended = (
        output.transpose(2, 0, 1, 3)
        .reshape(1, suffix, groups_per_head * width)
        .astype(jnp.bfloat16)
    )
    arrived, arrived_slot = shifted((suffix_key_value, new_slots), "store", stores // 2)
    new_store = lax.dynamic_update_slice_in_dim(kv_pages, arrived, arrived_slot[0], 0)
    return (attended, new_store)


def dot_nt(a, b):
    return lax.dot_general(a, b, (((1,), (1,)), ((), ())), preferred_element_type=jnp.float32)


def iota(shape, dim):
    return lax.broadcasted_iota(jnp.int32, shape, dim)


def pack_stats(top, total):
    lane = iota((HEAD_SIZE, HEAD_SIZE), 1)
    row = iota((STAT_ROWS, HEAD_SIZE), 0)
    col = iota((STAT_ROWS, HEAD_SIZE), 1)
    tile = jnp.zeros((STAT_ROWS, HEAD_SIZE), jnp.float32)
    for j, (m, l) in enumerate(zip(top, total)):
        high = l.astype(jnp.bfloat16).astype(jnp.float32)
        low = l - high
        mixed = jnp.where(lane == 0, m, jnp.where(lane == 1, high, low)).astype(jnp.bfloat16)
        pick = ((row == col * 4 + j) & (col < 3)).astype(jnp.float32).astype(jnp.bfloat16)
        tile = tile + dot_nt(pick, mixed)
    return tile.astype(jnp.bfloat16)


def unpack_stats(tile):
    row = iota((STAT_ROWS, 8 * HEAD_SIZE), 0)
    block = iota((STAT_ROWS, 8 * HEAD_SIZE), 1) // HEAD_SIZE
    j = block // 2
    stat = block % 2
    spread = (
        ((row == j) & (stat == 0)) | ((row == j + 4) & (stat == 1)) | ((row == j + 8) & (stat == 1))
    )
    spread = spread.astype(jnp.float32).astype(jnp.bfloat16)
    turned = tile.astype(jnp.float32).T.astype(jnp.bfloat16)
    wide = jnp.dot(turned, spread, preferred_element_type=jnp.float32)
    part = lambda b: wide[:, b * HEAD_SIZE:(b + 1) * HEAD_SIZE]
    return [part(2 * j) for j in range(4)], [part(2 * j + 1) for j in range(4)]


def partial_rows(q, k, v, live, own, factor):
    s = dot_nt(q, k)
    s = jnp.where(live, s, DEAD)
    top = jnp.max(s, axis=-1, keepdims=True)
    if own is not None:
        k_own, v_own, causal = own
        s_own = jnp.where(causal, dot_nt(q, k_own), DEAD)
        top = jnp.maximum(top, jnp.max(s_own, axis=-1, keepdims=True))
    top = jnp.maximum(top * factor, FLOOR).astype(jnp.bfloat16).astype(jnp.float32)
    p = jnp.exp2(s * factor - top).astype(jnp.bfloat16)
    ones = jnp.ones((k.shape[0], HEAD_SIZE), jnp.bfloat16)
    out = jnp.dot(p, jnp.concatenate([v, ones], 1), preferred_element_type=jnp.float32)
    if own is not None:
        p = jnp.exp2(s_own * factor - top).astype(jnp.bfloat16)
        ones = jnp.ones((k_own.shape[0], HEAD_SIZE), jnp.bfloat16)
        out = out + jnp.dot(p, jnp.concatenate([v_own, ones], 1), preferred_element_type=jnp.float32)
    top = jnp.broadcast_to(top, (q.shape[0], HEAD_SIZE))
    return out[:, :HEAD_SIZE], top, out[:, HEAD_SIZE:]


def attend_kernel(sizes, parts, own, wire, *refs):
    kv_heads, groups, suffix, cap, page_len = sizes
    refs = list(refs)
    meta = refs.pop(0)
    queries = [[refs.pop(0) for _ in range(n)] for n in parts]
    own_kv = refs.pop(0) if own else None
    pages = refs.pop(0)
    outs = [(refs.pop(0), refs.pop(0)) for _ in parts]
    held, sems = refs
    copies = [
        [
            pltpu.make_async_copy(pages.at[meta[n, c]], held.at[n, c], sems.at[n, c])
            for c in range(cap)
        ]
        for n in range(len(parts))
    ]
    for request in copies:
        for copy in request:
            copy.start()
    factor = HEAD_SIZE ** (-0.5) * LOG2E
    keys = cap * page_len
    for n, halves in enumerate(queries):
        for copy in copies[n]:
            copy.wait()
        live = iota((1, keys), 1) < meta[n, cap] * page_len
        heads_each = kv_heads // len(halves)
        acc_ref, stat_ref = outs[n]
        for h in range(kv_heads):
            q_ref = halves[h // heads_each]
            first = (h % heads_each) * groups
            lanes = slice(h * HEAD_SIZE, (h + 1) * HEAD_SIZE)
            k = held[n, :, 0, :, lanes].reshape(keys, HEAD_SIZE)
            v = held[n, :, 1, :, lanes].reshape(keys, HEAD_SIZE)
            tops, totals = [], []
            rows = groups * suffix
            per_block = HEAD_SIZE // suffix
            for j in range(rows // HEAD_SIZE):
                q = jnp.concatenate(
                    [
                        q_ref[:, (first + g) * HEAD_SIZE:(first + g + 1) * HEAD_SIZE]
                        for g in range(j * per_block, (j + 1) * per_block)
                    ],
                    0,
                )
                extra = None
                if own:
                    at = iota((HEAD_SIZE, suffix), 0) % suffix
                    extra = (own_kv[0, :, lanes], own_kv[1, :, lanes], iota((HEAD_SIZE, suffix), 1) <= at)
                acc, top, total = partial_rows(q, k, v, live, extra, factor)
                acc_ref[h, j * HEAD_SIZE:(j + 1) * HEAD_SIZE, :] = acc.astype(acc_ref.dtype)
                tops.append(top)
                totals.append(total)
            tile = pack_stats(tops, totals)
            if wire:
                stat_ref[h] = tile
            else:
                stat_ref[h] = tile


def attend(sizes, meta, queries, own_kv, kv_pages, wire=False):
    kv_heads, groups, suffix, cap, page_len = sizes
    parts = [len(q) for q in queries]
    flat = [x for q in queries for x in q]
    own = own_kv is not None
    shapes = []
    rows = groups * suffix
    for _ in parts:
        shapes.append(jax.ShapeDtypeStruct((kv_heads, rows, HEAD_SIZE), jnp.float32))
        shapes.append(jax.ShapeDtypeStruct((kv_heads, STAT_ROWS, HEAD_SIZE), jnp.bfloat16))
    keys = cap * page_len
    count = len(parts)
    out = pl.pallas_call(
        functools.partial(attend_kernel, sizes, parts, own, wire),
        out_shape=shapes,
        in_specs=[SMEM] + [VMEM] * (len(flat) + own) + [HBM],
        out_specs=[VMEM] * len(shapes),
        scratch_shapes=[
            pltpu.VMEM((count, cap) + kv_pages.shape[1:], jnp.bfloat16),
            pltpu.SemaphoreType.DMA((count, cap)),
        ],
        compiler_params=pltpu.CompilerParams(vmem_limit_bytes=48 * 1024 * 1024),
        cost_estimate=pl.CostEstimate(
            flops=count * kv_heads * rows * keys * HEAD_SIZE * 8,
            bytes_accessed=count * kv_heads * (rows * 6 + keys * 4) * HEAD_SIZE,
            transcendentals=count * kv_heads * rows * keys,
        ),
    )(meta, *flat, *([own_kv] if own else []), kv_pages)
    return [(out[2 * n], out[2 * n + 1]) for n in range(count)]


def blend(parts):
    top = functools.reduce(jnp.maximum, [m for _, m, _ in parts])
    scales = [jnp.exp2(m - top) for _, m, _ in parts]
    acc = sum(a * f for (a, _, _), f in zip(parts, scales))
    total = sum(l * f for (_, _, l), f in zip(parts, scales))
    return acc, top, total


def block_of(j):
    return slice(j * HEAD_SIZE, (j + 1) * HEAD_SIZE)


def pack_kernel(first, heads, acc_ref, stat_ref, out_ref):
    rows = acc_ref.shape[1]
    for h in range(heads):
        out_ref[h, :rows, :] = acc_ref[first + h].astype(jnp.bfloat16)
        out_ref[h, rows:, :] = stat_ref[first + h]


def merge_kernel(first, heads, in_ref, acc_ref, stat_ref, out_ref):
    rows = acc_ref.shape[1]
    for h in range(heads):
        in_top, in_total = unpack_stats(in_ref[h, rows:, :])
        my_top, my_total = unpack_stats(stat_ref[first + h])
        tops, totals = [], []
        for j in range(rows // HEAD_SIZE):
            acc, top, total = blend(
                [
                    (in_ref[h, block_of(j), :].astype(jnp.float32), in_top[j], in_total[j]),
                    (acc_ref[first + h, block_of(j), :], my_top[j], my_total[j]),
                ]
            )
            out_ref[h, block_of(j), :] = acc.astype(jnp.bfloat16)
            tops.append(top)
            totals.append(total)
        out_ref[h, rows:, :] = pack_stats(tops, totals)


def final_kernel(heads_each, suffix, *refs):
    arrivals, (acc_ref, stat_ref, out_ref) = refs[:-3], refs[-3:]
    kv_heads, rows = acc_ref.shape[:2]
    groups = rows // suffix
    for h in range(kv_heads):
        here = arrivals[h // heads_each::kv_heads // heads_each]
        stats = [unpack_stats(ref[h % heads_each, rows:, :]) for ref in here]
        stats.append(unpack_stats(stat_ref[h]))
        for j in range(rows // HEAD_SIZE):
            blocks = [ref[h % heads_each, block_of(j), :].astype(jnp.float32) for ref in here]
            blocks.append(acc_ref[h, block_of(j), :])
            acc, _, total = blend([(a, t[j], l[j]) for a, (t, l) in zip(blocks, stats)])
            out = (acc / total).astype(jnp.bfloat16)
            for i in range(HEAD_SIZE // suffix):
                g = h * groups + j * (HEAD_SIZE // suffix) + i
                out_ref[0, :, block_of(g)] = out[i * suffix:(i + 1) * suffix]


def call(kernel, shape, *args):
    size = sum(a.size * a.dtype.itemsize for a in args)
    return pl.pallas_call(
        kernel,
        out_shape=shape,
        in_specs=[VMEM] * len(args),
        out_specs=VMEM,
        compiler_params=pltpu.CompilerParams(vmem_limit_bytes=48 * 1024 * 1024),
        cost_estimate=pl.CostEstimate(flops=size, bytes_accessed=2 * size, transcendentals=size // 8),
    )(*args)


def queries_travel(queries, suffix_key_value, kv_pages, page_table, prefix_pages, new_slots):
    stores = lax.axis_size("store")
    pages_dev, _, page_len, width = kv_pages.shape
    maxp = page_table.shape[1]
    cap = maxp // stores
    kv_heads = width // HEAD_SIZE
    suffix = queries.shape[1]
    groups = queries.shape[2] // width
    sizes = (kv_heads, groups, suffix, cap, page_len)
    half = stores // 2
    me = lax.axis_index("store")

    order = list(range(0, stores, 2)) + list(range(1, stores, 2))[::-1]
    up = [(order[i], order[(i + 1) % stores]) for i in range(stores)]
    down = [(order[i], order[i - 1]) for i in range(stores)]
    place = [order.index(i) for i in range(stores)]
    my_place = jnp.asarray(place, jnp.int32)[me]
    order_now = jnp.asarray(order, jnp.int32)

    mine_row = jnp.concatenate([page_table, prefix_pages[:, None]], 1)
    rows = lax.all_gather(mine_row, "store", axis=0, tiled=True)

    def listing(rows):
        table, length = rows[:, :maxp], rows[:, maxp:]
        entries = jnp.arange(maxp, dtype=jnp.int32)
        held = table // pages_dev == me
        before = entries[:, None] < entries[None, :]
        rank = jnp.sum((held[:, :, None] & before[None]).astype(jnp.int32), 1)
        placed = held[:, :, None] & (rank[:, :, None] == jnp.arange(cap, dtype=jnp.int32))
        ids = jnp.sum(jnp.where(placed, (table % pages_dev)[:, :, None], 0), 1)
        live = jnp.sum((held & (entries[None] < length)).astype(jnp.int32), 1, keepdims=True)
        return jnp.concatenate([ids, live], 1)

    lists = listing(rows)

    def listed(*distances):
        which = [order_now[(my_place - d) % stores] for d in distances]
        return jnp.stack([lists[w] for w in which])

    heads_each = kv_heads // 2
    cut = heads_each * groups * HEAD_SIZE
    mine = [queries[0, :, :cut], queries[0, :, cut:]]
    ups, downs = list(mine), list(mine)
    partials = {}
    partials[0], = attend(sizes, listing(mine_row), [[queries[0]]], suffix_key_value[0], kv_pages)
    for step in range(1, half):
        ups = [lax.ppermute(x, "store", up) for x in ups]
        downs = [lax.ppermute(x, "store", down) for x in downs]
        got = attend(sizes, listed(step, -step), [ups, downs], None, kv_pages)
        partials[step], partials[-step] = got
    ups[0] = lax.ppermute(ups[0], "store", up)
    downs[1] = lax.ppermute(downs[1], "store", down)
    (far,) = attend(sizes, listed(half), [[ups[0], downs[1]]], None, kv_pages)

    rows_head = groups * suffix
    wire = jax.ShapeDtypeStruct((heads_each, rows_head + STAT_ROWS, HEAD_SIZE), jnp.bfloat16)

    def packed(part, side):
        return call(functools.partial(pack_kernel, side * heads_each, heads_each), wire, *part)

    def merged(block, part, side):
        return call(
            functools.partial(merge_kernel, side * heads_each, heads_each), wire, block, *part
        )

    flows = {}
    for side in range(2):
        for sign, route in ((1, down), (-1, up)):
            if (side == 0) == (sign == 1):
                block = packed(far, side)
                distance = half
            else:
                block = packed(partials[sign * (half - 1)], side)
                distance = half - 1
            while True:
                block = lax.ppermute(block, "store", route)
                distance -= 1
                if distance == 0:
                    break
                block = merged(block, partials[sign * distance], side)
            flows[sign, side] = block
    attended = call(
        functools.partial(final_kernel, heads_each, suffix),
        jax.ShapeDtypeStruct(queries.shape, queries.dtype),
        flows[1, 0], flows[1, 1], flows[-1, 0], flows[-1, 1], *partials[0],
    )
    arrived, arrived_slot = shifted((suffix_key_value, new_slots), "store", stores // 2)
    new_store = lax.dynamic_update_slice_in_dim(kv_pages, arrived, arrived_slot[0], 0)
    return (attended, new_store)


def on_device(queries, suffix_key_value, kv_pages, page_table, prefix_pages, new_slots):
    stores = lax.axis_size("store")
    pulled = page_table.shape[1] // stores * kv_pages[0].size
    pushed = 2 * queries[0].size
    arrays = (queries, suffix_key_value, kv_pages, page_table, prefix_pages, new_slots)
    if pulled >= pushed and stores % 2 == 0:
        return queries_travel(*arrays)
    return pages_travel(*arrays)


def solution(mesh):
    return jax.shard_map(
        on_device,
        mesh=mesh,
        in_specs=(
            P(("groups", "store"), None, "tensor"),
            P(("groups", "store"), None, None, "tensor"),
            P(("groups", "store"), None, None, "tensor"),
            P(("groups", "store"), None),
            P(("groups", "store")),
            P(("groups", "store")),
        ),
        out_specs=(
            P(("groups", "store"), None, "tensor"),
            P(("groups", "store"), None, None, "tensor"),
        ),
        check_vma=False,
    )
```

```python
import functools

import jax
import jax.numpy as jnp
from jax import lax
from jax.experimental import pallas as pl
from jax.experimental.pallas import tpu as pltpu
from jax.sharding import PartitionSpec as P

HEAD_SIZE = 128
LOG2E = 1.4426950408889634
DEAD = -1e30
FLOOR = -1e29
STAT_ROWS = 16
VMEM = pl.BlockSpec(memory_space=pltpu.VMEM)
SMEM = pl.BlockSpec(memory_space=pltpu.SMEM)
HBM = pl.BlockSpec(memory_space=pltpu.HBM)


def shifted(block, axis, distance):
    devices = range(lax.axis_size(axis))
    route = [((i - distance) % len(devices), i) for i in devices]
    return lax.ppermute(block, axis, route)


def block_update(state, head_count, key_rows, value_rows, live, scale):
    top_old, total_old, acc_old = state
    scores = (
        jnp.einsum("qhgd,khd->hgqk", head_count, key_rows, preferred_element_type=jnp.float32)
        * scale
    )
    scores = jnp.where(live, scores, -1e30)
    top_new = jnp.maximum(top_old, jnp.max(scores, axis=-1))
    weights = jnp.where(live, jnp.exp(scores - top_new[..., None]), 0.0)
    factor = jnp.exp(top_old - top_new)
    total_new = total_old * factor + jnp.sum(weights, axis=-1)
    product = jnp.einsum(
        "hgqk,khd->hgqd",
        weights.astype(jnp.bfloat16),
        value_rows,
        preferred_element_type=jnp.float32,
    )
    return (top_new, total_new, acc_old * factor[..., None] + product)


def pages_travel(queries, suffix_key_value, kv_pages, page_table, prefix_pages, new_slots):
    stores = lax.axis_size("store")
    pages_dev = kv_pages.shape[0]
    maxp = page_table.shape[1]
    cap = maxp // stores
    page_len = kv_pages.shape[2]
    width = kv_pages.shape[3]
    kv_heads = width // HEAD_SIZE
    suffix = queries.shape[1]
    groups_per_head = queries.shape[2] // width
    scale = HEAD_SIZE ** (-0.5)
    length = prefix_pages[0]
    table = page_table[0]
    owners = table // pages_dev
    local_ids = table % pages_dev
    entries = jnp.arange(maxp, dtype=jnp.int32)
    same_owner = (owners[:, None] == owners[None, :]) & (entries[:, None] < entries[None, :])
    ranks = jnp.sum(same_owner.astype(jnp.int32), axis=0)
    slots = owners * cap + ranks
    placed = slots[:, None] == entries[None, :]
    slot_entry = jnp.sum(jnp.where(placed, entries[:, None], 0), axis=0)
    wanted = jnp.sum(jnp.where(placed, local_ids[:, None], 0), axis=0)
    asked = lax.all_to_all(
        wanted.reshape(stores, cap), "store", split_axis=0, concat_axis=0, tiled=True
    )
    served = kv_pages[asked.reshape(-1)].reshape(stores, cap, 2, page_len, width)
    received = lax.all_to_all(served, "store", split_axis=0, concat_axis=0, tiled=True).reshape(
        maxp, 2, page_len, width
    )
    head_count = queries[0].reshape(suffix, kv_heads, groups_per_head, HEAD_SIZE)
    own_keys = suffix_key_value[0, 0].reshape(suffix, kv_heads, HEAD_SIZE)
    own_values = suffix_key_value[0, 1].reshape(suffix, kv_heads, HEAD_SIZE)
    rows = jnp.arange(suffix, dtype=jnp.int32)
    causal = rows[None, :] <= rows[:, None]
    start_state = (
        jnp.full((kv_heads, groups_per_head, suffix), -1e30, jnp.float32),
        jnp.zeros((kv_heads, groups_per_head, suffix), jnp.float32),
        jnp.zeros((kv_heads, groups_per_head, suffix, HEAD_SIZE), jnp.float32),
    )
    state = block_update(start_state, head_count, own_keys, own_values, causal, scale)
    block_pages = min(8, maxp)
    live_pages = slot_entry < length
    trips = maxp // block_pages

    def step_block(index, carry):
        first = index * block_pages
        block = lax.dynamic_slice_in_dim(received, first, block_pages, 0)
        alive = lax.dynamic_slice_in_dim(live_pages, first, block_pages, 0)
        alive = jnp.broadcast_to(alive[:, None], (block_pages, page_len)).reshape(
            1, block_pages * page_len
        )
        block_keys = block[:, 0].reshape(block_pages * page_len, kv_heads, HEAD_SIZE)
        block_values = block[:, 1].reshape(block_pages * page_len, kv_heads, HEAD_SIZE)
        return block_update(carry, head_count, block_keys, block_values, alive, scale)

    top_final, total_final, acc_final = lax.fori_loop(0, trips, step_block, state)
    output = acc_final / total_final[..., None]
    attended = (
        output.transpose(2, 0, 1, 3)
        .reshape(1, suffix, groups_per_head * width)
        .astype(jnp.bfloat16)
    )
    arrived, arrived_slot = shifted((suffix_key_value, new_slots), "store", stores // 2)
    new_store = lax.dynamic_update_slice_in_dim(kv_pages, arrived, arrived_slot[0], 0)
    return (attended, new_store)


def dot_nt(a, b):
    return lax.dot_general(a, b, (((1,), (1,)), ((), ())), preferred_element_type=jnp.float32)


def block_of(j):
    return slice(j * HEAD_SIZE, (j + 1) * HEAD_SIZE)


def iota(shape, dim):
    return lax.broadcasted_iota(jnp.int32, shape, dim)


def pack_stats(top, total):
    lane = iota((HEAD_SIZE, HEAD_SIZE), 1)
    row = iota((STAT_ROWS, HEAD_SIZE), 0)
    col = iota((STAT_ROWS, HEAD_SIZE), 1)
    tile = jnp.zeros((STAT_ROWS, HEAD_SIZE), jnp.float32)
    for j, (m, l) in enumerate(zip(top, total)):
        high = l.astype(jnp.bfloat16).astype(jnp.float32)
        low = l - high
        mixed = jnp.where(lane == 0, m, jnp.where(lane == 1, high, low)).astype(jnp.bfloat16)
        pick = ((row == col * 4 + j) & (col < 3)).astype(jnp.float32).astype(jnp.bfloat16)
        tile = tile + dot_nt(pick, mixed)
    return tile.astype(jnp.bfloat16)


def unpack_stats(tile):
    row = iota((STAT_ROWS, 8 * HEAD_SIZE), 0)
    block = iota((STAT_ROWS, 8 * HEAD_SIZE), 1) // HEAD_SIZE
    j = block // 2
    stat = block % 2
    spread = (
        ((row == j) & (stat == 0)) | ((row == j + 4) & (stat == 1)) | ((row == j + 8) & (stat == 1))
    )
    spread = spread.astype(jnp.float32).astype(jnp.bfloat16)
    turned = tile.astype(jnp.float32).T.astype(jnp.bfloat16)
    wide = jnp.dot(turned, spread, preferred_element_type=jnp.float32)
    part = lambda b: wide[:, b * HEAD_SIZE:(b + 1) * HEAD_SIZE]
    return [part(2 * j) for j in range(4)], [part(2 * j + 1) for j in range(4)]


def partial_rows(q, k, v, live, own, factor):
    s = dot_nt(q, k)
    s = jnp.where(live, s, DEAD)
    top = jnp.max(s, axis=-1, keepdims=True)
    if own is not None:
        k_own, v_own, causal = own
        s_own = jnp.where(causal, dot_nt(q, k_own), DEAD)
        top = jnp.maximum(top, jnp.max(s_own, axis=-1, keepdims=True))
    top = jnp.maximum(top * factor, FLOOR).astype(jnp.bfloat16).astype(jnp.float32)
    p = jnp.exp2(s * factor - top).astype(jnp.bfloat16)
    ones = jnp.ones((k.shape[0], HEAD_SIZE), jnp.bfloat16)
    out = jnp.dot(p, jnp.concatenate([v, ones], 1), preferred_element_type=jnp.float32)
    if own is not None:
        p = jnp.exp2(s_own * factor - top).astype(jnp.bfloat16)
        ones = jnp.ones((k_own.shape[0], HEAD_SIZE), jnp.bfloat16)
        out = out + jnp.dot(p, jnp.concatenate([v_own, ones], 1), preferred_element_type=jnp.float32)
    top = jnp.broadcast_to(top, (q.shape[0], HEAD_SIZE))
    return out[:, :HEAD_SIZE], top, out[:, HEAD_SIZE:]


def attend_kernel(sizes, parts, own, *refs):
    kv_heads, groups, suffix, cap, page_len = sizes
    refs = list(refs)
    meta = refs.pop(0)
    queries = [[refs.pop(0) for _ in range(n)] for n in parts]
    own_kv = refs.pop(0) if own else None
    pages = refs.pop(0)
    outs = [(refs.pop(0), refs.pop(0)) for _ in parts]
    stored = refs.pop(0) if own else None
    held, sems = refs[:2]
    copies = [
        [
            pltpu.make_async_copy(pages.at[meta[n, c]], held.at[n, c], sems.at[n, c])
            for c in range(cap)
        ]
        for n in range(len(parts))
    ]
    for request in copies:
        for copy in request:
            copy.start()
    if own:
        keep = pltpu.make_async_copy(pages, stored, refs[2])
        keep.start()
    factor = HEAD_SIZE ** (-0.5) * LOG2E
    keys = cap * page_len
    for n, halves in enumerate(queries):
        for copy in copies[n]:
            copy.wait()
        live = iota((1, keys), 1) < meta[n, cap] * page_len
        heads_each = kv_heads // len(halves)
        acc_ref, stat_ref = outs[n]
        for h in range(kv_heads):
            q_ref = halves[h // heads_each]
            first = (h % heads_each) * groups
            lanes = slice(h * HEAD_SIZE, (h + 1) * HEAD_SIZE)
            k = held[n, :, 0, :, lanes].reshape(keys, HEAD_SIZE)
            v = held[n, :, 1, :, lanes].reshape(keys, HEAD_SIZE)
            rows = groups * suffix
            q = jnp.concatenate([q_ref[:, block_of(first + g)] for g in range(groups)], 0)
            extra = None
            if own:
                at = iota((rows, suffix), 0) % suffix
                causal = iota((rows, suffix), 1) <= at
                extra = (own_kv[0, :, lanes], own_kv[1, :, lanes], causal)
            acc, top, total = partial_rows(q, k, v, live, extra, factor)
            acc_ref[h] = acc
            blocks = [block_of(j) for j in range(rows // HEAD_SIZE)]
            stat_ref[h] = pack_stats([top[j] for j in blocks], [total[j] for j in blocks])
    if own:
        keep.wait()


def attend(sizes, meta, queries, own_kv, kv_pages):
    kv_heads, groups, suffix, cap, page_len = sizes
    parts = [len(q) for q in queries]
    flat = [x for q in queries for x in q]
    own = own_kv is not None
    shapes = []
    rows = groups * suffix
    for _ in parts:
        shapes.append(jax.ShapeDtypeStruct((kv_heads, rows, HEAD_SIZE), jnp.float32))
        shapes.append(jax.ShapeDtypeStruct((kv_heads, STAT_ROWS, HEAD_SIZE), jnp.bfloat16))
    keys = cap * page_len
    count = len(parts)
    scratch = [
        pltpu.VMEM((count, cap) + kv_pages.shape[1:], jnp.bfloat16),
        pltpu.SemaphoreType.DMA((count, cap)),
    ]
    specs = [VMEM] * len(shapes)
    if own:
        shapes.append(jax.ShapeDtypeStruct(kv_pages.shape, kv_pages.dtype))
        specs.append(HBM)
        scratch.append(pltpu.SemaphoreType.DMA)
    out = pl.pallas_call(
        functools.partial(attend_kernel, sizes, parts, own),
        out_shape=shapes,
        in_specs=[SMEM] + [VMEM] * (len(flat) + own) + [HBM],
        out_specs=specs,
        scratch_shapes=scratch,
        compiler_params=pltpu.CompilerParams(vmem_limit_bytes=48 * 1024 * 1024),
        cost_estimate=pl.CostEstimate(
            flops=count * kv_heads * rows * keys * HEAD_SIZE * 8,
            bytes_accessed=count * kv_heads * (rows * 6 + keys * 4) * HEAD_SIZE,
            transcendentals=count * kv_heads * rows * keys,
        ),
    )(meta, *flat, *([own_kv] if own else []), kv_pages)
    return [(out[2 * n], out[2 * n + 1]) for n in range(count)] + list(out[2 * count:])


def place_kernel(half, column, me_ref, lists_ref, page_ref, old_ref, out_ref, sem):
    me = me_ref[0]
    from_below = (me >= half) == (me % 2 == 0)
    slot = jnp.where(from_below, lists_ref[0, column], lists_ref[1, column])
    copy = pltpu.make_async_copy(page_ref.at[0], out_ref.at[slot], sem)
    copy.start()
    copy.wait()


def place_page(half, column, me, lists, page, store):
    return pl.pallas_call(
        functools.partial(place_kernel, half, column),
        out_shape=jax.ShapeDtypeStruct(store.shape, store.dtype),
        in_specs=[SMEM, SMEM, VMEM, HBM],
        out_specs=HBM,
        scratch_shapes=[pltpu.SemaphoreType.DMA],
        input_output_aliases={3: 0},
        cost_estimate=pl.CostEstimate(flops=0, bytes_accessed=2 * page.size, transcendentals=0),
    )(me, lists, page, store)


def blend(parts):
    top = functools.reduce(jnp.maximum, [m for _, m, _ in parts])
    scales = [jnp.exp2(m - top) for _, m, _ in parts]
    acc = sum(a * f for (a, _, _), f in zip(parts, scales))
    total = sum(l * f for (_, _, l), f in zip(parts, scales))
    return acc, top, total


def pack_kernel(first, heads, acc_ref, stat_ref, out_ref):
    rows = acc_ref.shape[1]
    for h in range(heads):
        out_ref[h, :rows, :] = acc_ref[first + h].astype(jnp.bfloat16)
        out_ref[h, rows:, :] = stat_ref[first + h]


def merge_kernel(first, heads, in_ref, acc_ref, stat_ref, out_ref, out_stat_ref=None):
    rows = acc_ref.shape[1]
    for h in range(heads):
        in_top, in_total = unpack_stats(in_ref[h, rows:, :])
        my_top, my_total = unpack_stats(stat_ref[first + h])
        tops, totals = [], []
        for j in range(rows // HEAD_SIZE):
            acc, top, total = blend(
                [
                    (in_ref[h, block_of(j), :].astype(jnp.float32), in_top[j], in_total[j]),
                    (acc_ref[first + h, block_of(j), :], my_top[j], my_total[j]),
                ]
            )
            out_ref[h, block_of(j), :] = acc.astype(out_ref.dtype)
            tops.append(top)
            totals.append(total)
        if out_stat_ref is None:
            out_ref[h, rows:, :] = pack_stats(tops, totals)
        else:
            out_stat_ref[h] = pack_stats(tops, totals)


def final_kernel(suffix, *refs):
    sides, out_ref = (refs[0:3], refs[3:6]), refs[6]
    for side, (in_ref, acc_ref, stat_ref) in enumerate(sides):
        heads, rows = acc_ref.shape[:2]
        groups = rows // suffix
        for h in range(heads):
            in_top, in_total = unpack_stats(in_ref[h, rows:, :])
            my_top, my_total = unpack_stats(stat_ref[h])
            for j in range(rows // HEAD_SIZE):
                acc, _, total = blend(
                    [
                        (in_ref[h, block_of(j), :].astype(jnp.float32), in_top[j], in_total[j]),
                        (acc_ref[h, block_of(j), :], my_top[j], my_total[j]),
                    ]
                )
                out = (acc / total).astype(jnp.bfloat16)
                for i in range(HEAD_SIZE // suffix):
                    g = (side * heads + h) * groups + j * (HEAD_SIZE // suffix) + i
                    out_ref[0, :, block_of(g)] = out[i * suffix:(i + 1) * suffix]


def call(kernel, shape, *args):
    size = sum(a.size * a.dtype.itemsize for a in args)
    return pl.pallas_call(
        kernel,
        out_shape=shape,
        in_specs=[VMEM] * len(args),
        out_specs=[VMEM] * len(shape) if isinstance(shape, list) else VMEM,
        compiler_params=pltpu.CompilerParams(vmem_limit_bytes=48 * 1024 * 1024),
        cost_estimate=pl.CostEstimate(flops=size, bytes_accessed=2 * size, transcendentals=size // 8),
    )(*args)


def queries_travel(queries, suffix_key_value, kv_pages, page_table, prefix_pages, new_slots):
    stores = lax.axis_size("store")
    pages_dev, _, page_len, width = kv_pages.shape
    maxp = page_table.shape[1]
    cap = maxp // stores
    kv_heads = width // HEAD_SIZE
    suffix = queries.shape[1]
    groups = queries.shape[2] // width
    sizes = (kv_heads, groups, suffix, cap, page_len)
    half = stores // 2
    me = lax.axis_index("store")

    order = list(range(0, stores, 2)) + list(range(1, stores, 2))[::-1]
    up = [(order[i], order[(i + 1) % stores]) for i in range(stores)]
    down = [(order[i], order[i - 1]) for i in range(stores)]

    table, length = page_table[0], prefix_pages[0]
    entries = jnp.arange(maxp, dtype=jnp.int32)
    owners = table // pages_dev
    before = (owners[:, None] == owners[None, :]) & (entries[:, None] < entries[None, :])
    rank = jnp.sum(before.astype(jnp.int32), 0)
    place = jnp.arange(HEAD_SIZE, dtype=jnp.int32)
    field = jnp.where(place[:, None] < cap, rank[None, :] == place[:, None], place[:, None] == cap)
    value = jnp.where(
        place[:, None] < cap, (table % pages_dev)[None], (entries < length).astype(jnp.int32)[None]
    )
    owned = owners[None, :] == jnp.arange(suffix, dtype=jnp.int32)[:, None]
    lists = jnp.sum(jnp.where(owned[:, None, :] & field[None], value[None], 0), -1)
    lists = jnp.where(place[None, :] == cap + 1, new_slots[0], lists)

    heads_each = kv_heads // 2
    cut = heads_each * groups * HEAD_SIZE
    mine = [
        jnp.concatenate([queries[0, :, :cut], lists.astype(queries.dtype)], 1),
        queries[0, :, cut:],
    ]

    def listed(*arrays):
        rows = [lax.dynamic_slice(x, (me, cut), (1, HEAD_SIZE)) for x in arrays]
        return jnp.concatenate(rows).astype(jnp.int32)

    def after(values, token):
        return lax.optimization_barrier((values, token))

    ups, downs = list(mine), list(mine)
    partials, lists_of = {}, {}
    for step in range(1, half):
        ups = [lax.ppermute(x, "store", up) for x in ups]
        downs = [lax.ppermute(x, "store", down) for x in downs]
        if step == 1:
            partials[0], store = attend(
                sizes,
                lax.dynamic_slice(lists, (me, 0), (1, HEAD_SIZE)),
                [[queries[0]]],
                suffix_key_value[0],
                kv_pages,
            )
            (ups, downs), partials[0] = after((ups, downs), partials[0])
        else:
            (ups, downs), (partials[step - 1], partials[1 - step]) = after(
                (ups, downs), (partials[step - 1], partials[1 - step])
            )
        lists_of[step] = listed(ups[0], downs[0])
        got = attend(sizes, lists_of[step], [ups, downs], None, kv_pages)
        partials[step], partials[-step] = got
    ups[0] = lax.ppermute(ups[0], "store", up)
    downs[1] = lax.ppermute(downs[1], "store", down)
    (ups, downs), (partials[half - 1], partials[1 - half]) = after(
        (ups, downs), (partials[half - 1], partials[1 - half])
    )
    (far,) = attend(sizes, listed(ups[0]), [[ups[0], downs[1]]], None, kv_pages)

    rows_head = groups * suffix
    wire = jax.ShapeDtypeStruct((heads_each, rows_head + STAT_ROWS, HEAD_SIZE), jnp.bfloat16)

    def packed(part, side):
        return call(functools.partial(pack_kernel, side * heads_each, heads_each), wire, *part)

    def merged(block, part, side):
        return call(
            functools.partial(merge_kernel, side * heads_each, heads_each), wire, block, *part
        )

    late, early = {}, {}
    blocks = {}
    for side, sign in ((0, 1), (1, -1)):
        blocks[side, sign] = packed(far, side), half
        blocks[1 - side, sign] = packed(partials[sign * (half - 1)], 1 - side), half - 1
    for (side, sign), (block, distance) in blocks.items():
        route = down if sign == 1 else up
        first = distance
        while True:
            block = lax.ppermute(block, "store", route)
            distance -= 1
            if distance == 0:
                break
            block = merged(block, partials[sign * distance], side)
        (late if first == half else early)[side] = block
    kept = [
        jax.ShapeDtypeStruct((heads_each, rows_head, HEAD_SIZE), jnp.float32),
        jax.ShapeDtypeStruct((heads_each, STAT_ROWS, HEAD_SIZE), jnp.bfloat16),
    ]
    rest = [
        call(
            functools.partial(merge_kernel, side * heads_each, heads_each),
            kept, early[side], *partials[0],
        )
        for side in range(2)
    ]
    attended = call(
        functools.partial(final_kernel, suffix),
        jax.ShapeDtypeStruct(queries.shape, queries.dtype),
        late[0], *rest[0], late[1], *rest[1],
    )

    page, _ = after(suffix_key_value, partials[half - 1])
    arrived = shifted(page, "store", half)
    new_store = place_page(half, cap + 1, me[None], lists_of[stores // 4], arrived, store)
    return (attended, new_store)


def on_device(queries, suffix_key_value, kv_pages, page_table, prefix_pages, new_slots):
    stores = lax.axis_size("store")
    pulled = page_table.shape[1] // stores * kv_pages[0].size
    pushed = 2 * queries[0].size
    arrays = (queries, suffix_key_value, kv_pages, page_table, prefix_pages, new_slots)
    if pulled >= pushed and stores % 4 == 0:
        return queries_travel(*arrays)
    return pages_travel(*arrays)


def solution(mesh):
    return jax.shard_map(
        on_device,
        mesh=mesh,
        in_specs=(
            P(("groups", "store"), None, "tensor"),
            P(("groups", "store"), None, None, "tensor"),
            P(("groups", "store"), None, None, "tensor"),
            P(("groups", "store"), None),
            P(("groups", "store")),
            P(("groups", "store")),
        ),
        out_specs=(
            P(("groups", "store"), None, "tensor"),
            P(("groups", "store"), None, None, "tensor"),
        ),
        check_vma=False,
    )
```

```python
import functools

import jax
import jax.numpy as jnp
from jax import lax
from jax.experimental import pallas as pl
from jax.experimental.pallas import tpu as pltpu
from jax.sharding import PartitionSpec as P

HEAD_SIZE = 128
LOG2E = 1.4426950408889634
DEAD = -1e30
FLOOR = -1e29
STAT_ROWS = 16
VMEM = pl.BlockSpec(memory_space=pltpu.VMEM)
SMEM = pl.BlockSpec(memory_space=pltpu.SMEM)
HBM = pl.BlockSpec(memory_space=pltpu.HBM)


def shifted(block, axis, distance):
    devices = range(lax.axis_size(axis))
    route = [((i - distance) % len(devices), i) for i in devices]
    return lax.ppermute(block, axis, route)


def block_update(state, head_count, key_rows, value_rows, live, scale):
    top_old, total_old, acc_old = state
    scores = (
        jnp.einsum("qhgd,khd->hgqk", head_count, key_rows, preferred_element_type=jnp.float32)
        * scale
    )
    scores = jnp.where(live, scores, -1e30)
    top_new = jnp.maximum(top_old, jnp.max(scores, axis=-1))
    weights = jnp.where(live, jnp.exp(scores - top_new[..., None]), 0.0)
    factor = jnp.exp(top_old - top_new)
    total_new = total_old * factor + jnp.sum(weights, axis=-1)
    product = jnp.einsum(
        "hgqk,khd->hgqd",
        weights.astype(jnp.bfloat16),
        value_rows,
        preferred_element_type=jnp.float32,
    )
    return (top_new, total_new, acc_old * factor[..., None] + product)


def pages_travel(queries, suffix_key_value, kv_pages, page_table, prefix_pages, new_slots):
    stores = lax.axis_size("store")
    pages_dev = kv_pages.shape[0]
    maxp = page_table.shape[1]
    cap = maxp // stores
    page_len = kv_pages.shape[2]
    width = kv_pages.shape[3]
    kv_heads = width // HEAD_SIZE
    suffix = queries.shape[1]
    groups_per_head = queries.shape[2] // width
    scale = HEAD_SIZE ** (-0.5)
    length = prefix_pages[0]
    table = page_table[0]
    owners = table // pages_dev
    local_ids = table % pages_dev
    entries = jnp.arange(maxp, dtype=jnp.int32)
    same_owner = (owners[:, None] == owners[None, :]) & (entries[:, None] < entries[None, :])
    ranks = jnp.sum(same_owner.astype(jnp.int32), axis=0)
    slots = owners * cap + ranks
    placed = slots[:, None] == entries[None, :]
    slot_entry = jnp.sum(jnp.where(placed, entries[:, None], 0), axis=0)
    wanted = jnp.sum(jnp.where(placed, local_ids[:, None], 0), axis=0)
    asked = lax.all_to_all(
        wanted.reshape(stores, cap), "store", split_axis=0, concat_axis=0, tiled=True
    )
    served = kv_pages[asked.reshape(-1)].reshape(stores, cap, 2, page_len, width)
    received = lax.all_to_all(served, "store", split_axis=0, concat_axis=0, tiled=True).reshape(
        maxp, 2, page_len, width
    )
    head_count = queries[0].reshape(suffix, kv_heads, groups_per_head, HEAD_SIZE)
    own_keys = suffix_key_value[0, 0].reshape(suffix, kv_heads, HEAD_SIZE)
    own_values = suffix_key_value[0, 1].reshape(suffix, kv_heads, HEAD_SIZE)
    rows = jnp.arange(suffix, dtype=jnp.int32)
    causal = rows[None, :] <= rows[:, None]
    start_state = (
        jnp.full((kv_heads, groups_per_head, suffix), -1e30, jnp.float32),
        jnp.zeros((kv_heads, groups_per_head, suffix), jnp.float32),
        jnp.zeros((kv_heads, groups_per_head, suffix, HEAD_SIZE), jnp.float32),
    )
    state = block_update(start_state, head_count, own_keys, own_values, causal, scale)
    block_pages = min(8, maxp)
    live_pages = slot_entry < length
    trips = maxp // block_pages

    def step_block(index, carry):
        first = index * block_pages
        block = lax.dynamic_slice_in_dim(received, first, block_pages, 0)
        alive = lax.dynamic_slice_in_dim(live_pages, first, block_pages, 0)
        alive = jnp.broadcast_to(alive[:, None], (block_pages, page_len)).reshape(
            1, block_pages * page_len
        )
        block_keys = block[:, 0].reshape(block_pages * page_len, kv_heads, HEAD_SIZE)
        block_values = block[:, 1].reshape(block_pages * page_len, kv_heads, HEAD_SIZE)
        return block_update(carry, head_count, block_keys, block_values, alive, scale)

    top_final, total_final, acc_final = lax.fori_loop(0, trips, step_block, state)
    output = acc_final / total_final[..., None]
    attended = (
        output.transpose(2, 0, 1, 3)
        .reshape(1, suffix, groups_per_head * width)
        .astype(jnp.bfloat16)
    )
    arrived, arrived_slot = shifted((suffix_key_value, new_slots), "store", stores // 2)
    new_store = lax.dynamic_update_slice_in_dim(kv_pages, arrived, arrived_slot[0], 0)
    return (attended, new_store)


def dot_nt(a, b):
    return lax.dot_general(a, b, (((1,), (1,)), ((), ())), preferred_element_type=jnp.float32)


def block_of(j):
    return slice(j * HEAD_SIZE, (j + 1) * HEAD_SIZE)


def iota(shape, dim):
    return lax.broadcasted_iota(jnp.int32, shape, dim)


def pack_stats(top, total):
    diagonal = iota((HEAD_SIZE, HEAD_SIZE), 0) == iota((HEAD_SIZE, HEAD_SIZE), 1)
    row = iota((STAT_ROWS, HEAD_SIZE), 0)
    tile = jnp.zeros((STAT_ROWS, HEAD_SIZE), jnp.float32)

    def along(x):
        return jnp.sum(jnp.where(diagonal, x, 0.0), 0, keepdims=True)

    for j, (m, l) in enumerate(zip(top, total)):
        l = along(l)
        high = l.astype(jnp.bfloat16).astype(jnp.float32)
        for t, x in enumerate((along(m), high, l - high)):
            tile = jnp.where(row == 4 * t + j, x, tile)
    return tile.astype(jnp.bfloat16)


def unpack_stats(tile):
    row = iota((STAT_ROWS, 8 * HEAD_SIZE), 0)
    block = iota((STAT_ROWS, 8 * HEAD_SIZE), 1) // HEAD_SIZE
    j = block // 2
    stat = block % 2
    spread = (
        ((row == j) & (stat == 0)) | ((row == j + 4) & (stat == 1)) | ((row == j + 8) & (stat == 1))
    )
    spread = spread.astype(jnp.float32).astype(jnp.bfloat16)
    turned = tile.astype(jnp.float32).T.astype(jnp.bfloat16)
    wide = jnp.dot(turned, spread, preferred_element_type=jnp.float32)
    part = lambda b: wide[:, b * HEAD_SIZE:(b + 1) * HEAD_SIZE]
    return [part(2 * j) for j in range(4)], [part(2 * j + 1) for j in range(4)]


def attend_kernel(sizes, parts, own, *refs):
    kv_heads, groups, suffix, cap, page_len = sizes
    refs = list(refs)
    meta = refs.pop(0)
    queries = [[refs.pop(0) for _ in range(n)] for n in parts]
    own_kv = refs.pop(0) if own else None
    pages = refs.pop(0)
    outs = [(refs.pop(0), refs.pop(0)) for _ in parts]
    stored = refs.pop(0) if own else None
    held, sems, scores = refs[:3]
    if own:
        late_scores, store_sem = refs[3:]
    copies = [
        [
            pltpu.make_async_copy(pages.at[meta[n, c]], held.at[n, c], sems.at[n, c])
            for c in range(cap)
        ]
        for n in range(len(parts))
    ]
    for request in copies:
        for copy in request:
            copy.start()
    if own:
        keep = pltpu.make_async_copy(pages, stored, store_sem)
        keep.start()
    factor = HEAD_SIZE ** (-0.5) * LOG2E
    keys = cap * page_len
    rows = groups * suffix
    jobs = [(n, h) for n in range(len(parts)) for h in range(kv_heads)]

    def lanes(h):
        return slice(h * HEAD_SIZE, (h + 1) * HEAD_SIZE)

    def score(i):
        n, h = jobs[i]
        if h == 0:
            for copy in copies[n]:
                copy.wait()
        heads_each = kv_heads // len(queries[n])
        q_ref, first = queries[n][h // heads_each], (h % heads_each) * groups
        q = jnp.concatenate([q_ref[:, block_of(first + g)] for g in range(groups)], 0)
        k = held[n, :, 0, :, lanes(h)].reshape(keys, HEAD_SIZE)
        scores[i % 2, :, :keys] = dot_nt(q, k)
        if own:
            at = iota((rows, suffix), 0) % suffix
            causal = iota((rows, suffix), 1) <= at
            late_scores[i % 2] = jnp.where(causal, dot_nt(q, own_kv[0, :, lanes(h)]), DEAD)

    def weigh(i):
        n, h = jobs[i]
        live = iota((1, keys), 1) < meta[n, cap] * page_len
        s = jnp.where(live, scores[i % 2], DEAD)
        top = jnp.max(s, axis=-1, keepdims=True)
        if own:
            top = jnp.maximum(top, jnp.max(late_scores[i % 2], axis=-1, keepdims=True))
        top = jnp.maximum(top * factor, FLOOR).astype(jnp.bfloat16).astype(jnp.float32)
        p = jnp.exp2(s * factor - top).astype(jnp.bfloat16)
        v = held[n, :, 1, :, lanes(h)].reshape(keys, HEAD_SIZE)
        v = jnp.concatenate([v, jnp.ones_like(v)], 1)
        out = jnp.dot(p, v, preferred_element_type=jnp.float32)
        if own:
            p = jnp.exp2(late_scores[i % 2] * factor - top).astype(jnp.bfloat16)
            v = own_kv[1, :, lanes(h)]
            v = jnp.concatenate([v, jnp.ones_like(v)], 1)
            out = out + jnp.dot(p, v, preferred_element_type=jnp.float32)
        acc_ref, stat_ref = outs[n]
        acc_ref[h] = out[:, :HEAD_SIZE]
        total = out[:, HEAD_SIZE:]
        top = jnp.broadcast_to(top, total.shape)
        blocks = [block_of(j) for j in range(rows // HEAD_SIZE)]
        stat_ref[h] = pack_stats([top[j] for j in blocks], [total[j] for j in blocks])

    for i in range(len(jobs) + 1):
        if i < len(jobs):
            score(i)
        if i > 0:
            weigh(i - 1)
    if own:
        keep.wait()


def attend(sizes, meta, queries, own_kv, kv_pages):
    kv_heads, groups, suffix, cap, page_len = sizes
    parts = [len(q) for q in queries]
    flat = [x for q in queries for x in q]
    own = own_kv is not None
    shapes = []
    rows = groups * suffix
    for _ in parts:
        shapes.append(jax.ShapeDtypeStruct((kv_heads, rows, HEAD_SIZE), jnp.float32))
        shapes.append(jax.ShapeDtypeStruct((kv_heads, STAT_ROWS, HEAD_SIZE), jnp.bfloat16))
    keys = cap * page_len
    count = len(parts)
    scratch = [
        pltpu.VMEM((count, cap) + kv_pages.shape[1:], jnp.bfloat16),
        pltpu.SemaphoreType.DMA((count, cap)),
        pltpu.VMEM((2, rows, keys), jnp.float32),
    ]
    specs = [VMEM] * len(shapes)
    if own:
        shapes.append(jax.ShapeDtypeStruct(kv_pages.shape, kv_pages.dtype))
        specs.append(HBM)
        scratch.append(pltpu.VMEM((2, rows, suffix), jnp.float32))
        scratch.append(pltpu.SemaphoreType.DMA)
    out = pl.pallas_call(
        functools.partial(attend_kernel, sizes, parts, own),
        out_shape=shapes,
        in_specs=[SMEM] + [VMEM] * (len(flat) + own) + [HBM],
        out_specs=specs,
        scratch_shapes=scratch,
        compiler_params=pltpu.CompilerParams(vmem_limit_bytes=48 * 1024 * 1024),
        cost_estimate=pl.CostEstimate(
            flops=count * kv_heads * rows * keys * HEAD_SIZE * 8,
            bytes_accessed=count * kv_heads * (rows * 6 + keys * 4) * HEAD_SIZE,
            transcendentals=count * kv_heads * rows * keys,
        ),
    )(meta, *flat, *([own_kv] if own else []), kv_pages)
    return [(out[2 * n], out[2 * n + 1]) for n in range(count)] + list(out[2 * count:])


def place_kernel(half, column, me_ref, lists_ref, page_ref, old_ref, out_ref, sem):
    me = me_ref[0]
    from_below = (me >= half) == (me % 2 == 0)
    slot = jnp.where(from_below, lists_ref[0, column], lists_ref[1, column])
    copy = pltpu.make_async_copy(page_ref.at[0], out_ref.at[slot], sem)
    copy.start()
    copy.wait()


def place_page(half, column, me, lists, page, store):
    return pl.pallas_call(
        functools.partial(place_kernel, half, column),
        out_shape=jax.ShapeDtypeStruct(store.shape, store.dtype),
        in_specs=[SMEM, SMEM, VMEM, HBM],
        out_specs=HBM,
        scratch_shapes=[pltpu.SemaphoreType.DMA],
        input_output_aliases={3: 0},
        cost_estimate=pl.CostEstimate(flops=0, bytes_accessed=2 * page.size, transcendentals=0),
    )(me, lists, page, store)


def blend(parts):
    top = functools.reduce(jnp.maximum, [m for _, m, _ in parts])
    scales = [jnp.exp2(m - top) for _, m, _ in parts]
    acc = sum(a * f for (a, _, _), f in zip(parts, scales))
    total = sum(l * f for (_, _, l), f in zip(parts, scales))
    return acc, top, total


def pack_kernel(first, heads, acc_ref, stat_ref, out_ref):
    rows = acc_ref.shape[1]
    for h in range(heads):
        out_ref[h, :rows, :] = acc_ref[first + h].astype(jnp.bfloat16)
        out_ref[h, rows:, :] = stat_ref[first + h]


def merge_kernel(first, heads, in_ref, acc_ref, stat_ref, out_ref, out_stat_ref=None):
    rows = acc_ref.shape[1]
    for h in range(heads):
        in_top, in_total = unpack_stats(in_ref[h, rows:, :])
        my_top, my_total = unpack_stats(stat_ref[first + h])
        tops, totals = [], []
        for j in range(rows // HEAD_SIZE):
            acc, top, total = blend(
                [
                    (in_ref[h, block_of(j), :].astype(jnp.float32), in_top[j], in_total[j]),
                    (acc_ref[first + h, block_of(j), :], my_top[j], my_total[j]),
                ]
            )
            out_ref[h, block_of(j), :] = acc.astype(out_ref.dtype)
            tops.append(top)
            totals.append(total)
        if out_stat_ref is None:
            out_ref[h, rows:, :] = pack_stats(tops, totals)
        else:
            out_stat_ref[h] = pack_stats(tops, totals)


def final_kernel(suffix, *refs):
    sides, out_ref = (refs[0:3], refs[3:6]), refs[6]
    for side, (in_ref, acc_ref, stat_ref) in enumerate(sides):
        heads, rows = acc_ref.shape[:2]
        groups = rows // suffix
        for h in range(heads):
            in_top, in_total = unpack_stats(in_ref[h, rows:, :])
            my_top, my_total = unpack_stats(stat_ref[h])
            for j in range(rows // HEAD_SIZE):
                acc, _, total = blend(
                    [
                        (in_ref[h, block_of(j), :].astype(jnp.float32), in_top[j], in_total[j]),
                        (acc_ref[h, block_of(j), :], my_top[j], my_total[j]),
                    ]
                )
                out = (acc / total).astype(jnp.bfloat16)
                for i in range(HEAD_SIZE // suffix):
                    g = (side * heads + h) * groups + j * (HEAD_SIZE // suffix) + i
                    out_ref[0, :, block_of(g)] = out[i * suffix:(i + 1) * suffix]


def call(kernel, shape, *args):
    size = sum(a.size * a.dtype.itemsize for a in args)
    return pl.pallas_call(
        kernel,
        out_shape=shape,
        in_specs=[VMEM] * len(args),
        out_specs=[VMEM] * len(shape) if isinstance(shape, list) else VMEM,
        compiler_params=pltpu.CompilerParams(vmem_limit_bytes=48 * 1024 * 1024),
        cost_estimate=pl.CostEstimate(flops=size, bytes_accessed=2 * size, transcendentals=size // 8),
    )(*args)


def prepare_kernel(cut, cap, pages_dev, length_ref, slot_ref, table_ref, q_ref, first_ref, second_ref):
    maxp = table_ref.shape[1]
    suffix = q_ref.shape[1]
    second_ref[...] = q_ref[0, :, cut:]
    first_ref[:, :cut] = q_ref[0, :, :cut]
    table = table_ref[...]
    owner = lax.div(table, pages_dev)
    local = (table - owner * pages_dev).astype(jnp.float32)
    owner = owner.astype(jnp.float32)
    down, along = iota((maxp, maxp), 0), iota((maxp, maxp), 1)

    def turned(x):
        return jnp.sum(jnp.where(down == along, x, 0.0), 1, keepdims=True)

    before = (turned(owner) == owner) & (along < down)
    rank = jnp.sum(jnp.where(before, 1.0, 0.0), 1, keepdims=True)
    place = iota((maxp, HEAD_SIZE), 1)
    live = jnp.where(iota((maxp, HEAD_SIZE), 0) < length_ref[0], 1.0, 0.0)
    ids = jnp.where(rank == place.astype(jnp.float32), turned(local), 0.0)
    fields = jnp.where(place < cap, ids, jnp.where(place == cap, live, 0.0))
    owned = jnp.where(owner == iota((suffix, maxp), 0).astype(jnp.float32), 1.0, 0.0)
    lists = jnp.dot(
        owned.astype(jnp.bfloat16), fields.astype(jnp.bfloat16), preferred_element_type=jnp.float32
    )
    slot = slot_ref[0].astype(jnp.float32)
    lists = jnp.where(iota(lists.shape, 1) == cap + 1, slot, lists)
    first_ref[:, cut:] = lists.astype(jnp.bfloat16)


def prepare(cut, cap, pages_dev, queries, page_table, prefix_pages, new_slots):
    suffix, columns = queries.shape[1:]
    return pl.pallas_call(
        functools.partial(prepare_kernel, cut, cap, pages_dev),
        out_shape=[
            jax.ShapeDtypeStruct((suffix, cut + HEAD_SIZE), queries.dtype),
            jax.ShapeDtypeStruct((suffix, columns - cut), queries.dtype),
        ],
        in_specs=[SMEM, SMEM, VMEM, VMEM],
        out_specs=[VMEM, VMEM],
    )(prefix_pages, new_slots, page_table, queries)


def queries_travel(queries, suffix_key_value, kv_pages, page_table, prefix_pages, new_slots):
    stores = lax.axis_size("store")
    pages_dev, _, page_len, width = kv_pages.shape
    maxp = page_table.shape[1]
    cap = maxp // stores
    kv_heads = width // HEAD_SIZE
    suffix = queries.shape[1]
    groups = queries.shape[2] // width
    sizes = (kv_heads, groups, suffix, cap, page_len)
    half = stores // 2
    me = lax.axis_index("store")

    order = list(range(0, stores, 2)) + list(range(1, stores, 2))[::-1]
    up = [(order[i], order[(i + 1) % stores]) for i in range(stores)]
    down = [(order[i], order[i - 1]) for i in range(stores)]

    heads_each = kv_heads // 2
    cut = heads_each * groups * HEAD_SIZE
    mine = prepare(cut, cap, pages_dev, queries, page_table, prefix_pages, new_slots)

    def listed(*arrays):
        rows = [lax.dynamic_slice(x, (me, cut), (1, HEAD_SIZE)) for x in arrays]
        return jnp.concatenate(rows).astype(jnp.int32)

    def after(values, token):
        return lax.optimization_barrier((values, token))

    ups, downs = list(mine), list(mine)
    partials, lists_of = {}, {}
    for step in range(1, half):
        ups = [lax.ppermute(x, "store", up) for x in ups]
        downs = [lax.ppermute(x, "store", down) for x in downs]
        if step == 1:
            partials[0], store = attend(
                sizes,
                listed(mine[0]),
                [mine],
                suffix_key_value[0],
                kv_pages,
            )
            (ups, downs), partials[0] = after((ups, downs), partials[0])
        else:
            (ups, downs), (partials[step - 1], partials[1 - step]) = after(
                (ups, downs), (partials[step - 1], partials[1 - step])
            )
        lists_of[step] = listed(ups[0], downs[0])
        got = attend(sizes, lists_of[step], [ups, downs], None, kv_pages)
        partials[step], partials[-step] = got
    ups[0] = lax.ppermute(ups[0], "store", up)
    downs[1] = lax.ppermute(downs[1], "store", down)

    rows_head = groups * suffix
    wire = jax.ShapeDtypeStruct((heads_each, rows_head + STAT_ROWS, HEAD_SIZE), jnp.bfloat16)

    def packed(part, side):
        return call(functools.partial(pack_kernel, side * heads_each, heads_each), wire, *part)

    def merged(block, part, side):
        return call(
            functools.partial(merge_kernel, side * heads_each, heads_each), wire, block, *part
        )

    routes = {1: down, -1: up}
    nearer = {sign: packed(partials[sign * (half - 1)], side) for side, sign in ((1, 1), (0, -1))}
    hop = {sign: lax.ppermute(block, "store", routes[sign]) for sign, block in nearer.items()}
    page, _ = after(suffix_key_value, partials[half - 2])
    arrived = shifted(page, "store", half)
    (ups, downs), (_, arrived) = after((ups, downs), (nearer, arrived))
    (far,) = attend(sizes, listed(ups[0]), [[ups[0], downs[1]]], None, kv_pages)
    store = place_page(half, cap + 1, me[None], lists_of[stores // 4], arrived, store)

    side_of = {1: {"late": 0, "early": 1}, -1: {"late": 1, "early": 0}}
    turns = [("early", half - 1)]
    for distance in range(half, 0, -1):
        turns += [("late", distance)] + [("early", distance - 2)] * (distance > 2)
    flows = {("early", sign): hop[sign] for sign in routes}
    sent = None
    for flow, distance in turns[1:]:
        blocks = {}
        if flow == "late" and distance == half:
            far, hop = after(far, hop)
            for sign in routes:
                flows["early", sign] = hop[sign]
                blocks[sign] = packed(far, side_of[sign][flow])
        else:
            came = {sign: flows[flow, sign] for sign in routes}
            if distance == 1:
                ended = {sign: flows["early", sign] for sign in routes}
                came, ended = after(came, ended)
                flows.update({("early", sign): ended[sign] for sign in routes})
            came, _ = after(came, sent)
            for sign in routes:
                blocks[sign] = merged(
                    came[sign], partials[sign * distance], side_of[sign][flow]
                )
        for sign in routes:
            flows[flow, sign] = lax.ppermute(blocks[sign], "store", routes[sign])
        sent = blocks
    late = {side_of[sign]["late"]: flows["late", sign] for sign in routes}
    early, _ = after({side_of[sign]["early"]: flows["early", sign] for sign in routes}, sent)
    kept = [
        jax.ShapeDtypeStruct((heads_each, rows_head, HEAD_SIZE), jnp.float32),
        jax.ShapeDtypeStruct((heads_each, STAT_ROWS, HEAD_SIZE), jnp.bfloat16),
    ]
    rest = [
        call(
            functools.partial(merge_kernel, side * heads_each, heads_each),
            kept, early[side], *partials[0],
        )
        for side in range(2)
    ]
    attended = call(
        functools.partial(final_kernel, suffix),
        jax.ShapeDtypeStruct(queries.shape, queries.dtype),
        late[0], *rest[0], late[1], *rest[1],
    )

    return (attended, store)


def on_device(queries, suffix_key_value, kv_pages, page_table, prefix_pages, new_slots):
    stores = lax.axis_size("store")
    pulled = page_table.shape[1] // stores * kv_pages[0].size
    pushed = 2 * queries[0].size
    arrays = (queries, suffix_key_value, kv_pages, page_table, prefix_pages, new_slots)
    if pulled >= pushed and stores % 4 == 0:
        return queries_travel(*arrays)
    return pages_travel(*arrays)


def solution(mesh):
    return jax.shard_map(
        on_device,
        mesh=mesh,
        in_specs=(
            P(("groups", "store"), None, "tensor"),
            P(("groups", "store"), None, None, "tensor"),
            P(("groups", "store"), None, None, "tensor"),
            P(("groups", "store"), None),
            P(("groups", "store")),
            P(("groups", "store")),
        ),
        out_specs=(
            P(("groups", "store"), None, "tensor"),
            P(("groups", "store"), None, None, "tensor"),
        ),
        check_vma=False,
    )
```

```python
import functools

import jax
import jax.numpy as jnp
from jax import lax
from jax.experimental import pallas as pl
from jax.experimental.pallas import tpu as pltpu
from jax.sharding import PartitionSpec as P

HEAD_SIZE = 128
LOG2E = 1.4426950408889634
DEAD = -1e30
FLOOR = -1e29
STAT_ROWS = 16
LIGHT = pl.CostEstimate(flops=1, bytes_accessed=1, transcendentals=0)
VMEM = pl.BlockSpec(memory_space=pltpu.VMEM)
SMEM = pl.BlockSpec(memory_space=pltpu.SMEM)
HBM = pl.BlockSpec(memory_space=pltpu.HBM)


def shifted(block, axis, distance):
    devices = range(lax.axis_size(axis))
    route = [((i - distance) % len(devices), i) for i in devices]
    return lax.ppermute(block, axis, route)


def block_update(state, head_count, key_rows, value_rows, live, scale):
    top_old, total_old, acc_old = state
    scores = (
        jnp.einsum("qhgd,khd->hgqk", head_count, key_rows, preferred_element_type=jnp.float32)
        * scale
    )
    scores = jnp.where(live, scores, -1e30)
    top_new = jnp.maximum(top_old, jnp.max(scores, axis=-1))
    weights = jnp.where(live, jnp.exp(scores - top_new[..., None]), 0.0)
    factor = jnp.exp(top_old - top_new)
    total_new = total_old * factor + jnp.sum(weights, axis=-1)
    product = jnp.einsum(
        "hgqk,khd->hgqd",
        weights.astype(jnp.bfloat16),
        value_rows,
        preferred_element_type=jnp.float32,
    )
    return (top_new, total_new, acc_old * factor[..., None] + product)


def pages_travel(queries, suffix_key_value, kv_pages, page_table, prefix_pages, new_slots):
    stores = lax.axis_size("store")
    pages_dev = kv_pages.shape[0]
    maxp = page_table.shape[1]
    cap = maxp // stores
    page_len = kv_pages.shape[2]
    width = kv_pages.shape[3]
    kv_heads = width // HEAD_SIZE
    suffix = queries.shape[1]
    groups_per_head = queries.shape[2] // width
    scale = HEAD_SIZE ** (-0.5)
    length = prefix_pages[0]
    table = page_table[0]
    owners = table // pages_dev
    local_ids = table % pages_dev
    entries = jnp.arange(maxp, dtype=jnp.int32)
    same_owner = (owners[:, None] == owners[None, :]) & (entries[:, None] < entries[None, :])
    ranks = jnp.sum(same_owner.astype(jnp.int32), axis=0)
    slots = owners * cap + ranks
    placed = slots[:, None] == entries[None, :]
    slot_entry = jnp.sum(jnp.where(placed, entries[:, None], 0), axis=0)
    wanted = jnp.sum(jnp.where(placed, local_ids[:, None], 0), axis=0)
    asked = lax.all_to_all(
        wanted.reshape(stores, cap), "store", split_axis=0, concat_axis=0, tiled=True
    )
    served = kv_pages[asked.reshape(-1)].reshape(stores, cap, 2, page_len, width)
    received = lax.all_to_all(served, "store", split_axis=0, concat_axis=0, tiled=True).reshape(
        maxp, 2, page_len, width
    )
    head_count = queries[0].reshape(suffix, kv_heads, groups_per_head, HEAD_SIZE)
    own_keys = suffix_key_value[0, 0].reshape(suffix, kv_heads, HEAD_SIZE)
    own_values = suffix_key_value[0, 1].reshape(suffix, kv_heads, HEAD_SIZE)
    rows = jnp.arange(suffix, dtype=jnp.int32)
    causal = rows[None, :] <= rows[:, None]
    start_state = (
        jnp.full((kv_heads, groups_per_head, suffix), -1e30, jnp.float32),
        jnp.zeros((kv_heads, groups_per_head, suffix), jnp.float32),
        jnp.zeros((kv_heads, groups_per_head, suffix, HEAD_SIZE), jnp.float32),
    )
    state = block_update(start_state, head_count, own_keys, own_values, causal, scale)
    block_pages = min(8, maxp)
    live_pages = slot_entry < length
    trips = maxp // block_pages

    def step_block(index, carry):
        first = index * block_pages
        block = lax.dynamic_slice_in_dim(received, first, block_pages, 0)
        alive = lax.dynamic_slice_in_dim(live_pages, first, block_pages, 0)
        alive = jnp.broadcast_to(alive[:, None], (block_pages, page_len)).reshape(
            1, block_pages * page_len
        )
        block_keys = block[:, 0].reshape(block_pages * page_len, kv_heads, HEAD_SIZE)
        block_values = block[:, 1].reshape(block_pages * page_len, kv_heads, HEAD_SIZE)
        return block_update(carry, head_count, block_keys, block_values, alive, scale)

    top_final, total_final, acc_final = lax.fori_loop(0, trips, step_block, state)
    output = acc_final / total_final[..., None]
    attended = (
        output.transpose(2, 0, 1, 3)
        .reshape(1, suffix, groups_per_head * width)
        .astype(jnp.bfloat16)
    )
    arrived, arrived_slot = shifted((suffix_key_value, new_slots), "store", stores // 2)
    new_store = lax.dynamic_update_slice_in_dim(kv_pages, arrived, arrived_slot[0], 0)
    return (attended, new_store)


def dot_nt(a, b):
    return lax.dot_general(a, b, (((1,), (1,)), ((), ())), preferred_element_type=jnp.float32)


def block_of(j):
    return slice(j * HEAD_SIZE, (j + 1) * HEAD_SIZE)


def iota(shape, dim):
    return lax.broadcasted_iota(jnp.int32, shape, dim)


def pack_stats(top, total):
    diagonal = iota((HEAD_SIZE, HEAD_SIZE), 0) == iota((HEAD_SIZE, HEAD_SIZE), 1)
    row = iota((STAT_ROWS, HEAD_SIZE), 0)
    tile = jnp.zeros((STAT_ROWS, HEAD_SIZE), jnp.float32)

    def along(x):
        return jnp.sum(jnp.where(diagonal, x, 0.0), 0, keepdims=True)

    for j, (m, l) in enumerate(zip(top, total)):
        l = along(l)
        high = l.astype(jnp.bfloat16).astype(jnp.float32)
        for t, x in enumerate((along(m), high, l - high)):
            tile = jnp.where(row == 4 * t + j, x, tile)
    return tile.astype(jnp.bfloat16)


def unpack_stats(tile):
    row = iota((STAT_ROWS, 8 * HEAD_SIZE), 0)
    block = iota((STAT_ROWS, 8 * HEAD_SIZE), 1) // HEAD_SIZE
    j = block // 2
    stat = block % 2
    spread = (
        ((row == j) & (stat == 0)) | ((row == j + 4) & (stat == 1)) | ((row == j + 8) & (stat == 1))
    )
    spread = spread.astype(jnp.float32).astype(jnp.bfloat16)
    turned = tile.astype(jnp.float32).T.astype(jnp.bfloat16)
    wide = jnp.dot(turned, spread, preferred_element_type=jnp.float32)
    part = lambda b: wide[:, b * HEAD_SIZE:(b + 1) * HEAD_SIZE]
    return [part(2 * j) for j in range(4)], [part(2 * j + 1) for j in range(4)]


def attend_kernel(sizes, jobs, *refs):
    groups, suffix, cap, page_len, count, own = sizes
    refs = list(refs)
    meta = refs.pop(0)
    queries = [refs.pop(0) for _ in range(count)]
    if own:
        own_kv, pages = refs.pop(0), refs.pop(0)
    else:
        held = refs.pop(0)
    results = len({job[-1] for job in jobs})
    outs = [(refs.pop(0), refs.pop(0)) for _ in range(results)]
    if own:
        held, stored, scores, late_scores, sems = refs
        fetch = pltpu.make_async_copy(pages, held, sems.at[0])
        fetch.start()
        fetch.wait()
        keep = pltpu.make_async_copy(held, stored, sems.at[1])
        keep.start()
    else:
        (scores,) = refs
    factor = HEAD_SIZE ** (-0.5) * LOG2E
    keys = cap * page_len
    rows = groups * suffix
    filled = [0] * results
    spots = []
    for job in jobs:
        spots.append(filled[job[-1]])
        filled[job[-1]] += 1

    def stacked(n, part, h):
        return jnp.concatenate([held[meta[n, c], part, :, block_of(h)] for c in range(cap)], 0)

    def score(i):
        n, array, first, h, _ = jobs[i]
        q_ref = queries[array]
        q = jnp.concatenate([q_ref[:, block_of(first * groups + g)] for g in range(groups)], 0)
        scores[i % 2] = dot_nt(q, stacked(n, 0, h))
        if own:
            at = iota((rows, suffix), 0) % suffix
            causal = iota((rows, suffix), 1) <= at
            late_scores[i % 2] = jnp.where(causal, dot_nt(q, own_kv[0, :, block_of(h)]), DEAD)

    def weigh(i):
        n, _, _, h, result = jobs[i]
        live = iota((1, keys), 1) < meta[n, cap] * page_len
        s = jnp.where(live, scores[i % 2], DEAD)
        top = jnp.max(s, axis=-1, keepdims=True)
        if own:
            top = jnp.maximum(top, jnp.max(late_scores[i % 2], axis=-1, keepdims=True))
        top = jnp.maximum(top * factor, FLOOR).astype(jnp.bfloat16).astype(jnp.float32)
        p = jnp.exp2(s * factor - top).astype(jnp.bfloat16)
        v = stacked(n, 1, h)
        v = jnp.concatenate([v, jnp.ones_like(v)], 1)
        out = jnp.dot(p, v, preferred_element_type=jnp.float32)
        if own:
            p = jnp.exp2(late_scores[i % 2] * factor - top).astype(jnp.bfloat16)
            v = own_kv[1, :, block_of(h)]
            v = jnp.concatenate([v, jnp.ones_like(v)], 1)
            out = out + jnp.dot(p, v, preferred_element_type=jnp.float32)
        acc_ref, stat_ref = outs[result]
        spot = spots[i]
        acc_ref[spot] = out[:, :HEAD_SIZE]
        total = out[:, HEAD_SIZE:]
        top = jnp.broadcast_to(top, total.shape)
        blocks = [block_of(j) for j in range(rows // HEAD_SIZE)]
        stat_ref[spot] = pack_stats([top[j] for j in blocks], [total[j] for j in blocks])

    for i in range(len(jobs) + 1):
        if i < len(jobs):
            score(i)
        if i > 0:
            weigh(i - 1)
    if own:
        keep.wait()


def attend(shape, jobs, meta, queries, held, own=None):
    groups, suffix, cap, page_len = shape
    rows, keys = groups * suffix, cap * page_len
    results = len({job[-1] for job in jobs})
    heads = len(jobs) // results
    shapes, specs = [], []
    for _ in range(results):
        shapes.append(jax.ShapeDtypeStruct((heads, rows, HEAD_SIZE), jnp.float32))
        shapes.append(jax.ShapeDtypeStruct((heads, STAT_ROWS, HEAD_SIZE), jnp.bfloat16))
        specs += [VMEM, VMEM]
    scratch = [pltpu.VMEM((2, rows, keys), jnp.float32)]
    more = [held]
    if own is not None:
        more = [own, held]
        shapes += [jax.ShapeDtypeStruct(held.shape, held.dtype)] * 2
        specs += [VMEM, HBM]
        scratch.append(pltpu.VMEM((2, rows, suffix), jnp.float32))
        scratch.append(pltpu.SemaphoreType.DMA((2,)))
    out = pl.pallas_call(
        functools.partial(attend_kernel, shape + (len(queries), own is not None), jobs),
        out_shape=shapes,
        in_specs=[SMEM] + [VMEM] * len(queries) + ([VMEM] if own is None else [VMEM, HBM]),
        out_specs=specs,
        scratch_shapes=scratch,
        compiler_params=pltpu.CompilerParams(vmem_limit_bytes=40 * 1024 * 1024),
        cost_estimate=LIGHT,
    )(meta, *queries, *more)
    return [(out[2 * n], out[2 * n + 1]) for n in range(results)] + list(out[2 * results:])


def place_kernel(half, column, me_ref, lists_ref, page_ref, old_ref, out_ref, sem):
    me = me_ref[0]
    from_below = (me >= half) == (me % 2 == 0)
    slot = jnp.where(from_below, lists_ref[0, column], lists_ref[1, column])
    copy = pltpu.make_async_copy(page_ref.at[0], out_ref.at[slot], sem)
    copy.start()
    copy.wait()


def place_page(half, column, me, lists, page, store):
    return pl.pallas_call(
        functools.partial(place_kernel, half, column),
        out_shape=jax.ShapeDtypeStruct(store.shape, store.dtype),
        in_specs=[SMEM, SMEM, VMEM, HBM],
        out_specs=HBM,
        scratch_shapes=[pltpu.SemaphoreType.DMA],
        input_output_aliases={3: 0},
        cost_estimate=LIGHT,
    )(me, lists, page, store)


def blend(parts):
    top = functools.reduce(jnp.maximum, [m for _, m, _ in parts])
    scales = [jnp.exp2(m - top) for _, m, _ in parts]
    acc = sum(a * f for (a, _, _), f in zip(parts, scales))
    total = sum(l * f for (_, _, l), f in zip(parts, scales))
    return acc, top, total


def pack_kernel(acc_ref, stat_ref, out_ref):
    heads, rows = acc_ref.shape[:2]
    for h in range(heads):
        out_ref[h, :rows, :] = acc_ref[h].astype(jnp.bfloat16)
        out_ref[h, rows:, :] = stat_ref[h]


def merge_kernel(in_ref, acc_ref, stat_ref, out_ref, out_stat_ref=None):
    heads, rows = acc_ref.shape[:2]
    for h in range(heads):
        in_top, in_total = unpack_stats(in_ref[h, rows:, :])
        my_top, my_total = unpack_stats(stat_ref[h])
        tops, totals = [], []
        for j in range(rows // HEAD_SIZE):
            acc, top, total = blend(
                [
                    (in_ref[h, block_of(j), :].astype(jnp.float32), in_top[j], in_total[j]),
                    (acc_ref[h, block_of(j), :], my_top[j], my_total[j]),
                ]
            )
            out_ref[h, block_of(j), :] = acc.astype(out_ref.dtype)
            tops.append(top)
            totals.append(total)
        if out_stat_ref is None:
            out_ref[h, rows:, :] = pack_stats(tops, totals)
        else:
            out_stat_ref[h] = pack_stats(tops, totals)


def final_kernel(suffix, *refs):
    sides, out_ref = (refs[0:3], refs[3:6]), refs[6]
    for side, (in_ref, acc_ref, stat_ref) in enumerate(sides):
        heads, rows = acc_ref.shape[:2]
        groups = rows // suffix
        for h in range(heads):
            in_top, in_total = unpack_stats(in_ref[h, rows:, :])
            my_top, my_total = unpack_stats(stat_ref[h])
            for j in range(rows // HEAD_SIZE):
                acc, _, total = blend(
                    [
                        (in_ref[h, block_of(j), :].astype(jnp.float32), in_top[j], in_total[j]),
                        (acc_ref[h, block_of(j), :], my_top[j], my_total[j]),
                    ]
                )
                out = (acc / total).astype(jnp.bfloat16)
                for i in range(HEAD_SIZE // suffix):
                    g = (side * heads + h) * groups + j * (HEAD_SIZE // suffix) + i
                    out_ref[0, :, block_of(g)] = out[i * suffix:(i + 1) * suffix]


def call(kernel, shape, *args):
    size = sum(a.size * a.dtype.itemsize for a in args)
    return pl.pallas_call(
        kernel,
        out_shape=shape,
        in_specs=[VMEM] * len(args),
        out_specs=[VMEM] * len(shape) if isinstance(shape, list) else VMEM,
        compiler_params=pltpu.CompilerParams(vmem_limit_bytes=48 * 1024 * 1024),
        cost_estimate=pl.CostEstimate(flops=size, bytes_accessed=2 * size, transcendentals=0),
    )(*args)


def prepare_kernel(cut, cap, pages_dev, length_ref, slot_ref, table_ref, q_ref, first_ref, second_ref):
    maxp = table_ref.shape[1]
    suffix = q_ref.shape[1]
    second_ref[...] = q_ref[0, :, cut:]
    first_ref[:, :cut] = q_ref[0, :, :cut]
    table = table_ref[...]
    owner = lax.div(table, pages_dev)
    local = (table - owner * pages_dev).astype(jnp.float32)
    owner = owner.astype(jnp.float32)
    down, along = iota((maxp, maxp), 0), iota((maxp, maxp), 1)

    def turned(x):
        return jnp.sum(jnp.where(down == along, x, 0.0), 1, keepdims=True)

    before = (turned(owner) == owner) & (along < down)
    rank = jnp.sum(jnp.where(before, 1.0, 0.0), 1, keepdims=True)
    place = iota((maxp, HEAD_SIZE), 1)
    live = jnp.where(iota((maxp, HEAD_SIZE), 0) < length_ref[0], 1.0, 0.0)
    ids = jnp.where(rank == place.astype(jnp.float32), turned(local), 0.0)
    fields = jnp.where(place < cap, ids, jnp.where(place == cap, live, 0.0))
    owned = jnp.where(owner == iota((suffix, maxp), 0).astype(jnp.float32), 1.0, 0.0)
    lists = jnp.dot(
        owned.astype(jnp.bfloat16), fields.astype(jnp.bfloat16), preferred_element_type=jnp.float32
    )
    slot = slot_ref[0].astype(jnp.float32)
    lists = jnp.where(iota(lists.shape, 1) == cap + 1, slot, lists)
    first_ref[:, cut:] = lists.astype(jnp.bfloat16)


def prepare(cut, cap, pages_dev, queries, page_table, prefix_pages, new_slots):
    suffix, columns = queries.shape[1:]
    return pl.pallas_call(
        functools.partial(prepare_kernel, cut, cap, pages_dev),
        out_shape=[
            jax.ShapeDtypeStruct((suffix, cut + HEAD_SIZE), queries.dtype),
            jax.ShapeDtypeStruct((suffix, columns - cut), queries.dtype),
        ],
        in_specs=[SMEM, SMEM, VMEM, VMEM],
        out_specs=[VMEM, VMEM],
        cost_estimate=LIGHT,
    )(prefix_pages, new_slots, page_table, queries)


def queries_travel(queries, suffix_key_value, kv_pages, page_table, prefix_pages, new_slots):
    stores = lax.axis_size("store")
    pages_dev, _, page_len, width = kv_pages.shape
    maxp = page_table.shape[1]
    cap = maxp // stores
    kv_heads = width // HEAD_SIZE
    suffix = queries.shape[1]
    groups = queries.shape[2] // width
    shape = (groups, suffix, cap, page_len)
    half = stores // 2
    me = lax.axis_index("store")
    heads_each = kv_heads // 2
    cut = heads_each * groups * HEAD_SIZE

    order = list(range(0, stores, 2)) + list(range(1, stores, 2))[::-1]
    up = [(order[i], order[(i + 1) % stores]) for i in range(stores)]
    down = [(order[i], order[i - 1]) for i in range(stores)]
    routes = {1: up, -1: down}

    def listed(*arrays):
        rows = [lax.dynamic_slice(x, (me, cut), (1, HEAD_SIZE)) for x in arrays]
        return jnp.concatenate(rows).astype(jnp.int32)

    def after(values, token):
        return lax.optimization_barrier((values, token))[0]

    arrived = shifted(suffix_key_value, "store", half)
    mine = prepare(cut, cap, pages_dev, queries, page_table, prefix_pages, new_slots)

    moving = {
        (side, sign): lax.ppermute(mine[side], "store", routes[sign])
        for side in range(2)
        for sign in routes
    }
    jobs = [(0, side, h, side * heads_each + h, side) for side in range(2) for h in range(heads_each)]
    first, second = after(mine, arrived)
    *own, held, store = attend(
        shape, jobs, listed(first), [first, second], kv_pages, suffix_key_value[0]
    )
    parts = {(0, side): own[side] for side in range(2)}
    token = own
    lists_of = {}
    sent = {}
    for step in range(1, half):
        for side in range(2):
            came = {sign: after(moving[side, sign], token) for sign in routes}
            for sign in routes:
                if step < half - 1 or (side == 0) == (sign == 1):
                    moving[side, sign] = lax.ppermute(came[sign], "store", routes[sign])
            if side == 0:
                lists_of[step] = listed(came[1], came[-1])
            jobs = [(n, n, h, side * heads_each + h, n) for n in range(2) for h in range(heads_each)]
            got = attend(shape, jobs, lists_of[step], [came[1], came[-1]], held)
            parts[step, side], parts[-step, side] = got
            token = got
            if step == half - 1:
                sign = 1 if side == 1 else -1
                sent["early", sign] = packed(parts[sign * step, side])
                token = sent["early", sign]
    came = after([moving[0, 1], moving[1, -1]], token)
    jobs = [(0, side, h, side * heads_each + h, side) for side in range(2) for h in range(heads_each)]
    far = attend(shape, jobs, listed(came[0]), came, held)
    token = far

    back = {1: down, -1: up}
    side_of = {("late", 1): 0, ("late", -1): 1, ("early", 1): 1, ("early", -1): 0}
    flows = {key: lax.ppermute(block, "store", back[key[1]]) for key, block in sent.items()}
    store = place_page(
        half, cap + 1, me[None], lists_of[stores // 4], arrived, after(store, token)
    )
    turns = [("late", half)]
    for distance in range(half - 1, 0, -1):
        turns += [("early", distance - 1)] * (distance > 1) + [("late", distance)]
    for flow, distance in turns:
        if distance == half:
            far, ended = lax.optimization_barrier((far, {sign: flows["early", sign] for sign in back}))
            flows.update({("early", sign): ended[sign] for sign in back})
            blocks = {sign: packed(far[side_of[flow, sign]]) for sign in back}
        else:
            came = {sign: flows[flow, sign] for sign in back}
            if distance == 1 and flow == "late":
                ended = {sign: flows["early", sign] for sign in back}
                came, ended = lax.optimization_barrier((came, ended))
                flows.update({("early", sign): ended[sign] for sign in back})
            came = after(came, token)
            blocks = {
                sign: merged(came[sign], parts[sign * distance, side_of[flow, sign]])
                for sign in back
            }
        for sign in back:
            flows[flow, sign] = lax.ppermute(blocks[sign], "store", back[sign])
        token = blocks
    rest, late = [None, None], [None, None]
    for sign in (1, -1):
        side = side_of["early", sign]
        rest[side] = kept(after(flows["early", sign], token), parts[0, side])
        late[1 - side] = flows["late", sign]
    attended = call(
        functools.partial(final_kernel, suffix),
        jax.ShapeDtypeStruct(queries.shape, queries.dtype),
        late[0], *rest[0], late[1], *rest[1],
    )
    return (attended, store)


def wire_of(part):
    heads, rows, columns = part[0].shape
    return jax.ShapeDtypeStruct((heads, rows + STAT_ROWS, columns), jnp.bfloat16)


def packed(part):
    return call(pack_kernel, wire_of(part), *part)


def merged(block, part):
    return call(merge_kernel, wire_of(part), block, *part)


def kept(block, part):
    return call(merge_kernel, [jax.ShapeDtypeStruct(x.shape, x.dtype) for x in part], block, *part)


def on_device(queries, suffix_key_value, kv_pages, page_table, prefix_pages, new_slots):
    stores = lax.axis_size("store")
    pulled = page_table.shape[1] // stores * kv_pages[0].size
    pushed = 2 * queries[0].size
    arrays = (queries, suffix_key_value, kv_pages, page_table, prefix_pages, new_slots)
    if pulled >= pushed and stores % 4 == 0:
        return queries_travel(*arrays)
    return pages_travel(*arrays)


def solution(mesh):
    return jax.shard_map(
        on_device,
        mesh=mesh,
        in_specs=(
            P(("groups", "store"), None, "tensor"),
            P(("groups", "store"), None, None, "tensor"),
            P(("groups", "store"), None, None, "tensor"),
            P(("groups", "store"), None),
            P(("groups", "store")),
            P(("groups", "store")),
        ),
        out_specs=(
            P(("groups", "store"), None, "tensor"),
            P(("groups", "store"), None, None, "tensor"),
        ),
        check_vma=False,
    )
```

```python
import functools

import jax
import jax.numpy as jnp
from jax import lax
from jax.experimental import pallas as pl
from jax.experimental.pallas import tpu as pltpu
from jax.sharding import PartitionSpec as P

HEAD_SIZE = 128
LOG2E = 1.4426950408889634
DEAD = -1e30
FLOOR = -1e29
STAT_ROWS = 16
GRANT = 20 * 1024 * 1024
LIGHT = pl.CostEstimate(flops=1, bytes_accessed=1, transcendentals=0)
VMEM = pl.BlockSpec(memory_space=pltpu.VMEM)
SMEM = pl.BlockSpec(memory_space=pltpu.SMEM)
HBM = pl.BlockSpec(memory_space=pltpu.HBM)


def shifted(block, axis, distance):
    devices = range(lax.axis_size(axis))
    route = [((i - distance) % len(devices), i) for i in devices]
    return lax.ppermute(block, axis, route)


def block_update(state, head_count, key_rows, value_rows, live, scale):
    top_old, total_old, acc_old = state
    scores = (
        jnp.einsum("qhgd,khd->hgqk", head_count, key_rows, preferred_element_type=jnp.float32)
        * scale
    )
    scores = jnp.where(live, scores, -1e30)
    top_new = jnp.maximum(top_old, jnp.max(scores, axis=-1))
    weights = jnp.where(live, jnp.exp(scores - top_new[..., None]), 0.0)
    factor = jnp.exp(top_old - top_new)
    total_new = total_old * factor + jnp.sum(weights, axis=-1)
    product = jnp.einsum(
        "hgqk,khd->hgqd",
        weights.astype(jnp.bfloat16),
        value_rows,
        preferred_element_type=jnp.float32,
    )
    return (top_new, total_new, acc_old * factor[..., None] + product)


def pages_travel(queries, suffix_key_value, kv_pages, page_table, prefix_pages, new_slots):
    stores = lax.axis_size("store")
    pages_dev = kv_pages.shape[0]
    maxp = page_table.shape[1]
    cap = maxp // stores
    page_len = kv_pages.shape[2]
    width = kv_pages.shape[3]
    kv_heads = width // HEAD_SIZE
    suffix = queries.shape[1]
    groups_per_head = queries.shape[2] // width
    scale = HEAD_SIZE ** (-0.5)
    length = prefix_pages[0]
    table = page_table[0]
    owners = table // pages_dev
    local_ids = table % pages_dev
    entries = jnp.arange(maxp, dtype=jnp.int32)
    same_owner = (owners[:, None] == owners[None, :]) & (entries[:, None] < entries[None, :])
    ranks = jnp.sum(same_owner.astype(jnp.int32), axis=0)
    slots = owners * cap + ranks
    placed = slots[:, None] == entries[None, :]
    slot_entry = jnp.sum(jnp.where(placed, entries[:, None], 0), axis=0)
    wanted = jnp.sum(jnp.where(placed, local_ids[:, None], 0), axis=0)
    asked = lax.all_to_all(
        wanted.reshape(stores, cap), "store", split_axis=0, concat_axis=0, tiled=True
    )
    served = kv_pages[asked.reshape(-1)].reshape(stores, cap, 2, page_len, width)
    received = lax.all_to_all(served, "store", split_axis=0, concat_axis=0, tiled=True).reshape(
        maxp, 2, page_len, width
    )
    head_count = queries[0].reshape(suffix, kv_heads, groups_per_head, HEAD_SIZE)
    own_keys = suffix_key_value[0, 0].reshape(suffix, kv_heads, HEAD_SIZE)
    own_values = suffix_key_value[0, 1].reshape(suffix, kv_heads, HEAD_SIZE)
    rows = jnp.arange(suffix, dtype=jnp.int32)
    causal = rows[None, :] <= rows[:, None]
    start_state = (
        jnp.full((kv_heads, groups_per_head, suffix), -1e30, jnp.float32),
        jnp.zeros((kv_heads, groups_per_head, suffix), jnp.float32),
        jnp.zeros((kv_heads, groups_per_head, suffix, HEAD_SIZE), jnp.float32),
    )
    state = block_update(start_state, head_count, own_keys, own_values, causal, scale)
    block_pages = min(8, maxp)
    live_pages = slot_entry < length
    trips = maxp // block_pages

    def step_block(index, carry):
        first = index * block_pages
        block = lax.dynamic_slice_in_dim(received, first, block_pages, 0)
        alive = lax.dynamic_slice_in_dim(live_pages, first, block_pages, 0)
        alive = jnp.broadcast_to(alive[:, None], (block_pages, page_len)).reshape(
            1, block_pages * page_len
        )
        block_keys = block[:, 0].reshape(block_pages * page_len, kv_heads, HEAD_SIZE)
        block_values = block[:, 1].reshape(block_pages * page_len, kv_heads, HEAD_SIZE)
        return block_update(carry, head_count, block_keys, block_values, alive, scale)

    top_final, total_final, acc_final = lax.fori_loop(0, trips, step_block, state)
    output = acc_final / total_final[..., None]
    attended = (
        output.transpose(2, 0, 1, 3)
        .reshape(1, suffix, groups_per_head * width)
        .astype(jnp.bfloat16)
    )
    arrived, arrived_slot = shifted((suffix_key_value, new_slots), "store", stores // 2)
    new_store = lax.dynamic_update_slice_in_dim(kv_pages, arrived, arrived_slot[0], 0)
    return (attended, new_store)


def dot_nt(a, b):
    return lax.dot_general(a, b, (((1,), (1,)), ((), ())), preferred_element_type=jnp.float32)


def block_of(j):
    return slice(j * HEAD_SIZE, (j + 1) * HEAD_SIZE)


def iota(shape, dim):
    return lax.broadcasted_iota(jnp.int32, shape, dim)


def pack_stats(top, total):
    diagonal = iota((HEAD_SIZE, HEAD_SIZE), 0) == iota((HEAD_SIZE, HEAD_SIZE), 1)
    row = iota((STAT_ROWS, HEAD_SIZE), 0)
    tile = jnp.zeros((STAT_ROWS, HEAD_SIZE), jnp.float32)

    def along(x):
        return jnp.sum(jnp.where(diagonal, x, 0.0), 0, keepdims=True)

    for j, (m, l) in enumerate(zip(top, total)):
        l = along(l)
        high = l.astype(jnp.bfloat16).astype(jnp.float32)
        for t, x in enumerate((along(m), high, l - high)):
            tile = jnp.where(row == 4 * t + j, x, tile)
    return tile.astype(jnp.bfloat16)


def unpack_stats(tile):
    row = iota((STAT_ROWS, 8 * HEAD_SIZE), 0)
    block = iota((STAT_ROWS, 8 * HEAD_SIZE), 1) // HEAD_SIZE
    j = block // 2
    stat = block % 2
    spread = (
        ((row == j) & (stat == 0)) | ((row == j + 4) & (stat == 1)) | ((row == j + 8) & (stat == 1))
    )
    spread = spread.astype(jnp.float32).astype(jnp.bfloat16)
    turned = tile.astype(jnp.float32).T.astype(jnp.bfloat16)
    wide = jnp.dot(turned, spread, preferred_element_type=jnp.float32)
    part = lambda b: wide[:, b * HEAD_SIZE:(b + 1) * HEAD_SIZE]
    return [part(2 * j) for j in range(4)], [part(2 * j + 1) for j in range(4)]


def attend_kernel(sizes, jobs, *refs):
    groups, suffix, cap, page_len, count, own = sizes
    refs = list(refs)
    meta = refs.pop(0)
    queries = [refs.pop(0) for _ in range(count)]
    if own:
        own_kv = refs.pop(0)
    held = refs.pop(0)
    results = len({job[-1] for job in jobs})
    outs = [(refs.pop(0), refs.pop(0)) for _ in range(results)]
    if own:
        stored, scores, late_scores, sem = refs
        keep = pltpu.make_async_copy(held, stored, sem)
        keep.start()
    else:
        (scores,) = refs
    factor = HEAD_SIZE ** (-0.5) * LOG2E
    keys = cap * page_len
    rows = groups * suffix
    filled = [0] * results
    spots = []
    for job in jobs:
        spots.append(filled[job[-1]])
        filled[job[-1]] += 1

    def stacked(n, part, h):
        return jnp.concatenate([held[meta[n, c], part, :, block_of(h)] for c in range(cap)], 0)

    def score(i):
        n, array, first, h, _ = jobs[i]
        q_ref = queries[array]
        q = jnp.concatenate([q_ref[:, block_of(first * groups + g)] for g in range(groups)], 0)
        scores[i % 2] = dot_nt(q, stacked(n, 0, h))
        if own:
            at = iota((rows, suffix), 0) % suffix
            causal = iota((rows, suffix), 1) <= at
            late_scores[i % 2] = jnp.where(causal, dot_nt(q, own_kv[0, :, block_of(h)]), DEAD)

    def weigh(i):
        n, _, _, h, result = jobs[i]
        live = iota((1, keys), 1) < meta[n, cap] * page_len
        s = jnp.where(live, scores[i % 2], DEAD)
        top = jnp.max(s, axis=-1, keepdims=True)
        if own:
            top = jnp.maximum(top, jnp.max(late_scores[i % 2], axis=-1, keepdims=True))
        top = jnp.maximum(top * factor, FLOOR).astype(jnp.bfloat16).astype(jnp.float32)
        p = jnp.exp2(s * factor - top).astype(jnp.bfloat16)
        v = stacked(n, 1, h)
        v = jnp.concatenate([v, jnp.ones_like(v)], 1)
        out = jnp.dot(p, v, preferred_element_type=jnp.float32)
        if own:
            p = jnp.exp2(late_scores[i % 2] * factor - top).astype(jnp.bfloat16)
            v = own_kv[1, :, block_of(h)]
            v = jnp.concatenate([v, jnp.ones_like(v)], 1)
            out = out + jnp.dot(p, v, preferred_element_type=jnp.float32)
        acc_ref, stat_ref = outs[result]
        spot = spots[i]
        acc_ref[spot] = out[:, :HEAD_SIZE]
        total = out[:, HEAD_SIZE:]
        top = jnp.broadcast_to(top, total.shape)
        blocks = [block_of(j) for j in range(rows // HEAD_SIZE)]
        stat_ref[spot] = pack_stats([top[j] for j in blocks], [total[j] for j in blocks])

    for i in range(len(jobs) + 1):
        if i < len(jobs):
            score(i)
        if i > 0:
            weigh(i - 1)
    if own:
        keep.wait()


def attend(shape, jobs, meta, queries, held, own=None):
    groups, suffix, cap, page_len = shape
    rows, keys = groups * suffix, cap * page_len
    results = len({job[-1] for job in jobs})
    heads = len(jobs) // results
    shapes, specs = [], []
    for _ in range(results):
        shapes.append(jax.ShapeDtypeStruct((heads, rows, HEAD_SIZE), jnp.float32))
        shapes.append(jax.ShapeDtypeStruct((heads, STAT_ROWS, HEAD_SIZE), jnp.bfloat16))
        specs += [VMEM, VMEM]
    scratch = [pltpu.VMEM((2, rows, keys), jnp.float32)]
    more = [held]
    if own is not None:
        more = [own, held]
        shapes.append(jax.ShapeDtypeStruct(held.shape, held.dtype))
        specs.append(HBM)
        scratch.append(pltpu.VMEM((2, rows, suffix), jnp.float32))
        scratch.append(pltpu.SemaphoreType.DMA)
    out = pl.pallas_call(
        functools.partial(attend_kernel, shape + (len(queries), own is not None), jobs),
        out_shape=shapes,
        in_specs=[SMEM] + [VMEM] * (len(queries) + len(more)),
        out_specs=specs,
        scratch_shapes=scratch,
        compiler_params=pltpu.CompilerParams(vmem_limit_bytes=GRANT),
        cost_estimate=pl.CostEstimate(
            flops=len(jobs) * rows * keys * HEAD_SIZE * 8,
            bytes_accessed=len(jobs) * (rows * 6 + keys * 4) * HEAD_SIZE,
            transcendentals=len(jobs) * rows * keys,
        ),
    )(meta, *queries, *more)
    return [(out[2 * n], out[2 * n + 1]) for n in range(results)] + list(out[2 * results:])


def place_kernel(half, column, me_ref, lists_ref, page_ref, old_ref, out_ref, sem):
    me = me_ref[0]
    from_below = (me >= half) == (me % 2 == 0)
    slot = jnp.where(from_below, lists_ref[0, column], lists_ref[1, column])
    copy = pltpu.make_async_copy(page_ref.at[0], out_ref.at[slot], sem)
    copy.start()
    copy.wait()


def place_page(half, column, me, lists, page, store):
    return pl.pallas_call(
        functools.partial(place_kernel, half, column),
        out_shape=jax.ShapeDtypeStruct(store.shape, store.dtype),
        in_specs=[SMEM, SMEM, VMEM, HBM],
        out_specs=HBM,
        scratch_shapes=[pltpu.SemaphoreType.DMA],
        input_output_aliases={3: 0},
        compiler_params=pltpu.CompilerParams(vmem_limit_bytes=GRANT),
        cost_estimate=LIGHT,
    )(me, lists, page, store)


def blend(parts):
    top = functools.reduce(jnp.maximum, [m for _, m, _ in parts])
    scales = [jnp.exp2(m - top) for _, m, _ in parts]
    acc = sum(a * f for (a, _, _), f in zip(parts, scales))
    total = sum(l * f for (_, _, l), f in zip(parts, scales))
    return acc, top, total


def pack_kernel(acc_ref, stat_ref, out_ref):
    heads, rows = acc_ref.shape[:2]
    for h in range(heads):
        out_ref[h, :rows, :] = acc_ref[h].astype(jnp.bfloat16)
        out_ref[h, rows:, :] = stat_ref[h]


def merge_kernel(in_ref, acc_ref, stat_ref, out_ref, out_stat_ref=None):
    heads, rows = acc_ref.shape[:2]
    for h in range(heads):
        in_top, in_total = unpack_stats(in_ref[h, rows:, :])
        my_top, my_total = unpack_stats(stat_ref[h])
        tops, totals = [], []
        for j in range(rows // HEAD_SIZE):
            acc, top, total = blend(
                [
                    (in_ref[h, block_of(j), :].astype(jnp.float32), in_top[j], in_total[j]),
                    (acc_ref[h, block_of(j), :], my_top[j], my_total[j]),
                ]
            )
            out_ref[h, block_of(j), :] = acc.astype(out_ref.dtype)
            tops.append(top)
            totals.append(total)
        if out_stat_ref is None:
            out_ref[h, rows:, :] = pack_stats(tops, totals)
        else:
            out_stat_ref[h] = pack_stats(tops, totals)


def final_kernel(suffix, *refs):
    sides, out_ref = (refs[0:3], refs[3:6]), refs[6]
    for side, (in_ref, acc_ref, stat_ref) in enumerate(sides):
        heads, rows = acc_ref.shape[:2]
        groups = rows // suffix
        for h in range(heads):
            in_top, in_total = unpack_stats(in_ref[h, rows:, :])
            my_top, my_total = unpack_stats(stat_ref[h])
            for j in range(rows // HEAD_SIZE):
                acc, _, total = blend(
                    [
                        (in_ref[h, block_of(j), :].astype(jnp.float32), in_top[j], in_total[j]),
                        (acc_ref[h, block_of(j), :], my_top[j], my_total[j]),
                    ]
                )
                out = (acc / total).astype(jnp.bfloat16)
                for i in range(HEAD_SIZE // suffix):
                    g = (side * heads + h) * groups + j * (HEAD_SIZE // suffix) + i
                    out_ref[0, :, block_of(g)] = out[i * suffix:(i + 1) * suffix]


def call(kernel, shape, *args):
    size = sum(a.size * a.dtype.itemsize for a in args)
    return pl.pallas_call(
        kernel,
        out_shape=shape,
        in_specs=[VMEM] * len(args),
        out_specs=[VMEM] * len(shape) if isinstance(shape, list) else VMEM,
        compiler_params=pltpu.CompilerParams(vmem_limit_bytes=GRANT),
        cost_estimate=pl.CostEstimate(flops=size, bytes_accessed=2 * size, transcendentals=0),
    )(*args)


def prepare_kernel(cut, cap, pages_dev, length_ref, slot_ref, table_ref, q_ref, first_ref, second_ref):
    maxp = table_ref.shape[1]
    suffix = q_ref.shape[1]
    second_ref[...] = q_ref[0, :, cut:]
    first_ref[:, :cut] = q_ref[0, :, :cut]
    table = table_ref[...]
    owner = lax.div(table, pages_dev)
    local = (table - owner * pages_dev).astype(jnp.float32)
    owner = owner.astype(jnp.float32)
    down, along = iota((maxp, maxp), 0), iota((maxp, maxp), 1)

    def turned(x):
        return jnp.sum(jnp.where(down == along, x, 0.0), 1, keepdims=True)

    before = (turned(owner) == owner) & (along < down)
    rank = jnp.sum(jnp.where(before, 1.0, 0.0), 1, keepdims=True)
    place = iota((maxp, HEAD_SIZE), 1)
    live = jnp.where(iota((maxp, HEAD_SIZE), 0) < length_ref[0], 1.0, 0.0)
    ids = jnp.where(rank == place.astype(jnp.float32), turned(local), 0.0)
    fields = jnp.where(place < cap, ids, jnp.where(place == cap, live, 0.0))
    owned = jnp.where(owner == iota((suffix, maxp), 0).astype(jnp.float32), 1.0, 0.0)
    lists = jnp.dot(
        owned.astype(jnp.bfloat16), fields.astype(jnp.bfloat16), preferred_element_type=jnp.float32
    )
    slot = slot_ref[0].astype(jnp.float32)
    lists = jnp.where(iota(lists.shape, 1) == cap + 1, slot, lists)
    first_ref[:, cut:] = lists.astype(jnp.bfloat16)


def prepare(cut, cap, pages_dev, queries, page_table, prefix_pages, new_slots):
    suffix, columns = queries.shape[1:]
    return pl.pallas_call(
        functools.partial(prepare_kernel, cut, cap, pages_dev),
        out_shape=[
            jax.ShapeDtypeStruct((suffix, cut + HEAD_SIZE), queries.dtype),
            jax.ShapeDtypeStruct((suffix, columns - cut), queries.dtype),
        ],
        in_specs=[SMEM, SMEM, VMEM, VMEM],
        out_specs=[VMEM, VMEM],
        compiler_params=pltpu.CompilerParams(vmem_limit_bytes=GRANT),
        cost_estimate=pl.CostEstimate(flops=1, bytes_accessed=1 << 24, transcendentals=0),
    )(prefix_pages, new_slots, page_table, queries)


def queries_travel(queries, suffix_key_value, kv_pages, page_table, prefix_pages, new_slots):
    stores = lax.axis_size("store")
    pages_dev, _, page_len, width = kv_pages.shape
    maxp = page_table.shape[1]
    cap = maxp // stores
    kv_heads = width // HEAD_SIZE
    suffix = queries.shape[1]
    groups = queries.shape[2] // width
    shape = (groups, suffix, cap, page_len)
    half = stores // 2
    me = lax.axis_index("store")
    heads_each = kv_heads // 2
    cut = heads_each * groups * HEAD_SIZE

    order = list(range(0, stores, 2)) + list(range(1, stores, 2))[::-1]
    up = [(order[i], order[(i + 1) % stores]) for i in range(stores)]
    down = [(order[i], order[i - 1]) for i in range(stores)]
    routes = {1: up, -1: down}

    def listed(*arrays):
        rows = [lax.dynamic_slice(x, (me, cut), (1, HEAD_SIZE)) for x in arrays]
        return jnp.concatenate(rows).astype(jnp.int32)

    def after(values, token):
        return lax.optimization_barrier((values, token))[0]

    arrived = shifted(suffix_key_value, "store", half)
    mine = prepare(cut, cap, pages_dev, queries, page_table, prefix_pages, new_slots)

    moving = {
        (side, sign): lax.ppermute(mine[side], "store", routes[sign])
        for side in range(2)
        for sign in routes
    }
    jobs = [(0, side, h, side * heads_each + h, side) for side in range(2) for h in range(heads_each)]
    held = kv_pages
    *own, store = attend(shape, jobs, listed(mine[0]), mine, held, suffix_key_value[0])
    parts = {(0, side): own[side] for side in range(2)}
    token = [own, arrived]
    lists_of = {}
    sent = {}
    for step in range(1, half):
        for side in range(2):
            came = {sign: after(moving[side, sign], token) for sign in routes}
            for sign in routes:
                if step < half - 1 or (side == 0) == (sign == 1):
                    moving[side, sign] = lax.ppermute(came[sign], "store", routes[sign])
            if side == 0:
                lists_of[step] = listed(came[1], came[-1])
            jobs = [(n, n, h, side * heads_each + h, n) for n in range(2) for h in range(heads_each)]
            got = attend(shape, jobs, lists_of[step], [came[1], came[-1]], held)
            parts[step, side], parts[-step, side] = got
            token = got
            if step == half - 1:
                sign = 1 if side == 1 else -1
                sent["early", sign] = packed(parts[sign * step, side])
                token = sent["early", sign]
    came = after([moving[0, 1], moving[1, -1]], token)
    jobs = [(0, side, h, side * heads_each + h, side) for side in range(2) for h in range(heads_each)]
    far = attend(shape, jobs, listed(came[0]), came, held)
    token = far

    back = {1: down, -1: up}
    side_of = {("late", 1): 0, ("late", -1): 1, ("early", 1): 1, ("early", -1): 0}
    flows = {key: lax.ppermute(block, "store", back[key[1]]) for key, block in sent.items()}
    store = place_page(
        half, cap + 1, me[None], lists_of[stores // 4], arrived, after(store, token)
    )
    turns = [("late", half)]
    for distance in range(half - 1, 0, -1):
        turns += [("early", distance - 1)] * (distance > 1) + [("late", distance)]
    for flow, distance in turns:
        if distance == half:
            far, ended = lax.optimization_barrier((far, {sign: flows["early", sign] for sign in back}))
            flows.update({("early", sign): ended[sign] for sign in back})
            blocks = {sign: packed(far[side_of[flow, sign]]) for sign in back}
        else:
            came = {sign: flows[flow, sign] for sign in back}
            if distance == 1 and flow == "late":
                ended = {sign: flows["early", sign] for sign in back}
                came, ended = lax.optimization_barrier((came, ended))
                flows.update({("early", sign): ended[sign] for sign in back})
            came = after(came, token)
            blocks = {
                sign: merged(came[sign], parts[sign * distance, side_of[flow, sign]])
                for sign in back
            }
        for sign in back:
            flows[flow, sign] = lax.ppermute(blocks[sign], "store", back[sign])
        token = blocks
    rest, late = [None, None], [None, None]
    for sign in (1, -1):
        side = side_of["early", sign]
        rest[side] = kept(after(flows["early", sign], token), parts[0, side])
        late[1 - side] = flows["late", sign]
    attended = call(
        functools.partial(final_kernel, suffix),
        jax.ShapeDtypeStruct(queries.shape, queries.dtype),
        late[0], *rest[0], late[1], *rest[1],
    )
    return (attended, store)


def wire_of(part):
    heads, rows, columns = part[0].shape
    return jax.ShapeDtypeStruct((heads, rows + STAT_ROWS, columns), jnp.bfloat16)


def packed(part):
    return call(pack_kernel, wire_of(part), *part)


def merged(block, part):
    return call(merge_kernel, wire_of(part), block, *part)


def kept(block, part):
    return call(merge_kernel, [jax.ShapeDtypeStruct(x.shape, x.dtype) for x in part], block, *part)


def on_device(queries, suffix_key_value, kv_pages, page_table, prefix_pages, new_slots):
    stores = lax.axis_size("store")
    pulled = page_table.shape[1] // stores * kv_pages[0].size
    pushed = 2 * queries[0].size
    arrays = (queries, suffix_key_value, kv_pages, page_table, prefix_pages, new_slots)
    if pulled >= pushed and stores % 4 == 0:
        return queries_travel(*arrays)
    return pages_travel(*arrays)


def solution(mesh):
    return jax.shard_map(
        on_device,
        mesh=mesh,
        in_specs=(
            P(("groups", "store"), None, "tensor"),
            P(("groups", "store"), None, None, "tensor"),
            P(("groups", "store"), None, None, "tensor"),
            P(("groups", "store"), None),
            P(("groups", "store")),
            P(("groups", "store")),
        ),
        out_specs=(
            P(("groups", "store"), None, "tensor"),
            P(("groups", "store"), None, None, "tensor"),
        ),
        check_vma=False,
    )
```

```python
import functools

import jax
import jax.numpy as jnp
from jax import lax
from jax.experimental import pallas as pl
from jax.experimental.pallas import tpu as pltpu
from jax.sharding import PartitionSpec as P

HEAD_SIZE = 128
LOG2E = 1.4426950408889634
DEAD = -1e30
FLOOR = -1e29
STAT_ROWS = 16
GRANT = 20 * 1024 * 1024
LIGHT = pl.CostEstimate(flops=1, bytes_accessed=1, transcendentals=0)
VMEM = pl.BlockSpec(memory_space=pltpu.VMEM)
SMEM = pl.BlockSpec(memory_space=pltpu.SMEM)
HBM = pl.BlockSpec(memory_space=pltpu.HBM)


def shifted(block, axis, distance):
    devices = range(lax.axis_size(axis))
    route = [((i - distance) % len(devices), i) for i in devices]
    return lax.ppermute(block, axis, route)


def block_update(state, head_count, key_rows, value_rows, live, scale):
    top_old, total_old, acc_old = state
    scores = (
        jnp.einsum("qhgd,khd->hgqk", head_count, key_rows, preferred_element_type=jnp.float32)
        * scale
    )
    scores = jnp.where(live, scores, -1e30)
    top_new = jnp.maximum(top_old, jnp.max(scores, axis=-1))
    weights = jnp.where(live, jnp.exp(scores - top_new[..., None]), 0.0)
    factor = jnp.exp(top_old - top_new)
    total_new = total_old * factor + jnp.sum(weights, axis=-1)
    product = jnp.einsum(
        "hgqk,khd->hgqd",
        weights.astype(jnp.bfloat16),
        value_rows,
        preferred_element_type=jnp.float32,
    )
    return (top_new, total_new, acc_old * factor[..., None] + product)


def pages_travel(queries, suffix_key_value, kv_pages, page_table, prefix_pages, new_slots):
    stores = lax.axis_size("store")
    pages_dev = kv_pages.shape[0]
    maxp = page_table.shape[1]
    cap = maxp // stores
    page_len = kv_pages.shape[2]
    width = kv_pages.shape[3]
    kv_heads = width // HEAD_SIZE
    suffix = queries.shape[1]
    groups_per_head = queries.shape[2] // width
    scale = HEAD_SIZE ** (-0.5)
    length = prefix_pages[0]
    table = page_table[0]
    owners = table // pages_dev
    local_ids = table % pages_dev
    entries = jnp.arange(maxp, dtype=jnp.int32)
    same_owner = (owners[:, None] == owners[None, :]) & (entries[:, None] < entries[None, :])
    ranks = jnp.sum(same_owner.astype(jnp.int32), axis=0)
    slots = owners * cap + ranks
    placed = slots[:, None] == entries[None, :]
    slot_entry = jnp.sum(jnp.where(placed, entries[:, None], 0), axis=0)
    wanted = jnp.sum(jnp.where(placed, local_ids[:, None], 0), axis=0)
    asked = lax.all_to_all(
        wanted.reshape(stores, cap), "store", split_axis=0, concat_axis=0, tiled=True
    )
    served = kv_pages[asked.reshape(-1)].reshape(stores, cap, 2, page_len, width)
    received = lax.all_to_all(served, "store", split_axis=0, concat_axis=0, tiled=True).reshape(
        maxp, 2, page_len, width
    )
    head_count = queries[0].reshape(suffix, kv_heads, groups_per_head, HEAD_SIZE)
    own_keys = suffix_key_value[0, 0].reshape(suffix, kv_heads, HEAD_SIZE)
    own_values = suffix_key_value[0, 1].reshape(suffix, kv_heads, HEAD_SIZE)
    rows = jnp.arange(suffix, dtype=jnp.int32)
    causal = rows[None, :] <= rows[:, None]
    start_state = (
        jnp.full((kv_heads, groups_per_head, suffix), -1e30, jnp.float32),
        jnp.zeros((kv_heads, groups_per_head, suffix), jnp.float32),
        jnp.zeros((kv_heads, groups_per_head, suffix, HEAD_SIZE), jnp.float32),
    )
    state = block_update(start_state, head_count, own_keys, own_values, causal, scale)
    block_pages = min(8, maxp)
    live_pages = slot_entry < length
    trips = maxp // block_pages

    def step_block(index, carry):
        first = index * block_pages
        block = lax.dynamic_slice_in_dim(received, first, block_pages, 0)
        alive = lax.dynamic_slice_in_dim(live_pages, first, block_pages, 0)
        alive = jnp.broadcast_to(alive[:, None], (block_pages, page_len)).reshape(
            1, block_pages * page_len
        )
        block_keys = block[:, 0].reshape(block_pages * page_len, kv_heads, HEAD_SIZE)
        block_values = block[:, 1].reshape(block_pages * page_len, kv_heads, HEAD_SIZE)
        return block_update(carry, head_count, block_keys, block_values, alive, scale)

    top_final, total_final, acc_final = lax.fori_loop(0, trips, step_block, state)
    output = acc_final / total_final[..., None]
    attended = (
        output.transpose(2, 0, 1, 3)
        .reshape(1, suffix, groups_per_head * width)
        .astype(jnp.bfloat16)
    )
    arrived, arrived_slot = shifted((suffix_key_value, new_slots), "store", stores // 2)
    new_store = lax.dynamic_update_slice_in_dim(kv_pages, arrived, arrived_slot[0], 0)
    return (attended, new_store)


def dot_nt(a, b):
    return lax.dot_general(a, b, (((1,), (1,)), ((), ())), preferred_element_type=jnp.float32)


def block_of(j):
    return slice(j * HEAD_SIZE, (j + 1) * HEAD_SIZE)


def iota(shape, dim):
    return lax.broadcasted_iota(jnp.int32, shape, dim)


def pack_stats(top, total):
    diagonal = iota((HEAD_SIZE, HEAD_SIZE), 0) == iota((HEAD_SIZE, HEAD_SIZE), 1)
    row = iota((STAT_ROWS, HEAD_SIZE), 0)
    tile = jnp.zeros((STAT_ROWS, HEAD_SIZE), jnp.float32)

    def along(x):
        return jnp.sum(jnp.where(diagonal, x, 0.0), 0, keepdims=True)

    for j, (m, l) in enumerate(zip(top, total)):
        l = along(l)
        high = l.astype(jnp.bfloat16).astype(jnp.float32)
        for t, x in enumerate((along(m), high, l - high)):
            tile = jnp.where(row == 4 * t + j, x, tile)
    return tile.astype(jnp.bfloat16)


def unpack_stats(tile):
    row = iota((STAT_ROWS, 8 * HEAD_SIZE), 0)
    block = iota((STAT_ROWS, 8 * HEAD_SIZE), 1) // HEAD_SIZE
    j = block // 2
    stat = block % 2
    spread = (
        ((row == j) & (stat == 0)) | ((row == j + 4) & (stat == 1)) | ((row == j + 8) & (stat == 1))
    )
    spread = spread.astype(jnp.float32).astype(jnp.bfloat16)
    turned = tile.astype(jnp.float32).T.astype(jnp.bfloat16)
    wide = jnp.dot(turned, spread, preferred_element_type=jnp.float32)
    part = lambda b: wide[:, b * HEAD_SIZE:(b + 1) * HEAD_SIZE]
    return [part(2 * j) for j in range(4)], [part(2 * j + 1) for j in range(4)]


def attend_kernel(sizes, jobs, *refs):
    groups, suffix, cap, page_len, count, own, keeping = sizes
    refs = list(refs)
    meta = refs.pop(0)
    queries = [refs.pop(0) for _ in range(count)]
    if own:
        own_kv = refs.pop(0)
    held = refs.pop(0)
    results = len({job[-1] for job in jobs})
    outs = [(refs.pop(0), refs.pop(0)) for _ in range(results)]
    stored = refs.pop(0) if keeping else None
    scores = refs.pop(0)
    late_scores = refs.pop(0) if own else None
    if keeping:
        keep = pltpu.make_async_copy(held, stored, refs.pop(0))
        keep.start()
    factor = HEAD_SIZE ** (-0.5) * LOG2E
    keys = cap * page_len
    rows = groups * suffix
    filled = [0] * results
    spots = []
    for job in jobs:
        spots.append(filled[job[-1]])
        filled[job[-1]] += 1

    def stacked(n, part, h):
        return jnp.concatenate([held[meta[n, c], part, :, block_of(h)] for c in range(cap)], 0)

    def score(i):
        n, array, first, h, _ = jobs[i]
        q_ref = queries[array]
        q = jnp.concatenate([q_ref[:, block_of(first * groups + g)] for g in range(groups)], 0)
        scores[i % 2] = dot_nt(q, stacked(n, 0, h))
        if own:
            at = iota((rows, suffix), 0) % suffix
            causal = iota((rows, suffix), 1) <= at
            late_scores[i % 2] = jnp.where(causal, dot_nt(q, own_kv[0, :, block_of(h)]), DEAD)

    def weigh(i):
        n, _, _, h, result = jobs[i]
        live = iota((1, keys), 1) < meta[n, cap] * page_len
        s = jnp.where(live, scores[i % 2], DEAD)
        top = jnp.max(s, axis=-1, keepdims=True)
        if own:
            top = jnp.maximum(top, jnp.max(late_scores[i % 2], axis=-1, keepdims=True))
        top = jnp.maximum(top * factor, FLOOR).astype(jnp.bfloat16).astype(jnp.float32)
        p = jnp.exp2(s * factor - top).astype(jnp.bfloat16)
        v = stacked(n, 1, h)
        v = jnp.concatenate([v, jnp.ones_like(v)], 1)
        out = jnp.dot(p, v, preferred_element_type=jnp.float32)
        if own:
            p = jnp.exp2(late_scores[i % 2] * factor - top).astype(jnp.bfloat16)
            v = own_kv[1, :, block_of(h)]
            v = jnp.concatenate([v, jnp.ones_like(v)], 1)
            out = out + jnp.dot(p, v, preferred_element_type=jnp.float32)
        acc_ref, stat_ref = outs[result]
        spot = spots[i]
        acc_ref[spot] = out[:, :HEAD_SIZE]
        total = out[:, HEAD_SIZE:]
        top = jnp.broadcast_to(top, total.shape)
        blocks = [block_of(j) for j in range(rows // HEAD_SIZE)]
        stat_ref[spot] = pack_stats([top[j] for j in blocks], [total[j] for j in blocks])

    for i in range(len(jobs) + 1):
        if i < len(jobs):
            score(i)
        if i > 0:
            weigh(i - 1)
    if keeping:
        keep.wait()


def attend(shape, jobs, meta, queries, held, own=None, keeping=False):
    groups, suffix, cap, page_len = shape
    rows, keys = groups * suffix, cap * page_len
    results = len({job[-1] for job in jobs})
    heads = len(jobs) // results
    shapes, specs = [], []
    for _ in range(results):
        shapes.append(jax.ShapeDtypeStruct((heads, rows, HEAD_SIZE), jnp.float32))
        shapes.append(jax.ShapeDtypeStruct((heads, STAT_ROWS, HEAD_SIZE), jnp.bfloat16))
        specs += [VMEM, VMEM]
    scratch = [pltpu.VMEM((2, rows, keys), jnp.float32)]
    more = [held]
    if own is not None:
        more = [own, held]
        scratch.append(pltpu.VMEM((2, rows, suffix), jnp.float32))
    if keeping:
        shapes.append(jax.ShapeDtypeStruct(held.shape, held.dtype))
        specs.append(HBM)
        scratch.append(pltpu.SemaphoreType.DMA)
    out = pl.pallas_call(
        functools.partial(attend_kernel, shape + (len(queries), own is not None, keeping), jobs),
        out_shape=shapes,
        in_specs=[SMEM] + [VMEM] * (len(queries) + len(more)),
        out_specs=specs,
        scratch_shapes=scratch,
        compiler_params=pltpu.CompilerParams(vmem_limit_bytes=GRANT),
        cost_estimate=pl.CostEstimate(
            flops=len(jobs) * rows * keys * HEAD_SIZE * 8,
            bytes_accessed=len(jobs) * (rows * 6 + keys * 4) * HEAD_SIZE,
            transcendentals=len(jobs) * rows * keys,
        ),
    )(meta, *queries, *more)
    return [(out[2 * n], out[2 * n + 1]) for n in range(results)] + list(out[2 * results:])


def place_kernel(half, column, me_ref, lists_ref, page_ref, old_ref, out_ref, sem):
    me = me_ref[0]
    from_below = (me >= half) == (me % 2 == 0)
    slot = jnp.where(from_below, lists_ref[0, column], lists_ref[1, column])
    copy = pltpu.make_async_copy(page_ref.at[0], out_ref.at[slot], sem)
    copy.start()
    copy.wait()


def place_page(half, column, me, lists, page, store):
    return pl.pallas_call(
        functools.partial(place_kernel, half, column),
        out_shape=jax.ShapeDtypeStruct(store.shape, store.dtype),
        in_specs=[SMEM, SMEM, VMEM, HBM],
        out_specs=HBM,
        scratch_shapes=[pltpu.SemaphoreType.DMA],
        input_output_aliases={3: 0},
        compiler_params=pltpu.CompilerParams(vmem_limit_bytes=GRANT),
        cost_estimate=LIGHT,
    )(me, lists, page, store)


def blend(parts):
    top = functools.reduce(jnp.maximum, [m for _, m, _ in parts])
    scales = [jnp.exp2(m - top) for _, m, _ in parts]
    acc = sum(a * f for (a, _, _), f in zip(parts, scales))
    total = sum(l * f for (_, _, l), f in zip(parts, scales))
    return acc, top, total


def pack_kernel(acc_ref, stat_ref, out_ref):
    heads, rows = acc_ref.shape[:2]
    for h in range(heads):
        out_ref[h, :rows, :] = acc_ref[h].astype(jnp.bfloat16)
        out_ref[h, rows:, :] = stat_ref[h]


def merge_kernel(in_ref, acc_ref, stat_ref, out_ref, out_stat_ref=None):
    heads, rows = acc_ref.shape[:2]
    for h in range(heads):
        in_top, in_total = unpack_stats(in_ref[h, rows:, :])
        my_top, my_total = unpack_stats(stat_ref[h])
        tops, totals = [], []
        for j in range(rows // HEAD_SIZE):
            acc, top, total = blend(
                [
                    (in_ref[h, block_of(j), :].astype(jnp.float32), in_top[j], in_total[j]),
                    (acc_ref[h, block_of(j), :], my_top[j], my_total[j]),
                ]
            )
            out_ref[h, block_of(j), :] = acc.astype(out_ref.dtype)
            tops.append(top)
            totals.append(total)
        if out_stat_ref is None:
            out_ref[h, rows:, :] = pack_stats(tops, totals)
        else:
            out_stat_ref[h] = pack_stats(tops, totals)


def final_kernel(suffix, *refs):
    sides, out_ref = (refs[0:3], refs[3:6]), refs[6]
    for side, (in_ref, acc_ref, stat_ref) in enumerate(sides):
        heads, rows = acc_ref.shape[:2]
        groups = rows // suffix
        for h in range(heads):
            in_top, in_total = unpack_stats(in_ref[h, rows:, :])
            my_top, my_total = unpack_stats(stat_ref[h])
            for j in range(rows // HEAD_SIZE):
                acc, _, total = blend(
                    [
                        (in_ref[h, block_of(j), :].astype(jnp.float32), in_top[j], in_total[j]),
                        (acc_ref[h, block_of(j), :], my_top[j], my_total[j]),
                    ]
                )
                out = (acc / total).astype(jnp.bfloat16)
                for i in range(HEAD_SIZE // suffix):
                    g = (side * heads + h) * groups + j * (HEAD_SIZE // suffix) + i
                    out_ref[0, :, block_of(g)] = out[i * suffix:(i + 1) * suffix]


def call(kernel, shape, *args):
    size = sum(a.size * a.dtype.itemsize for a in args)
    return pl.pallas_call(
        kernel,
        out_shape=shape,
        in_specs=[VMEM] * len(args),
        out_specs=[VMEM] * len(shape) if isinstance(shape, list) else VMEM,
        compiler_params=pltpu.CompilerParams(vmem_limit_bytes=GRANT),
        cost_estimate=pl.CostEstimate(flops=size, bytes_accessed=2 * size, transcendentals=0),
    )(*args)


def prepare_kernel(cut, cap, pages_dev, length_ref, slot_ref, table_ref, q_ref, first_ref, second_ref):
    maxp = table_ref.shape[1]
    suffix = q_ref.shape[1]
    second_ref[...] = q_ref[0, :, cut:]
    first_ref[:, :cut] = q_ref[0, :, :cut]
    table = table_ref[...]
    owner = lax.div(table, pages_dev)
    local = (table - owner * pages_dev).astype(jnp.float32)
    owner = owner.astype(jnp.float32)
    down, along = iota((maxp, maxp), 0), iota((maxp, maxp), 1)

    def turned(x):
        return jnp.sum(jnp.where(down == along, x, 0.0), 1, keepdims=True)

    before = (turned(owner) == owner) & (along < down)
    rank = jnp.sum(jnp.where(before, 1.0, 0.0), 1, keepdims=True)
    place = iota((maxp, HEAD_SIZE), 1)
    live = jnp.where(iota((maxp, HEAD_SIZE), 0) < length_ref[0], 1.0, 0.0)
    ids = jnp.where(rank == place.astype(jnp.float32), turned(local), 0.0)
    fields = jnp.where(place < cap, ids, jnp.where(place == cap, live, 0.0))
    owned = jnp.where(owner == iota((suffix, maxp), 0).astype(jnp.float32), 1.0, 0.0)
    lists = jnp.dot(
        owned.astype(jnp.bfloat16), fields.astype(jnp.bfloat16), preferred_element_type=jnp.float32
    )
    slot = slot_ref[0].astype(jnp.float32)
    lists = jnp.where(iota(lists.shape, 1) == cap + 1, slot, lists)
    first_ref[:, cut:] = lists.astype(jnp.bfloat16)


def prepare(cut, cap, pages_dev, queries, page_table, prefix_pages, new_slots):
    suffix, columns = queries.shape[1:]
    return pl.pallas_call(
        functools.partial(prepare_kernel, cut, cap, pages_dev),
        out_shape=[
            jax.ShapeDtypeStruct((suffix, cut + HEAD_SIZE), queries.dtype),
            jax.ShapeDtypeStruct((suffix, columns - cut), queries.dtype),
        ],
        in_specs=[SMEM, SMEM, VMEM, VMEM],
        out_specs=[VMEM, VMEM],
        compiler_params=pltpu.CompilerParams(vmem_limit_bytes=GRANT),
        cost_estimate=pl.CostEstimate(flops=1, bytes_accessed=1 << 24, transcendentals=0),
    )(prefix_pages, new_slots, page_table, queries)


def queries_travel(queries, suffix_key_value, kv_pages, page_table, prefix_pages, new_slots):
    stores = lax.axis_size("store")
    pages_dev, _, page_len, width = kv_pages.shape
    maxp = page_table.shape[1]
    cap = maxp // stores
    kv_heads = width // HEAD_SIZE
    suffix = queries.shape[1]
    groups = queries.shape[2] // width
    shape = (groups, suffix, cap, page_len)
    half = stores // 2
    me = lax.axis_index("store")
    heads_each = kv_heads // 2
    cut = heads_each * groups * HEAD_SIZE

    order = list(range(0, stores, 2)) + list(range(1, stores, 2))[::-1]
    up = [(order[i], order[(i + 1) % stores]) for i in range(stores)]
    down = [(order[i], order[i - 1]) for i in range(stores)]
    routes = {1: up, -1: down}

    def listed(*arrays):
        rows = [lax.dynamic_slice(x, (me, cut), (1, HEAD_SIZE)) for x in arrays]
        return jnp.concatenate(rows).astype(jnp.int32)

    def after(values, token):
        return lax.optimization_barrier((values, token))[0]

    arrived = shifted(suffix_key_value, "store", half)
    mine = prepare(cut, cap, pages_dev, queries, page_table, prefix_pages, new_slots)

    moving = {
        (side, sign): lax.ppermute(mine[side], "store", routes[sign])
        for side in range(2)
        for sign in routes
    }
    held = kv_pages
    parts = {}
    token = []
    lists_of = {}
    sent = {}
    for step in range(1, half):
        for side in range(2):
            came = {sign: after(moving[side, sign], token) for sign in routes}
            for sign in routes:
                if step < half - 1 or (side == 0) == (sign == 1):
                    moving[side, sign] = lax.ppermute(came[sign], "store", routes[sign])
            if side == 0:
                lists_of[step] = listed(came[1], came[-1])
            jobs = [(n, n, h, side * heads_each + h, n) for n in range(2) for h in range(heads_each)]
            keeping = (step, side) == (1, 1)
            got = attend(shape, jobs, lists_of[step], [came[1], came[-1]], held, None, keeping)
            if keeping:
                store = got.pop()
            parts[step, side], parts[-step, side] = got
            token = got
            if (step, side) == (half // 2, 0):
                token = [got, arrived]
            if step == half - 1:
                sign = 1 if side == 1 else -1
                sent["early", sign] = packed(parts[sign * step, side])
                token = sent["early", sign]
    came = after([moving[0, 1], moving[1, -1]], token)
    jobs = [(0, side, h, side * heads_each + h, side) for side in range(2) for h in range(heads_each)]
    far = attend(shape, jobs, listed(came[0]), came, held)
    token = far

    back = {1: down, -1: up}
    side_of = {("late", 1): 0, ("late", -1): 1, ("early", 1): 1, ("early", -1): 0}
    flows = {key: lax.ppermute(block, "store", back[key[1]]) for key, block in sent.items()}
    store = place_page(
        half, cap + 1, me[None], lists_of[stores // 4], arrived, after(store, token)
    )
    turns = [("late", half)]
    for distance in range(half - 1, 0, -1):
        turns += [("early", distance - 1)] * (distance > 1) + [("late", distance)]
    for flow, distance in turns:
        if distance == half:
            far, ended = lax.optimization_barrier((far, {sign: flows["early", sign] for sign in back}))
            flows.update({("early", sign): ended[sign] for sign in back})
            blocks = {sign: packed(far[side_of[flow, sign]]) for sign in back}
        else:
            came = {sign: flows[flow, sign] for sign in back}
            if distance == 1 and flow == "late":
                ended = {sign: flows["early", sign] for sign in back}
                came, ended = lax.optimization_barrier((came, ended))
                flows.update({("early", sign): ended[sign] for sign in back})
            came = after(came, token)
            blocks = {
                sign: merged(came[sign], parts[sign * distance, side_of[flow, sign]])
                for sign in back
            }
        for sign in back:
            flows[flow, sign] = lax.ppermute(blocks[sign], "store", back[sign])
        token = blocks
        if flow == "early" and distance <= 2:
            side = 2 - distance
            jobs = [(0, 0, h, side * heads_each + h, 0) for h in range(heads_each)]
            parts[0, side], = attend(
                shape, jobs, listed(mine[0]), [after(mine[side], token)], held, suffix_key_value[0]
            )
            token = [blocks, parts[0, side]]
    rest, late = [None, None], [None, None]
    for sign in (1, -1):
        side = side_of["early", sign]
        rest[side] = kept(after(flows["early", sign], token), parts[0, side])
        late[1 - side] = flows["late", sign]
    attended = call(
        functools.partial(final_kernel, suffix),
        jax.ShapeDtypeStruct(queries.shape, queries.dtype),
        late[0], *rest[0], late[1], *rest[1],
    )
    return (attended, store)


def wire_of(part):
    heads, rows, columns = part[0].shape
    return jax.ShapeDtypeStruct((heads, rows + STAT_ROWS, columns), jnp.bfloat16)


def packed(part):
    return call(pack_kernel, wire_of(part), *part)


def merged(block, part):
    return call(merge_kernel, wire_of(part), block, *part)


def kept(block, part):
    return call(merge_kernel, [jax.ShapeDtypeStruct(x.shape, x.dtype) for x in part], block, *part)


def on_device(queries, suffix_key_value, kv_pages, page_table, prefix_pages, new_slots):
    stores = lax.axis_size("store")
    pulled = page_table.shape[1] // stores * kv_pages[0].size
    pushed = 2 * queries[0].size
    arrays = (queries, suffix_key_value, kv_pages, page_table, prefix_pages, new_slots)
    if pulled >= pushed and stores % 8 == 0:
        return queries_travel(*arrays)
    return pages_travel(*arrays)


def solution(mesh):
    return jax.shard_map(
        on_device,
        mesh=mesh,
        in_specs=(
            P(("groups", "store"), None, "tensor"),
            P(("groups", "store"), None, None, "tensor"),
            P(("groups", "store"), None, None, "tensor"),
            P(("groups", "store"), None),
            P(("groups", "store")),
            P(("groups", "store")),
        ),
        out_specs=(
            P(("groups", "store"), None, "tensor"),
            P(("groups", "store"), None, None, "tensor"),
        ),
        check_vma=False,
    )
```

```python
import functools

import jax
import jax.numpy as jnp
from jax import lax
from jax.experimental import pallas as pl
from jax.experimental.pallas import tpu as pltpu
from jax.sharding import PartitionSpec as P

HEAD_SIZE = 128
LOG2E = 1.4426950408889634
DEAD = -1e30
FLOOR = -1e29
STAT_ROWS = 16
GRANT = 20 * 1024 * 1024
LIGHT = pl.CostEstimate(flops=1, bytes_accessed=1, transcendentals=0)
VMEM = pl.BlockSpec(memory_space=pltpu.VMEM)
SMEM = pl.BlockSpec(memory_space=pltpu.SMEM)
HBM = pl.BlockSpec(memory_space=pltpu.HBM)


def shifted(block, axis, distance):
    devices = range(lax.axis_size(axis))
    route = [((i - distance) % len(devices), i) for i in devices]
    return lax.ppermute(block, axis, route)


def block_update(state, head_count, key_rows, value_rows, live, scale):
    top_old, total_old, acc_old = state
    scores = (
        jnp.einsum("qhgd,khd->hgqk", head_count, key_rows, preferred_element_type=jnp.float32)
        * scale
    )
    scores = jnp.where(live, scores, -1e30)
    top_new = jnp.maximum(top_old, jnp.max(scores, axis=-1))
    weights = jnp.where(live, jnp.exp(scores - top_new[..., None]), 0.0)
    factor = jnp.exp(top_old - top_new)
    total_new = total_old * factor + jnp.sum(weights, axis=-1)
    product = jnp.einsum(
        "hgqk,khd->hgqd",
        weights.astype(jnp.bfloat16),
        value_rows,
        preferred_element_type=jnp.float32,
    )
    return (top_new, total_new, acc_old * factor[..., None] + product)


def pages_travel(queries, suffix_key_value, kv_pages, page_table, prefix_pages, new_slots):
    stores = lax.axis_size("store")
    pages_dev = kv_pages.shape[0]
    maxp = page_table.shape[1]
    cap = maxp // stores
    page_len = kv_pages.shape[2]
    width = kv_pages.shape[3]
    kv_heads = width // HEAD_SIZE
    suffix = queries.shape[1]
    groups_per_head = queries.shape[2] // width
    scale = HEAD_SIZE ** (-0.5)
    length = prefix_pages[0]
    table = page_table[0]
    owners = table // pages_dev
    local_ids = table % pages_dev
    entries = jnp.arange(maxp, dtype=jnp.int32)
    same_owner = (owners[:, None] == owners[None, :]) & (entries[:, None] < entries[None, :])
    ranks = jnp.sum(same_owner.astype(jnp.int32), axis=0)
    slots = owners * cap + ranks
    placed = slots[:, None] == entries[None, :]
    slot_entry = jnp.sum(jnp.where(placed, entries[:, None], 0), axis=0)
    wanted = jnp.sum(jnp.where(placed, local_ids[:, None], 0), axis=0)
    asked = lax.all_to_all(
        wanted.reshape(stores, cap), "store", split_axis=0, concat_axis=0, tiled=True
    )
    served = kv_pages[asked.reshape(-1)].reshape(stores, cap, 2, page_len, width)
    received = lax.all_to_all(served, "store", split_axis=0, concat_axis=0, tiled=True).reshape(
        maxp, 2, page_len, width
    )
    head_count = queries[0].reshape(suffix, kv_heads, groups_per_head, HEAD_SIZE)
    own_keys = suffix_key_value[0, 0].reshape(suffix, kv_heads, HEAD_SIZE)
    own_values = suffix_key_value[0, 1].reshape(suffix, kv_heads, HEAD_SIZE)
    rows = jnp.arange(suffix, dtype=jnp.int32)
    causal = rows[None, :] <= rows[:, None]
    start_state = (
        jnp.full((kv_heads, groups_per_head, suffix), -1e30, jnp.float32),
        jnp.zeros((kv_heads, groups_per_head, suffix), jnp.float32),
        jnp.zeros((kv_heads, groups_per_head, suffix, HEAD_SIZE), jnp.float32),
    )
    state = block_update(start_state, head_count, own_keys, own_values, causal, scale)
    block_pages = min(8, maxp)
    live_pages = slot_entry < length
    trips = maxp // block_pages

    def step_block(index, carry):
        first = index * block_pages
        block = lax.dynamic_slice_in_dim(received, first, block_pages, 0)
        alive = lax.dynamic_slice_in_dim(live_pages, first, block_pages, 0)
        alive = jnp.broadcast_to(alive[:, None], (block_pages, page_len)).reshape(
            1, block_pages * page_len
        )
        block_keys = block[:, 0].reshape(block_pages * page_len, kv_heads, HEAD_SIZE)
        block_values = block[:, 1].reshape(block_pages * page_len, kv_heads, HEAD_SIZE)
        return block_update(carry, head_count, block_keys, block_values, alive, scale)

    top_final, total_final, acc_final = lax.fori_loop(0, trips, step_block, state)
    output = acc_final / total_final[..., None]
    attended = (
        output.transpose(2, 0, 1, 3)
        .reshape(1, suffix, groups_per_head * width)
        .astype(jnp.bfloat16)
    )
    arrived, arrived_slot = shifted((suffix_key_value, new_slots), "store", stores // 2)
    new_store = lax.dynamic_update_slice_in_dim(kv_pages, arrived, arrived_slot[0], 0)
    return (attended, new_store)


def dot_nt(a, b):
    return lax.dot_general(a, b, (((1,), (1,)), ((), ())), preferred_element_type=jnp.float32)


def block_of(j):
    return slice(j * HEAD_SIZE, (j + 1) * HEAD_SIZE)


def iota(shape, dim):
    return lax.broadcasted_iota(jnp.int32, shape, dim)


def pack_stats(top, total):
    diagonal = iota((HEAD_SIZE, HEAD_SIZE), 0) == iota((HEAD_SIZE, HEAD_SIZE), 1)
    row = iota((STAT_ROWS, HEAD_SIZE), 0)
    tile = jnp.zeros((STAT_ROWS, HEAD_SIZE), jnp.float32)

    def along(x):
        return jnp.sum(jnp.where(diagonal, x, 0.0), 0, keepdims=True)

    for j, (m, l) in enumerate(zip(top, total)):
        l = along(l)
        high = l.astype(jnp.bfloat16).astype(jnp.float32)
        for t, x in enumerate((along(m), high, l - high)):
            tile = jnp.where(row == 4 * t + j, x, tile)
    return tile.astype(jnp.bfloat16)


def unpack_stats(tile):
    row = iota((STAT_ROWS, 8 * HEAD_SIZE), 0)
    block = iota((STAT_ROWS, 8 * HEAD_SIZE), 1) // HEAD_SIZE
    j = block // 2
    stat = block % 2
    spread = (
        ((row == j) & (stat == 0)) | ((row == j + 4) & (stat == 1)) | ((row == j + 8) & (stat == 1))
    )
    spread = spread.astype(jnp.float32).astype(jnp.bfloat16)
    turned = tile.astype(jnp.float32).T.astype(jnp.bfloat16)
    wide = jnp.dot(turned, spread, preferred_element_type=jnp.float32)
    part = lambda b: wide[:, b * HEAD_SIZE:(b + 1) * HEAD_SIZE]
    return [part(2 * j) for j in range(4)], [part(2 * j + 1) for j in range(4)]


def attend_kernel(sizes, jobs, *refs):
    groups, suffix, cap, page_len, count, own, keeping = sizes
    refs = list(refs)
    meta = refs.pop(0)
    who = None if own else refs.pop(0)
    queries = [refs.pop(0) for _ in range(count)]
    if own:
        own_kv = refs.pop(0)
    held = refs.pop(0)
    results = len({job[-1] for job in jobs})
    outs = [(refs.pop(0), refs.pop(0)) for _ in range(results)]
    stored = refs.pop(0) if keeping else None
    scores = refs.pop(0)
    late_scores = refs.pop(0) if own else None
    if keeping:
        keep = pltpu.make_async_copy(held, stored, refs.pop(0))
        keep.start()
    factor = HEAD_SIZE ** (-0.5) * LOG2E
    keys = cap * page_len
    rows = groups * suffix
    filled = [0] * results
    spots = []
    for job in jobs:
        spots.append(filled[job[-1]])
        filled[job[-1]] += 1

    def stacked(n, part, h):
        return jnp.concatenate([held[wanted(n, c), part, :, block_of(h)] for c in range(cap)], 0)

    def wanted(n, field):
        return meta[0 if own else who[n], field]

    def score(i):
        n, array, first, h, _ = jobs[i]
        q_ref = queries[array]
        if not own:
            q_ref = q_ref.at[who[n]]
        q = jnp.concatenate([q_ref[:, block_of(first * groups + g)] for g in range(groups)], 0)
        scores[i % 2] = dot_nt(q, stacked(n, 0, h))
        if own:
            at = iota((rows, suffix), 0) % suffix
            causal = iota((rows, suffix), 1) <= at
            late_scores[i % 2] = jnp.where(causal, dot_nt(q, own_kv[0, :, block_of(h)]), DEAD)

    def weigh(i):
        n, _, _, h, result = jobs[i]
        live = iota((1, keys), 1) < wanted(n, cap) * page_len
        s = jnp.where(live, scores[i % 2], DEAD)
        top = jnp.max(s, axis=-1, keepdims=True)
        if own:
            top = jnp.maximum(top, jnp.max(late_scores[i % 2], axis=-1, keepdims=True))
        top = jnp.maximum(top * factor, FLOOR).astype(jnp.bfloat16).astype(jnp.float32)
        p = jnp.exp2(s * factor - top).astype(jnp.bfloat16)
        v = stacked(n, 1, h)
        v = jnp.concatenate([v, jnp.ones_like(v)], 1)
        out = jnp.dot(p, v, preferred_element_type=jnp.float32)
        if own:
            p = jnp.exp2(late_scores[i % 2] * factor - top).astype(jnp.bfloat16)
            v = own_kv[1, :, block_of(h)]
            v = jnp.concatenate([v, jnp.ones_like(v)], 1)
            out = out + jnp.dot(p, v, preferred_element_type=jnp.float32)
        acc_ref, stat_ref = outs[result]
        spot = spots[i]
        acc_ref[spot] = out[:, :HEAD_SIZE]
        total = out[:, HEAD_SIZE:]
        top = jnp.broadcast_to(top, total.shape)
        blocks = [block_of(j) for j in range(rows // HEAD_SIZE)]
        stat_ref[spot] = pack_stats([top[j] for j in blocks], [total[j] for j in blocks])

    for i in range(len(jobs) + 1):
        if i < len(jobs):
            score(i)
        if i > 0:
            weigh(i - 1)
    if keeping:
        keep.wait()


def attend(shape, jobs, meta, queries, held, own=None, keeping=False):
    groups, suffix, cap, page_len = shape
    rows, keys = groups * suffix, cap * page_len
    results = len({job[-1] for job in jobs})
    heads = len(jobs) // results
    shapes, specs = [], []
    for _ in range(results):
        shapes.append(jax.ShapeDtypeStruct((heads, rows, HEAD_SIZE), jnp.float32))
        shapes.append(jax.ShapeDtypeStruct((heads, STAT_ROWS, HEAD_SIZE), jnp.bfloat16))
        specs += [VMEM, VMEM]
    scratch = [pltpu.VMEM((2, rows, keys), jnp.float32)]
    more = [held]
    if own is not None:
        more = [own, held]
        scratch.append(pltpu.VMEM((2, rows, suffix), jnp.float32))
    if keeping:
        shapes.append(jax.ShapeDtypeStruct(held.shape, held.dtype))
        specs.append(HBM)
        scratch.append(pltpu.SemaphoreType.DMA)
    out = pl.pallas_call(
        functools.partial(attend_kernel, shape + (len(queries), own is not None, keeping), jobs),
        out_shape=shapes,
        in_specs=[SMEM] * len(meta) + [VMEM] * (len(queries) + len(more)),
        out_specs=specs,
        scratch_shapes=scratch,
        compiler_params=pltpu.CompilerParams(vmem_limit_bytes=GRANT),
        cost_estimate=pl.CostEstimate(
            flops=len(jobs) * rows * keys * HEAD_SIZE * 8,
            bytes_accessed=len(jobs) * (rows * 6 + keys * 4) * HEAD_SIZE,
            transcendentals=len(jobs) * rows * keys,
        ),
    )(*meta, *queries, *more)
    return [(out[2 * n], out[2 * n + 1]) for n in range(results)] + list(out[2 * results:])


def place_kernel(half, column, me_ref, lists_ref, page_ref, old_ref, out_ref, sem):
    me = me_ref[0]
    slot = lists_ref[jnp.where(me >= half, me - half, me + half), column]
    copy = pltpu.make_async_copy(page_ref.at[0], out_ref.at[slot], sem)
    copy.start()
    copy.wait()


def place_page(half, column, me, lists, page, store):
    return pl.pallas_call(
        functools.partial(place_kernel, half, column),
        out_shape=jax.ShapeDtypeStruct(store.shape, store.dtype),
        in_specs=[SMEM, SMEM, VMEM, HBM],
        out_specs=HBM,
        scratch_shapes=[pltpu.SemaphoreType.DMA],
        input_output_aliases={3: 0},
        compiler_params=pltpu.CompilerParams(vmem_limit_bytes=GRANT),
        cost_estimate=LIGHT,
    )(me, lists, page, store)


def blend(parts):
    top = functools.reduce(jnp.maximum, [m for _, m, _ in parts])
    scales = [jnp.exp2(m - top) for _, m, _ in parts]
    acc = sum(a * f for (a, _, _), f in zip(parts, scales))
    total = sum(l * f for (_, _, l), f in zip(parts, scales))
    return acc, top, total


def pack_kernel(acc_ref, stat_ref, out_ref):
    heads, rows = acc_ref.shape[:2]
    for h in range(heads):
        out_ref[h, :rows, :] = acc_ref[h].astype(jnp.bfloat16)
        out_ref[h, rows:, :] = stat_ref[h]


def merge_kernel(in_ref, acc_ref, stat_ref, out_ref, out_stat_ref=None):
    heads, rows = acc_ref.shape[:2]
    for h in range(heads):
        in_top, in_total = unpack_stats(in_ref[h, rows:, :])
        my_top, my_total = unpack_stats(stat_ref[h])
        tops, totals = [], []
        for j in range(rows // HEAD_SIZE):
            acc, top, total = blend(
                [
                    (in_ref[h, block_of(j), :].astype(jnp.float32), in_top[j], in_total[j]),
                    (acc_ref[h, block_of(j), :], my_top[j], my_total[j]),
                ]
            )
            out_ref[h, block_of(j), :] = acc.astype(out_ref.dtype)
            tops.append(top)
            totals.append(total)
        if out_stat_ref is None:
            out_ref[h, rows:, :] = pack_stats(tops, totals)
        else:
            out_stat_ref[h] = pack_stats(tops, totals)


def final_kernel(suffix, *refs):
    sides, out_ref = (refs[0:3], refs[3:6]), refs[6]
    for side, (in_ref, acc_ref, stat_ref) in enumerate(sides):
        heads, rows = acc_ref.shape[:2]
        groups = rows // suffix
        for h in range(heads):
            in_top, in_total = unpack_stats(in_ref[h, rows:, :])
            my_top, my_total = unpack_stats(stat_ref[h])
            for j in range(rows // HEAD_SIZE):
                acc, _, total = blend(
                    [
                        (in_ref[h, block_of(j), :].astype(jnp.float32), in_top[j], in_total[j]),
                        (acc_ref[h, block_of(j), :], my_top[j], my_total[j]),
                    ]
                )
                out = (acc / total).astype(jnp.bfloat16)
                for i in range(HEAD_SIZE // suffix):
                    g = (side * heads + h) * groups + j * (HEAD_SIZE // suffix) + i
                    out_ref[0, :, block_of(g)] = out[i * suffix:(i + 1) * suffix]


def call(kernel, shape, *args):
    size = sum(a.size * a.dtype.itemsize for a in args)
    return pl.pallas_call(
        kernel,
        out_shape=shape,
        in_specs=[VMEM] * len(args),
        out_specs=[VMEM] * len(shape) if isinstance(shape, list) else VMEM,
        compiler_params=pltpu.CompilerParams(vmem_limit_bytes=GRANT),
        cost_estimate=pl.CostEstimate(flops=size, bytes_accessed=2 * size, transcendentals=0),
    )(*args)


def prepare_kernel(cut, cap, pages_dev, length_ref, slot_ref, table_ref, q_ref, first_ref, second_ref):
    maxp = table_ref.shape[1]
    suffix = q_ref.shape[1]
    second_ref[...] = q_ref[0, :, cut:]
    first_ref[:, :cut] = q_ref[0, :, :cut]
    table = table_ref[...]
    owner = lax.div(table, pages_dev)
    local = (table - owner * pages_dev).astype(jnp.float32)
    owner = owner.astype(jnp.float32)
    down, along = iota((maxp, maxp), 0), iota((maxp, maxp), 1)

    def turned(x):
        return jnp.sum(jnp.where(down == along, x, 0.0), 1, keepdims=True)

    before = (turned(owner) == owner) & (along < down)
    rank = jnp.sum(jnp.where(before, 1.0, 0.0), 1, keepdims=True)
    place = iota((maxp, HEAD_SIZE), 1)
    live = jnp.where(iota((maxp, HEAD_SIZE), 0) < length_ref[0], 1.0, 0.0)
    ids = jnp.where(rank == place.astype(jnp.float32), turned(local), 0.0)
    fields = jnp.where(place < cap, ids, jnp.where(place == cap, live, 0.0))
    owned = jnp.where(owner == iota((suffix, maxp), 0).astype(jnp.float32), 1.0, 0.0)
    lists = jnp.dot(
        owned.astype(jnp.bfloat16), fields.astype(jnp.bfloat16), preferred_element_type=jnp.float32
    )
    slot = slot_ref[0].astype(jnp.float32)
    lists = jnp.where(iota(lists.shape, 1) == cap + 1, slot, lists)
    first_ref[:, cut:] = lists.astype(jnp.bfloat16)


def prepare(cut, cap, pages_dev, queries, page_table, prefix_pages, new_slots):
    suffix, columns = queries.shape[1:]
    return pl.pallas_call(
        functools.partial(prepare_kernel, cut, cap, pages_dev),
        out_shape=[
            jax.ShapeDtypeStruct((suffix, cut + HEAD_SIZE), queries.dtype),
            jax.ShapeDtypeStruct((suffix, columns - cut), queries.dtype),
        ],
        in_specs=[SMEM, SMEM, VMEM, VMEM],
        out_specs=[VMEM, VMEM],
        compiler_params=pltpu.CompilerParams(vmem_limit_bytes=GRANT),
        cost_estimate=pl.CostEstimate(flops=1, bytes_accessed=1 << 24, transcendentals=0),
    )(prefix_pages, new_slots, page_table, queries)


def queries_travel(queries, suffix_key_value, kv_pages, page_table, prefix_pages, new_slots):
    stores = lax.axis_size("store")
    pages_dev, _, page_len, width = kv_pages.shape
    maxp = page_table.shape[1]
    cap = maxp // stores
    kv_heads = width // HEAD_SIZE
    suffix = queries.shape[1]
    groups = queries.shape[2] // width
    shape = (groups, suffix, cap, page_len)
    half = stores // 2
    me = lax.axis_index("store")
    heads_each = kv_heads // 2
    cut = heads_each * groups * HEAD_SIZE

    order = list(range(0, stores, 2)) + list(range(1, stores, 2))[::-1]
    up = [(order[i], order[(i + 1) % stores]) for i in range(stores)]
    down = [(order[i], order[i - 1]) for i in range(stores)]
    routes = {1: up, -1: down}

    def after(values, token):
        return lax.optimization_barrier((values, token))[0]

    arrived = shifted(suffix_key_value, "store", half)
    mine = prepare(cut, cap, pages_dev, queries, page_table, prefix_pages, new_slots)
    gathered = [lax.all_gather(x, "store") for x in mine]

    lists = lax.dynamic_slice(gathered[0], (0, me, cut), (stores, 1, HEAD_SIZE))
    lists = lists.reshape(stores, HEAD_SIZE).astype(jnp.int32)
    whose = [[order[(order.index(i) - d) % stores] for d in range(stores)] for i in range(stores)]
    whose = jnp.asarray(whose, jnp.int32)[me]
    held = kv_pages

    def attended_to(side, distances, token, keeping=False):
        jobs = [
            (d % stores, 0, h, side * heads_each + h, n)
            for n, d in enumerate(distances)
            for h in range(heads_each)
        ]
        got = attend(
            shape, jobs, [lists, whose], [after(gathered[side], token)], held, None, keeping
        )
        parts.update({(d, side): got[n] for n, d in enumerate(distances)})
        return got

    def attended_own(side, token):
        jobs = [(0, 0, h, side * heads_each + h, 0) for h in range(heads_each)]
        mine_list = lax.dynamic_slice(mine[0], (me, cut), (1, HEAD_SIZE)).astype(jnp.int32)
        got = attend(
            shape, jobs, [mine_list], [after(mine[side], token)], held, suffix_key_value[0]
        )
        parts[0, side] = got[0]
        return got

    parts = {}
    far, near = half, half - 1
    token = attended_to(0, [far, -near, near, 1 - near], [], True)
    store = token.pop()
    token = attended_to(0, list(range(near - 1, 0, -1)) + list(range(2 - near, 0)), token)
    token = attended_to(1, [far, near], token)
    sent = {("early", 1): packed(parts[near, 1]), ("early", -1): packed(parts[-near, 0])}
    extra = {
        ("late", half): lambda t: attended_to(1, [-near, near - 1], t),
        ("early", near - 1): lambda t: attended_to(1, [1 - near] + list(range(near - 2, 0, -1)), t),
        ("late", near): lambda t: attended_to(1, list(range(2 - near, 0)), t),
        ("early", near - 2): lambda t: attended_own(0, t),
        ("late", near - 1): lambda t: attended_own(1, t),
    }

    back = {1: down, -1: up}
    side_of = {("late", 1): 0, ("late", -1): 1, ("early", 1): 1, ("early", -1): 0}
    flows = {key: lax.ppermute(block, "store", back[key[1]]) for key, block in sent.items()}
    store = place_page(half, cap + 1, me[None], lists, arrived, after(store, token))
    turns = [("late", half)]
    for distance in range(half - 1, 0, -1):
        turns += [("early", distance - 1)] * (distance > 1) + [("late", distance)]
    for flow, distance in turns:
        if distance == half:
            blocks = {sign: packed(parts[half, side_of[flow, sign]]) for sign in back}
        else:
            came = {sign: flows[flow, sign] for sign in back}
            if distance == 1 and flow == "late":
                ended = {sign: flows["early", sign] for sign in back}
                came, ended = lax.optimization_barrier((came, ended))
                flows.update({("early", sign): ended[sign] for sign in back})
            came = after(came, token)
            blocks = {
                sign: merged(came[sign], parts[sign * distance, side_of[flow, sign]])
                for sign in back
            }
        for sign in back:
            flows[flow, sign] = lax.ppermute(blocks[sign], "store", back[sign])
        token = blocks
        if (flow, distance) in extra:
            token = [blocks, extra[flow, distance](token)]
    rest, late = [None, None], [None, None]
    for sign in (1, -1):
        side = side_of["early", sign]
        rest[side] = kept(after(flows["early", sign], token), parts[0, side])
        late[1 - side] = flows["late", sign]
    attended = call(
        functools.partial(final_kernel, suffix),
        jax.ShapeDtypeStruct(queries.shape, queries.dtype),
        late[0], *rest[0], late[1], *rest[1],
    )
    return (attended, store)


def wire_of(part):
    heads, rows, columns = part[0].shape
    return jax.ShapeDtypeStruct((heads, rows + STAT_ROWS, columns), jnp.bfloat16)


def packed(part):
    return call(pack_kernel, wire_of(part), *part)


def merged(block, part):
    return call(merge_kernel, wire_of(part), block, *part)


def kept(block, part):
    return call(merge_kernel, [jax.ShapeDtypeStruct(x.shape, x.dtype) for x in part], block, *part)


def on_device(queries, suffix_key_value, kv_pages, page_table, prefix_pages, new_slots):
    stores = lax.axis_size("store")
    pulled = page_table.shape[1] // stores * kv_pages[0].size
    pushed = 2 * queries[0].size
    arrays = (queries, suffix_key_value, kv_pages, page_table, prefix_pages, new_slots)
    if pulled >= pushed and stores % 8 == 0:
        return queries_travel(*arrays)
    return pages_travel(*arrays)


def solution(mesh):
    return jax.shard_map(
        on_device,
        mesh=mesh,
        in_specs=(
            P(("groups", "store"), None, "tensor"),
            P(("groups", "store"), None, None, "tensor"),
            P(("groups", "store"), None, None, "tensor"),
            P(("groups", "store"), None),
            P(("groups", "store")),
            P(("groups", "store")),
        ),
        out_specs=(
            P(("groups", "store"), None, "tensor"),
            P(("groups", "store"), None, None, "tensor"),
        ),
        check_vma=False,
    )
```

```python
import functools

import jax
import jax.numpy as jnp
from jax import lax
from jax.experimental import pallas as pl
from jax.experimental.pallas import tpu as pltpu
from jax.sharding import PartitionSpec as P

HEAD_SIZE = 128
LOG2E = 1.4426950408889634
DEAD = -1e30
FLOOR = -1e29
STAT_ROWS = 16
GRANT = 20 * 1024 * 1024
LIGHT = pl.CostEstimate(flops=1, bytes_accessed=1, transcendentals=0)
VMEM = pl.BlockSpec(memory_space=pltpu.VMEM)
SMEM = pl.BlockSpec(memory_space=pltpu.SMEM)
HBM = pl.BlockSpec(memory_space=pltpu.HBM)


def shifted(block, axis, distance):
    devices = range(lax.axis_size(axis))
    route = [((i - distance) % len(devices), i) for i in devices]
    return lax.ppermute(block, axis, route)


def block_update(state, head_count, key_rows, value_rows, live, scale):
    top_old, total_old, acc_old = state
    scores = (
        jnp.einsum("qhgd,khd->hgqk", head_count, key_rows, preferred_element_type=jnp.float32)
        * scale
    )
    scores = jnp.where(live, scores, -1e30)
    top_new = jnp.maximum(top_old, jnp.max(scores, axis=-1))
    weights = jnp.where(live, jnp.exp(scores - top_new[..., None]), 0.0)
    factor = jnp.exp(top_old - top_new)
    total_new = total_old * factor + jnp.sum(weights, axis=-1)
    product = jnp.einsum(
        "hgqk,khd->hgqd",
        weights.astype(jnp.bfloat16),
        value_rows,
        preferred_element_type=jnp.float32,
    )
    return (top_new, total_new, acc_old * factor[..., None] + product)


def pages_travel(queries, suffix_key_value, kv_pages, page_table, prefix_pages, new_slots):
    stores = lax.axis_size("store")
    pages_dev = kv_pages.shape[0]
    maxp = page_table.shape[1]
    cap = maxp // stores
    page_len = kv_pages.shape[2]
    width = kv_pages.shape[3]
    kv_heads = width // HEAD_SIZE
    suffix = queries.shape[1]
    groups_per_head = queries.shape[2] // width
    scale = HEAD_SIZE ** (-0.5)
    length = prefix_pages[0]
    table = page_table[0]
    owners = table // pages_dev
    local_ids = table % pages_dev
    entries = jnp.arange(maxp, dtype=jnp.int32)
    same_owner = (owners[:, None] == owners[None, :]) & (entries[:, None] < entries[None, :])
    ranks = jnp.sum(same_owner.astype(jnp.int32), axis=0)
    slots = owners * cap + ranks
    placed = slots[:, None] == entries[None, :]
    slot_entry = jnp.sum(jnp.where(placed, entries[:, None], 0), axis=0)
    wanted = jnp.sum(jnp.where(placed, local_ids[:, None], 0), axis=0)
    asked = lax.all_to_all(
        wanted.reshape(stores, cap), "store", split_axis=0, concat_axis=0, tiled=True
    )
    served = kv_pages[asked.reshape(-1)].reshape(stores, cap, 2, page_len, width)
    received = lax.all_to_all(served, "store", split_axis=0, concat_axis=0, tiled=True).reshape(
        maxp, 2, page_len, width
    )
    head_count = queries[0].reshape(suffix, kv_heads, groups_per_head, HEAD_SIZE)
    own_keys = suffix_key_value[0, 0].reshape(suffix, kv_heads, HEAD_SIZE)
    own_values = suffix_key_value[0, 1].reshape(suffix, kv_heads, HEAD_SIZE)
    rows = jnp.arange(suffix, dtype=jnp.int32)
    causal = rows[None, :] <= rows[:, None]
    start_state = (
        jnp.full((kv_heads, groups_per_head, suffix), -1e30, jnp.float32),
        jnp.zeros((kv_heads, groups_per_head, suffix), jnp.float32),
        jnp.zeros((kv_heads, groups_per_head, suffix, HEAD_SIZE), jnp.float32),
    )
    state = block_update(start_state, head_count, own_keys, own_values, causal, scale)
    block_pages = min(8, maxp)
    live_pages = slot_entry < length
    trips = maxp // block_pages

    def step_block(index, carry):
        first = index * block_pages
        block = lax.dynamic_slice_in_dim(received, first, block_pages, 0)
        alive = lax.dynamic_slice_in_dim(live_pages, first, block_pages, 0)
        alive = jnp.broadcast_to(alive[:, None], (block_pages, page_len)).reshape(
            1, block_pages * page_len
        )
        block_keys = block[:, 0].reshape(block_pages * page_len, kv_heads, HEAD_SIZE)
        block_values = block[:, 1].reshape(block_pages * page_len, kv_heads, HEAD_SIZE)
        return block_update(carry, head_count, block_keys, block_values, alive, scale)

    top_final, total_final, acc_final = lax.fori_loop(0, trips, step_block, state)
    output = acc_final / total_final[..., None]
    attended = (
        output.transpose(2, 0, 1, 3)
        .reshape(1, suffix, groups_per_head * width)
        .astype(jnp.bfloat16)
    )
    arrived, arrived_slot = shifted((suffix_key_value, new_slots), "store", stores // 2)
    new_store = lax.dynamic_update_slice_in_dim(kv_pages, arrived, arrived_slot[0], 0)
    return (attended, new_store)


def dot_nt(a, b):
    return lax.dot_general(a, b, (((1,), (1,)), ((), ())), preferred_element_type=jnp.float32)


def block_of(j):
    return slice(j * HEAD_SIZE, (j + 1) * HEAD_SIZE)


def iota(shape, dim):
    return lax.broadcasted_iota(jnp.int32, shape, dim)


def pack_stats(top, total):
    diagonal = iota((HEAD_SIZE, HEAD_SIZE), 0) == iota((HEAD_SIZE, HEAD_SIZE), 1)
    row = iota((STAT_ROWS, HEAD_SIZE), 0)
    tile = jnp.zeros((STAT_ROWS, HEAD_SIZE), jnp.float32)

    def along(x):
        return jnp.sum(jnp.where(diagonal, x, 0.0), 0, keepdims=True)

    for j, (m, l) in enumerate(zip(top, total)):
        l = along(l)
        high = l.astype(jnp.bfloat16).astype(jnp.float32)
        for t, x in enumerate((along(m), high, l - high)):
            tile = jnp.where(row == 4 * t + j, x, tile)
    return tile.astype(jnp.bfloat16)


def unpack_stats(tile):
    row = iota((STAT_ROWS, 8 * HEAD_SIZE), 0)
    block = iota((STAT_ROWS, 8 * HEAD_SIZE), 1) // HEAD_SIZE
    j = block // 2
    stat = block % 2
    spread = (
        ((row == j) & (stat == 0)) | ((row == j + 4) & (stat == 1)) | ((row == j + 8) & (stat == 1))
    )
    spread = spread.astype(jnp.float32).astype(jnp.bfloat16)
    turned = tile.astype(jnp.float32).T.astype(jnp.bfloat16)
    wide = jnp.dot(turned, spread, preferred_element_type=jnp.float32)
    part = lambda b: wide[:, b * HEAD_SIZE:(b + 1) * HEAD_SIZE]
    return [part(2 * j) for j in range(4)], [part(2 * j + 1) for j in range(4)]


def attend_kernel(sizes, jobs, *refs):
    groups, suffix, cap, page_len, count, own, keeping = sizes
    refs = list(refs)
    meta = refs.pop(0)
    queries = [refs.pop(0) for _ in range(count)]
    if own:
        own_kv = refs.pop(0)
    held = refs.pop(0)
    results = len({job[-1] for job in jobs})
    outs = [(refs.pop(0), refs.pop(0)) for _ in range(results)]
    stored = refs.pop(0) if keeping else None
    scores = refs.pop(0)
    late_scores = refs.pop(0) if own else None
    if keeping:
        keep = pltpu.make_async_copy(held, stored, refs.pop(0))
        keep.start()
    factor = HEAD_SIZE ** (-0.5) * LOG2E
    keys = cap * page_len
    rows = groups * suffix
    filled = [0] * results
    spots = []
    for job in jobs:
        spots.append(filled[job[-1]])
        filled[job[-1]] += 1

    def stacked(n, part, h):
        return jnp.concatenate([held[meta[n, c], part, :, block_of(h)] for c in range(cap)], 0)

    def score(i):
        n, array, first, h, _ = jobs[i]
        q_ref = queries[array]
        q = jnp.concatenate([q_ref[:, block_of(first * groups + g)] for g in range(groups)], 0)
        scores[i % 2] = dot_nt(q, stacked(n, 0, h))
        if own:
            at = iota((rows, suffix), 0) % suffix
            causal = iota((rows, suffix), 1) <= at
            late_scores[i % 2] = jnp.where(causal, dot_nt(q, own_kv[0, :, block_of(h)]), DEAD)

    def weigh(i):
        n, _, _, h, result = jobs[i]
        live = iota((1, keys), 1) < meta[n, cap] * page_len
        s = jnp.where(live, scores[i % 2], DEAD)
        top = jnp.max(s, axis=-1, keepdims=True)
        if own:
            top = jnp.maximum(top, jnp.max(late_scores[i % 2], axis=-1, keepdims=True))
        top = jnp.maximum(top * factor, FLOOR).astype(jnp.bfloat16).astype(jnp.float32)
        p = jnp.exp2(s * factor - top).astype(jnp.bfloat16)
        v = stacked(n, 1, h)
        v = jnp.concatenate([v, jnp.ones_like(v)], 1)
        out = jnp.dot(p, v, preferred_element_type=jnp.float32)
        if own:
            p = jnp.exp2(late_scores[i % 2] * factor - top).astype(jnp.bfloat16)
            v = own_kv[1, :, block_of(h)]
            v = jnp.concatenate([v, jnp.ones_like(v)], 1)
            out = out + jnp.dot(p, v, preferred_element_type=jnp.float32)
        acc_ref, stat_ref = outs[result]
        spot = spots[i]
        acc_ref[spot] = out[:, :HEAD_SIZE]
        total = out[:, HEAD_SIZE:]
        top = jnp.broadcast_to(top, total.shape)
        blocks = [block_of(j) for j in range(rows // HEAD_SIZE)]
        stat_ref[spot] = pack_stats([top[j] for j in blocks], [total[j] for j in blocks])

    for i in range(len(jobs) + 1):
        if i < len(jobs):
            score(i)
        if i > 0:
            weigh(i - 1)
    if keeping:
        keep.wait()


def attend(shape, jobs, meta, queries, held, own=None, keeping=False):
    groups, suffix, cap, page_len = shape
    rows, keys = groups * suffix, cap * page_len
    results = len({job[-1] for job in jobs})
    heads = len(jobs) // results
    shapes, specs = [], []
    for _ in range(results):
        shapes.append(jax.ShapeDtypeStruct((heads, rows, HEAD_SIZE), jnp.float32))
        shapes.append(jax.ShapeDtypeStruct((heads, STAT_ROWS, HEAD_SIZE), jnp.bfloat16))
        specs += [VMEM, VMEM]
    scratch = [pltpu.VMEM((2, rows, keys), jnp.float32)]
    more = [held]
    if own is not None:
        more = [own, held]
        scratch.append(pltpu.VMEM((2, rows, suffix), jnp.float32))
    if keeping:
        shapes.append(jax.ShapeDtypeStruct(held.shape, held.dtype))
        specs.append(HBM)
        scratch.append(pltpu.SemaphoreType.DMA)
    out = pl.pallas_call(
        functools.partial(attend_kernel, shape + (len(queries), own is not None, keeping), jobs),
        out_shape=shapes,
        in_specs=[SMEM] + [VMEM] * (len(queries) + len(more)),
        out_specs=specs,
        scratch_shapes=scratch,
        compiler_params=pltpu.CompilerParams(vmem_limit_bytes=GRANT),
        cost_estimate=pl.CostEstimate(
            flops=len(jobs) * rows * keys * HEAD_SIZE * 8,
            bytes_accessed=len(jobs) * (rows * 6 + keys * 4) * HEAD_SIZE,
            transcendentals=len(jobs) * rows * keys,
        ),
    )(meta, *queries, *more)
    return [(out[2 * n], out[2 * n + 1]) for n in range(results)] + list(out[2 * results:])


def place_kernel(half, column, me_ref, lists_ref, page_ref, old_ref, out_ref, sem):
    me = me_ref[0]
    from_below = (me >= half) == (me % 2 == 0)
    slot = jnp.where(from_below, lists_ref[0, column], lists_ref[1, column])
    copy = pltpu.make_async_copy(page_ref.at[0], out_ref.at[slot], sem)
    copy.start()
    copy.wait()


def place_page(half, column, me, lists, page, store):
    return pl.pallas_call(
        functools.partial(place_kernel, half, column),
        out_shape=jax.ShapeDtypeStruct(store.shape, store.dtype),
        in_specs=[SMEM, SMEM, VMEM, HBM],
        out_specs=HBM,
        scratch_shapes=[pltpu.SemaphoreType.DMA],
        input_output_aliases={3: 0},
        compiler_params=pltpu.CompilerParams(vmem_limit_bytes=GRANT),
        cost_estimate=LIGHT,
    )(me, lists, page, store)


def blend(parts):
    top = functools.reduce(jnp.maximum, [m for _, m, _ in parts])
    scales = [jnp.exp2(m - top) for _, m, _ in parts]
    acc = sum(a * f for (a, _, _), f in zip(parts, scales))
    total = sum(l * f for (_, _, l), f in zip(parts, scales))
    return acc, top, total


def pack_kernel(acc_ref, stat_ref, out_ref):
    heads, rows = acc_ref.shape[:2]
    for h in range(heads):
        out_ref[h, :rows, :] = acc_ref[h].astype(jnp.bfloat16)
        out_ref[h, rows:, :] = stat_ref[h]


def merge_kernel(in_ref, acc_ref, stat_ref, out_ref, out_stat_ref=None):
    heads, rows = acc_ref.shape[:2]
    for h in range(heads):
        in_top, in_total = unpack_stats(in_ref[h, rows:, :])
        my_top, my_total = unpack_stats(stat_ref[h])
        tops, totals = [], []
        for j in range(rows // HEAD_SIZE):
            acc, top, total = blend(
                [
                    (in_ref[h, block_of(j), :].astype(jnp.float32), in_top[j], in_total[j]),
                    (acc_ref[h, block_of(j), :], my_top[j], my_total[j]),
                ]
            )
            out_ref[h, block_of(j), :] = acc.astype(out_ref.dtype)
            tops.append(top)
            totals.append(total)
        if out_stat_ref is None:
            out_ref[h, rows:, :] = pack_stats(tops, totals)
        else:
            out_stat_ref[h] = pack_stats(tops, totals)


def final_kernel(suffix, *refs):
    sides, out_ref = (refs[0:3], refs[3:6]), refs[6]
    for side, (in_ref, acc_ref, stat_ref) in enumerate(sides):
        heads, rows = acc_ref.shape[:2]
        groups = rows // suffix
        for h in range(heads):
            in_top, in_total = unpack_stats(in_ref[h, rows:, :])
            my_top, my_total = unpack_stats(stat_ref[h])
            for j in range(rows // HEAD_SIZE):
                acc, _, total = blend(
                    [
                        (in_ref[h, block_of(j), :].astype(jnp.float32), in_top[j], in_total[j]),
                        (acc_ref[h, block_of(j), :], my_top[j], my_total[j]),
                    ]
                )
                out = (acc / total).astype(jnp.bfloat16)
                for i in range(HEAD_SIZE // suffix):
                    g = (side * heads + h) * groups + j * (HEAD_SIZE // suffix) + i
                    out_ref[0, :, block_of(g)] = out[i * suffix:(i + 1) * suffix]


def call(kernel, shape, *args):
    size = sum(a.size * a.dtype.itemsize for a in args)
    return pl.pallas_call(
        kernel,
        out_shape=shape,
        in_specs=[VMEM] * len(args),
        out_specs=[VMEM] * len(shape) if isinstance(shape, list) else VMEM,
        compiler_params=pltpu.CompilerParams(vmem_limit_bytes=GRANT),
        cost_estimate=pl.CostEstimate(flops=size, bytes_accessed=2 * size, transcendentals=0),
    )(*args)


def prepare_kernel(cut, cap, pages_dev, length_ref, slot_ref, table_ref, q_ref, first_ref, second_ref):
    maxp = table_ref.shape[1]
    suffix = q_ref.shape[1]
    second_ref[...] = q_ref[0, :, cut:]
    first_ref[:, :cut] = q_ref[0, :, :cut]
    table = table_ref[...]
    owner = lax.div(table, pages_dev)
    local = (table - owner * pages_dev).astype(jnp.float32)
    owner = owner.astype(jnp.float32)
    down, along = iota((maxp, maxp), 0), iota((maxp, maxp), 1)

    def turned(x):
        return jnp.sum(jnp.where(down == along, x, 0.0), 1, keepdims=True)

    before = (turned(owner) == owner) & (along < down)
    rank = jnp.sum(jnp.where(before, 1.0, 0.0), 1, keepdims=True)
    place = iota((maxp, HEAD_SIZE), 1)
    live = jnp.where(iota((maxp, HEAD_SIZE), 0) < length_ref[0], 1.0, 0.0)
    ids = jnp.where(rank == place.astype(jnp.float32), turned(local), 0.0)
    fields = jnp.where(place < cap, ids, jnp.where(place == cap, live, 0.0))
    owned = jnp.where(owner == iota((suffix, maxp), 0).astype(jnp.float32), 1.0, 0.0)
    lists = jnp.dot(
        owned.astype(jnp.bfloat16), fields.astype(jnp.bfloat16), preferred_element_type=jnp.float32
    )
    slot = slot_ref[0].astype(jnp.float32)
    lists = jnp.where(iota(lists.shape, 1) == cap + 1, slot, lists)
    first_ref[:, cut:] = lists.astype(jnp.bfloat16)


def prepare(cut, cap, pages_dev, queries, page_table, prefix_pages, new_slots):
    suffix, columns = queries.shape[1:]
    return pl.pallas_call(
        functools.partial(prepare_kernel, cut, cap, pages_dev),
        out_shape=[
            jax.ShapeDtypeStruct((suffix, cut + HEAD_SIZE), queries.dtype),
            jax.ShapeDtypeStruct((suffix, columns - cut), queries.dtype),
        ],
        in_specs=[SMEM, SMEM, VMEM, VMEM],
        out_specs=[VMEM, VMEM],
        compiler_params=pltpu.CompilerParams(vmem_limit_bytes=GRANT),
        cost_estimate=pl.CostEstimate(flops=1, bytes_accessed=1 << 24, transcendentals=0),
    )(prefix_pages, new_slots, page_table, queries)


def queries_travel(queries, suffix_key_value, kv_pages, page_table, prefix_pages, new_slots):
    stores = lax.axis_size("store")
    pages_dev, _, page_len, width = kv_pages.shape
    maxp = page_table.shape[1]
    cap = maxp // stores
    kv_heads = width // HEAD_SIZE
    suffix = queries.shape[1]
    groups = queries.shape[2] // width
    shape = (groups, suffix, cap, page_len)
    half = stores // 2
    me = lax.axis_index("store")
    heads_each = kv_heads // 2
    cut = heads_each * groups * HEAD_SIZE

    order = list(range(0, stores, 2)) + list(range(1, stores, 2))[::-1]
    up = [(order[i], order[(i + 1) % stores]) for i in range(stores)]
    down = [(order[i], order[i - 1]) for i in range(stores)]
    routes = {1: up, -1: down}

    def listed(*arrays):
        rows = [lax.dynamic_slice(x, (me, cut), (1, HEAD_SIZE)) for x in arrays]
        return jnp.concatenate(rows).astype(jnp.int32)

    def after(values, token):
        return lax.optimization_barrier((values, token))[0]

    mine = prepare(cut, cap, pages_dev, queries, page_table, prefix_pages, new_slots)

    moving = {
        (side, sign): lax.ppermute(mine[side], "store", routes[sign])
        for side in range(2)
        for sign in routes
    }
    held = kv_pages
    parts = {}
    token = []
    lists_of = {}
    sent = {}
    for step in range(1, half):
        for side in range(2):
            came = {sign: after(moving[side, sign], token) for sign in routes}
            for sign in routes:
                if step < half - 1 or (side == 0) == (sign == 1):
                    moving[side, sign] = lax.ppermute(came[sign], "store", routes[sign])
            if side == 0:
                lists_of[step] = listed(came[1], came[-1])
            jobs = [(n, n, h, side * heads_each + h, n) for n in range(2) for h in range(heads_each)]
            got = attend(shape, jobs, lists_of[step], [came[1], came[-1]], held)
            parts[step, side], parts[-step, side] = got
            token = got
            if (step, side) == (half - 2, 1):
                arrived = shifted(after(suffix_key_value, token), "store", half)
            if step == half - 1:
                sign = 1 if side == 1 else -1
                sent["early", sign] = packed(parts[sign * step, side])
                token = sent["early", sign]
    came = after([moving[0, 1], moving[1, -1]], [token, arrived])
    jobs = [(0, side, h, side * heads_each + h, side) for side in range(2) for h in range(heads_each)]
    far = attend(shape, jobs, listed(came[0]), came, held)
    token = far

    back = {1: down, -1: up}
    side_of = {("late", 1): 0, ("late", -1): 1, ("early", 1): 1, ("early", -1): 0}
    flows = {key: lax.ppermute(block, "store", back[key[1]]) for key, block in sent.items()}
    turns = [("late", half)]
    for distance in range(half - 1, 0, -1):
        turns += [("early", distance - 1)] * (distance > 1) + [("late", distance)]
    for flow, distance in turns:
        if distance == half:
            far, ended = lax.optimization_barrier((far, {sign: flows["early", sign] for sign in back}))
            flows.update({("early", sign): ended[sign] for sign in back})
            blocks = {sign: packed(far[side_of[flow, sign]]) for sign in back}
        else:
            came = {sign: flows[flow, sign] for sign in back}
            if distance == 1 and flow == "late":
                ended = {sign: flows["early", sign] for sign in back}
                came, ended = lax.optimization_barrier((came, ended))
                flows.update({("early", sign): ended[sign] for sign in back})
            came = after(came, token)
            blocks = {
                sign: merged(came[sign], parts[sign * distance, side_of[flow, sign]])
                for sign in back
            }
        for sign in back:
            flows[flow, sign] = lax.ppermute(blocks[sign], "store", back[sign])
        token = blocks
        if flow == "early" and distance <= 2:
            side = 2 - distance
            jobs = [(0, 0, h, side * heads_each + h, 0) for h in range(heads_each)]
            parts[0, side], *kept_pages = attend(
                shape,
                jobs,
                listed(mine[0]),
                [after(mine[side], token)],
                held,
                suffix_key_value[0],
                side == 0,
            )
            token = [blocks, parts[0, side]]
            if kept_pages:
                store, = kept_pages
    store = place_page(
        half, cap + 1, me[None], lists_of[stores // 4], arrived, after(store, token)
    )
    rest, late = [None, None], [None, None]
    for sign in (1, -1):
        side = side_of["early", sign]
        rest[side] = kept(after(flows["early", sign], token), parts[0, side])
        late[1 - side] = flows["late", sign]
    attended = call(
        functools.partial(final_kernel, suffix),
        jax.ShapeDtypeStruct(queries.shape, queries.dtype),
        late[0], *rest[0], late[1], *rest[1],
    )
    return (attended, store)


def wire_of(part):
    heads, rows, columns = part[0].shape
    return jax.ShapeDtypeStruct((heads, rows + STAT_ROWS, columns), jnp.bfloat16)


def packed(part):
    return call(pack_kernel, wire_of(part), *part)


def merged(block, part):
    return call(merge_kernel, wire_of(part), block, *part)


def kept(block, part):
    return call(merge_kernel, [jax.ShapeDtypeStruct(x.shape, x.dtype) for x in part], block, *part)


def on_device(queries, suffix_key_value, kv_pages, page_table, prefix_pages, new_slots):
    stores = lax.axis_size("store")
    pulled = page_table.shape[1] // stores * kv_pages[0].size
    pushed = 2 * queries[0].size
    arrays = (queries, suffix_key_value, kv_pages, page_table, prefix_pages, new_slots)
    if pulled >= pushed and stores % 8 == 0:
        return queries_travel(*arrays)
    return pages_travel(*arrays)


def solution(mesh):
    return jax.shard_map(
        on_device,
        mesh=mesh,
        in_specs=(
            P(("groups", "store"), None, "tensor"),
            P(("groups", "store"), None, None, "tensor"),
            P(("groups", "store"), None, None, "tensor"),
            P(("groups", "store"), None),
            P(("groups", "store")),
            P(("groups", "store")),
        ),
        out_specs=(
            P(("groups", "store"), None, "tensor"),
            P(("groups", "store"), None, None, "tensor"),
        ),
        check_vma=False,
    )
```

```python
import functools

import jax
import jax.numpy as jnp
from jax import lax
from jax.experimental import pallas as pl
from jax.experimental.pallas import tpu as pltpu
from jax.sharding import PartitionSpec as P

HEAD_SIZE = 128
LOG2E = 1.4426950408889634
DEAD = -1e30
FLOOR = -1e29
STAT_ROWS = 16
GRANT = 20 * 1024 * 1024
LIGHT = pl.CostEstimate(flops=1, bytes_accessed=1, transcendentals=0)
VMEM = pl.BlockSpec(memory_space=pltpu.VMEM)
SMEM = pl.BlockSpec(memory_space=pltpu.SMEM)
HBM = pl.BlockSpec(memory_space=pltpu.HBM)


def shifted(block, axis, distance):
    devices = range(lax.axis_size(axis))
    route = [((i - distance) % len(devices), i) for i in devices]
    return lax.ppermute(block, axis, route)


def block_update(state, head_count, key_rows, value_rows, live, scale):
    top_old, total_old, acc_old = state
    scores = (
        jnp.einsum("qhgd,khd->hgqk", head_count, key_rows, preferred_element_type=jnp.float32)
        * scale
    )
    scores = jnp.where(live, scores, -1e30)
    top_new = jnp.maximum(top_old, jnp.max(scores, axis=-1))
    weights = jnp.where(live, jnp.exp(scores - top_new[..., None]), 0.0)
    factor = jnp.exp(top_old - top_new)
    total_new = total_old * factor + jnp.sum(weights, axis=-1)
    product = jnp.einsum(
        "hgqk,khd->hgqd",
        weights.astype(jnp.bfloat16),
        value_rows,
        preferred_element_type=jnp.float32,
    )
    return (top_new, total_new, acc_old * factor[..., None] + product)


def pages_travel(queries, suffix_key_value, kv_pages, page_table, prefix_pages, new_slots):
    stores = lax.axis_size("store")
    pages_dev = kv_pages.shape[0]
    maxp = page_table.shape[1]
    cap = maxp // stores
    page_len = kv_pages.shape[2]
    width = kv_pages.shape[3]
    kv_heads = width // HEAD_SIZE
    suffix = queries.shape[1]
    groups_per_head = queries.shape[2] // width
    scale = HEAD_SIZE ** (-0.5)
    length = prefix_pages[0]
    table = page_table[0]
    owners = table // pages_dev
    local_ids = table % pages_dev
    entries = jnp.arange(maxp, dtype=jnp.int32)
    same_owner = (owners[:, None] == owners[None, :]) & (entries[:, None] < entries[None, :])
    ranks = jnp.sum(same_owner.astype(jnp.int32), axis=0)
    slots = owners * cap + ranks
    placed = slots[:, None] == entries[None, :]
    slot_entry = jnp.sum(jnp.where(placed, entries[:, None], 0), axis=0)
    wanted = jnp.sum(jnp.where(placed, local_ids[:, None], 0), axis=0)
    asked = lax.all_to_all(
        wanted.reshape(stores, cap), "store", split_axis=0, concat_axis=0, tiled=True
    )
    served = kv_pages[asked.reshape(-1)].reshape(stores, cap, 2, page_len, width)
    received = lax.all_to_all(served, "store", split_axis=0, concat_axis=0, tiled=True).reshape(
        maxp, 2, page_len, width
    )
    head_count = queries[0].reshape(suffix, kv_heads, groups_per_head, HEAD_SIZE)
    own_keys = suffix_key_value[0, 0].reshape(suffix, kv_heads, HEAD_SIZE)
    own_values = suffix_key_value[0, 1].reshape(suffix, kv_heads, HEAD_SIZE)
    rows = jnp.arange(suffix, dtype=jnp.int32)
    causal = rows[None, :] <= rows[:, None]
    start_state = (
        jnp.full((kv_heads, groups_per_head, suffix), -1e30, jnp.float32),
        jnp.zeros((kv_heads, groups_per_head, suffix), jnp.float32),
        jnp.zeros((kv_heads, groups_per_head, suffix, HEAD_SIZE), jnp.float32),
    )
    state = block_update(start_state, head_count, own_keys, own_values, causal, scale)
    block_pages = min(8, maxp)
    live_pages = slot_entry < length
    trips = maxp // block_pages

    def step_block(index, carry):
        first = index * block_pages
        block = lax.dynamic_slice_in_dim(received, first, block_pages, 0)
        alive = lax.dynamic_slice_in_dim(live_pages, first, block_pages, 0)
        alive = jnp.broadcast_to(alive[:, None], (block_pages, page_len)).reshape(
            1, block_pages * page_len
        )
        block_keys = block[:, 0].reshape(block_pages * page_len, kv_heads, HEAD_SIZE)
        block_values = block[:, 1].reshape(block_pages * page_len, kv_heads, HEAD_SIZE)
        return block_update(carry, head_count, block_keys, block_values, alive, scale)

    top_final, total_final, acc_final = lax.fori_loop(0, trips, step_block, state)
    output = acc_final / total_final[..., None]
    attended = (
        output.transpose(2, 0, 1, 3)
        .reshape(1, suffix, groups_per_head * width)
        .astype(jnp.bfloat16)
    )
    arrived, arrived_slot = shifted((suffix_key_value, new_slots), "store", stores // 2)
    new_store = lax.dynamic_update_slice_in_dim(kv_pages, arrived, arrived_slot[0], 0)
    return (attended, new_store)


def dot_nt(a, b):
    return lax.dot_general(a, b, (((1,), (1,)), ((), ())), preferred_element_type=jnp.float32)


def block_of(j):
    return slice(j * HEAD_SIZE, (j + 1) * HEAD_SIZE)


def iota(shape, dim):
    return lax.broadcasted_iota(jnp.int32, shape, dim)


def pack_stats(top, total):
    diagonal = iota((HEAD_SIZE, HEAD_SIZE), 0) == iota((HEAD_SIZE, HEAD_SIZE), 1)
    row = iota((STAT_ROWS, HEAD_SIZE), 0)
    tile = jnp.zeros((STAT_ROWS, HEAD_SIZE), jnp.float32)

    def along(x):
        return jnp.sum(jnp.where(diagonal, x, 0.0), 0, keepdims=True)

    for j, (m, l) in enumerate(zip(top, total)):
        l = along(l)
        high = l.astype(jnp.bfloat16).astype(jnp.float32)
        for t, x in enumerate((along(m), high, l - high)):
            tile = jnp.where(row == 4 * t + j, x, tile)
    return tile.astype(jnp.bfloat16)


def unpack_stats(tile):
    row = iota((STAT_ROWS, 8 * HEAD_SIZE), 0)
    block = iota((STAT_ROWS, 8 * HEAD_SIZE), 1) // HEAD_SIZE
    j = block // 2
    stat = block % 2
    spread = (
        ((row == j) & (stat == 0)) | ((row == j + 4) & (stat == 1)) | ((row == j + 8) & (stat == 1))
    )
    spread = spread.astype(jnp.float32).astype(jnp.bfloat16)
    turned = tile.astype(jnp.float32).T.astype(jnp.bfloat16)
    wide = jnp.dot(turned, spread, preferred_element_type=jnp.float32)
    part = lambda b: wide[:, b * HEAD_SIZE:(b + 1) * HEAD_SIZE]
    return [part(2 * j) for j in range(4)], [part(2 * j + 1) for j in range(4)]


def attend_kernel(sizes, jobs, *refs):
    groups, suffix, cap, page_len, count, own, keeping = sizes
    refs = list(refs)
    meta = refs.pop(0)
    queries = [refs.pop(0) for _ in range(count)]
    if own:
        own_kv = refs.pop(0)
    held = refs.pop(0)
    results = len({job[-1] for job in jobs})
    outs = [(refs.pop(0), refs.pop(0)) for _ in range(results)]
    stored = refs.pop(0) if keeping else None
    scores = refs.pop(0)
    late_scores = refs.pop(0) if own else None
    if keeping:
        keep = pltpu.make_async_copy(held, stored, refs.pop(0))
        keep.start()
    factor = HEAD_SIZE ** (-0.5) * LOG2E
    keys = cap * page_len
    rows = groups * suffix
    filled = [0] * results
    spots = []
    for job in jobs:
        spots.append(filled[job[-1]])
        filled[job[-1]] += 1

    def stacked(n, part, h):
        return jnp.concatenate([held[meta[n, c], part, :, block_of(h)] for c in range(cap)], 0)

    def score(i):
        n, array, first, h, _ = jobs[i]
        q_ref = queries[array]
        q = jnp.concatenate([q_ref[:, block_of(first * groups + g)] for g in range(groups)], 0)
        scores[i % 2] = dot_nt(q, stacked(n, 0, h))
        if own:
            at = iota((rows, suffix), 0) % suffix
            causal = iota((rows, suffix), 1) <= at
            late_scores[i % 2] = jnp.where(causal, dot_nt(q, own_kv[0, :, block_of(h)]), DEAD)

    def weigh(i):
        n, _, _, h, result = jobs[i]
        live = iota((1, keys), 1) < meta[n, cap] * page_len
        s = jnp.where(live, scores[i % 2], DEAD)
        top = jnp.max(s, axis=-1, keepdims=True)
        if own:
            top = jnp.maximum(top, jnp.max(late_scores[i % 2], axis=-1, keepdims=True))
        top = jnp.maximum(top * factor, FLOOR).astype(jnp.bfloat16).astype(jnp.float32)
        p = jnp.exp2(s * factor - top).astype(jnp.bfloat16)
        v = stacked(n, 1, h)
        v = jnp.concatenate([v, jnp.ones_like(v)], 1)
        out = jnp.dot(p, v, preferred_element_type=jnp.float32)
        if own:
            p = jnp.exp2(late_scores[i % 2] * factor - top).astype(jnp.bfloat16)
            v = own_kv[1, :, block_of(h)]
            v = jnp.concatenate([v, jnp.ones_like(v)], 1)
            out = out + jnp.dot(p, v, preferred_element_type=jnp.float32)
        acc_ref, stat_ref = outs[result]
        spot = spots[i]
        acc_ref[spot] = out[:, :HEAD_SIZE]
        total = out[:, HEAD_SIZE:]
        top = jnp.broadcast_to(top, total.shape)
        blocks = [block_of(j) for j in range(rows // HEAD_SIZE)]
        stat_ref[spot] = pack_stats([top[j] for j in blocks], [total[j] for j in blocks])

    for i in range(len(jobs) + 1):
        if i < len(jobs):
            score(i)
        if i > 0:
            weigh(i - 1)
    if keeping:
        keep.wait()


def attend(shape, jobs, meta, queries, held, own=None, keeping=False):
    groups, suffix, cap, page_len = shape
    rows, keys = groups * suffix, cap * page_len
    results = len({job[-1] for job in jobs})
    heads = len(jobs) // results
    shapes, specs = [], []
    for _ in range(results):
        shapes.append(jax.ShapeDtypeStruct((heads, rows, HEAD_SIZE), jnp.float32))
        shapes.append(jax.ShapeDtypeStruct((heads, STAT_ROWS, HEAD_SIZE), jnp.bfloat16))
        specs += [VMEM, VMEM]
    scratch = [pltpu.VMEM((2, rows, keys), jnp.float32)]
    more = [held]
    if own is not None:
        more = [own, held]
        scratch.append(pltpu.VMEM((2, rows, suffix), jnp.float32))
    if keeping:
        shapes.append(jax.ShapeDtypeStruct(held.shape, held.dtype))
        specs.append(HBM)
        scratch.append(pltpu.SemaphoreType.DMA)
    weight = 16 if own is not None and not keeping else 1
    out = pl.pallas_call(
        functools.partial(attend_kernel, shape + (len(queries), own is not None, keeping), jobs),
        out_shape=shapes,
        in_specs=[SMEM] + [VMEM] * (len(queries) + len(more)),
        out_specs=specs,
        scratch_shapes=scratch,
        compiler_params=pltpu.CompilerParams(vmem_limit_bytes=GRANT),
        cost_estimate=pl.CostEstimate(
            flops=weight * len(jobs) * rows * keys * HEAD_SIZE * 8,
            bytes_accessed=weight * len(jobs) * (rows * 6 + keys * 4) * HEAD_SIZE,
            transcendentals=weight * len(jobs) * rows * keys,
        ),
    )(meta, *queries, *more)
    return [(out[2 * n], out[2 * n + 1]) for n in range(results)] + list(out[2 * results:])


def place_kernel(half, column, me_ref, lists_ref, page_ref, old_ref, out_ref, sem):
    me = me_ref[0]
    from_below = (me >= half) == (me % 2 == 0)
    slot = jnp.where(from_below, lists_ref[0, column], lists_ref[1, column])
    copy = pltpu.make_async_copy(page_ref.at[0], out_ref.at[slot], sem)
    copy.start()
    copy.wait()


def place_page(half, column, me, lists, page, store):
    return pl.pallas_call(
        functools.partial(place_kernel, half, column),
        out_shape=jax.ShapeDtypeStruct(store.shape, store.dtype),
        in_specs=[SMEM, SMEM, VMEM, HBM],
        out_specs=HBM,
        scratch_shapes=[pltpu.SemaphoreType.DMA],
        input_output_aliases={3: 0},
        compiler_params=pltpu.CompilerParams(vmem_limit_bytes=GRANT),
        cost_estimate=LIGHT,
    )(me, lists, page, store)


def blend(parts):
    top = functools.reduce(jnp.maximum, [m for _, m, _ in parts])
    scales = [jnp.exp2(m - top) for _, m, _ in parts]
    acc = sum(a * f for (a, _, _), f in zip(parts, scales))
    total = sum(l * f for (_, _, l), f in zip(parts, scales))
    return acc, top, total


def pack_kernel(acc_ref, stat_ref, out_ref):
    heads, rows = acc_ref.shape[:2]
    for h in range(heads):
        out_ref[h, :rows, :] = acc_ref[h].astype(jnp.bfloat16)
        out_ref[h, rows:, :] = stat_ref[h]


def merge_kernel(in_ref, acc_ref, stat_ref, out_ref, out_stat_ref=None):
    heads, rows = acc_ref.shape[:2]
    for h in range(heads):
        in_top, in_total = unpack_stats(in_ref[h, rows:, :])
        my_top, my_total = unpack_stats(stat_ref[h])
        tops, totals = [], []
        for j in range(rows // HEAD_SIZE):
            acc, top, total = blend(
                [
                    (in_ref[h, block_of(j), :].astype(jnp.float32), in_top[j], in_total[j]),
                    (acc_ref[h, block_of(j), :], my_top[j], my_total[j]),
                ]
            )
            out_ref[h, block_of(j), :] = acc.astype(out_ref.dtype)
            tops.append(top)
            totals.append(total)
        if out_stat_ref is None:
            out_ref[h, rows:, :] = pack_stats(tops, totals)
        else:
            out_stat_ref[h] = pack_stats(tops, totals)


def final_kernel(suffix, *refs):
    sides, out_ref = (refs[0:3], refs[3:6]), refs[6]
    for side, (in_ref, acc_ref, stat_ref) in enumerate(sides):
        heads, rows = acc_ref.shape[:2]
        groups = rows // suffix
        for h in range(heads):
            in_top, in_total = unpack_stats(in_ref[h, rows:, :])
            my_top, my_total = unpack_stats(stat_ref[h])
            for j in range(rows // HEAD_SIZE):
                acc, _, total = blend(
                    [
                        (in_ref[h, block_of(j), :].astype(jnp.float32), in_top[j], in_total[j]),
                        (acc_ref[h, block_of(j), :], my_top[j], my_total[j]),
                    ]
                )
                out = (acc / total).astype(jnp.bfloat16)
                for i in range(HEAD_SIZE // suffix):
                    g = (side * heads + h) * groups + j * (HEAD_SIZE // suffix) + i
                    out_ref[0, :, block_of(g)] = out[i * suffix:(i + 1) * suffix]


def call(kernel, shape, *args):
    size = sum(a.size * a.dtype.itemsize for a in args)
    return pl.pallas_call(
        kernel,
        out_shape=shape,
        in_specs=[VMEM] * len(args),
        out_specs=[VMEM] * len(shape) if isinstance(shape, list) else VMEM,
        compiler_params=pltpu.CompilerParams(vmem_limit_bytes=GRANT),
        cost_estimate=pl.CostEstimate(flops=size, bytes_accessed=2 * size, transcendentals=0),
    )(*args)


def prepare_kernel(cut, cap, pages_dev, length_ref, slot_ref, table_ref, q_ref, first_ref, second_ref):
    maxp = table_ref.shape[1]
    suffix = q_ref.shape[1]
    second_ref[...] = q_ref[0, :, cut:]
    first_ref[:, :cut] = q_ref[0, :, :cut]
    table = table_ref[...]
    owner = lax.div(table, pages_dev)
    local = (table - owner * pages_dev).astype(jnp.float32)
    owner = owner.astype(jnp.float32)
    down, along = iota((maxp, maxp), 0), iota((maxp, maxp), 1)

    def turned(x):
        return jnp.sum(jnp.where(down == along, x, 0.0), 1, keepdims=True)

    before = (turned(owner) == owner) & (along < down)
    rank = jnp.sum(jnp.where(before, 1.0, 0.0), 1, keepdims=True)
    place = iota((maxp, HEAD_SIZE), 1)
    live = jnp.where(iota((maxp, HEAD_SIZE), 0) < length_ref[0], 1.0, 0.0)
    ids = jnp.where(rank == place.astype(jnp.float32), turned(local), 0.0)
    fields = jnp.where(place < cap, ids, jnp.where(place == cap, live, 0.0))
    owned = jnp.where(owner == iota((suffix, maxp), 0).astype(jnp.float32), 1.0, 0.0)
    lists = jnp.dot(
        owned.astype(jnp.bfloat16), fields.astype(jnp.bfloat16), preferred_element_type=jnp.float32
    )
    slot = slot_ref[0].astype(jnp.float32)
    lists = jnp.where(iota(lists.shape, 1) == cap + 1, slot, lists)
    first_ref[:, cut:] = lists.astype(jnp.bfloat16)


def prepare(cut, cap, pages_dev, queries, page_table, prefix_pages, new_slots):
    suffix, columns = queries.shape[1:]
    return pl.pallas_call(
        functools.partial(prepare_kernel, cut, cap, pages_dev),
        out_shape=[
            jax.ShapeDtypeStruct((suffix, cut + HEAD_SIZE), queries.dtype),
            jax.ShapeDtypeStruct((suffix, columns - cut), queries.dtype),
        ],
        in_specs=[SMEM, SMEM, VMEM, VMEM],
        out_specs=[VMEM, VMEM],
        compiler_params=pltpu.CompilerParams(vmem_limit_bytes=GRANT),
    )(prefix_pages, new_slots, page_table, queries)


def queries_travel(queries, suffix_key_value, kv_pages, page_table, prefix_pages, new_slots):
    stores = lax.axis_size("store")
    pages_dev, _, page_len, width = kv_pages.shape
    maxp = page_table.shape[1]
    cap = maxp // stores
    kv_heads = width // HEAD_SIZE
    suffix = queries.shape[1]
    groups = queries.shape[2] // width
    shape = (groups, suffix, cap, page_len)
    half = stores // 2
    me = lax.axis_index("store")
    heads_each = kv_heads // 2
    cut = heads_each * groups * HEAD_SIZE

    order = list(range(0, stores, 2)) + list(range(1, stores, 2))[::-1]
    up = [(order[i], order[(i + 1) % stores]) for i in range(stores)]
    down = [(order[i], order[i - 1]) for i in range(stores)]
    routes = {1: up, -1: down}

    def listed(*arrays):
        rows = [lax.dynamic_slice(x, (me, cut), (1, HEAD_SIZE)) for x in arrays]
        return jnp.concatenate(rows).astype(jnp.int32)

    def after(values, token):
        return lax.optimization_barrier((values, token))[0]

    arrived = shifted(suffix_key_value, "store", half)
    mine = prepare(cut, cap, pages_dev, queries, page_table, prefix_pages, new_slots)

    moving = {
        (side, sign): lax.ppermute(mine[side], "store", routes[sign])
        for side in range(2)
        for sign in routes
    }
    held = kv_pages
    parts = {}

    def attend_own(side, token, keeping):
        jobs = [(0, 0, h, side * heads_each + h, 0) for h in range(heads_each)]
        lists = listed(mine[0])
        own = suffix_key_value[0]
        parts[0, side], *pages = attend(
            shape, jobs, lists, [after(mine[side], token)], held, own, keeping
        )
        return pages

    attend_own(0, arrived, False)
    token = parts[0, 0]
    lists_of = {}
    sent = {}
    for step in range(1, half):
        for side in range(2):
            came = {sign: after(moving[side, sign], token) for sign in routes}
            for sign in routes:
                if step < half - 1 or (side == 0) == (sign == 1):
                    moving[side, sign] = lax.ppermute(came[sign], "store", routes[sign])
            if side == 0:
                lists_of[step] = listed(came[1], came[-1])
            jobs = [(n, n, h, side * heads_each + h, n) for n in range(2) for h in range(heads_each)]
            got = attend(shape, jobs, lists_of[step], [came[1], came[-1]], held)
            parts[step, side], parts[-step, side] = got
            token = got
            if step == half - 1:
                sign = 1 if side == 1 else -1
                sent["early", sign] = packed(parts[sign * step, side])
                token = sent["early", sign]
    came = after([moving[0, 1], moving[1, -1]], token)
    jobs = [(0, side, h, side * heads_each + h, side) for side in range(2) for h in range(heads_each)]
    far = attend(shape, jobs, listed(came[0]), came, held)
    token = far

    back = {1: down, -1: up}
    side_of = {("late", 1): 0, ("late", -1): 1, ("early", 1): 1, ("early", -1): 0}
    flows = {key: lax.ppermute(block, "store", back[key[1]]) for key, block in sent.items()}
    turns = [("late", half)]
    for distance in range(half - 1, 0, -1):
        turns += [("early", distance - 1)] * (distance > 1) + [("late", distance)]
    for flow, distance in turns:
        if distance == half:
            blocks = {sign: packed(far[side_of[flow, sign]]) for sign in back}
        else:
            came = {sign: flows[flow, sign] for sign in back}
            if distance == 1 and flow == "late":
                ended = {sign: flows["early", sign] for sign in back}
                came, ended = lax.optimization_barrier((came, ended))
                flows.update({("early", sign): ended[sign] for sign in back})
            came = after(came, token)
            blocks = {
                sign: merged(came[sign], parts[sign * distance, side_of[flow, sign]])
                for sign in back
            }
        for sign in back:
            flows[flow, sign] = lax.ppermute(blocks[sign], "store", back[sign])
        token = blocks
        if flow == "early" and distance == 1:
            (store,) = attend_own(1, token, True)
            token = [token, store]
    store = place_page(
        half, cap + 1, me[None], lists_of[stores // 4], arrived, after(store, token)
    )
    rest, late = [None, None], [None, None]
    for sign in (1, -1):
        side = side_of["early", sign]
        rest[side] = kept(after(flows["early", sign], token), parts[0, side])
        late[1 - side] = flows["late", sign]
    attended = call(
        functools.partial(final_kernel, suffix),
        jax.ShapeDtypeStruct(queries.shape, queries.dtype),
        late[0], *rest[0], late[1], *rest[1],
    )
    return (attended, store)


def wire_of(part):
    heads, rows, columns = part[0].shape
    return jax.ShapeDtypeStruct((heads, rows + STAT_ROWS, columns), jnp.bfloat16)


def packed(part):
    return call(pack_kernel, wire_of(part), *part)


def merged(block, part):
    return call(merge_kernel, wire_of(part), block, *part)


def kept(block, part):
    return call(merge_kernel, [jax.ShapeDtypeStruct(x.shape, x.dtype) for x in part], block, *part)


def on_device(queries, suffix_key_value, kv_pages, page_table, prefix_pages, new_slots):
    stores = lax.axis_size("store")
    pulled = page_table.shape[1] // stores * kv_pages[0].size
    pushed = 2 * queries[0].size
    arrays = (queries, suffix_key_value, kv_pages, page_table, prefix_pages, new_slots)
    if pulled >= pushed and stores % 8 == 0:
        return queries_travel(*arrays)
    return pages_travel(*arrays)


def solution(mesh):
    return jax.shard_map(
        on_device,
        mesh=mesh,
        in_specs=(
            P(("groups", "store"), None, "tensor"),
            P(("groups", "store"), None, None, "tensor"),
            P(("groups", "store"), None, None, "tensor"),
            P(("groups", "store"), None),
            P(("groups", "store")),
            P(("groups", "store")),
        ),
        out_specs=(
            P(("groups", "store"), None, "tensor"),
            P(("groups", "store"), None, None, "tensor"),
        ),
        check_vma=False,
    )
```

```python
import functools

import jax
import jax.numpy as jnp
from jax import lax
from jax.experimental import pallas as pl
from jax.experimental.pallas import tpu as pltpu
from jax.sharding import PartitionSpec as P

HEAD_SIZE = 128
LOG2E = 1.4426950408889634
DEAD = -1e30
FLOOR = -1e29
STAT_ROWS = 16
LIST_ROWS = 16
GRANT = 20 * 1024 * 1024
LIGHT = pl.CostEstimate(flops=1, bytes_accessed=1, transcendentals=0)
VMEM = pl.BlockSpec(memory_space=pltpu.VMEM)
SMEM = pl.BlockSpec(memory_space=pltpu.SMEM)
HBM = pl.BlockSpec(memory_space=pltpu.HBM)


def shifted(block, axis, distance):
    devices = range(lax.axis_size(axis))
    route = [((i - distance) % len(devices), i) for i in devices]
    return lax.ppermute(block, axis, route)


def block_update(state, head_count, key_rows, value_rows, live, scale):
    top_old, total_old, acc_old = state
    scores = (
        jnp.einsum("qhgd,khd->hgqk", head_count, key_rows, preferred_element_type=jnp.float32)
        * scale
    )
    scores = jnp.where(live, scores, -1e30)
    top_new = jnp.maximum(top_old, jnp.max(scores, axis=-1))
    weights = jnp.where(live, jnp.exp(scores - top_new[..., None]), 0.0)
    factor = jnp.exp(top_old - top_new)
    total_new = total_old * factor + jnp.sum(weights, axis=-1)
    product = jnp.einsum(
        "hgqk,khd->hgqd",
        weights.astype(jnp.bfloat16),
        value_rows,
        preferred_element_type=jnp.float32,
    )
    return (top_new, total_new, acc_old * factor[..., None] + product)


def pages_travel(queries, suffix_key_value, kv_pages, page_table, prefix_pages, new_slots):
    stores = lax.axis_size("store")
    pages_dev = kv_pages.shape[0]
    maxp = page_table.shape[1]
    cap = maxp // stores
    page_len = kv_pages.shape[2]
    width = kv_pages.shape[3]
    kv_heads = width // HEAD_SIZE
    suffix = queries.shape[1]
    groups_per_head = queries.shape[2] // width
    scale = HEAD_SIZE ** (-0.5)
    length = prefix_pages[0]
    table = page_table[0]
    owners = table // pages_dev
    local_ids = table % pages_dev
    entries = jnp.arange(maxp, dtype=jnp.int32)
    same_owner = (owners[:, None] == owners[None, :]) & (entries[:, None] < entries[None, :])
    ranks = jnp.sum(same_owner.astype(jnp.int32), axis=0)
    slots = owners * cap + ranks
    placed = slots[:, None] == entries[None, :]
    slot_entry = jnp.sum(jnp.where(placed, entries[:, None], 0), axis=0)
    wanted = jnp.sum(jnp.where(placed, local_ids[:, None], 0), axis=0)
    asked = lax.all_to_all(
        wanted.reshape(stores, cap), "store", split_axis=0, concat_axis=0, tiled=True
    )
    served = kv_pages[asked.reshape(-1)].reshape(stores, cap, 2, page_len, width)
    received = lax.all_to_all(served, "store", split_axis=0, concat_axis=0, tiled=True).reshape(
        maxp, 2, page_len, width
    )
    head_count = queries[0].reshape(suffix, kv_heads, groups_per_head, HEAD_SIZE)
    own_keys = suffix_key_value[0, 0].reshape(suffix, kv_heads, HEAD_SIZE)
    own_values = suffix_key_value[0, 1].reshape(suffix, kv_heads, HEAD_SIZE)
    rows = jnp.arange(suffix, dtype=jnp.int32)
    causal = rows[None, :] <= rows[:, None]
    start_state = (
        jnp.full((kv_heads, groups_per_head, suffix), -1e30, jnp.float32),
        jnp.zeros((kv_heads, groups_per_head, suffix), jnp.float32),
        jnp.zeros((kv_heads, groups_per_head, suffix, HEAD_SIZE), jnp.float32),
    )
    state = block_update(start_state, head_count, own_keys, own_values, causal, scale)
    block_pages = min(8, maxp)
    live_pages = slot_entry < length
    trips = maxp // block_pages

    def step_block(index, carry):
        first = index * block_pages
        block = lax.dynamic_slice_in_dim(received, first, block_pages, 0)
        alive = lax.dynamic_slice_in_dim(live_pages, first, block_pages, 0)
        alive = jnp.broadcast_to(alive[:, None], (block_pages, page_len)).reshape(
            1, block_pages * page_len
        )
        block_keys = block[:, 0].reshape(block_pages * page_len, kv_heads, HEAD_SIZE)
        block_values = block[:, 1].reshape(block_pages * page_len, kv_heads, HEAD_SIZE)
        return block_update(carry, head_count, block_keys, block_values, alive, scale)

    top_final, total_final, acc_final = lax.fori_loop(0, trips, step_block, state)
    output = acc_final / total_final[..., None]
    attended = (
        output.transpose(2, 0, 1, 3)
        .reshape(1, suffix, groups_per_head * width)
        .astype(jnp.bfloat16)
    )
    arrived, arrived_slot = shifted((suffix_key_value, new_slots), "store", stores // 2)
    new_store = lax.dynamic_update_slice_in_dim(kv_pages, arrived, arrived_slot[0], 0)
    return (attended, new_store)


def dot_nt(a, b):
    return lax.dot_general(a, b, (((1,), (1,)), ((), ())), preferred_element_type=jnp.float32)


def block_of(j):
    return slice(j * HEAD_SIZE, (j + 1) * HEAD_SIZE)


def iota(shape, dim):
    return lax.broadcasted_iota(jnp.int32, shape, dim)


def pack_stats(top, total):
    diagonal = iota((HEAD_SIZE, HEAD_SIZE), 0) == iota((HEAD_SIZE, HEAD_SIZE), 1)
    row = iota((STAT_ROWS, HEAD_SIZE), 0)
    tile = jnp.zeros((STAT_ROWS, HEAD_SIZE), jnp.float32)

    def along(x):
        return jnp.sum(jnp.where(diagonal, x, 0.0), 0, keepdims=True)

    for j, (m, l) in enumerate(zip(top, total)):
        l = along(l)
        high = l.astype(jnp.bfloat16).astype(jnp.float32)
        for t, x in enumerate((along(m), high, l - high)):
            tile = jnp.where(row == 4 * t + j, x, tile)
    return tile.astype(jnp.bfloat16)


def unpack_stats(tile):
    row = iota((STAT_ROWS, 8 * HEAD_SIZE), 0)
    block = iota((STAT_ROWS, 8 * HEAD_SIZE), 1) // HEAD_SIZE
    j = block // 2
    stat = block % 2
    spread = (
        ((row == j) & (stat == 0)) | ((row == j + 4) & (stat == 1)) | ((row == j + 8) & (stat == 1))
    )
    spread = spread.astype(jnp.float32).astype(jnp.bfloat16)
    turned = tile.astype(jnp.float32).T.astype(jnp.bfloat16)
    wide = jnp.dot(turned, spread, preferred_element_type=jnp.float32)
    part = lambda b: wide[:, b * HEAD_SIZE:(b + 1) * HEAD_SIZE]
    return [part(2 * j) for j in range(4)], [part(2 * j + 1) for j in range(4)]


def attend_kernel(sizes, jobs, *refs):
    groups, suffix, cap, page_len, count, own, keeping = sizes
    refs = list(refs)
    meta = refs.pop(0)
    queries = [refs.pop(0) for _ in range(count)]
    if own:
        own_kv = refs.pop(0)
    held = refs.pop(0)
    results = len({job[-1] for job in jobs})
    outs = [(refs.pop(0), refs.pop(0)) for _ in range(results)]
    stored = refs.pop(0) if keeping else None
    scores = refs.pop(0)
    late_scores = refs.pop(0) if own else None
    if keeping:
        keep = pltpu.make_async_copy(held, stored, refs.pop(0))
        keep.start()
    factor = HEAD_SIZE ** (-0.5) * LOG2E
    keys = cap * page_len
    rows = groups * suffix
    filled = [0] * results
    spots = []
    for job in jobs:
        spots.append(filled[job[-1]])
        filled[job[-1]] += 1

    def stacked(n, part, h):
        return jnp.concatenate([held[meta[n, c], part, :, block_of(h)] for c in range(cap)], 0)

    def score(i):
        n, array, first, h, _ = jobs[i]
        q_ref = queries[array]
        q = q_ref[first * rows:(first + 1) * rows, :]
        scores[i % 2] = dot_nt(q, stacked(n, 0, h))
        if own:
            at = iota((rows, suffix), 0) % suffix
            causal = iota((rows, suffix), 1) <= at
            late_scores[i % 2] = jnp.where(causal, dot_nt(q, own_kv[0, :, block_of(h)]), DEAD)

    def weigh(i):
        n, _, _, h, result = jobs[i]
        live = iota((1, keys), 1) < meta[n, cap] * page_len
        s = jnp.where(live, scores[i % 2], DEAD)
        top = jnp.max(s, axis=-1, keepdims=True)
        if own:
            top = jnp.maximum(top, jnp.max(late_scores[i % 2], axis=-1, keepdims=True))
        top = jnp.maximum(top * factor, FLOOR).astype(jnp.bfloat16).astype(jnp.float32)
        p = jnp.exp2(s * factor - top).astype(jnp.bfloat16)
        v = stacked(n, 1, h)
        v = jnp.concatenate([v, jnp.ones_like(v)], 1)
        out = jnp.dot(p, v, preferred_element_type=jnp.float32)
        if own:
            p = jnp.exp2(late_scores[i % 2] * factor - top).astype(jnp.bfloat16)
            v = own_kv[1, :, block_of(h)]
            v = jnp.concatenate([v, jnp.ones_like(v)], 1)
            out = out + jnp.dot(p, v, preferred_element_type=jnp.float32)
        acc_ref, stat_ref = outs[result]
        spot = spots[i]
        acc_ref[spot] = out[:, :HEAD_SIZE]
        total = out[:, HEAD_SIZE:]
        top = jnp.broadcast_to(top, total.shape)
        blocks = [block_of(j) for j in range(rows // HEAD_SIZE)]
        stat_ref[spot] = pack_stats([top[j] for j in blocks], [total[j] for j in blocks])

    for i in range(len(jobs) + 1):
        if i < len(jobs):
            score(i)
        if i > 0:
            weigh(i - 1)
    if keeping:
        keep.wait()


def attend(shape, jobs, meta, queries, held, own=None, keeping=False):
    groups, suffix, cap, page_len = shape
    rows, keys = groups * suffix, cap * page_len
    results = len({job[-1] for job in jobs})
    heads = len(jobs) // results
    shapes, specs = [], []
    for _ in range(results):
        shapes.append(jax.ShapeDtypeStruct((heads, rows, HEAD_SIZE), jnp.float32))
        shapes.append(jax.ShapeDtypeStruct((heads, STAT_ROWS, HEAD_SIZE), jnp.bfloat16))
        specs += [VMEM, VMEM]
    scratch = [pltpu.VMEM((2, rows, keys), jnp.float32)]
    more = [held]
    if own is not None:
        more = [own, held]
        scratch.append(pltpu.VMEM((2, rows, suffix), jnp.float32))
    if keeping:
        shapes.append(jax.ShapeDtypeStruct(held.shape, held.dtype))
        specs.append(HBM)
        scratch.append(pltpu.SemaphoreType.DMA)
    weight = 16 if own is not None and not keeping else 1
    out = pl.pallas_call(
        functools.partial(attend_kernel, shape + (len(queries), own is not None, keeping), jobs),
        out_shape=shapes,
        in_specs=[SMEM] + [VMEM] * (len(queries) + len(more)),
        out_specs=specs,
        scratch_shapes=scratch,
        compiler_params=pltpu.CompilerParams(vmem_limit_bytes=GRANT),
        cost_estimate=pl.CostEstimate(
            flops=weight * len(jobs) * rows * keys * HEAD_SIZE * 8,
            bytes_accessed=weight * len(jobs) * (rows * 6 + keys * 4) * HEAD_SIZE,
            transcendentals=weight * len(jobs) * rows * keys,
        ),
    )(meta, *queries, *more)
    return [(out[2 * n], out[2 * n + 1]) for n in range(results)] + list(out[2 * results:])


def place_kernel(half, column, me_ref, lists_ref, page_ref, old_ref, out_ref, sem):
    me = me_ref[0]
    from_below = (me >= half) == (me % 2 == 0)
    slot = jnp.where(from_below, lists_ref[0, column], lists_ref[1, column])
    copy = pltpu.make_async_copy(page_ref.at[0], out_ref.at[slot], sem)
    copy.start()
    copy.wait()


def place_page(half, column, me, lists, page, store):
    return pl.pallas_call(
        functools.partial(place_kernel, half, column),
        out_shape=jax.ShapeDtypeStruct(store.shape, store.dtype),
        in_specs=[SMEM, SMEM, VMEM, HBM],
        out_specs=HBM,
        scratch_shapes=[pltpu.SemaphoreType.DMA],
        input_output_aliases={3: 0},
        compiler_params=pltpu.CompilerParams(vmem_limit_bytes=GRANT),
        cost_estimate=LIGHT,
    )(me, lists, page, store)


def blend(parts):
    top = functools.reduce(jnp.maximum, [m for _, m, _ in parts])
    scales = [jnp.exp2(m - top) for _, m, _ in parts]
    acc = sum(a * f for (a, _, _), f in zip(parts, scales))
    total = sum(l * f for (_, _, l), f in zip(parts, scales))
    return acc, top, total


def pack_kernel(acc_ref, stat_ref, out_ref):
    heads, rows = acc_ref.shape[:2]
    for h in range(heads):
        out_ref[h, :rows, :] = acc_ref[h].astype(jnp.bfloat16)
        out_ref[h, rows:, :] = stat_ref[h]


def merge_kernel(in_ref, acc_ref, stat_ref, out_ref, out_stat_ref=None):
    heads, rows = acc_ref.shape[:2]
    for h in range(heads):
        in_top, in_total = unpack_stats(in_ref[h, rows:, :])
        my_top, my_total = unpack_stats(stat_ref[h])
        tops, totals = [], []
        for j in range(rows // HEAD_SIZE):
            acc, top, total = blend(
                [
                    (in_ref[h, block_of(j), :].astype(jnp.float32), in_top[j], in_total[j]),
                    (acc_ref[h, block_of(j), :], my_top[j], my_total[j]),
                ]
            )
            out_ref[h, block_of(j), :] = acc.astype(out_ref.dtype)
            tops.append(top)
            totals.append(total)
        if out_stat_ref is None:
            out_ref[h, rows:, :] = pack_stats(tops, totals)
        else:
            out_stat_ref[h] = pack_stats(tops, totals)


def final_kernel(suffix, *refs):
    sides, (out_ref, done, sems) = (refs[0:3], refs[3:6]), refs[6:]
    copies = []
    for side, (in_ref, acc_ref, stat_ref) in enumerate(sides):
        heads, rows = acc_ref.shape[:2]
        groups = rows // suffix
        for h in range(heads):
            in_top, in_total = unpack_stats(in_ref[h, rows:, :])
            my_top, my_total = unpack_stats(stat_ref[h])
            for j in range(rows // HEAD_SIZE):
                acc, _, total = blend(
                    [
                        (in_ref[h, block_of(j), :].astype(jnp.float32), in_top[j], in_total[j]),
                        (acc_ref[h, block_of(j), :], my_top[j], my_total[j]),
                    ]
                )
                out = (acc / total).astype(jnp.bfloat16)
                for i in range(HEAD_SIZE // suffix):
                    g = (side * heads + h) * groups + j * (HEAD_SIZE // suffix) + i
                    done[0, :, block_of(g)] = out[i * suffix:(i + 1) * suffix]
            head = side * heads + h
            span = pl.ds(head * groups * HEAD_SIZE, groups * HEAD_SIZE)
            copies.append(
                pltpu.make_async_copy(done.at[:, :, span], out_ref.at[:, :, span], sems.at[head])
            )
            copies[-1].start()
    for copy in copies:
        copy.wait()


def finish(suffix, like, *args):
    heads = sum(x.shape[0] for x in args[1::3])
    return pl.pallas_call(
        functools.partial(final_kernel, suffix),
        out_shape=jax.ShapeDtypeStruct(like.shape, like.dtype),
        in_specs=[VMEM] * len(args),
        out_specs=HBM,
        scratch_shapes=[
            pltpu.VMEM(like.shape, like.dtype),
            pltpu.SemaphoreType.DMA((heads,)),
        ],
        compiler_params=pltpu.CompilerParams(vmem_limit_bytes=GRANT),
    )(*args)


def call(kernel, shape, *args):
    size = sum(a.size * a.dtype.itemsize for a in args)
    return pl.pallas_call(
        kernel,
        out_shape=shape,
        in_specs=[VMEM] * len(args),
        out_specs=[VMEM] * len(shape) if isinstance(shape, list) else VMEM,
        compiler_params=pltpu.CompilerParams(vmem_limit_bytes=GRANT),
        cost_estimate=pl.CostEstimate(flops=size, bytes_accessed=2 * size, transcendentals=0),
    )(*args)


def prepare_kernel(cap, pages_dev, length_ref, slot_ref, table_ref, q_ref, first_ref, second_ref):
    maxp = table_ref.shape[1]
    suffix = q_ref.shape[1]
    rows = second_ref.shape[0]
    blocks = rows // suffix
    for g in range(blocks):
        into = slice(g * suffix, (g + 1) * suffix)
        first_ref[into, :] = q_ref[0, :, block_of(g)]
        second_ref[into, :] = q_ref[0, :, block_of(blocks + g)]
    table = table_ref[...]
    owner = lax.div(table, pages_dev)
    local = (table - owner * pages_dev).astype(jnp.float32)
    owner = owner.astype(jnp.float32)
    down, along = iota((maxp, maxp), 0), iota((maxp, maxp), 1)

    def turned(x):
        return jnp.sum(jnp.where(down == along, x, 0.0), 1, keepdims=True)

    before = (turned(owner) == owner) & (along < down)
    rank = jnp.sum(jnp.where(before, 1.0, 0.0), 1, keepdims=True)
    place = iota((maxp, HEAD_SIZE), 1)
    live = jnp.where(iota((maxp, HEAD_SIZE), 0) < length_ref[0], 1.0, 0.0)
    ids = jnp.where(rank == place.astype(jnp.float32), turned(local), 0.0)
    fields = jnp.where(place < cap, ids, jnp.where(place == cap, live, 0.0))
    owned = jnp.where(owner == iota((LIST_ROWS, maxp), 0).astype(jnp.float32), 1.0, 0.0)
    lists = jnp.dot(
        owned.astype(jnp.bfloat16), fields.astype(jnp.bfloat16), preferred_element_type=jnp.float32
    )
    slot = slot_ref[0].astype(jnp.float32)
    lists = jnp.where(iota(lists.shape, 1) == cap + 1, slot, lists)
    first_ref[rows:, :] = lists.astype(jnp.bfloat16)


def prepare(cap, pages_dev, queries, page_table, prefix_pages, new_slots):
    rows = queries.size // HEAD_SIZE // 2
    return pl.pallas_call(
        functools.partial(prepare_kernel, cap, pages_dev),
        out_shape=[
            jax.ShapeDtypeStruct((rows + LIST_ROWS, HEAD_SIZE), queries.dtype),
            jax.ShapeDtypeStruct((rows, HEAD_SIZE), queries.dtype),
        ],
        in_specs=[SMEM, SMEM, VMEM, VMEM],
        out_specs=[VMEM, VMEM],
        compiler_params=pltpu.CompilerParams(vmem_limit_bytes=GRANT),
    )(prefix_pages, new_slots, page_table, queries)


def queries_travel(queries, suffix_key_value, kv_pages, page_table, prefix_pages, new_slots):
    stores = lax.axis_size("store")
    pages_dev, _, page_len, width = kv_pages.shape
    maxp = page_table.shape[1]
    cap = maxp // stores
    kv_heads = width // HEAD_SIZE
    suffix = queries.shape[1]
    groups = queries.shape[2] // width
    shape = (groups, suffix, cap, page_len)
    half = stores // 2
    me = lax.axis_index("store")
    heads_each = kv_heads // 2
    below = heads_each * groups * suffix

    order = list(range(0, stores, 2)) + list(range(1, stores, 2))[::-1]
    up = [(order[i], order[(i + 1) % stores]) for i in range(stores)]
    down = [(order[i], order[i - 1]) for i in range(stores)]
    routes = {1: up, -1: down}

    def listed(*arrays):
        rows = [lax.dynamic_slice(x, (below + me, 0), (1, HEAD_SIZE)) for x in arrays]
        return jnp.concatenate(rows).astype(jnp.int32)

    def after(values, token):
        return lax.optimization_barrier((values, token))[0]

    mine = prepare(cap, pages_dev, queries, page_table, prefix_pages, new_slots)
    arrived = shifted(after(suffix_key_value, mine), "store", half)

    moving = {
        (side, sign): lax.ppermute(mine[side], "store", routes[sign])
        for side in range(2)
        for sign in routes
    }
    held = kv_pages
    parts = {}

    def attend_own(side, token, keeping):
        jobs = [(0, 0, h, side * heads_each + h, 0) for h in range(heads_each)]
        lists = listed(mine[0])
        own = suffix_key_value[0]
        parts[0, side], *pages = attend(
            shape, jobs, lists, [after(mine[side], token)], held, own, keeping
        )
        return pages

    attend_own(0, arrived, False)
    token = parts[0, 0]
    lists_of = {}
    sent = {}
    for step in range(1, half):
        for side in range(2):
            came = {sign: after(moving[side, sign], token) for sign in routes}
            for sign in routes:
                if step < half - 1 or (side == 0) == (sign == 1):
                    moving[side, sign] = lax.ppermute(came[sign], "store", routes[sign])
            if side == 0:
                lists_of[step] = listed(came[1], came[-1])
            jobs = [(n, n, h, side * heads_each + h, n) for n in range(2) for h in range(heads_each)]
            got = attend(shape, jobs, lists_of[step], [came[1], came[-1]], held)
            parts[step, side], parts[-step, side] = got
            token = got
            if step == half - 1:
                sign = 1 if side == 1 else -1
                sent["early", sign] = packed(parts[sign * step, side])
                token = sent["early", sign]
    lists, far = None, []
    for side, sign in ((0, 1), (1, -1)):
        came = after(moving[side, sign], token)
        lists = listed(came) if side == 0 else lists
        jobs = [(0, 0, h, side * heads_each + h, 0) for h in range(heads_each)]
        part, = attend(shape, jobs, lists, [came], held)
        far.append(packed(part))
        token = far

    back = {1: down, -1: up}
    side_of = {("late", 1): 0, ("late", -1): 1, ("early", 1): 1, ("early", -1): 0}
    flows = {key: lax.ppermute(block, "store", back[key[1]]) for key, block in sent.items()}
    turns = [("late", half)]
    for distance in range(half - 1, 0, -1):
        turns += [("early", distance - 1)] * (distance > 1) + [("late", distance)]
    for flow, distance in turns:
        if distance == half:
            blocks = {sign: far[side_of[flow, sign]] for sign in back}
        else:
            came = {sign: flows[flow, sign] for sign in back}
            if distance == 1 and flow == "late":
                ended = {sign: flows["early", sign] for sign in back}
                came, ended = lax.optimization_barrier((came, ended))
                flows.update({("early", sign): ended[sign] for sign in back})
            came = after(came, token)
            blocks = {
                sign: merged(came[sign], parts[sign * distance, side_of[flow, sign]])
                for sign in back
            }
        for sign in back:
            flows[flow, sign] = lax.ppermute(blocks[sign], "store", back[sign])
        token = blocks
        if flow == "late" and distance == 2:
            (store,) = attend_own(1, token, True)
            token = [token, store]
    store = place_page(
        half, cap + 1, me[None], lists_of[stores // 4], arrived, after(store, token)
    )
    rest, late = [None, None], [None, None]
    for sign in (1, -1):
        side = side_of["early", sign]
        rest[side] = kept(after(flows["early", sign], token), parts[0, side])
        late[1 - side] = flows["late", sign]
    attended = finish(suffix, queries, late[0], *rest[0], late[1], *rest[1])
    return (attended, store)


def wire_of(part):
    heads, rows, columns = part[0].shape
    return jax.ShapeDtypeStruct((heads, rows + STAT_ROWS, columns), jnp.bfloat16)


def packed(part):
    return call(pack_kernel, wire_of(part), *part)


def merged(block, part):
    return call(merge_kernel, wire_of(part), block, *part)


def kept(block, part):
    return call(merge_kernel, [jax.ShapeDtypeStruct(x.shape, x.dtype) for x in part], block, *part)


def on_device(queries, suffix_key_value, kv_pages, page_table, prefix_pages, new_slots):
    stores = lax.axis_size("store")
    pulled = page_table.shape[1] // stores * kv_pages[0].size
    pushed = 2 * queries[0].size
    arrays = (queries, suffix_key_value, kv_pages, page_table, prefix_pages, new_slots)
    if pulled >= pushed and stores % 8 == 0 and stores <= LIST_ROWS:
        return queries_travel(*arrays)
    return pages_travel(*arrays)


def solution(mesh):
    return jax.shard_map(
        on_device,
        mesh=mesh,
        in_specs=(
            P(("groups", "store"), None, "tensor"),
            P(("groups", "store"), None, None, "tensor"),
            P(("groups", "store"), None, None, "tensor"),
            P(("groups", "store"), None),
            P(("groups", "store")),
            P(("groups", "store")),
        ),
        out_specs=(
            P(("groups", "store"), None, "tensor"),
            P(("groups", "store"), None, None, "tensor"),
        ),
        check_vma=False,
    )
```

```python
import functools

import jax
import jax.numpy as jnp
from jax import lax
from jax.experimental import pallas as pl
from jax.experimental.pallas import tpu as pltpu
from jax.sharding import PartitionSpec as P

HEAD_SIZE = 128
LOG2E = 1.4426950408889634
DEAD = -1e30
FLOOR = -1e29
STAT_ROWS = 16
LIST_ROWS = 16
GRANT = 20 * 1024 * 1024
LIGHT = pl.CostEstimate(flops=1, bytes_accessed=1, transcendentals=0)
VMEM = pl.BlockSpec(memory_space=pltpu.VMEM)
SMEM = pl.BlockSpec(memory_space=pltpu.SMEM)
HBM = pl.BlockSpec(memory_space=pltpu.HBM)


def shifted(block, axis, distance):
    devices = range(lax.axis_size(axis))
    route = [((i - distance) % len(devices), i) for i in devices]
    return lax.ppermute(block, axis, route)


def block_update(state, head_count, key_rows, value_rows, live, scale):
    top_old, total_old, acc_old = state
    scores = (
        jnp.einsum("qhgd,khd->hgqk", head_count, key_rows, preferred_element_type=jnp.float32)
        * scale
    )
    scores = jnp.where(live, scores, -1e30)
    top_new = jnp.maximum(top_old, jnp.max(scores, axis=-1))
    weights = jnp.where(live, jnp.exp(scores - top_new[..., None]), 0.0)
    factor = jnp.exp(top_old - top_new)
    total_new = total_old * factor + jnp.sum(weights, axis=-1)
    product = jnp.einsum(
        "hgqk,khd->hgqd",
        weights.astype(jnp.bfloat16),
        value_rows,
        preferred_element_type=jnp.float32,
    )
    return (top_new, total_new, acc_old * factor[..., None] + product)


def pages_travel(queries, suffix_key_value, kv_pages, page_table, prefix_pages, new_slots):
    stores = lax.axis_size("store")
    pages_dev = kv_pages.shape[0]
    maxp = page_table.shape[1]
    cap = maxp // stores
    page_len = kv_pages.shape[2]
    width = kv_pages.shape[3]
    kv_heads = width // HEAD_SIZE
    suffix = queries.shape[1]
    groups_per_head = queries.shape[2] // width
    scale = HEAD_SIZE ** (-0.5)
    length = prefix_pages[0]
    table = page_table[0]
    owners = table // pages_dev
    local_ids = table % pages_dev
    entries = jnp.arange(maxp, dtype=jnp.int32)
    same_owner = (owners[:, None] == owners[None, :]) & (entries[:, None] < entries[None, :])
    ranks = jnp.sum(same_owner.astype(jnp.int32), axis=0)
    slots = owners * cap + ranks
    placed = slots[:, None] == entries[None, :]
    slot_entry = jnp.sum(jnp.where(placed, entries[:, None], 0), axis=0)
    wanted = jnp.sum(jnp.where(placed, local_ids[:, None], 0), axis=0)
    asked = lax.all_to_all(
        wanted.reshape(stores, cap), "store", split_axis=0, concat_axis=0, tiled=True
    )
    served = kv_pages[asked.reshape(-1)].reshape(stores, cap, 2, page_len, width)
    received = lax.all_to_all(served, "store", split_axis=0, concat_axis=0, tiled=True).reshape(
        maxp, 2, page_len, width
    )
    head_count = queries[0].reshape(suffix, kv_heads, groups_per_head, HEAD_SIZE)
    own_keys = suffix_key_value[0, 0].reshape(suffix, kv_heads, HEAD_SIZE)
    own_values = suffix_key_value[0, 1].reshape(suffix, kv_heads, HEAD_SIZE)
    rows = jnp.arange(suffix, dtype=jnp.int32)
    causal = rows[None, :] <= rows[:, None]
    start_state = (
        jnp.full((kv_heads, groups_per_head, suffix), -1e30, jnp.float32),
        jnp.zeros((kv_heads, groups_per_head, suffix), jnp.float32),
        jnp.zeros((kv_heads, groups_per_head, suffix, HEAD_SIZE), jnp.float32),
    )
    state = block_update(start_state, head_count, own_keys, own_values, causal, scale)
    block_pages = min(8, maxp)
    live_pages = slot_entry < length
    trips = maxp // block_pages

    def step_block(index, carry):
        first = index * block_pages
        block = lax.dynamic_slice_in_dim(received, first, block_pages, 0)
        alive = lax.dynamic_slice_in_dim(live_pages, first, block_pages, 0)
        alive = jnp.broadcast_to(alive[:, None], (block_pages, page_len)).reshape(
            1, block_pages * page_len
        )
        block_keys = block[:, 0].reshape(block_pages * page_len, kv_heads, HEAD_SIZE)
        block_values = block[:, 1].reshape(block_pages * page_len, kv_heads, HEAD_SIZE)
        return block_update(carry, head_count, block_keys, block_values, alive, scale)

    top_final, total_final, acc_final = lax.fori_loop(0, trips, step_block, state)
    output = acc_final / total_final[..., None]
    attended = (
        output.transpose(2, 0, 1, 3)
        .reshape(1, suffix, groups_per_head * width)
        .astype(jnp.bfloat16)
    )
    arrived, arrived_slot = shifted((suffix_key_value, new_slots), "store", stores // 2)
    new_store = lax.dynamic_update_slice_in_dim(kv_pages, arrived, arrived_slot[0], 0)
    return (attended, new_store)


def dot_nt(a, b):
    return lax.dot_general(a, b, (((1,), (1,)), ((), ())), preferred_element_type=jnp.float32)


def block_of(j):
    return slice(j * HEAD_SIZE, (j + 1) * HEAD_SIZE)


def iota(shape, dim):
    return lax.broadcasted_iota(jnp.int32, shape, dim)


def pack_stats(top, total):
    diagonal = iota((HEAD_SIZE, HEAD_SIZE), 0) == iota((HEAD_SIZE, HEAD_SIZE), 1)
    row = iota((STAT_ROWS, HEAD_SIZE), 0)
    tile = jnp.zeros((STAT_ROWS, HEAD_SIZE), jnp.float32)

    def along(x):
        return jnp.sum(jnp.where(diagonal, x, 0.0), 0, keepdims=True)

    for j, (m, l) in enumerate(zip(top, total)):
        l = along(l)
        high = l.astype(jnp.bfloat16).astype(jnp.float32)
        for t, x in enumerate((along(m), high, l - high)):
            tile = jnp.where(row == 4 * t + j, x, tile)
    return tile.astype(jnp.bfloat16)


def unpack_stats(tile):
    row = iota((STAT_ROWS, 8 * HEAD_SIZE), 0)
    block = iota((STAT_ROWS, 8 * HEAD_SIZE), 1) // HEAD_SIZE
    j = block // 2
    stat = block % 2
    spread = (
        ((row == j) & (stat == 0)) | ((row == j + 4) & (stat == 1)) | ((row == j + 8) & (stat == 1))
    )
    spread = spread.astype(jnp.float32).astype(jnp.bfloat16)
    turned = tile.astype(jnp.float32).T.astype(jnp.bfloat16)
    wide = jnp.dot(turned, spread, preferred_element_type=jnp.float32)
    part = lambda b: wide[:, b * HEAD_SIZE:(b + 1) * HEAD_SIZE]
    return [part(2 * j) for j in range(4)], [part(2 * j + 1) for j in range(4)]


def attend_kernel(sizes, own, keeping, *refs):
    heads, rows, suffix, cap, page_len = sizes
    refs = list(refs)
    meta, q_ref = refs.pop(0), refs.pop(0)
    own_kv = refs.pop(0) if own else None
    held, acc_ref, stat_ref = refs.pop(0), refs.pop(0), refs.pop(0)
    stored = refs.pop(0) if keeping else None
    scores = refs.pop(0)
    late_scores = refs.pop(0) if own else None
    if keeping:
        keep = pltpu.make_async_copy(held, stored, refs.pop(0))
        keep.start()
    factor = HEAD_SIZE ** (-0.5) * LOG2E
    keys = cap * page_len

    def stacked(part, h):
        return jnp.concatenate([held[meta[0, c], part, :, block_of(h)] for c in range(cap)], 0)

    def score(h):
        q = q_ref[h * rows:(h + 1) * rows, :]
        scores[h % 2] = dot_nt(q, stacked(0, h))
        if own:
            at = iota((rows, suffix), 0) % suffix
            causal = iota((rows, suffix), 1) <= at
            late_scores[h % 2] = jnp.where(causal, dot_nt(q, own_kv[0, :, block_of(h)]), DEAD)

    def weigh(h):
        live = iota((1, keys), 1) < meta[0, cap] * page_len
        s = jnp.where(live, scores[h % 2], DEAD)
        top = jnp.max(s, axis=-1, keepdims=True)
        if own:
            top = jnp.maximum(top, jnp.max(late_scores[h % 2], axis=-1, keepdims=True))
        top = jnp.maximum(top * factor, FLOOR).astype(jnp.bfloat16).astype(jnp.float32)
        p = jnp.exp2(s * factor - top).astype(jnp.bfloat16)
        v = stacked(1, h)
        v = jnp.concatenate([v, jnp.ones_like(v)], 1)
        out = jnp.dot(p, v, preferred_element_type=jnp.float32)
        if own:
            p = jnp.exp2(late_scores[h % 2] * factor - top).astype(jnp.bfloat16)
            v = own_kv[1, :, block_of(h)]
            v = jnp.concatenate([v, jnp.ones_like(v)], 1)
            out = out + jnp.dot(p, v, preferred_element_type=jnp.float32)
        acc_ref[h] = out[:, :HEAD_SIZE]
        total = out[:, HEAD_SIZE:]
        top = jnp.broadcast_to(top, total.shape)
        blocks = [block_of(j) for j in range(rows // HEAD_SIZE)]
        stat_ref[h] = pack_stats([top[j] for j in blocks], [total[j] for j in blocks])

    for h in range(heads + 1):
        if h < heads:
            score(h)
        if h > 0:
            weigh(h - 1)
    if keeping:
        keep.wait()


def attend(sizes, meta, queries, held, own=None, keeping=False, weight=1):
    heads, rows, suffix, cap, page_len = sizes
    keys = cap * page_len
    shapes = [
        jax.ShapeDtypeStruct((heads, rows, HEAD_SIZE), jnp.float32),
        jax.ShapeDtypeStruct((heads, STAT_ROWS, HEAD_SIZE), jnp.bfloat16),
    ]
    specs = [VMEM, VMEM]
    scratch = [pltpu.VMEM((2, rows, keys), jnp.float32)]
    more = [held]
    if own is not None:
        more = [own, held]
        scratch.append(pltpu.VMEM((2, rows, suffix), jnp.float32))
    if keeping:
        shapes.append(jax.ShapeDtypeStruct(held.shape, held.dtype))
        specs.append(HBM)
        scratch.append(pltpu.SemaphoreType.DMA)
    acc, stat, *pages = pl.pallas_call(
        functools.partial(attend_kernel, sizes, own is not None, keeping),
        out_shape=shapes,
        in_specs=[SMEM] + [VMEM] * (1 + len(more)),
        out_specs=specs,
        scratch_shapes=scratch,
        compiler_params=pltpu.CompilerParams(vmem_limit_bytes=GRANT),
        cost_estimate=pl.CostEstimate(
            flops=weight * heads * rows * keys * HEAD_SIZE * 8,
            bytes_accessed=weight * heads * (rows * 6 + keys * 4) * HEAD_SIZE,
            transcendentals=weight * heads * rows * keys,
        ),
    )(meta, queries, *more)
    return (acc, stat), *pages


def place_kernel(column, near_ref, below_ref, above_ref, page_ref, old_ref, out_ref, sem):
    slot = jnp.where(near_ref[0] == 1, below_ref[0, column], above_ref[0, column])
    copy = pltpu.make_async_copy(page_ref.at[0], out_ref.at[slot], sem)
    copy.start()
    copy.wait()


def place_page(column, near, below, above, page, store):
    return pl.pallas_call(
        functools.partial(place_kernel, column),
        out_shape=jax.ShapeDtypeStruct(store.shape, store.dtype),
        in_specs=[SMEM, SMEM, SMEM, VMEM, HBM],
        out_specs=HBM,
        scratch_shapes=[pltpu.SemaphoreType.DMA],
        input_output_aliases={4: 0},
        compiler_params=pltpu.CompilerParams(vmem_limit_bytes=GRANT),
        cost_estimate=LIGHT,
    )(near, below, above, page, store)


def blend(parts):
    top = functools.reduce(jnp.maximum, [m for _, m, _ in parts])
    scales = [jnp.exp2(m - top) for _, m, _ in parts]
    acc = sum(a * f for (a, _, _), f in zip(parts, scales))
    total = sum(l * f for (_, _, l), f in zip(parts, scales))
    return acc, top, total


def pack_kernel(acc_ref, stat_ref, out_ref):
    heads, rows = acc_ref.shape[:2]
    for h in range(heads):
        out_ref[h, :rows, :] = acc_ref[h].astype(jnp.bfloat16)
        out_ref[h, rows:, :] = stat_ref[h]


def merge_kernel(in_ref, acc_ref, stat_ref, out_ref):
    heads, rows = acc_ref.shape[:2]
    for h in range(heads):
        in_top, in_total = unpack_stats(in_ref[h, rows:, :])
        my_top, my_total = unpack_stats(stat_ref[h])
        tops, totals = [], []
        for j in range(rows // HEAD_SIZE):
            acc, top, total = blend(
                [
                    (in_ref[h, block_of(j), :].astype(jnp.float32), in_top[j], in_total[j]),
                    (acc_ref[h, block_of(j), :], my_top[j], my_total[j]),
                ]
            )
            out_ref[h, block_of(j), :] = acc.astype(out_ref.dtype)
            tops.append(top)
            totals.append(total)
        out_ref[h, rows:, :] = pack_stats(tops, totals)


def final_kernel(suffix, in_ref, acc_ref, stat_ref, out_ref, done, sems):
    heads, rows = acc_ref.shape[:2]
    groups = rows // suffix
    copies = []
    for h in range(heads):
        in_top, in_total = unpack_stats(in_ref[h, rows:, :])
        my_top, my_total = unpack_stats(stat_ref[h])
        for j in range(rows // HEAD_SIZE):
            acc, _, total = blend(
                [
                    (in_ref[h, block_of(j), :].astype(jnp.float32), in_top[j], in_total[j]),
                    (acc_ref[h, block_of(j), :], my_top[j], my_total[j]),
                ]
            )
            out = (acc / total).astype(jnp.bfloat16)
            for i in range(HEAD_SIZE // suffix):
                g = h * groups + j * (HEAD_SIZE // suffix) + i
                done[0, :, block_of(g)] = out[i * suffix:(i + 1) * suffix]
        span = pl.ds(h * groups * HEAD_SIZE, groups * HEAD_SIZE)
        copies.append(
            pltpu.make_async_copy(done.at[:, :, span], out_ref.at[:, :, span], sems.at[h])
        )
        copies[-1].start()
    for copy in copies:
        copy.wait()


def finish(suffix, like, block, part):
    return pl.pallas_call(
        functools.partial(final_kernel, suffix),
        out_shape=jax.ShapeDtypeStruct(like.shape, like.dtype),
        in_specs=[VMEM] * 3,
        out_specs=HBM,
        scratch_shapes=[
            pltpu.VMEM(like.shape, like.dtype),
            pltpu.SemaphoreType.DMA((part[0].shape[0],)),
        ],
        compiler_params=pltpu.CompilerParams(vmem_limit_bytes=GRANT),
    )(block, *part)


def call(kernel, shape, *args):
    size = sum(a.size * a.dtype.itemsize for a in args)
    return pl.pallas_call(
        kernel,
        out_shape=shape,
        in_specs=[VMEM] * len(args),
        out_specs=[VMEM] * len(shape) if isinstance(shape, list) else VMEM,
        compiler_params=pltpu.CompilerParams(vmem_limit_bytes=GRANT),
        cost_estimate=pl.CostEstimate(flops=size, bytes_accessed=2 * size, transcendentals=0),
    )(*args)


def prepare_kernel(cap, pages_dev, length_ref, slot_ref, table_ref, q_ref, out_ref):
    maxp = table_ref.shape[1]
    suffix = q_ref.shape[1]
    rows = out_ref.shape[0] - LIST_ROWS
    for g in range(rows // suffix):
        out_ref[g * suffix:(g + 1) * suffix, :] = q_ref[0, :, block_of(g)]
    table = table_ref[...]
    owner = lax.div(table, pages_dev)
    local = (table - owner * pages_dev).astype(jnp.float32)
    owner = owner.astype(jnp.float32)
    down, along = iota((maxp, maxp), 0), iota((maxp, maxp), 1)

    def turned(x):
        return jnp.sum(jnp.where(down == along, x, 0.0), 1, keepdims=True)

    before = (turned(owner) == owner) & (along < down)
    rank = jnp.sum(jnp.where(before, 1.0, 0.0), 1, keepdims=True)
    place = iota((maxp, HEAD_SIZE), 1)
    live = jnp.where(iota((maxp, HEAD_SIZE), 0) < length_ref[0], 1.0, 0.0)
    ids = jnp.where(rank == place.astype(jnp.float32), turned(local), 0.0)
    fields = jnp.where(place < cap, ids, jnp.where(place == cap, live, 0.0))
    owned = jnp.where(owner == iota((LIST_ROWS, maxp), 0).astype(jnp.float32), 1.0, 0.0)
    lists = jnp.dot(
        owned.astype(jnp.bfloat16), fields.astype(jnp.bfloat16), preferred_element_type=jnp.float32
    )
    slot = slot_ref[0].astype(jnp.float32)
    lists = jnp.where(iota(lists.shape, 1) == cap + 1, slot, lists)
    out_ref[rows:, :] = lists.astype(jnp.bfloat16)


def prepare(cap, pages_dev, queries, page_table, prefix_pages, new_slots):
    rows = queries.size // HEAD_SIZE
    return pl.pallas_call(
        functools.partial(prepare_kernel, cap, pages_dev),
        out_shape=jax.ShapeDtypeStruct((rows + LIST_ROWS, HEAD_SIZE), queries.dtype),
        in_specs=[SMEM, SMEM, VMEM, VMEM],
        out_specs=VMEM,
        compiler_params=pltpu.CompilerParams(vmem_limit_bytes=GRANT),
    )(prefix_pages, new_slots, page_table, queries)


def queries_travel(queries, suffix_key_value, kv_pages, page_table, prefix_pages, new_slots):
    stores = lax.axis_size("store")
    cores = lax.axis_size("tensor")
    pages_dev, _, page_len, width = kv_pages.shape
    cap = page_table.shape[1] // stores
    heads = width // HEAD_SIZE
    suffix = queries.shape[1]
    rows = queries.shape[2] // width * suffix
    sizes = (heads, rows, suffix, cap, page_len)
    half = stores // 2
    me = lax.axis_index("store")

    order = list(range(0, stores, 2)) + list(range(1, stores, 2))[::-1]
    route = [
        (order[i] * cores + core, order[(i + 1 - 2 * (core % 2)) % stores] * cores + core)
        for core in range(cores)
        for i in range(stores)
    ]

    def onward(x):
        return lax.ppermute(x, ("store", "tensor"), route)

    def listed(x):
        row = lax.dynamic_slice(x, (heads * rows + me, 0), (1, HEAD_SIZE))
        return row.astype(jnp.int32)

    def after(values, token):
        return lax.optimization_barrier((values, token))[0]

    mine = prepare(cap, pages_dev, queries, page_table, prefix_pages, new_slots)
    moving = onward(mine)
    arrived = shifted(after(suffix_key_value, mine), "store", half)

    own, store = attend(
        sizes, listed(mine), mine, kv_pages, suffix_key_value[0], True, weight=8
    )
    token = own
    partial = None
    lists = {}
    for step in range(1, stores):
        came = after(moving, token)
        if step < stores - 1:
            moving = onward(came)
        lists[step] = listed(came)
        part, = attend(sizes, lists[step], came, kv_pages)
        if step == 1:
            block = packed(after(part, arrived))
        else:
            block = merged(after(partial, part), part)
        partial = onward(block)
        token = block
    attended = finish(suffix, queries, partial, own)

    near = ((me >= half) == (me % 2 == 0)) == (lax.axis_index("tensor") % 2 == 0)
    quarter = stores // 4
    store = place_page(
        cap + 1,
        near.astype(jnp.int32)[None],
        lists[quarter],
        lists[stores - quarter],
        arrived,
        after(store, token),
    )
    return (attended, store)


def wire_of(part):
    heads, rows, columns = part[0].shape
    return jax.ShapeDtypeStruct((heads, rows + STAT_ROWS, columns), jnp.bfloat16)


def packed(part):
    return call(pack_kernel, wire_of(part), *part)


def merged(block, part):
    return call(merge_kernel, wire_of(part), block, *part)


def on_device(queries, suffix_key_value, kv_pages, page_table, prefix_pages, new_slots):
    stores = lax.axis_size("store")
    pulled = page_table.shape[1] // stores * kv_pages[0].size
    pushed = 2 * queries[0].size
    arrays = (queries, suffix_key_value, kv_pages, page_table, prefix_pages, new_slots)
    if pulled >= pushed and stores % 8 == 0 and stores <= LIST_ROWS:
        return queries_travel(*arrays)
    return pages_travel(*arrays)


def solution(mesh):
    return jax.shard_map(
        on_device,
        mesh=mesh,
        in_specs=(
            P(("groups", "store"), None, "tensor"),
            P(("groups", "store"), None, None, "tensor"),
            P(("groups", "store"), None, None, "tensor"),
            P(("groups", "store"), None),
            P(("groups", "store")),
            P(("groups", "store")),
        ),
        out_specs=(
            P(("groups", "store"), None, "tensor"),
            P(("groups", "store"), None, None, "tensor"),
        ),
        check_vma=False,
    )
```

```python
import functools

import jax
import jax.numpy as jnp
from jax import lax
from jax.experimental import pallas as pl
from jax.experimental.pallas import tpu as pltpu
from jax.sharding import PartitionSpec as P

HEAD_SIZE = 128
LOG2E = 1.4426950408889634
DEAD = -1e30
FLOOR = -1e29
STAT_ROWS = 16
LIST_ROWS = 16
GRANT = 20 * 1024 * 1024
LIGHT = pl.CostEstimate(flops=1, bytes_accessed=1, transcendentals=0)
VMEM = pl.BlockSpec(memory_space=pltpu.VMEM)
SMEM = pl.BlockSpec(memory_space=pltpu.SMEM)
HBM = pl.BlockSpec(memory_space=pltpu.HBM)


def shifted(block, axis, distance):
    devices = range(lax.axis_size(axis))
    route = [((i - distance) % len(devices), i) for i in devices]
    return lax.ppermute(block, axis, route)


def block_update(state, head_count, key_rows, value_rows, live, scale):
    top_old, total_old, acc_old = state
    scores = (
        jnp.einsum("qhgd,khd->hgqk", head_count, key_rows, preferred_element_type=jnp.float32)
        * scale
    )
    scores = jnp.where(live, scores, -1e30)
    top_new = jnp.maximum(top_old, jnp.max(scores, axis=-1))
    weights = jnp.where(live, jnp.exp(scores - top_new[..., None]), 0.0)
    factor = jnp.exp(top_old - top_new)
    total_new = total_old * factor + jnp.sum(weights, axis=-1)
    product = jnp.einsum(
        "hgqk,khd->hgqd",
        weights.astype(jnp.bfloat16),
        value_rows,
        preferred_element_type=jnp.float32,
    )
    return (top_new, total_new, acc_old * factor[..., None] + product)


def pages_travel(queries, suffix_key_value, kv_pages, page_table, prefix_pages, new_slots):
    stores = lax.axis_size("store")
    pages_dev = kv_pages.shape[0]
    maxp = page_table.shape[1]
    cap = maxp // stores
    page_len = kv_pages.shape[2]
    width = kv_pages.shape[3]
    kv_heads = width // HEAD_SIZE
    suffix = queries.shape[1]
    groups_per_head = queries.shape[2] // width
    scale = HEAD_SIZE ** (-0.5)
    length = prefix_pages[0]
    table = page_table[0]
    owners = table // pages_dev
    local_ids = table % pages_dev
    entries = jnp.arange(maxp, dtype=jnp.int32)
    same_owner = (owners[:, None] == owners[None, :]) & (entries[:, None] < entries[None, :])
    ranks = jnp.sum(same_owner.astype(jnp.int32), axis=0)
    slots = owners * cap + ranks
    placed = slots[:, None] == entries[None, :]
    slot_entry = jnp.sum(jnp.where(placed, entries[:, None], 0), axis=0)
    wanted = jnp.sum(jnp.where(placed, local_ids[:, None], 0), axis=0)
    asked = lax.all_to_all(
        wanted.reshape(stores, cap), "store", split_axis=0, concat_axis=0, tiled=True
    )
    served = kv_pages[asked.reshape(-1)].reshape(stores, cap, 2, page_len, width)
    received = lax.all_to_all(served, "store", split_axis=0, concat_axis=0, tiled=True).reshape(
        maxp, 2, page_len, width
    )
    head_count = queries[0].reshape(suffix, kv_heads, groups_per_head, HEAD_SIZE)
    own_keys = suffix_key_value[0, 0].reshape(suffix, kv_heads, HEAD_SIZE)
    own_values = suffix_key_value[0, 1].reshape(suffix, kv_heads, HEAD_SIZE)
    rows = jnp.arange(suffix, dtype=jnp.int32)
    causal = rows[None, :] <= rows[:, None]
    start_state = (
        jnp.full((kv_heads, groups_per_head, suffix), -1e30, jnp.float32),
        jnp.zeros((kv_heads, groups_per_head, suffix), jnp.float32),
        jnp.zeros((kv_heads, groups_per_head, suffix, HEAD_SIZE), jnp.float32),
    )
    state = block_update(start_state, head_count, own_keys, own_values, causal, scale)
    block_pages = min(8, maxp)
    live_pages = slot_entry < length
    trips = maxp // block_pages

    def step_block(index, carry):
        first = index * block_pages
        block = lax.dynamic_slice_in_dim(received, first, block_pages, 0)
        alive = lax.dynamic_slice_in_dim(live_pages, first, block_pages, 0)
        alive = jnp.broadcast_to(alive[:, None], (block_pages, page_len)).reshape(
            1, block_pages * page_len
        )
        block_keys = block[:, 0].reshape(block_pages * page_len, kv_heads, HEAD_SIZE)
        block_values = block[:, 1].reshape(block_pages * page_len, kv_heads, HEAD_SIZE)
        return block_update(carry, head_count, block_keys, block_values, alive, scale)

    top_final, total_final, acc_final = lax.fori_loop(0, trips, step_block, state)
    output = acc_final / total_final[..., None]
    attended = (
        output.transpose(2, 0, 1, 3)
        .reshape(1, suffix, groups_per_head * width)
        .astype(jnp.bfloat16)
    )
    arrived, arrived_slot = shifted((suffix_key_value, new_slots), "store", stores // 2)
    new_store = lax.dynamic_update_slice_in_dim(kv_pages, arrived, arrived_slot[0], 0)
    return (attended, new_store)


def dot_nt(a, b):
    return lax.dot_general(a, b, (((1,), (1,)), ((), ())), preferred_element_type=jnp.float32)


def block_of(j):
    return slice(j * HEAD_SIZE, (j + 1) * HEAD_SIZE)


def iota(shape, dim):
    return lax.broadcasted_iota(jnp.int32, shape, dim)


def pack_stats(top, total):
    diagonal = iota((HEAD_SIZE, HEAD_SIZE), 0) == iota((HEAD_SIZE, HEAD_SIZE), 1)
    row = iota((STAT_ROWS, HEAD_SIZE), 0)
    tile = jnp.zeros((STAT_ROWS, HEAD_SIZE), jnp.float32)

    def along(x):
        return jnp.sum(jnp.where(diagonal, x, 0.0), 0, keepdims=True)

    for j, (m, l) in enumerate(zip(top, total)):
        l = along(l)
        high = l.astype(jnp.bfloat16).astype(jnp.float32)
        for t, x in enumerate((along(m), high, l - high)):
            tile = jnp.where(row == 4 * t + j, x, tile)
    return tile.astype(jnp.bfloat16)


def unpack_stats(tile):
    row = iota((STAT_ROWS, 8 * HEAD_SIZE), 0)
    block = iota((STAT_ROWS, 8 * HEAD_SIZE), 1) // HEAD_SIZE
    j = block // 2
    stat = block % 2
    spread = (
        ((row == j) & (stat == 0)) | ((row == j + 4) & (stat == 1)) | ((row == j + 8) & (stat == 1))
    )
    spread = spread.astype(jnp.float32).astype(jnp.bfloat16)
    turned = tile.astype(jnp.float32).T.astype(jnp.bfloat16)
    wide = jnp.dot(turned, spread, preferred_element_type=jnp.float32)
    part = lambda b: wide[:, b * HEAD_SIZE:(b + 1) * HEAD_SIZE]
    return [part(2 * j) for j in range(4)], [part(2 * j + 1) for j in range(4)]


def attend_kernel(sizes, own, keeping, *refs):
    heads, rows, suffix, cap, page_len = sizes
    refs = list(refs)
    meta, q_ref = refs.pop(0), refs.pop(0)
    own_kv = refs.pop(0) if own else None
    held = refs.pop(0)
    if keeping and keeping[0]:
        refs.pop(0)
    acc_ref, stat_ref = refs.pop(0), refs.pop(0)
    stored = refs.pop(0) if keeping else None
    scores = refs.pop(0)
    late_scores = refs.pop(0) if own else None
    if keeping:
        span = pl.ds(*keeping)
        keep = pltpu.make_async_copy(held.at[span], stored.at[span], refs.pop(0))
        keep.start()
    factor = HEAD_SIZE ** (-0.5) * LOG2E
    keys = cap * page_len

    def stacked(part, h):
        return jnp.concatenate([held[meta[0, c], part, :, block_of(h)] for c in range(cap)], 0)

    def score(h):
        if own:
            groups = rows // suffix
            q = [q_ref[0, :, block_of(h * groups + g)] for g in range(groups)]
            q = jnp.concatenate(q, 0)
        else:
            q = q_ref[h * rows:(h + 1) * rows, :]
        scores[h % 2] = dot_nt(q, stacked(0, h))
        if own:
            at = iota((rows, suffix), 0) % suffix
            causal = iota((rows, suffix), 1) <= at
            late_scores[h % 2] = jnp.where(causal, dot_nt(q, own_kv[0, :, block_of(h)]), DEAD)

    def weigh(h):
        live = iota((1, keys), 1) < meta[0, cap] * page_len
        s = jnp.where(live, scores[h % 2], DEAD)
        top = jnp.max(s, axis=-1, keepdims=True)
        if own:
            top = jnp.maximum(top, jnp.max(late_scores[h % 2], axis=-1, keepdims=True))
        top = jnp.maximum(top * factor, FLOOR).astype(jnp.bfloat16).astype(jnp.float32)
        p = jnp.exp2(s * factor - top).astype(jnp.bfloat16)
        v = stacked(1, h)
        v = jnp.concatenate([v, jnp.ones_like(v)], 1)
        out = jnp.dot(p, v, preferred_element_type=jnp.float32)
        if own:
            p = jnp.exp2(late_scores[h % 2] * factor - top).astype(jnp.bfloat16)
            v = own_kv[1, :, block_of(h)]
            v = jnp.concatenate([v, jnp.ones_like(v)], 1)
            out = out + jnp.dot(p, v, preferred_element_type=jnp.float32)
        acc_ref[h] = out[:, :HEAD_SIZE]
        total = out[:, HEAD_SIZE:]
        top = jnp.broadcast_to(top, total.shape)
        blocks = [block_of(j) for j in range(rows // HEAD_SIZE)]
        stat_ref[h] = pack_stats([top[j] for j in blocks], [total[j] for j in blocks])

    for h in range(heads + 1):
        if h < heads:
            score(h)
        if h > 0:
            weigh(h - 1)
    if keeping:
        keep.wait()


def attend(sizes, meta, queries, held, own=None, keeping=None, store=None):
    heads, rows, suffix, cap, page_len = sizes
    keys = cap * page_len
    shapes = [
        jax.ShapeDtypeStruct((heads, rows, HEAD_SIZE), jnp.float32),
        jax.ShapeDtypeStruct((heads, STAT_ROWS, HEAD_SIZE), jnp.bfloat16),
    ]
    in_specs, out_specs = [SMEM, VMEM, VMEM], [VMEM, VMEM]
    scratch = [pltpu.VMEM((2, rows, keys), jnp.float32)]
    args, aliases = [meta, queries, held], {}
    if own is not None:
        args.insert(2, own)
        in_specs.append(VMEM)
        scratch.append(pltpu.VMEM((2, rows, suffix), jnp.float32))
    if keeping:
        shapes.append(jax.ShapeDtypeStruct(held.shape, held.dtype))
        out_specs.append(HBM)
        scratch.append(pltpu.SemaphoreType.DMA)
    if store is not None:
        aliases[len(args)] = 2
        args.append(store)
        in_specs.append(HBM)
    acc, stat, *pages = pl.pallas_call(
        functools.partial(attend_kernel, sizes, own is not None, keeping),
        out_shape=shapes,
        in_specs=in_specs,
        out_specs=out_specs,
        scratch_shapes=scratch,
        input_output_aliases=aliases,
        compiler_params=pltpu.CompilerParams(vmem_limit_bytes=GRANT),
        cost_estimate=pl.CostEstimate(
            flops=heads * rows * keys * HEAD_SIZE * 8,
            bytes_accessed=heads * (rows * 6 + keys * 4) * HEAD_SIZE,
            transcendentals=heads * rows * keys,
        ),
    )(*args)
    return (acc, stat), *pages


def place_kernel(column, near_ref, below_ref, above_ref, page_ref, old_ref, out_ref, sem):
    slot = jnp.where(near_ref[0] == 1, below_ref[0, column], above_ref[0, column])
    copy = pltpu.make_async_copy(page_ref.at[0], out_ref.at[slot], sem)
    copy.start()
    copy.wait()


def place_page(column, near, below, above, page, store):
    return pl.pallas_call(
        functools.partial(place_kernel, column),
        out_shape=jax.ShapeDtypeStruct(store.shape, store.dtype),
        in_specs=[SMEM, SMEM, SMEM, VMEM, HBM],
        out_specs=HBM,
        scratch_shapes=[pltpu.SemaphoreType.DMA],
        input_output_aliases={4: 0},
        compiler_params=pltpu.CompilerParams(vmem_limit_bytes=GRANT),
        cost_estimate=LIGHT,
    )(near, below, above, page, store)


def blend(parts):
    top = functools.reduce(jnp.maximum, [m for _, m, _ in parts])
    scales = [jnp.exp2(m - top) for _, m, _ in parts]
    acc = sum(a * f for (a, _, _), f in zip(parts, scales))
    total = sum(l * f for (_, _, l), f in zip(parts, scales))
    return acc, top, total


def pack_kernel(acc_ref, stat_ref, out_ref):
    heads, rows = acc_ref.shape[:2]
    for h in range(heads):
        out_ref[h, :rows, :] = acc_ref[h].astype(jnp.bfloat16)
        out_ref[h, rows:, :] = stat_ref[h]


def merge_kernel(first, in_ref, acc_ref, stat_ref, out_ref):
    heads, rows = out_ref.shape[0], acc_ref.shape[1]
    for h in range(first, first + heads):
        in_top, in_total = unpack_stats(in_ref[h, rows:, :])
        my_top, my_total = unpack_stats(stat_ref[h])
        tops, totals = [], []
        for j in range(rows // HEAD_SIZE):
            acc, top, total = blend(
                [
                    (in_ref[h, block_of(j), :].astype(jnp.float32), in_top[j], in_total[j]),
                    (acc_ref[h, block_of(j), :], my_top[j], my_total[j]),
                ]
            )
            out_ref[h - first, block_of(j), :] = acc.astype(out_ref.dtype)
            tops.append(top)
            totals.append(total)
        out_ref[h - first, rows:, :] = pack_stats(tops, totals)


def final_kernel(suffix, first, in_ref, acc_ref, stat_ref, *refs):
    out_ref, done, sems = refs[-3:]
    heads, rows = in_ref.shape[0], acc_ref.shape[1]
    groups = rows // suffix
    copies = []
    for h in range(heads):
        in_top, in_total = unpack_stats(in_ref[h, rows:, :])
        my_top, my_total = unpack_stats(stat_ref[first + h])
        for j in range(rows // HEAD_SIZE):
            acc, _, total = blend(
                [
                    (in_ref[h, block_of(j), :].astype(jnp.float32), in_top[j], in_total[j]),
                    (acc_ref[first + h, block_of(j), :], my_top[j], my_total[j]),
                ]
            )
            out = (acc / total).astype(jnp.bfloat16)
            for i in range(HEAD_SIZE // suffix):
                g = h * groups + j * (HEAD_SIZE // suffix) + i
                done[0, :, block_of(g)] = out[i * suffix:(i + 1) * suffix]
        width = groups * HEAD_SIZE
        copies.append(
            pltpu.make_async_copy(
                done.at[:, :, pl.ds(h * width, width)],
                out_ref.at[:, :, pl.ds((first + h) * width, width)],
                sems.at[h],
            )
        )
        copies[-1].start()
    for copy in copies:
        copy.wait()


def finish(suffix, first, like, block, part, before=None):
    heads, rows = block.shape[0], part[0].shape[1]
    args = [block, *part] + ([] if before is None else [before])
    return pl.pallas_call(
        functools.partial(final_kernel, suffix, first),
        out_shape=jax.ShapeDtypeStruct(like.shape, like.dtype),
        in_specs=[VMEM] * 3 + [HBM] * (len(args) - 3),
        out_specs=HBM,
        scratch_shapes=[
            pltpu.VMEM((1, suffix, heads * rows // suffix * HEAD_SIZE), like.dtype),
            pltpu.SemaphoreType.DMA((heads,)),
        ],
        input_output_aliases={} if before is None else {3: 0},
        compiler_params=pltpu.CompilerParams(vmem_limit_bytes=GRANT),
    )(*args)


def call(kernel, shape, *args):
    size = sum(a.size * a.dtype.itemsize for a in args)
    return pl.pallas_call(
        kernel,
        out_shape=shape,
        in_specs=[VMEM] * len(args),
        out_specs=[VMEM] * len(shape) if isinstance(shape, list) else VMEM,
        compiler_params=pltpu.CompilerParams(vmem_limit_bytes=GRANT),
        cost_estimate=pl.CostEstimate(flops=size, bytes_accessed=2 * size, transcendentals=0),
    )(*args)


def lists_kernel(cap, pages_dev, length_ref, slot_ref, table_ref, out_ref):
    maxp = table_ref.shape[1]
    table = table_ref[...]
    owner = lax.div(table, pages_dev)
    local = (table - owner * pages_dev).astype(jnp.float32)
    owner = owner.astype(jnp.float32)
    down, along = iota((maxp, maxp), 0), iota((maxp, maxp), 1)

    def turned(x):
        return jnp.sum(jnp.where(down == along, x, 0.0), 1, keepdims=True)

    before = (turned(owner) == owner) & (along < down)
    rank = jnp.sum(jnp.where(before, 1.0, 0.0), 1, keepdims=True)
    place = iota((maxp, HEAD_SIZE), 1)
    live = jnp.where(iota((maxp, HEAD_SIZE), 0) < length_ref[0], 1.0, 0.0)
    ids = jnp.where(rank == place.astype(jnp.float32), turned(local), 0.0)
    fields = jnp.where(place < cap, ids, jnp.where(place == cap, live, 0.0))
    owned = jnp.where(owner == iota((LIST_ROWS, maxp), 0).astype(jnp.float32), 1.0, 0.0)
    lists = jnp.dot(
        owned.astype(jnp.bfloat16), fields.astype(jnp.bfloat16), preferred_element_type=jnp.float32
    )
    slot = slot_ref[0].astype(jnp.float32)
    lists = jnp.where(iota(lists.shape, 1) == cap + 1, slot, lists)
    out_ref[...] = lists.astype(jnp.bfloat16)


def list_pages(cap, pages_dev, page_table, prefix_pages, new_slots):
    return pl.pallas_call(
        functools.partial(lists_kernel, cap, pages_dev),
        out_shape=jax.ShapeDtypeStruct((LIST_ROWS, HEAD_SIZE), jnp.bfloat16),
        in_specs=[SMEM, SMEM, VMEM],
        out_specs=VMEM,
        compiler_params=pltpu.CompilerParams(vmem_limit_bytes=GRANT),
    )(prefix_pages, new_slots, page_table)


def join_kernel(q_ref, lists_ref, out_ref):
    suffix, columns = q_ref.shape[1:]
    for g in range(columns // HEAD_SIZE):
        out_ref[g * suffix:(g + 1) * suffix, :] = q_ref[0, :, block_of(g)]
    out_ref[columns // HEAD_SIZE * suffix:, :] = lists_ref[...]


def queries_travel(queries, suffix_key_value, kv_pages, page_table, prefix_pages, new_slots):
    stores = lax.axis_size("store")
    cores = lax.axis_size("tensor")
    pages_dev, _, page_len, width = kv_pages.shape
    cap = page_table.shape[1] // stores
    heads = width // HEAD_SIZE
    suffix = queries.shape[1]
    rows = queries.shape[2] // width * suffix
    sizes = (heads, rows, suffix, cap, page_len)
    half = stores // 2
    me = lax.axis_index("store")

    order = list(range(0, stores, 2)) + list(range(1, stores, 2))[::-1]
    route = [
        (order[i] * cores + core, order[(i + 1 - 2 * (core % 2)) % stores] * cores + core)
        for core in range(cores)
        for i in range(stores)
    ]

    def onward(x):
        return lax.ppermute(x, ("store", "tensor"), route)

    def listed(x, below):
        row = lax.dynamic_slice(x, (below + me, 0), (1, HEAD_SIZE))
        return row.astype(jnp.int32)

    def after(values, token):
        return lax.optimization_barrier((values, token))[0]

    first = onward(queries)
    mine = list_pages(cap, pages_dev, page_table, prefix_pages, new_slots)
    first_lists = onward(mine)
    arrived = shifted(after(suffix_key_value, mine), "store", half)
    moving = call(
        join_kernel,
        jax.ShapeDtypeStruct((heads * rows + LIST_ROWS, HEAD_SIZE), queries.dtype),
        first,
        first_lists,
    )

    token = []
    lists = {}
    for step in range(1, stores):
        came = after(moving, token)
        if step < stores - 1:
            moving = onward(came)
        lists[step] = listed(came, heads * rows)
        if step == 2:
            part, store = attend(
                sizes, lists[step], came, kv_pages, keeping=(0, pages_dev // 2)
            )
        elif step == 3:
            rest = (pages_dev // 2, pages_dev - pages_dev // 2)
            part, store = attend(sizes, lists[step], came, kv_pages, None, rest, store)
        else:
            part, = attend(sizes, lists[step], came, kv_pages)
        if step == 1:
            block = packed(after(part, arrived))
        elif step < stores - 1:
            block = merged(after(partial, part), part, 0, heads)
        else:
            came = after(partial, part)
            ends = [merged(came, part, first, heads // 2) for first in (0, heads // 2)]
            token = ends
            ends = [onward(x) for x in ends]
            break
        partial = onward(block)
        token = block

    own, = attend(
        sizes, listed(mine, 0), after(queries, token), kv_pages, suffix_key_value[0]
    )
    near = ((me >= half) == (me % 2 == 0)) == (lax.axis_index("tensor") % 2 == 0)
    quarter = stores // 4
    store = place_page(
        cap + 1,
        near.astype(jnp.int32)[None],
        lists[quarter],
        lists[stores - quarter],
        arrived,
        after(store, own),
    )
    attended = finish(suffix, 0, queries, after(ends[0], store), own)
    attended = finish(suffix, heads // 2, queries, ends[1], own, attended)
    return (attended, store)


def wire_of(part, heads):
    rows, columns = part[0].shape[1:]
    return jax.ShapeDtypeStruct((heads, rows + STAT_ROWS, columns), jnp.bfloat16)


def packed(part):
    return call(pack_kernel, wire_of(part, part[0].shape[0]), *part)


def merged(block, part, first, heads):
    return call(functools.partial(merge_kernel, first), wire_of(part, heads), block, *part)


def on_device(queries, suffix_key_value, kv_pages, page_table, prefix_pages, new_slots):
    stores = lax.axis_size("store")
    pulled = page_table.shape[1] // stores * kv_pages[0].size
    pushed = 2 * queries[0].size
    arrays = (queries, suffix_key_value, kv_pages, page_table, prefix_pages, new_slots)
    if pulled >= pushed and stores % 8 == 0 and stores <= LIST_ROWS:
        return queries_travel(*arrays)
    return pages_travel(*arrays)


def solution(mesh):
    return jax.shard_map(
        on_device,
        mesh=mesh,
        in_specs=(
            P(("groups", "store"), None, "tensor"),
            P(("groups", "store"), None, None, "tensor"),
            P(("groups", "store"), None, None, "tensor"),
            P(("groups", "store"), None),
            P(("groups", "store")),
            P(("groups", "store")),
        ),
        out_specs=(
            P(("groups", "store"), None, "tensor"),
            P(("groups", "store"), None, None, "tensor"),
        ),
        check_vma=False,
    )
```

```python
import functools

import jax
import jax.numpy as jnp
from jax import lax
from jax.experimental import pallas as pl
from jax.experimental.pallas import tpu as pltpu
from jax.sharding import PartitionSpec as P

HEAD_SIZE = 128
LOG2E = 1.4426950408889634
DEAD = -1e30
FLOOR = -1e29
STAT_ROWS = 16
LIST_ROWS = 16
GRANT = 20 * 1024 * 1024
LIGHT = pl.CostEstimate(flops=1, bytes_accessed=1, transcendentals=0)
VMEM = pl.BlockSpec(memory_space=pltpu.VMEM)
SMEM = pl.BlockSpec(memory_space=pltpu.SMEM)
HBM = pl.BlockSpec(memory_space=pltpu.HBM)


def shifted(block, axis, distance):
    devices = range(lax.axis_size(axis))
    route = [((i - distance) % len(devices), i) for i in devices]
    return lax.ppermute(block, axis, route)


def block_update(state, head_count, key_rows, value_rows, live, scale):
    top_old, total_old, acc_old = state
    scores = (
        jnp.einsum("qhgd,khd->hgqk", head_count, key_rows, preferred_element_type=jnp.float32)
        * scale
    )
    scores = jnp.where(live, scores, -1e30)
    top_new = jnp.maximum(top_old, jnp.max(scores, axis=-1))
    weights = jnp.where(live, jnp.exp(scores - top_new[..., None]), 0.0)
    factor = jnp.exp(top_old - top_new)
    total_new = total_old * factor + jnp.sum(weights, axis=-1)
    product = jnp.einsum(
        "hgqk,khd->hgqd",
        weights.astype(jnp.bfloat16),
        value_rows,
        preferred_element_type=jnp.float32,
    )
    return (top_new, total_new, acc_old * factor[..., None] + product)


def pages_travel(queries, suffix_key_value, kv_pages, page_table, prefix_pages, new_slots):
    stores = lax.axis_size("store")
    pages_dev = kv_pages.shape[0]
    maxp = page_table.shape[1]
    cap = maxp // stores
    page_len = kv_pages.shape[2]
    width = kv_pages.shape[3]
    kv_heads = width // HEAD_SIZE
    suffix = queries.shape[1]
    groups_per_head = queries.shape[2] // width
    scale = HEAD_SIZE ** (-0.5)
    length = prefix_pages[0]
    table = page_table[0]
    owners = table // pages_dev
    local_ids = table % pages_dev
    entries = jnp.arange(maxp, dtype=jnp.int32)
    same_owner = (owners[:, None] == owners[None, :]) & (entries[:, None] < entries[None, :])
    ranks = jnp.sum(same_owner.astype(jnp.int32), axis=0)
    slots = owners * cap + ranks
    placed = slots[:, None] == entries[None, :]
    slot_entry = jnp.sum(jnp.where(placed, entries[:, None], 0), axis=0)
    wanted = jnp.sum(jnp.where(placed, local_ids[:, None], 0), axis=0)
    asked = lax.all_to_all(
        wanted.reshape(stores, cap), "store", split_axis=0, concat_axis=0, tiled=True
    )
    served = kv_pages[asked.reshape(-1)].reshape(stores, cap, 2, page_len, width)
    received = lax.all_to_all(served, "store", split_axis=0, concat_axis=0, tiled=True).reshape(
        maxp, 2, page_len, width
    )
    head_count = queries[0].reshape(suffix, kv_heads, groups_per_head, HEAD_SIZE)
    own_keys = suffix_key_value[0, 0].reshape(suffix, kv_heads, HEAD_SIZE)
    own_values = suffix_key_value[0, 1].reshape(suffix, kv_heads, HEAD_SIZE)
    rows = jnp.arange(suffix, dtype=jnp.int32)
    causal = rows[None, :] <= rows[:, None]
    start_state = (
        jnp.full((kv_heads, groups_per_head, suffix), -1e30, jnp.float32),
        jnp.zeros((kv_heads, groups_per_head, suffix), jnp.float32),
        jnp.zeros((kv_heads, groups_per_head, suffix, HEAD_SIZE), jnp.float32),
    )
    state = block_update(start_state, head_count, own_keys, own_values, causal, scale)
    block_pages = min(8, maxp)
    live_pages = slot_entry < length
    trips = maxp // block_pages

    def step_block(index, carry):
        first = index * block_pages
        block = lax.dynamic_slice_in_dim(received, first, block_pages, 0)
        alive = lax.dynamic_slice_in_dim(live_pages, first, block_pages, 0)
        alive = jnp.broadcast_to(alive[:, None], (block_pages, page_len)).reshape(
            1, block_pages * page_len
        )
        block_keys = block[:, 0].reshape(block_pages * page_len, kv_heads, HEAD_SIZE)
        block_values = block[:, 1].reshape(block_pages * page_len, kv_heads, HEAD_SIZE)
        return block_update(carry, head_count, block_keys, block_values, alive, scale)

    top_final, total_final, acc_final = lax.fori_loop(0, trips, step_block, state)
    output = acc_final / total_final[..., None]
    attended = (
        output.transpose(2, 0, 1, 3)
        .reshape(1, suffix, groups_per_head * width)
        .astype(jnp.bfloat16)
    )
    arrived, arrived_slot = shifted((suffix_key_value, new_slots), "store", stores // 2)
    new_store = lax.dynamic_update_slice_in_dim(kv_pages, arrived, arrived_slot[0], 0)
    return (attended, new_store)


def dot_nt(a, b):
    return lax.dot_general(a, b, (((1,), (1,)), ((), ())), preferred_element_type=jnp.float32)


def block_of(j):
    return slice(j * HEAD_SIZE, (j + 1) * HEAD_SIZE)


def iota(shape, dim):
    return lax.broadcasted_iota(jnp.int32, shape, dim)


def pack_stats(top, total):
    diagonal = iota((HEAD_SIZE, HEAD_SIZE), 0) == iota((HEAD_SIZE, HEAD_SIZE), 1)
    row = iota((STAT_ROWS, HEAD_SIZE), 0)
    tile = jnp.zeros((STAT_ROWS, HEAD_SIZE), jnp.float32)

    def along(x):
        return jnp.sum(jnp.where(diagonal, x, 0.0), 0, keepdims=True)

    for j, (m, l) in enumerate(zip(top, total)):
        l = along(l)
        high = l.astype(jnp.bfloat16).astype(jnp.float32)
        for t, x in enumerate((along(m), high, l - high)):
            tile = jnp.where(row == 4 * t + j, x, tile)
    return tile.astype(jnp.bfloat16)


def unpack_stats(tile):
    row = iota((STAT_ROWS, 8 * HEAD_SIZE), 0)
    block = iota((STAT_ROWS, 8 * HEAD_SIZE), 1) // HEAD_SIZE
    j = block // 2
    stat = block % 2
    spread = (
        ((row == j) & (stat == 0)) | ((row == j + 4) & (stat == 1)) | ((row == j + 8) & (stat == 1))
    )
    spread = spread.astype(jnp.float32).astype(jnp.bfloat16)
    turned = tile.astype(jnp.float32).T.astype(jnp.bfloat16)
    wide = jnp.dot(turned, spread, preferred_element_type=jnp.float32)
    part = lambda b: wide[:, b * HEAD_SIZE:(b + 1) * HEAD_SIZE]
    return [part(2 * j) for j in range(4)], [part(2 * j + 1) for j in range(4)]


def attend_kernel(sizes, jobs, own, keeping, *refs):
    rows, suffix, cap, page_len, count = sizes
    refs = list(refs)
    meta = refs.pop(0)
    queries = [refs.pop(0) for _ in range(count)]
    own_kv = refs.pop(0) if own else None
    held = refs.pop(0)
    if keeping and keeping[0]:
        refs.pop(0)
    outs = [(refs.pop(0), refs.pop(0)) for _ in range(count)]
    stored = refs.pop(0) if keeping else None
    scores = refs.pop(0)
    late_scores = refs.pop(0) if own else None
    if keeping:
        span = pl.ds(*keeping)
        keep = pltpu.make_async_copy(held.at[span], stored.at[span], refs.pop(0))
        keep.start()
    factor = HEAD_SIZE ** (-0.5) * LOG2E
    keys = cap * page_len

    def stacked(n, part, h):
        return jnp.concatenate([held[meta[n, c], part, :, block_of(h)] for c in range(cap)], 0)

    def score(i):
        n, first, h = jobs[i]
        q = queries[n][first * rows:(first + 1) * rows, :]
        scores[i % 2] = dot_nt(q, stacked(n, 0, h))
        if own:
            at = iota((rows, suffix), 0) % suffix
            causal = iota((rows, suffix), 1) <= at
            late_scores[i % 2] = jnp.where(causal, dot_nt(q, own_kv[0, :, block_of(h)]), DEAD)

    def weigh(i):
        n, first, h = jobs[i]
        live = iota((1, keys), 1) < meta[n, cap] * page_len
        s = jnp.where(live, scores[i % 2], DEAD)
        top = jnp.max(s, axis=-1, keepdims=True)
        if own:
            top = jnp.maximum(top, jnp.max(late_scores[i % 2], axis=-1, keepdims=True))
        top = jnp.maximum(top * factor, FLOOR).astype(jnp.bfloat16).astype(jnp.float32)
        p = jnp.exp2(s * factor - top).astype(jnp.bfloat16)
        v = stacked(n, 1, h)
        v = jnp.concatenate([v, jnp.ones_like(v)], 1)
        out = jnp.dot(p, v, preferred_element_type=jnp.float32)
        if own:
            p = jnp.exp2(late_scores[i % 2] * factor - top).astype(jnp.bfloat16)
            v = own_kv[1, :, block_of(h)]
            v = jnp.concatenate([v, jnp.ones_like(v)], 1)
            out = out + jnp.dot(p, v, preferred_element_type=jnp.float32)
        acc_ref, stat_ref = outs[n]
        acc_ref[first] = out[:, :HEAD_SIZE]
        total = out[:, HEAD_SIZE:]
        top = jnp.broadcast_to(top, total.shape)
        blocks = [block_of(j) for j in range(rows // HEAD_SIZE)]
        stat_ref[first] = pack_stats([top[j] for j in blocks], [total[j] for j in blocks])

    for i in range(len(jobs) + 1):
        if i < len(jobs):
            score(i)
        if i > 0:
            weigh(i - 1)
    if keeping:
        keep.wait()


def attend(sizes, jobs, meta, queries, held, own=None, keeping=None, store=None):
    rows, suffix, cap, page_len = sizes
    keys, count = cap * page_len, len(queries)
    heads = len(jobs) // count
    shapes, out_specs = [], []
    for _ in queries:
        shapes.append(jax.ShapeDtypeStruct((heads, rows, HEAD_SIZE), jnp.float32))
        shapes.append(jax.ShapeDtypeStruct((heads, STAT_ROWS, HEAD_SIZE), jnp.bfloat16))
        out_specs += [VMEM, VMEM]
    scratch = [pltpu.VMEM((2, rows, keys), jnp.float32)]
    args, aliases = [meta, *queries], {}
    if own is not None:
        args.append(own)
        scratch.append(pltpu.VMEM((2, rows, suffix), jnp.float32))
    args.append(held)
    in_specs = [SMEM] + [VMEM] * (len(args) - 1)
    if keeping:
        shapes.append(jax.ShapeDtypeStruct(held.shape, held.dtype))
        out_specs.append(HBM)
        scratch.append(pltpu.SemaphoreType.DMA)
    if store is not None:
        aliases[len(args)] = 2 * count
        args.append(store)
        in_specs.append(HBM)
    out = pl.pallas_call(
        functools.partial(attend_kernel, sizes + (count,), jobs, own is not None, keeping),
        out_shape=shapes,
        in_specs=in_specs,
        out_specs=out_specs,
        scratch_shapes=scratch,
        input_output_aliases=aliases,
        compiler_params=pltpu.CompilerParams(vmem_limit_bytes=GRANT),
        cost_estimate=pl.CostEstimate(
            flops=len(jobs) * rows * keys * HEAD_SIZE * 8,
            bytes_accessed=len(jobs) * (rows * 6 + keys * 4) * HEAD_SIZE,
            transcendentals=len(jobs) * rows * keys,
        ),
    )(*args)
    return [(out[2 * n], out[2 * n + 1]) for n in range(count)] + list(out[2 * count:])


def place_kernel(half, column, me_ref, lists_ref, page_ref, old_ref, out_ref, sem):
    me = me_ref[0]
    from_below = (me >= half) == (me % 2 == 0)
    slot = jnp.where(from_below, lists_ref[0, column], lists_ref[1, column])
    copy = pltpu.make_async_copy(page_ref.at[0], out_ref.at[slot], sem)
    copy.start()
    copy.wait()


def place_page(half, column, me, lists, page, store):
    return pl.pallas_call(
        functools.partial(place_kernel, half, column),
        out_shape=jax.ShapeDtypeStruct(store.shape, store.dtype),
        in_specs=[SMEM, SMEM, VMEM, HBM],
        out_specs=HBM,
        scratch_shapes=[pltpu.SemaphoreType.DMA],
        input_output_aliases={3: 0},
        compiler_params=pltpu.CompilerParams(vmem_limit_bytes=GRANT),
        cost_estimate=LIGHT,
    )(me, lists, page, store)


def blend(parts):
    top = functools.reduce(jnp.maximum, [m for _, m, _ in parts])
    scales = [jnp.exp2(m - top) for _, m, _ in parts]
    acc = sum(a * f for (a, _, _), f in zip(parts, scales))
    total = sum(l * f for (_, _, l), f in zip(parts, scales))
    return acc, top, total


def pack_kernel(acc_ref, stat_ref, out_ref):
    heads, rows = acc_ref.shape[:2]
    for h in range(heads):
        out_ref[h, :rows, :] = acc_ref[h].astype(jnp.bfloat16)
        out_ref[h, rows:, :] = stat_ref[h]


def merge_kernel(in_ref, acc_ref, stat_ref, out_ref):
    heads, rows = acc_ref.shape[:2]
    for h in range(heads):
        in_top, in_total = unpack_stats(in_ref[h, rows:, :])
        my_top, my_total = unpack_stats(stat_ref[h])
        tops, totals = [], []
        for j in range(rows // HEAD_SIZE):
            acc, top, total = blend(
                [
                    (in_ref[h, block_of(j), :].astype(jnp.float32), in_top[j], in_total[j]),
                    (acc_ref[h, block_of(j), :], my_top[j], my_total[j]),
                ]
            )
            out_ref[h, block_of(j), :] = acc.astype(out_ref.dtype)
            tops.append(top)
            totals.append(total)
        out_ref[h, rows:, :] = pack_stats(tops, totals)


def final_kernel(suffix, first, in_ref, acc_ref, stat_ref, *refs):
    out_ref, done, sems = refs[-3:]
    heads, rows = in_ref.shape[0], acc_ref.shape[1]
    groups = rows // suffix
    copies = []
    for h in range(heads):
        in_top, in_total = unpack_stats(in_ref[h, rows:, :])
        my_top, my_total = unpack_stats(stat_ref[h])
        for j in range(rows // HEAD_SIZE):
            acc, _, total = blend(
                [
                    (in_ref[h, block_of(j), :].astype(jnp.float32), in_top[j], in_total[j]),
                    (acc_ref[h, block_of(j), :], my_top[j], my_total[j]),
                ]
            )
            out = (acc / total).astype(jnp.bfloat16)
            for i in range(HEAD_SIZE // suffix):
                g = h * groups + j * (HEAD_SIZE // suffix) + i
                done[0, :, block_of(g)] = out[i * suffix:(i + 1) * suffix]
        width = groups * HEAD_SIZE
        copies.append(
            pltpu.make_async_copy(
                done.at[:, :, pl.ds(h * width, width)],
                out_ref.at[:, :, pl.ds((first + h) * width, width)],
                sems.at[h],
            )
        )
        copies[-1].start()
    for copy in copies:
        copy.wait()


def finish(suffix, first, like, block, part, before=None):
    heads, rows = block.shape[0], part[0].shape[1]
    args = [block, *part] + ([] if before is None else [before])
    return pl.pallas_call(
        functools.partial(final_kernel, suffix, first),
        out_shape=jax.ShapeDtypeStruct(like.shape, like.dtype),
        in_specs=[VMEM] * 3 + [HBM] * (len(args) - 3),
        out_specs=HBM,
        scratch_shapes=[
            pltpu.VMEM((1, suffix, heads * rows // suffix * HEAD_SIZE), like.dtype),
            pltpu.SemaphoreType.DMA((heads,)),
        ],
        input_output_aliases={} if before is None else {3: 0},
        compiler_params=pltpu.CompilerParams(vmem_limit_bytes=GRANT),
    )(*args)


def call(kernel, shape, *args):
    size = sum(a.size * a.dtype.itemsize for a in args)
    return pl.pallas_call(
        kernel,
        out_shape=shape,
        in_specs=[VMEM] * len(args),
        out_specs=[VMEM] * len(shape) if isinstance(shape, list) else VMEM,
        compiler_params=pltpu.CompilerParams(vmem_limit_bytes=GRANT),
        cost_estimate=pl.CostEstimate(flops=size, bytes_accessed=2 * size, transcendentals=0),
    )(*args)


def prepare_kernel(cap, pages_dev, length_ref, slot_ref, table_ref, q_ref, first_ref, second_ref):
    maxp = table_ref.shape[1]
    suffix = q_ref.shape[1]
    rows = second_ref.shape[0] - LIST_ROWS
    blocks = rows // suffix
    for g in range(blocks):
        into = slice(g * suffix, (g + 1) * suffix)
        first_ref[into, :] = q_ref[0, :, block_of(g)]
        second_ref[into, :] = q_ref[0, :, block_of(blocks + g)]
    table = table_ref[...]
    owner = lax.div(table, pages_dev)
    local = (table - owner * pages_dev).astype(jnp.float32)
    owner = owner.astype(jnp.float32)
    down, along = iota((maxp, maxp), 0), iota((maxp, maxp), 1)

    def turned(x):
        return jnp.sum(jnp.where(down == along, x, 0.0), 1, keepdims=True)

    before = (turned(owner) == owner) & (along < down)
    rank = jnp.sum(jnp.where(before, 1.0, 0.0), 1, keepdims=True)
    place = iota((maxp, HEAD_SIZE), 1)
    live = jnp.where(iota((maxp, HEAD_SIZE), 0) < length_ref[0], 1.0, 0.0)
    ids = jnp.where(rank == place.astype(jnp.float32), turned(local), 0.0)
    fields = jnp.where(place < cap, ids, jnp.where(place == cap, live, 0.0))
    owned = jnp.where(owner == iota((LIST_ROWS, maxp), 0).astype(jnp.float32), 1.0, 0.0)
    lists = jnp.dot(
        owned.astype(jnp.bfloat16), fields.astype(jnp.bfloat16), preferred_element_type=jnp.float32
    )
    slot = slot_ref[0].astype(jnp.float32)
    lists = jnp.where(iota(lists.shape, 1) == cap + 1, slot, lists)
    first_ref[rows:, :] = lists.astype(jnp.bfloat16)
    second_ref[rows:, :] = lists.astype(jnp.bfloat16)


def prepare(cap, pages_dev, queries, page_table, prefix_pages, new_slots):
    rows = queries.size // HEAD_SIZE // 2
    return pl.pallas_call(
        functools.partial(prepare_kernel, cap, pages_dev),
        out_shape=[jax.ShapeDtypeStruct((rows + LIST_ROWS, HEAD_SIZE), queries.dtype)] * 2,
        in_specs=[SMEM, SMEM, VMEM, VMEM],
        out_specs=[VMEM, VMEM],
        compiler_params=pltpu.CompilerParams(vmem_limit_bytes=GRANT),
    )(prefix_pages, new_slots, page_table, queries)


def queries_travel(queries, suffix_key_value, kv_pages, page_table, prefix_pages, new_slots):
    stores = lax.axis_size("store")
    pages_dev, _, page_len, width = kv_pages.shape
    cap = page_table.shape[1] // stores
    suffix = queries.shape[1]
    rows = queries.shape[2] // width * suffix
    sizes = (rows, suffix, cap, page_len)
    half = stores // 2
    heads = width // HEAD_SIZE // 2
    me = lax.axis_index("store")

    order = list(range(0, stores, 2)) + list(range(1, stores, 2))[::-1]
    up = [(order[i], order[(i + 1) % stores]) for i in range(stores)]
    down = [(order[i], order[i - 1]) for i in range(stores)]
    routes = (up, down)
    sides = range(2)

    def onward(side, x):
        return lax.ppermute(x, "store", routes[side])

    def listed(arrays):
        found = [lax.dynamic_slice(x, (heads * rows + me, 0), (1, HEAD_SIZE)) for x in arrays]
        return jnp.concatenate(found).astype(jnp.int32)

    def after(values, token):
        return lax.optimization_barrier((values, token))[0]

    def attend_own(side, token):
        jobs = [(0, h, side * heads + h) for h in range(heads)]
        mine_here = after(mine[side], token)
        return attend(sizes, jobs, listed(mine[:1]), [mine_here], kv_pages, suffix_key_value[0])

    mine = prepare(cap, pages_dev, queries, page_table, prefix_pages, new_slots)
    moving = [onward(side, mine[side]) for side in sides]
    own = attend_own(0, [])
    token = own
    lists, partial = {}, None
    jobs = [(side, h, side * heads + h) for side in sides for h in range(heads)]
    pages = pages_dev // 2
    for step in range(1, stores):
        came = after(moving, token)
        if step < stores - 1:
            moving = [onward(side, came[side]) for side in sides]
        lists[step] = listed(came)
        if step == 2:
            *parts, store = attend(sizes, jobs, lists[step], came, kv_pages, None, (0, pages))
        elif step == 3:
            span = (pages, pages_dev - pages)
            *parts, store = attend(sizes, jobs, lists[step], came, kv_pages, None, span, store)
        else:
            parts = attend(sizes, jobs, lists[step], came, kv_pages)
        if step == 1:
            blocks = [packed(part) for part in parts]
        else:
            if step == stores - 1:
                parts = after(parts, arrived)
            blocks = [merged(after(partial[side], parts), parts[side]) for side in sides]
        partial = [onward(side, blocks[side]) for side in sides]
        token = blocks
        if step == half:
            own += attend_own(1, token)
            token = [blocks, own]
        if step == stores - 2:
            arrived = shifted(after(suffix_key_value, token), "store", half)
    near = lists[stores // 4]
    store = place_page(half, cap + 1, me[None], near, arrived, after(store, token))
    attended = finish(suffix, 0, queries, after(partial[0], store), own[0])
    attended = finish(suffix, heads, queries, partial[1], own[1], attended)
    return (attended, store)


def wire_of(part):
    heads, rows, columns = part[0].shape
    return jax.ShapeDtypeStruct((heads, rows + STAT_ROWS, columns), jnp.bfloat16)


def packed(part):
    return call(pack_kernel, wire_of(part), *part)


def merged(block, part):
    return call(merge_kernel, wire_of(part), block, *part)


def on_device(queries, suffix_key_value, kv_pages, page_table, prefix_pages, new_slots):
    stores = lax.axis_size("store")
    pulled = page_table.shape[1] // stores * kv_pages[0].size
    pushed = 2 * queries[0].size
    arrays = (queries, suffix_key_value, kv_pages, page_table, prefix_pages, new_slots)
    if pulled >= pushed and stores % 8 == 0 and stores <= LIST_ROWS:
        return queries_travel(*arrays)
    return pages_travel(*arrays)


def solution(mesh):
    return jax.shard_map(
        on_device,
        mesh=mesh,
        in_specs=(
            P(("groups", "store"), None, "tensor"),
            P(("groups", "store"), None, None, "tensor"),
            P(("groups", "store"), None, None, "tensor"),
            P(("groups", "store"), None),
            P(("groups", "store")),
            P(("groups", "store")),
        ),
        out_specs=(
            P(("groups", "store"), None, "tensor"),
            P(("groups", "store"), None, None, "tensor"),
        ),
        check_vma=False,
    )
```

```python
import functools

import jax
import jax.numpy as jnp
from jax import lax
from jax.experimental import pallas as pl
from jax.experimental.pallas import tpu as pltpu
from jax.sharding import PartitionSpec as P

HEAD_SIZE = 128
LOG2E = 1.4426950408889634
DEAD = -1e30
FLOOR = -1e29
STAT_ROWS = 16
LIST_ROWS = 16
GRANT = 20 * 1024 * 1024
LIGHT = pl.CostEstimate(flops=1, bytes_accessed=1, transcendentals=0)
VMEM = pl.BlockSpec(memory_space=pltpu.VMEM)
SMEM = pl.BlockSpec(memory_space=pltpu.SMEM)
HBM = pl.BlockSpec(memory_space=pltpu.HBM)


def shifted(block, axis, distance):
    devices = range(lax.axis_size(axis))
    route = [((i - distance) % len(devices), i) for i in devices]
    return lax.ppermute(block, axis, route)


def block_update(state, head_count, key_rows, value_rows, live, scale):
    top_old, total_old, acc_old = state
    scores = (
        jnp.einsum("qhgd,khd->hgqk", head_count, key_rows, preferred_element_type=jnp.float32)
        * scale
    )
    scores = jnp.where(live, scores, -1e30)
    top_new = jnp.maximum(top_old, jnp.max(scores, axis=-1))
    weights = jnp.where(live, jnp.exp(scores - top_new[..., None]), 0.0)
    factor = jnp.exp(top_old - top_new)
    total_new = total_old * factor + jnp.sum(weights, axis=-1)
    product = jnp.einsum(
        "hgqk,khd->hgqd",
        weights.astype(jnp.bfloat16),
        value_rows,
        preferred_element_type=jnp.float32,
    )
    return (top_new, total_new, acc_old * factor[..., None] + product)


def pages_travel(queries, suffix_key_value, kv_pages, page_table, prefix_pages, new_slots):
    stores = lax.axis_size("store")
    pages_dev = kv_pages.shape[0]
    maxp = page_table.shape[1]
    cap = maxp // stores
    page_len = kv_pages.shape[2]
    width = kv_pages.shape[3]
    kv_heads = width // HEAD_SIZE
    suffix = queries.shape[1]
    groups_per_head = queries.shape[2] // width
    scale = HEAD_SIZE ** (-0.5)
    length = prefix_pages[0]
    table = page_table[0]
    owners = table // pages_dev
    local_ids = table % pages_dev
    entries = jnp.arange(maxp, dtype=jnp.int32)
    same_owner = (owners[:, None] == owners[None, :]) & (entries[:, None] < entries[None, :])
    ranks = jnp.sum(same_owner.astype(jnp.int32), axis=0)
    slots = owners * cap + ranks
    placed = slots[:, None] == entries[None, :]
    slot_entry = jnp.sum(jnp.where(placed, entries[:, None], 0), axis=0)
    wanted = jnp.sum(jnp.where(placed, local_ids[:, None], 0), axis=0)
    asked = lax.all_to_all(
        wanted.reshape(stores, cap), "store", split_axis=0, concat_axis=0, tiled=True
    )
    served = kv_pages[asked.reshape(-1)].reshape(stores, cap, 2, page_len, width)
    received = lax.all_to_all(served, "store", split_axis=0, concat_axis=0, tiled=True).reshape(
        maxp, 2, page_len, width
    )
    head_count = queries[0].reshape(suffix, kv_heads, groups_per_head, HEAD_SIZE)
    own_keys = suffix_key_value[0, 0].reshape(suffix, kv_heads, HEAD_SIZE)
    own_values = suffix_key_value[0, 1].reshape(suffix, kv_heads, HEAD_SIZE)
    rows = jnp.arange(suffix, dtype=jnp.int32)
    causal = rows[None, :] <= rows[:, None]
    start_state = (
        jnp.full((kv_heads, groups_per_head, suffix), -1e30, jnp.float32),
        jnp.zeros((kv_heads, groups_per_head, suffix), jnp.float32),
        jnp.zeros((kv_heads, groups_per_head, suffix, HEAD_SIZE), jnp.float32),
    )
    state = block_update(start_state, head_count, own_keys, own_values, causal, scale)
    block_pages = min(8, maxp)
    live_pages = slot_entry < length
    trips = maxp // block_pages

    def step_block(index, carry):
        first = index * block_pages
        block = lax.dynamic_slice_in_dim(received, first, block_pages, 0)
        alive = lax.dynamic_slice_in_dim(live_pages, first, block_pages, 0)
        alive = jnp.broadcast_to(alive[:, None], (block_pages, page_len)).reshape(
            1, block_pages * page_len
        )
        block_keys = block[:, 0].reshape(block_pages * page_len, kv_heads, HEAD_SIZE)
        block_values = block[:, 1].reshape(block_pages * page_len, kv_heads, HEAD_SIZE)
        return block_update(carry, head_count, block_keys, block_values, alive, scale)

    top_final, total_final, acc_final = lax.fori_loop(0, trips, step_block, state)
    output = acc_final / total_final[..., None]
    attended = (
        output.transpose(2, 0, 1, 3)
        .reshape(1, suffix, groups_per_head * width)
        .astype(jnp.bfloat16)
    )
    arrived, arrived_slot = shifted((suffix_key_value, new_slots), "store", stores // 2)
    new_store = lax.dynamic_update_slice_in_dim(kv_pages, arrived, arrived_slot[0], 0)
    return (attended, new_store)


def dot_nt(a, b):
    return lax.dot_general(a, b, (((1,), (1,)), ((), ())), preferred_element_type=jnp.float32)


def block_of(j):
    return slice(j * HEAD_SIZE, (j + 1) * HEAD_SIZE)


def iota(shape, dim):
    return lax.broadcasted_iota(jnp.int32, shape, dim)


def pack_stats(top, total):
    diagonal = iota((HEAD_SIZE, HEAD_SIZE), 0) == iota((HEAD_SIZE, HEAD_SIZE), 1)
    row = iota((STAT_ROWS, HEAD_SIZE), 0)
    tile = jnp.zeros((STAT_ROWS, HEAD_SIZE), jnp.float32)

    def along(x):
        return jnp.sum(jnp.where(diagonal, x, 0.0), 0, keepdims=True)

    for j, (m, l) in enumerate(zip(top, total)):
        l = along(l)
        high = l.astype(jnp.bfloat16).astype(jnp.float32)
        for t, x in enumerate((along(m), high, l - high)):
            tile = jnp.where(row == 4 * t + j, x, tile)
    return tile.astype(jnp.bfloat16)


def unpack_stats(tile):
    row = iota((STAT_ROWS, 8 * HEAD_SIZE), 0)
    block = iota((STAT_ROWS, 8 * HEAD_SIZE), 1) // HEAD_SIZE
    j = block // 2
    stat = block % 2
    spread = (
        ((row == j) & (stat == 0)) | ((row == j + 4) & (stat == 1)) | ((row == j + 8) & (stat == 1))
    )
    spread = spread.astype(jnp.float32).astype(jnp.bfloat16)
    turned = tile.astype(jnp.float32).T.astype(jnp.bfloat16)
    wide = jnp.dot(turned, spread, preferred_element_type=jnp.float32)
    part = lambda b: wide[:, b * HEAD_SIZE:(b + 1) * HEAD_SIZE]
    return [part(2 * j) for j in range(4)], [part(2 * j + 1) for j in range(4)]


def attend_kernel(sizes, jobs, own, keeping, *refs):
    rows, suffix, cap, page_len, count = sizes
    refs = list(refs)
    meta = refs.pop(0)
    queries = [refs.pop(0) for _ in range(count)]
    own_kv = refs.pop(0) if own else None
    held = refs.pop(0)
    if keeping and keeping[0]:
        refs.pop(0)
    outs = [(refs.pop(0), refs.pop(0)) for _ in range(count)]
    stored = refs.pop(0) if keeping else None
    scores = refs.pop(0)
    late_scores = refs.pop(0) if own else None
    if keeping:
        span = pl.ds(*keeping)
        keep = pltpu.make_async_copy(held.at[span], stored.at[span], refs.pop(0))
        keep.start()
    factor = HEAD_SIZE ** (-0.5) * LOG2E
    keys = cap * page_len

    def stacked(n, part, h):
        return jnp.concatenate([held[meta[n, c], part, :, block_of(h)] for c in range(cap)], 0)

    def score(i):
        n, _, h = jobs[i]
        q = queries[n][h * rows:(h + 1) * rows, :]
        scores[i % 2] = dot_nt(q, stacked(n, 0, h))
        if own:
            at = iota((rows, suffix), 0) % suffix
            causal = iota((rows, suffix), 1) <= at
            late_scores[i % 2] = jnp.where(causal, dot_nt(q, own_kv[0, :, block_of(h)]), DEAD)

    def weigh(i):
        n, spot, h = jobs[i]
        live = iota((1, keys), 1) < meta[n, cap] * page_len
        s = jnp.where(live, scores[i % 2], DEAD)
        top = jnp.max(s, axis=-1, keepdims=True)
        if own:
            top = jnp.maximum(top, jnp.max(late_scores[i % 2], axis=-1, keepdims=True))
        top = jnp.maximum(top * factor, FLOOR).astype(jnp.bfloat16).astype(jnp.float32)
        p = jnp.exp2(s * factor - top).astype(jnp.bfloat16)
        v = stacked(n, 1, h)
        v = jnp.concatenate([v, jnp.ones_like(v)], 1)
        out = jnp.dot(p, v, preferred_element_type=jnp.float32)
        if own:
            p = jnp.exp2(late_scores[i % 2] * factor - top).astype(jnp.bfloat16)
            v = own_kv[1, :, block_of(h)]
            v = jnp.concatenate([v, jnp.ones_like(v)], 1)
            out = out + jnp.dot(p, v, preferred_element_type=jnp.float32)
        acc_ref, stat_ref = outs[n]
        acc_ref[spot] = out[:, :HEAD_SIZE]
        total = out[:, HEAD_SIZE:]
        top = jnp.broadcast_to(top, total.shape)
        blocks = [block_of(j) for j in range(rows // HEAD_SIZE)]
        stat_ref[spot] = pack_stats([top[j] for j in blocks], [total[j] for j in blocks])

    for i in range(len(jobs) + 1):
        if i < len(jobs):
            score(i)
        if i > 0:
            weigh(i - 1)
    if keeping:
        keep.wait()


def attend(sizes, jobs, meta, queries, held, own=None, keeping=None, store=None):
    rows, suffix, cap, page_len = sizes
    keys, count = cap * page_len, len(queries)
    heads = len(jobs) // count
    shapes, out_specs = [], []
    for _ in queries:
        shapes.append(jax.ShapeDtypeStruct((heads, rows, HEAD_SIZE), jnp.float32))
        shapes.append(jax.ShapeDtypeStruct((heads, STAT_ROWS, HEAD_SIZE), jnp.bfloat16))
        out_specs += [VMEM, VMEM]
    scratch = [pltpu.VMEM((2, rows, keys), jnp.float32)]
    args, aliases = [meta, *queries], {}
    if own is not None:
        args.append(own)
        scratch.append(pltpu.VMEM((2, rows, suffix), jnp.float32))
    args.append(held)
    in_specs = [SMEM] + [VMEM] * (len(args) - 1)
    if keeping:
        shapes.append(jax.ShapeDtypeStruct(held.shape, held.dtype))
        out_specs.append(HBM)
        scratch.append(pltpu.SemaphoreType.DMA)
    if store is not None:
        aliases[len(args)] = 2 * count
        args.append(store)
        in_specs.append(HBM)
    work = pl.CostEstimate(
        flops=len(jobs) * rows * keys * HEAD_SIZE * 8,
        bytes_accessed=len(jobs) * (rows * 6 + keys * 4) * HEAD_SIZE,
        transcendentals=len(jobs) * rows * keys,
    )
    out = pl.pallas_call(
        functools.partial(attend_kernel, sizes + (count,), jobs, own is not None, keeping),
        out_shape=shapes,
        in_specs=in_specs,
        out_specs=out_specs,
        scratch_shapes=scratch,
        input_output_aliases=aliases,
        compiler_params=pltpu.CompilerParams(vmem_limit_bytes=GRANT),
        cost_estimate=work,
    )(*args)
    return [(out[2 * n], out[2 * n + 1]) for n in range(count)] + list(out[2 * count:])


def place_kernel(half, column, me_ref, core_ref, near_ref, far_ref, page_ref, old_ref, out_ref, sem):
    me, core = me_ref[0], core_ref[0]
    is_near = ((me >= half) == (me % 2 == 0)) == (core % 2 == 0)
    slot = jnp.where(is_near, near_ref[0, column], far_ref[0, column])
    copy = pltpu.make_async_copy(page_ref.at[0], out_ref.at[slot], sem)
    copy.start()
    copy.wait()


def place_page(half, column, me, core, near, far, page, store):
    return pl.pallas_call(
        functools.partial(place_kernel, half, column),
        out_shape=jax.ShapeDtypeStruct(store.shape, store.dtype),
        in_specs=[SMEM] * 4 + [VMEM, HBM],
        out_specs=HBM,
        scratch_shapes=[pltpu.SemaphoreType.DMA],
        input_output_aliases={5: 0},
        compiler_params=pltpu.CompilerParams(vmem_limit_bytes=GRANT),
        cost_estimate=LIGHT,
    )(me[None], core[None], near, far, page, store)


def blend(parts):
    top = functools.reduce(jnp.maximum, [m for _, m, _ in parts])
    scales = [jnp.exp2(m - top) for _, m, _ in parts]
    acc = sum(a * f for (a, _, _), f in zip(parts, scales))
    total = sum(l * f for (_, _, l), f in zip(parts, scales))
    return acc, top, total


def pack_kernel(acc_ref, stat_ref, out_ref):
    heads, rows = acc_ref.shape[:2]
    for h in range(heads):
        out_ref[h, :rows, :] = acc_ref[h].astype(jnp.bfloat16)
        out_ref[h, rows:, :] = stat_ref[h]


def merge_kernel(in_first, first, in_ref, acc_ref, stat_ref, out_ref):
    heads, rows = out_ref.shape[0], acc_ref.shape[1]
    for h in range(heads):
        in_top, in_total = unpack_stats(in_ref[in_first + h, rows:, :])
        my_top, my_total = unpack_stats(stat_ref[first + h])
        tops, totals = [], []
        for j in range(rows // HEAD_SIZE):
            acc, top, total = blend(
                [
                    (in_ref[in_first + h, block_of(j), :].astype(jnp.float32), in_top[j], in_total[j]),
                    (acc_ref[first + h, block_of(j), :], my_top[j], my_total[j]),
                ]
            )
            out_ref[h, block_of(j), :] = acc.astype(out_ref.dtype)
            tops.append(top)
            totals.append(total)
        out_ref[h, rows:, :] = pack_stats(tops, totals)


def final_kernel(suffix, first, in_ref, acc_ref, stat_ref, *refs):
    out_ref, done, sems = refs[-3:]
    heads, rows = in_ref.shape[0], acc_ref.shape[1]
    groups = rows // suffix
    copies = []
    for h in range(heads):
        in_top, in_total = unpack_stats(in_ref[h, rows:, :])
        my_top, my_total = unpack_stats(stat_ref[h])
        for j in range(rows // HEAD_SIZE):
            acc, _, total = blend(
                [
                    (in_ref[h, block_of(j), :].astype(jnp.float32), in_top[j], in_total[j]),
                    (acc_ref[h, block_of(j), :], my_top[j], my_total[j]),
                ]
            )
            out = (acc / total).astype(jnp.bfloat16)
            for i in range(HEAD_SIZE // suffix):
                g = h * groups + j * (HEAD_SIZE // suffix) + i
                done[0, :, block_of(g)] = out[i * suffix:(i + 1) * suffix]
        width = groups * HEAD_SIZE
        copies.append(
            pltpu.make_async_copy(
                done.at[:, :, pl.ds(h * width, width)],
                out_ref.at[:, :, pl.ds((first + h) * width, width)],
                sems.at[h],
            )
        )
        copies[-1].start()
    for copy in copies:
        copy.wait()


def finish(suffix, first, like, block, part, before=None):
    heads, rows = block.shape[0], part[0].shape[1]
    args = [block, *part] + ([] if before is None else [before])
    return pl.pallas_call(
        functools.partial(final_kernel, suffix, first),
        out_shape=jax.ShapeDtypeStruct(like.shape, like.dtype),
        in_specs=[VMEM] * 3 + [HBM] * (len(args) - 3),
        out_specs=HBM,
        scratch_shapes=[
            pltpu.VMEM((1, suffix, heads * rows // suffix * HEAD_SIZE), like.dtype),
            pltpu.SemaphoreType.DMA((heads,)),
        ],
        input_output_aliases={} if before is None else {3: 0},
        compiler_params=pltpu.CompilerParams(vmem_limit_bytes=GRANT),
    )(*args)


def call(kernel, shape, *args):
    size = sum(a.size * a.dtype.itemsize for a in args)
    return pl.pallas_call(
        kernel,
        out_shape=shape,
        in_specs=[VMEM] * len(args),
        out_specs=[VMEM] * len(shape) if isinstance(shape, list) else VMEM,
        compiler_params=pltpu.CompilerParams(vmem_limit_bytes=GRANT),
        cost_estimate=pl.CostEstimate(flops=size, bytes_accessed=2 * size, transcendentals=0),
    )(*args)


def lists_kernel(cap, pages_dev, length_ref, slot_ref, table_ref, out_ref):
    maxp = table_ref.shape[1]
    table = table_ref[...]
    owner = lax.div(table, pages_dev)
    local = (table - owner * pages_dev).astype(jnp.float32)
    owner = owner.astype(jnp.float32)
    down, along = iota((maxp, maxp), 0), iota((maxp, maxp), 1)

    def turned(x):
        return jnp.sum(jnp.where(down == along, x, 0.0), 1, keepdims=True)

    before = (turned(owner) == owner) & (along < down)
    rank = jnp.sum(jnp.where(before, 1.0, 0.0), 1, keepdims=True)
    place = iota((maxp, HEAD_SIZE), 1)
    live = jnp.where(iota((maxp, HEAD_SIZE), 0) < length_ref[0], 1.0, 0.0)
    ids = jnp.where(rank == place.astype(jnp.float32), turned(local), 0.0)
    fields = jnp.where(place < cap, ids, jnp.where(place == cap, live, 0.0))
    owned = jnp.where(owner == iota((LIST_ROWS, maxp), 0).astype(jnp.float32), 1.0, 0.0)
    lists = jnp.dot(
        owned.astype(jnp.bfloat16), fields.astype(jnp.bfloat16), preferred_element_type=jnp.float32
    )
    slot = slot_ref[0].astype(jnp.float32)
    lists = jnp.where(iota(lists.shape, 1) == cap + 1, slot, lists)
    out_ref[...] = lists.astype(jnp.bfloat16)


def list_pages(cap, pages_dev, page_table, prefix_pages, new_slots):
    return pl.pallas_call(
        functools.partial(lists_kernel, cap, pages_dev),
        out_shape=jax.ShapeDtypeStruct((LIST_ROWS, HEAD_SIZE), jnp.bfloat16),
        in_specs=[SMEM, SMEM, VMEM],
        out_specs=VMEM,
        compiler_params=pltpu.CompilerParams(vmem_limit_bytes=GRANT),
    )(prefix_pages, new_slots, page_table)


def join_kernel(q_ref, lists_ref, out_ref):
    suffix, columns = q_ref.shape[1:]
    for g in range(columns // HEAD_SIZE):
        out_ref[g * suffix:(g + 1) * suffix, :] = q_ref[0, :, block_of(g)]
    out_ref[columns // HEAD_SIZE * suffix:, :] = lists_ref[...]


def queries_travel(queries, suffix_key_value, kv_pages, page_table, prefix_pages, new_slots):
    stores = lax.axis_size("store")
    cores = lax.axis_size("tensor")
    pages_dev, _, page_len, width = kv_pages.shape
    cap = page_table.shape[1] // stores
    heads = width // HEAD_SIZE
    suffix = queries.shape[1]
    rows = queries.shape[2] // width * suffix
    sizes = (rows, suffix, cap, page_len)
    half = stores // 2
    me = lax.axis_index("store")

    order = list(range(0, stores, 2)) + list(range(1, stores, 2))[::-1]
    route = [
        (order[i] * cores + core, order[(i + 1 - 2 * (core % 2)) % stores] * cores + core)
        for core in range(cores)
        for i in range(stores)
    ]

    def onward(x):
        return lax.ppermute(x, ("store", "tensor"), route)

    def listed(x, below):
        row = lax.dynamic_slice(x, (below + me, 0), (1, HEAD_SIZE))
        return row.astype(jnp.int32)

    def after(values, token):
        return lax.optimization_barrier((values, token))[0]

    def joined(x, rows_below):
        shape = jax.ShapeDtypeStruct((heads * rows + LIST_ROWS, HEAD_SIZE), queries.dtype)
        return call(join_kernel, shape, x, rows_below)

    first = onward(queries)
    mine = list_pages(cap, pages_dev, page_table, prefix_pages, new_slots)
    moving = joined(first, onward(mine))

    own_queries = None
    halves = [range(0, heads // 2), range(heads // 2, heads)]
    token = []
    lists, own = {}, []
    for step in range(1, stores):
        came = after(moving, token)
        if step < stores - 1:
            moving = onward(came)
        lists[step] = listed(came, heads * rows)
        if step == stores - 3:
            arrived = shifted(after(suffix_key_value, token), "store", half)
        jobs = [(0, h, h) for h in range(heads)]
        keeping, pages = None, pages_dev // 2
        if step == 1:
            keeping = (0, pages)
            part, store = attend(sizes, jobs, lists[step], [came], kv_pages, None, keeping)
        elif step == 2:
            keeping = (pages, pages_dev - pages)
            part, store = attend(sizes, jobs, lists[step], [came], kv_pages, None, keeping, store)
        else:
            part, = attend(sizes, jobs, lists[step], [came], kv_pages)
        if step == 1:
            blocks = [packed(part)]
        elif step < stores - 2:
            blocks = [merged(after(partial[0], part), part, 0, 0, heads)]
        else:
            blocks = []
            for n, half_heads in enumerate(halves):
                block, at = (partial[0], half_heads[0]) if len(partial) == 1 else (partial[n], 0)
                block = after(block, [part, blocks])
                blocks.append(merged(block, part, at, half_heads[0], len(half_heads)))
        partial = [onward(block) for block in blocks]
        token = blocks
        if step == stores - 2:
            token = [blocks, arrived]
        if step in (half - 1, half):
            if own_queries is None:
                own_queries = joined(after(queries, token), mine)
            jobs = [(0, n, h) for n, h in enumerate(halves[len(own)])]
            x = after(own_queries, token)
            own += attend(sizes, jobs, listed(mine, 0), [x], kv_pages, suffix_key_value[0])
            token = [blocks, own]

    quarter = stores // 4
    near, far = lists[quarter], lists[stores - quarter]
    core = lax.axis_index("tensor")
    store = place_page(half, cap + 1, me, core, near, far, arrived, after(store, token))
    attended = finish(suffix, 0, queries, after(partial[0], store), own[0])
    attended = finish(suffix, heads // 2, queries, partial[1], own[1], attended)
    return (attended, store)


def wire_of(part, heads):
    rows, columns = part[0].shape[1:]
    return jax.ShapeDtypeStruct((heads, rows + STAT_ROWS, columns), jnp.bfloat16)


def packed(part):
    return call(pack_kernel, wire_of(part, part[0].shape[0]), *part)


def merged(block, part, in_first, first, heads):
    kernel = functools.partial(merge_kernel, in_first, first)
    return call(kernel, wire_of(part, heads), block, *part)


def on_device(queries, suffix_key_value, kv_pages, page_table, prefix_pages, new_slots):
    stores = lax.axis_size("store")
    pulled = page_table.shape[1] // stores * kv_pages[0].size
    pushed = 2 * queries[0].size
    arrays = (queries, suffix_key_value, kv_pages, page_table, prefix_pages, new_slots)
    if pulled >= pushed and stores % 8 == 0 and stores <= LIST_ROWS:
        return queries_travel(*arrays)
    return pages_travel(*arrays)


def solution(mesh):
    return jax.shard_map(
        on_device,
        mesh=mesh,
        in_specs=(
            P(("groups", "store"), None, "tensor"),
            P(("groups", "store"), None, None, "tensor"),
            P(("groups", "store"), None, None, "tensor"),
            P(("groups", "store"), None),
            P(("groups", "store")),
            P(("groups", "store")),
        ),
        out_specs=(
            P(("groups", "store"), None, "tensor"),
            P(("groups", "store"), None, None, "tensor"),
        ),
        check_vma=False,
    )
```

```python
import functools

import jax
import jax.numpy as jnp
from jax import lax
from jax.experimental import pallas as pl
from jax.experimental.pallas import tpu as pltpu
from jax.sharding import PartitionSpec as P

HEAD_SIZE = 128
LOG2E = 1.4426950408889634
DEAD = -1e30
FLOOR = -1e29
STAT_ROWS = 16
LIST_ROWS = 16
GRANT = 20 * 1024 * 1024
LIGHT = pl.CostEstimate(flops=1, bytes_accessed=1, transcendentals=0)
VMEM = pl.BlockSpec(memory_space=pltpu.VMEM)
SMEM = pl.BlockSpec(memory_space=pltpu.SMEM)
HBM = pl.BlockSpec(memory_space=pltpu.HBM)


def shifted(block, axis, distance):
    devices = range(lax.axis_size(axis))
    route = [((i - distance) % len(devices), i) for i in devices]
    return lax.ppermute(block, axis, route)


def block_update(state, head_count, key_rows, value_rows, live, scale):
    top_old, total_old, acc_old = state
    scores = (
        jnp.einsum("qhgd,khd->hgqk", head_count, key_rows, preferred_element_type=jnp.float32)
        * scale
    )
    scores = jnp.where(live, scores, -1e30)
    top_new = jnp.maximum(top_old, jnp.max(scores, axis=-1))
    weights = jnp.where(live, jnp.exp(scores - top_new[..., None]), 0.0)
    factor = jnp.exp(top_old - top_new)
    total_new = total_old * factor + jnp.sum(weights, axis=-1)
    product = jnp.einsum(
        "hgqk,khd->hgqd",
        weights.astype(jnp.bfloat16),
        value_rows,
        preferred_element_type=jnp.float32,
    )
    return (top_new, total_new, acc_old * factor[..., None] + product)


def pages_travel(queries, suffix_key_value, kv_pages, page_table, prefix_pages, new_slots):
    stores = lax.axis_size("store")
    pages_dev = kv_pages.shape[0]
    maxp = page_table.shape[1]
    cap = maxp // stores
    page_len = kv_pages.shape[2]
    width = kv_pages.shape[3]
    kv_heads = width // HEAD_SIZE
    suffix = queries.shape[1]
    groups_per_head = queries.shape[2] // width
    scale = HEAD_SIZE ** (-0.5)
    length = prefix_pages[0]
    table = page_table[0]
    owners = table // pages_dev
    local_ids = table % pages_dev
    entries = jnp.arange(maxp, dtype=jnp.int32)
    same_owner = (owners[:, None] == owners[None, :]) & (entries[:, None] < entries[None, :])
    ranks = jnp.sum(same_owner.astype(jnp.int32), axis=0)
    slots = owners * cap + ranks
    placed = slots[:, None] == entries[None, :]
    slot_entry = jnp.sum(jnp.where(placed, entries[:, None], 0), axis=0)
    wanted = jnp.sum(jnp.where(placed, local_ids[:, None], 0), axis=0)
    asked = lax.all_to_all(
        wanted.reshape(stores, cap), "store", split_axis=0, concat_axis=0, tiled=True
    )
    served = kv_pages[asked.reshape(-1)].reshape(stores, cap, 2, page_len, width)
    received = lax.all_to_all(served, "store", split_axis=0, concat_axis=0, tiled=True).reshape(
        maxp, 2, page_len, width
    )
    head_count = queries[0].reshape(suffix, kv_heads, groups_per_head, HEAD_SIZE)
    own_keys = suffix_key_value[0, 0].reshape(suffix, kv_heads, HEAD_SIZE)
    own_values = suffix_key_value[0, 1].reshape(suffix, kv_heads, HEAD_SIZE)
    rows = jnp.arange(suffix, dtype=jnp.int32)
    causal = rows[None, :] <= rows[:, None]
    start_state = (
        jnp.full((kv_heads, groups_per_head, suffix), -1e30, jnp.float32),
        jnp.zeros((kv_heads, groups_per_head, suffix), jnp.float32),
        jnp.zeros((kv_heads, groups_per_head, suffix, HEAD_SIZE), jnp.float32),
    )
    state = block_update(start_state, head_count, own_keys, own_values, causal, scale)
    block_pages = min(8, maxp)
    live_pages = slot_entry < length
    trips = maxp // block_pages

    def step_block(index, carry):
        first = index * block_pages
        block = lax.dynamic_slice_in_dim(received, first, block_pages, 0)
        alive = lax.dynamic_slice_in_dim(live_pages, first, block_pages, 0)
        alive = jnp.broadcast_to(alive[:, None], (block_pages, page_len)).reshape(
            1, block_pages * page_len
        )
        block_keys = block[:, 0].reshape(block_pages * page_len, kv_heads, HEAD_SIZE)
        block_values = block[:, 1].reshape(block_pages * page_len, kv_heads, HEAD_SIZE)
        return block_update(carry, head_count, block_keys, block_values, alive, scale)

    top_final, total_final, acc_final = lax.fori_loop(0, trips, step_block, state)
    output = acc_final / total_final[..., None]
    attended = (
        output.transpose(2, 0, 1, 3)
        .reshape(1, suffix, groups_per_head * width)
        .astype(jnp.bfloat16)
    )
    arrived, arrived_slot = shifted((suffix_key_value, new_slots), "store", stores // 2)
    new_store = lax.dynamic_update_slice_in_dim(kv_pages, arrived, arrived_slot[0], 0)
    return (attended, new_store)


def dot_nt(a, b):
    return lax.dot_general(a, b, (((1,), (1,)), ((), ())), preferred_element_type=jnp.float32)


def block_of(j):
    return slice(j * HEAD_SIZE, (j + 1) * HEAD_SIZE)


def iota(shape, dim):
    return lax.broadcasted_iota(jnp.int32, shape, dim)


def pack_stats(top, total):
    diagonal = iota((HEAD_SIZE, HEAD_SIZE), 0) == iota((HEAD_SIZE, HEAD_SIZE), 1)
    row = iota((STAT_ROWS, HEAD_SIZE), 0)
    tile = jnp.zeros((STAT_ROWS, HEAD_SIZE), jnp.float32)

    def along(x):
        return jnp.sum(jnp.where(diagonal, x, 0.0), 0, keepdims=True)

    for j, (m, l) in enumerate(zip(top, total)):
        l = along(l)
        high = l.astype(jnp.bfloat16).astype(jnp.float32)
        for t, x in enumerate((along(m), high, l - high)):
            tile = jnp.where(row == 4 * t + j, x, tile)
    return tile.astype(jnp.bfloat16)


def unpack_stats(tile):
    row = iota((STAT_ROWS, 8 * HEAD_SIZE), 0)
    block = iota((STAT_ROWS, 8 * HEAD_SIZE), 1) // HEAD_SIZE
    j = block // 2
    stat = block % 2
    spread = (
        ((row == j) & (stat == 0)) | ((row == j + 4) & (stat == 1)) | ((row == j + 8) & (stat == 1))
    )
    spread = spread.astype(jnp.float32).astype(jnp.bfloat16)
    turned = tile.astype(jnp.float32).T.astype(jnp.bfloat16)
    wide = jnp.dot(turned, spread, preferred_element_type=jnp.float32)
    part = lambda b: wide[:, b * HEAD_SIZE:(b + 1) * HEAD_SIZE]
    return [part(2 * j) for j in range(4)], [part(2 * j + 1) for j in range(4)]


def attend_kernel(sizes, jobs, own, keeping, *refs):
    rows, suffix, cap, page_len, count = sizes
    refs = list(refs)
    meta = refs.pop(0)
    queries = [refs.pop(0) for _ in range(count)]
    own_kv = refs.pop(0) if own else None
    held = refs.pop(0)
    if keeping and keeping[0]:
        refs.pop(0)
    outs = [(refs.pop(0), refs.pop(0)) for _ in range(count)]
    stored = refs.pop(0) if keeping else None
    scores = refs.pop(0)
    late_scores = refs.pop(0) if own else None
    if keeping:
        span = pl.ds(*keeping)
        keep = pltpu.make_async_copy(held.at[span], stored.at[span], refs.pop(0))
        keep.start()
    factor = HEAD_SIZE ** (-0.5) * LOG2E
    keys = cap * page_len

    def stacked(n, part, h):
        return jnp.concatenate([held[meta[n, c], part, :, block_of(h)] for c in range(cap)], 0)

    def score(i):
        n, _, h = jobs[i]
        q = queries[n][h * rows:(h + 1) * rows, :]
        scores[i % 2] = dot_nt(q, stacked(n, 0, h))
        if own:
            at = iota((rows, suffix), 0) % suffix
            causal = iota((rows, suffix), 1) <= at
            late_scores[i % 2] = jnp.where(causal, dot_nt(q, own_kv[0, :, block_of(h)]), DEAD)

    def weigh(i):
        n, spot, h = jobs[i]
        live = iota((1, keys), 1) < meta[n, cap] * page_len
        s = jnp.where(live, scores[i % 2], DEAD)
        top = jnp.max(s, axis=-1, keepdims=True)
        if own:
            top = jnp.maximum(top, jnp.max(late_scores[i % 2], axis=-1, keepdims=True))
        top = jnp.maximum(top * factor, FLOOR).astype(jnp.bfloat16).astype(jnp.float32)
        p = jnp.exp2(s * factor - top).astype(jnp.bfloat16)
        v = stacked(n, 1, h)
        v = jnp.concatenate([v, jnp.ones_like(v)], 1)
        out = jnp.dot(p, v, preferred_element_type=jnp.float32)
        if own:
            p = jnp.exp2(late_scores[i % 2] * factor - top).astype(jnp.bfloat16)
            v = own_kv[1, :, block_of(h)]
            v = jnp.concatenate([v, jnp.ones_like(v)], 1)
            out = out + jnp.dot(p, v, preferred_element_type=jnp.float32)
        acc_ref, stat_ref = outs[n]
        acc_ref[spot] = out[:, :HEAD_SIZE]
        total = out[:, HEAD_SIZE:]
        top = jnp.broadcast_to(top, total.shape)
        blocks = [block_of(j) for j in range(rows // HEAD_SIZE)]
        stat_ref[spot] = pack_stats([top[j] for j in blocks], [total[j] for j in blocks])

    for i in range(len(jobs) + 1):
        if i < len(jobs):
            score(i)
        if i > 0:
            weigh(i - 1)
    if keeping:
        keep.wait()


def attend(sizes, jobs, meta, queries, held, own=None, keeping=None, store=None):
    rows, suffix, cap, page_len = sizes
    keys, count = cap * page_len, len(queries)
    heads = len(jobs) // count
    shapes, out_specs = [], []
    for _ in queries:
        shapes.append(jax.ShapeDtypeStruct((heads, rows, HEAD_SIZE), jnp.float32))
        shapes.append(jax.ShapeDtypeStruct((heads, STAT_ROWS, HEAD_SIZE), jnp.bfloat16))
        out_specs += [VMEM, VMEM]
    scratch = [pltpu.VMEM((2, rows, keys), jnp.float32)]
    args, aliases = [meta, *queries], {}
    if own is not None:
        args.append(own)
        scratch.append(pltpu.VMEM((2, rows, suffix), jnp.float32))
    args.append(held)
    in_specs = [SMEM] + [VMEM] * (len(args) - 1)
    if keeping:
        shapes.append(jax.ShapeDtypeStruct(held.shape, held.dtype))
        out_specs.append(HBM)
        scratch.append(pltpu.SemaphoreType.DMA)
    if store is not None:
        aliases[len(args)] = 2 * count
        args.append(store)
        in_specs.append(HBM)
    out = pl.pallas_call(
        functools.partial(attend_kernel, sizes + (count,), jobs, own is not None, keeping),
        out_shape=shapes,
        in_specs=in_specs,
        out_specs=out_specs,
        scratch_shapes=scratch,
        input_output_aliases=aliases,
        compiler_params=pltpu.CompilerParams(vmem_limit_bytes=GRANT),
        cost_estimate=pl.CostEstimate(
            flops=len(jobs) * rows * keys * HEAD_SIZE * 8,
            bytes_accessed=len(jobs) * (rows * 6 + keys * 4) * HEAD_SIZE,
            transcendentals=len(jobs) * rows * keys,
        ),
    )(*args)
    return [(out[2 * n], out[2 * n + 1]) for n in range(count)] + list(out[2 * count:])


def hold_kernel(pages_ref, before_ref, out_ref, sem):
    copy = pltpu.make_async_copy(pages_ref, out_ref, sem)
    copy.start()
    copy.wait()


def hold(pages, before):
    return pl.pallas_call(
        hold_kernel,
        out_shape=jax.ShapeDtypeStruct(pages.shape, pages.dtype),
        in_specs=[HBM, VMEM],
        out_specs=VMEM,
        scratch_shapes=[pltpu.SemaphoreType.DMA],
        compiler_params=pltpu.CompilerParams(vmem_limit_bytes=48 * 1024 * 1024),
        cost_estimate=LIGHT,
    )(pages, before)


def place_kernel(half, column, me_ref, core_ref, near_ref, far_ref, page_ref, old_ref, out_ref, sem):
    me, core = me_ref[0], core_ref[0]
    is_near = ((me >= half) == (me % 2 == 0)) == (core % 2 == 0)
    slot = jnp.where(is_near, near_ref[0, column], far_ref[0, column])
    copy = pltpu.make_async_copy(page_ref.at[0], out_ref.at[slot], sem)
    copy.start()
    copy.wait()


def place_page(half, column, me, core, near, far, page, store):
    return pl.pallas_call(
        functools.partial(place_kernel, half, column),
        out_shape=jax.ShapeDtypeStruct(store.shape, store.dtype),
        in_specs=[SMEM] * 4 + [VMEM, HBM],
        out_specs=HBM,
        scratch_shapes=[pltpu.SemaphoreType.DMA],
        input_output_aliases={5: 0},
        compiler_params=pltpu.CompilerParams(vmem_limit_bytes=GRANT),
        cost_estimate=LIGHT,
    )(me[None], core[None], near, far, page, store)


def blend(parts):
    top = functools.reduce(jnp.maximum, [m for _, m, _ in parts])
    scales = [jnp.exp2(m - top) for _, m, _ in parts]
    acc = sum(a * f for (a, _, _), f in zip(parts, scales))
    total = sum(l * f for (_, _, l), f in zip(parts, scales))
    return acc, top, total


def pack_kernel(acc_ref, stat_ref, out_ref):
    heads, rows = acc_ref.shape[:2]
    for h in range(heads):
        out_ref[h, :rows, :] = acc_ref[h].astype(jnp.bfloat16)
        out_ref[h, rows:, :] = stat_ref[h]


def merge_kernel(in_first, first, in_ref, acc_ref, stat_ref, out_ref):
    heads, rows = out_ref.shape[0], acc_ref.shape[1]
    for h in range(heads):
        in_top, in_total = unpack_stats(in_ref[in_first + h, rows:, :])
        my_top, my_total = unpack_stats(stat_ref[first + h])
        tops, totals = [], []
        for j in range(rows // HEAD_SIZE):
            acc, top, total = blend(
                [
                    (in_ref[in_first + h, block_of(j), :].astype(jnp.float32), in_top[j], in_total[j]),
                    (acc_ref[first + h, block_of(j), :], my_top[j], my_total[j]),
                ]
            )
            out_ref[h, block_of(j), :] = acc.astype(out_ref.dtype)
            tops.append(top)
            totals.append(total)
        out_ref[h, rows:, :] = pack_stats(tops, totals)


def final_kernel(suffix, first, in_ref, acc_ref, stat_ref, *refs):
    out_ref, done, sems = refs[-3:]
    heads, rows = in_ref.shape[0], acc_ref.shape[1]
    groups = rows // suffix
    copies = []
    for h in range(heads):
        in_top, in_total = unpack_stats(in_ref[h, rows:, :])
        my_top, my_total = unpack_stats(stat_ref[h])
        for j in range(rows // HEAD_SIZE):
            acc, _, total = blend(
                [
                    (in_ref[h, block_of(j), :].astype(jnp.float32), in_top[j], in_total[j]),
                    (acc_ref[h, block_of(j), :], my_top[j], my_total[j]),
                ]
            )
            out = (acc / total).astype(jnp.bfloat16)
            for i in range(HEAD_SIZE // suffix):
                g = h * groups + j * (HEAD_SIZE // suffix) + i
                done[0, :, block_of(g)] = out[i * suffix:(i + 1) * suffix]
        width = groups * HEAD_SIZE
        copies.append(
            pltpu.make_async_copy(
                done.at[:, :, pl.ds(h * width, width)],
                out_ref.at[:, :, pl.ds((first + h) * width, width)],
                sems.at[h],
            )
        )
        copies[-1].start()
    for copy in copies:
        copy.wait()


def finish(suffix, first, like, block, part, before=None):
    heads, rows = block.shape[0], part[0].shape[1]
    args = [block, *part] + ([] if before is None else [before])
    return pl.pallas_call(
        functools.partial(final_kernel, suffix, first),
        out_shape=jax.ShapeDtypeStruct(like.shape, like.dtype),
        in_specs=[VMEM] * 3 + [HBM] * (len(args) - 3),
        out_specs=HBM,
        scratch_shapes=[
            pltpu.VMEM((1, suffix, heads * rows // suffix * HEAD_SIZE), like.dtype),
            pltpu.SemaphoreType.DMA((heads,)),
        ],
        input_output_aliases={} if before is None else {3: 0},
        compiler_params=pltpu.CompilerParams(vmem_limit_bytes=GRANT),
    )(*args)


def call(kernel, shape, *args):
    size = sum(a.size * a.dtype.itemsize for a in args)
    return pl.pallas_call(
        kernel,
        out_shape=shape,
        in_specs=[VMEM] * len(args),
        out_specs=[VMEM] * len(shape) if isinstance(shape, list) else VMEM,
        compiler_params=pltpu.CompilerParams(vmem_limit_bytes=GRANT),
        cost_estimate=pl.CostEstimate(flops=size, bytes_accessed=2 * size, transcendentals=0),
    )(*args)


def lists_kernel(cap, pages_dev, length_ref, slot_ref, table_ref, out_ref):
    maxp = table_ref.shape[1]
    table = table_ref[...]
    owner = lax.div(table, pages_dev)
    local = (table - owner * pages_dev).astype(jnp.float32)
    owner = owner.astype(jnp.float32)
    down, along = iota((maxp, maxp), 0), iota((maxp, maxp), 1)

    def turned(x):
        return jnp.sum(jnp.where(down == along, x, 0.0), 1, keepdims=True)

    before = (turned(owner) == owner) & (along < down)
    rank = jnp.sum(jnp.where(before, 1.0, 0.0), 1, keepdims=True)
    place = iota((maxp, HEAD_SIZE), 1)
    live = jnp.where(iota((maxp, HEAD_SIZE), 0) < length_ref[0], 1.0, 0.0)
    ids = jnp.where(rank == place.astype(jnp.float32), turned(local), 0.0)
    fields = jnp.where(place < cap, ids, jnp.where(place == cap, live, 0.0))
    owned = jnp.where(owner == iota((LIST_ROWS, maxp), 0).astype(jnp.float32), 1.0, 0.0)
    lists = jnp.dot(
        owned.astype(jnp.bfloat16), fields.astype(jnp.bfloat16), preferred_element_type=jnp.float32
    )
    slot = slot_ref[0].astype(jnp.float32)
    lists = jnp.where(iota(lists.shape, 1) == cap + 1, slot, lists)
    out_ref[...] = lists.astype(jnp.bfloat16)


def list_pages(cap, pages_dev, page_table, prefix_pages, new_slots):
    return pl.pallas_call(
        functools.partial(lists_kernel, cap, pages_dev),
        out_shape=jax.ShapeDtypeStruct((LIST_ROWS, HEAD_SIZE), jnp.bfloat16),
        in_specs=[SMEM, SMEM, VMEM],
        out_specs=VMEM,
        compiler_params=pltpu.CompilerParams(vmem_limit_bytes=GRANT),
    )(prefix_pages, new_slots, page_table)


def join_kernel(q_ref, lists_ref, out_ref):
    suffix, columns = q_ref.shape[1:]
    for g in range(columns // HEAD_SIZE):
        out_ref[g * suffix:(g + 1) * suffix, :] = q_ref[0, :, block_of(g)]
    out_ref[columns // HEAD_SIZE * suffix:, :] = lists_ref[...]


def queries_travel(queries, suffix_key_value, kv_pages, page_table, prefix_pages, new_slots):
    stores = lax.axis_size("store")
    cores = lax.axis_size("tensor")
    pages_dev, _, page_len, width = kv_pages.shape
    cap = page_table.shape[1] // stores
    heads = width // HEAD_SIZE
    suffix = queries.shape[1]
    rows = queries.shape[2] // width * suffix
    sizes = (rows, suffix, cap, page_len)
    half = stores // 2
    me = lax.axis_index("store")

    order = list(range(0, stores, 2)) + list(range(1, stores, 2))[::-1]
    route = [
        (order[i] * cores + core, order[(i + 1 - 2 * (core % 2)) % stores] * cores + core)
        for core in range(cores)
        for i in range(stores)
    ]

    def onward(x):
        return lax.ppermute(x, ("store", "tensor"), route)

    def listed(x, below):
        row = lax.dynamic_slice(x, (below + me, 0), (1, HEAD_SIZE))
        return row.astype(jnp.int32)

    def after(values, token):
        return lax.optimization_barrier((values, token))[0]

    def joined(x, rows_below):
        shape = jax.ShapeDtypeStruct((heads * rows + LIST_ROWS, HEAD_SIZE), queries.dtype)
        return call(join_kernel, shape, x, rows_below)

    first = onward(queries)
    mine = list_pages(cap, pages_dev, page_table, prefix_pages, new_slots)
    held = hold(kv_pages, mine)
    moving = joined(after(first, held), onward(mine))

    own_queries = None
    halves = [range(0, heads // 2), range(heads // 2, heads)]
    token = []
    lists, own = {}, []
    for step in range(1, stores):
        came = after(moving, token)
        if step < stores - 1:
            moving = onward(came)
        lists[step] = listed(came, heads * rows)
        if step == stores - 2:
            arrived = shifted(after(suffix_key_value, token), "store", half)
        jobs = [(0, h, h) for h in range(heads)]
        keeping, pages = None, pages_dev // 2
        if step == 1:
            keeping = (0, pages)
            part, store = attend(sizes, jobs, lists[step], [came], held, None, keeping)
        elif step == 2:
            keeping = (pages, pages_dev - pages)
            part, store = attend(sizes, jobs, lists[step], [came], held, None, keeping, store)
        else:
            part, = attend(sizes, jobs, lists[step], [came], held)
        if step == 1:
            blocks = [packed(part)]
        elif step < stores - 1:
            blocks = [merged(after(partial[0], part), part, 0, 0, heads)]
        else:
            part = after(part, arrived) if step == stores - 1 else part
            blocks = []
            for n, half_heads in enumerate(halves):
                block, at = (partial[0], half_heads[0]) if len(partial) == 1 else (partial[n], 0)
                block = after(block, [part, blocks])
                blocks.append(merged(block, part, at, half_heads[0], len(half_heads)))
        partial = [onward(block) for block in blocks]
        token = blocks
        if step in (half - 1, half):
            if own_queries is None:
                own_queries = joined(after(queries, token), mine)
            jobs = [(0, n, h) for n, h in enumerate(halves[len(own)])]
            x = after(own_queries, token)
            own += attend(sizes, jobs, listed(mine, 0), [x], held, suffix_key_value[0])
            token = [blocks, own]

    quarter = stores // 4
    near, far = lists[quarter], lists[stores - quarter]
    core = lax.axis_index("tensor")
    store = place_page(half, cap + 1, me, core, near, far, arrived, after(store, token))
    attended = finish(suffix, 0, queries, after(partial[0], store), own[0])
    attended = finish(suffix, heads // 2, queries, partial[1], own[1], attended)
    return (attended, store)


def wire_of(part, heads):
    rows, columns = part[0].shape[1:]
    return jax.ShapeDtypeStruct((heads, rows + STAT_ROWS, columns), jnp.bfloat16)


def packed(part):
    return call(pack_kernel, wire_of(part, part[0].shape[0]), *part)


def merged(block, part, in_first, first, heads):
    kernel = functools.partial(merge_kernel, in_first, first)
    return call(kernel, wire_of(part, heads), block, *part)


def on_device(queries, suffix_key_value, kv_pages, page_table, prefix_pages, new_slots):
    stores = lax.axis_size("store")
    pulled = page_table.shape[1] // stores * kv_pages[0].size
    pushed = 2 * queries[0].size
    arrays = (queries, suffix_key_value, kv_pages, page_table, prefix_pages, new_slots)
    if pulled >= pushed and stores % 8 == 0 and stores <= LIST_ROWS:
        return queries_travel(*arrays)
    return pages_travel(*arrays)


def solution(mesh):
    return jax.shard_map(
        on_device,
        mesh=mesh,
        in_specs=(
            P(("groups", "store"), None, "tensor"),
            P(("groups", "store"), None, None, "tensor"),
            P(("groups", "store"), None, None, "tensor"),
            P(("groups", "store"), None),
            P(("groups", "store")),
            P(("groups", "store")),
        ),
        out_specs=(
            P(("groups", "store"), None, "tensor"),
            P(("groups", "store"), None, None, "tensor"),
        ),
        check_vma=False,
    )
```

```python
import functools

import jax
import jax.numpy as jnp
from jax import lax
from jax.experimental import pallas as pl
from jax.experimental.pallas import tpu as pltpu
from jax.sharding import PartitionSpec as P

HEAD_SIZE = 128
LOG2E = 1.4426950408889634
DEAD = -1e30
FLOOR = -1e29
STAT_ROWS = 16
LIST_ROWS = 16
GRANT = 20 * 1024 * 1024
LIGHT = pl.CostEstimate(flops=1, bytes_accessed=1, transcendentals=0)
VMEM = pl.BlockSpec(memory_space=pltpu.VMEM)
SMEM = pl.BlockSpec(memory_space=pltpu.SMEM)
HBM = pl.BlockSpec(memory_space=pltpu.HBM)


def shifted(block, axis, distance):
    devices = range(lax.axis_size(axis))
    route = [((i - distance) % len(devices), i) for i in devices]
    return lax.ppermute(block, axis, route)


def block_update(state, head_count, key_rows, value_rows, live, scale):
    top_old, total_old, acc_old = state
    scores = (
        jnp.einsum("qhgd,khd->hgqk", head_count, key_rows, preferred_element_type=jnp.float32)
        * scale
    )
    scores = jnp.where(live, scores, -1e30)
    top_new = jnp.maximum(top_old, jnp.max(scores, axis=-1))
    weights = jnp.where(live, jnp.exp(scores - top_new[..., None]), 0.0)
    factor = jnp.exp(top_old - top_new)
    total_new = total_old * factor + jnp.sum(weights, axis=-1)
    product = jnp.einsum(
        "hgqk,khd->hgqd",
        weights.astype(jnp.bfloat16),
        value_rows,
        preferred_element_type=jnp.float32,
    )
    return (top_new, total_new, acc_old * factor[..., None] + product)


def pages_travel(queries, suffix_key_value, kv_pages, page_table, prefix_pages, new_slots):
    stores = lax.axis_size("store")
    pages_dev = kv_pages.shape[0]
    maxp = page_table.shape[1]
    cap = maxp // stores
    page_len = kv_pages.shape[2]
    width = kv_pages.shape[3]
    kv_heads = width // HEAD_SIZE
    suffix = queries.shape[1]
    groups_per_head = queries.shape[2] // width
    scale = HEAD_SIZE ** (-0.5)
    length = prefix_pages[0]
    table = page_table[0]
    owners = table // pages_dev
    local_ids = table % pages_dev
    entries = jnp.arange(maxp, dtype=jnp.int32)
    same_owner = (owners[:, None] == owners[None, :]) & (entries[:, None] < entries[None, :])
    ranks = jnp.sum(same_owner.astype(jnp.int32), axis=0)
    slots = owners * cap + ranks
    placed = slots[:, None] == entries[None, :]
    slot_entry = jnp.sum(jnp.where(placed, entries[:, None], 0), axis=0)
    wanted = jnp.sum(jnp.where(placed, local_ids[:, None], 0), axis=0)
    asked = lax.all_to_all(
        wanted.reshape(stores, cap), "store", split_axis=0, concat_axis=0, tiled=True
    )
    served = kv_pages[asked.reshape(-1)].reshape(stores, cap, 2, page_len, width)
    received = lax.all_to_all(served, "store", split_axis=0, concat_axis=0, tiled=True).reshape(
        maxp, 2, page_len, width
    )
    head_count = queries[0].reshape(suffix, kv_heads, groups_per_head, HEAD_SIZE)
    own_keys = suffix_key_value[0, 0].reshape(suffix, kv_heads, HEAD_SIZE)
    own_values = suffix_key_value[0, 1].reshape(suffix, kv_heads, HEAD_SIZE)
    rows = jnp.arange(suffix, dtype=jnp.int32)
    causal = rows[None, :] <= rows[:, None]
    start_state = (
        jnp.full((kv_heads, groups_per_head, suffix), -1e30, jnp.float32),
        jnp.zeros((kv_heads, groups_per_head, suffix), jnp.float32),
        jnp.zeros((kv_heads, groups_per_head, suffix, HEAD_SIZE), jnp.float32),
    )
    state = block_update(start_state, head_count, own_keys, own_values, causal, scale)
    block_pages = min(8, maxp)
    live_pages = slot_entry < length
    trips = maxp // block_pages

    def step_block(index, carry):
        first = index * block_pages
        block = lax.dynamic_slice_in_dim(received, first, block_pages, 0)
        alive = lax.dynamic_slice_in_dim(live_pages, first, block_pages, 0)
        alive = jnp.broadcast_to(alive[:, None], (block_pages, page_len)).reshape(
            1, block_pages * page_len
        )
        block_keys = block[:, 0].reshape(block_pages * page_len, kv_heads, HEAD_SIZE)
        block_values = block[:, 1].reshape(block_pages * page_len, kv_heads, HEAD_SIZE)
        return block_update(carry, head_count, block_keys, block_values, alive, scale)

    top_final, total_final, acc_final = lax.fori_loop(0, trips, step_block, state)
    output = acc_final / total_final[..., None]
    attended = (
        output.transpose(2, 0, 1, 3)
        .reshape(1, suffix, groups_per_head * width)
        .astype(jnp.bfloat16)
    )
    arrived, arrived_slot = shifted((suffix_key_value, new_slots), "store", stores // 2)
    new_store = lax.dynamic_update_slice_in_dim(kv_pages, arrived, arrived_slot[0], 0)
    return (attended, new_store)


def dot_nt(a, b):
    return lax.dot_general(a, b, (((1,), (1,)), ((), ())), preferred_element_type=jnp.float32)


def block_of(j):
    return slice(j * HEAD_SIZE, (j + 1) * HEAD_SIZE)


def iota(shape, dim):
    return lax.broadcasted_iota(jnp.int32, shape, dim)


def pack_stats(top, total):
    diagonal = iota((HEAD_SIZE, HEAD_SIZE), 0) == iota((HEAD_SIZE, HEAD_SIZE), 1)
    row = iota((STAT_ROWS, HEAD_SIZE), 0)
    tile = jnp.zeros((STAT_ROWS, HEAD_SIZE), jnp.float32)

    def along(x):
        return jnp.sum(jnp.where(diagonal, x, 0.0), 0, keepdims=True)

    for j, (m, l) in enumerate(zip(top, total)):
        l = along(l)
        high = l.astype(jnp.bfloat16).astype(jnp.float32)
        for t, x in enumerate((along(m), high, l - high)):
            tile = jnp.where(row == 4 * t + j, x, tile)
    return tile.astype(jnp.bfloat16)


def unpack_stats(tile):
    row = iota((STAT_ROWS, 8 * HEAD_SIZE), 0)
    block = iota((STAT_ROWS, 8 * HEAD_SIZE), 1) // HEAD_SIZE
    j = block // 2
    stat = block % 2
    spread = (
        ((row == j) & (stat == 0)) | ((row == j + 4) & (stat == 1)) | ((row == j + 8) & (stat == 1))
    )
    spread = spread.astype(jnp.float32).astype(jnp.bfloat16)
    turned = tile.astype(jnp.float32).T.astype(jnp.bfloat16)
    wide = jnp.dot(turned, spread, preferred_element_type=jnp.float32)
    part = lambda b: wide[:, b * HEAD_SIZE:(b + 1) * HEAD_SIZE]
    return [part(2 * j) for j in range(4)], [part(2 * j + 1) for j in range(4)]


def attend_kernel(sizes, jobs, own, keeping, *refs):
    rows, suffix, cap, page_len, count = sizes
    refs = list(refs)
    meta = refs.pop(0)
    queries = [refs.pop(0) for _ in range(count)]
    own_kv = refs.pop(0) if own else None
    held = refs.pop(0)
    if keeping and keeping[0]:
        refs.pop(0)
    outs = [(refs.pop(0), refs.pop(0)) for _ in range(count)]
    stored = refs.pop(0) if keeping else None
    scores = refs.pop(0)
    late_scores = refs.pop(0) if own else None
    if keeping:
        span = pl.ds(*keeping)
        keep = pltpu.make_async_copy(held.at[span], stored.at[span], refs.pop(0))
        keep.start()
    factor = HEAD_SIZE ** (-0.5) * LOG2E
    keys = cap * page_len

    def stacked(n, part, h):
        return jnp.concatenate([held[meta[n, c], part, :, block_of(h)] for c in range(cap)], 0)

    def score(i):
        n, _, h = jobs[i]
        q = queries[n][h * rows:(h + 1) * rows, :]
        scores[i % 2] = dot_nt(q, stacked(n, 0, h))
        if own:
            at = iota((rows, suffix), 0) % suffix
            causal = iota((rows, suffix), 1) <= at
            late_scores[i % 2] = jnp.where(causal, dot_nt(q, own_kv[0, :, block_of(h)]), DEAD)

    def weigh(i):
        n, spot, h = jobs[i]
        live = iota((1, keys), 1) < meta[n, cap] * page_len
        s = jnp.where(live, scores[i % 2], DEAD)
        top = jnp.max(s, axis=-1, keepdims=True)
        if own:
            top = jnp.maximum(top, jnp.max(late_scores[i % 2], axis=-1, keepdims=True))
        top = jnp.maximum(top * factor, FLOOR).astype(jnp.bfloat16).astype(jnp.float32)
        p = jnp.exp2(s * factor - top).astype(jnp.bfloat16)
        v = stacked(n, 1, h)
        v = jnp.concatenate([v, jnp.ones_like(v)], 1)
        out = jnp.dot(p, v, preferred_element_type=jnp.float32)
        if own:
            p = jnp.exp2(late_scores[i % 2] * factor - top).astype(jnp.bfloat16)
            v = own_kv[1, :, block_of(h)]
            v = jnp.concatenate([v, jnp.ones_like(v)], 1)
            out = out + jnp.dot(p, v, preferred_element_type=jnp.float32)
        acc_ref, stat_ref = outs[n]
        acc_ref[spot] = out[:, :HEAD_SIZE]
        total = out[:, HEAD_SIZE:]
        top = jnp.broadcast_to(top, total.shape)
        blocks = [block_of(j) for j in range(rows // HEAD_SIZE)]
        stat_ref[spot] = pack_stats([top[j] for j in blocks], [total[j] for j in blocks])

    for i in range(len(jobs) + 1):
        if i < len(jobs):
            score(i)
        if i > 0:
            weigh(i - 1)
    if keeping:
        keep.wait()


def attend(sizes, jobs, meta, queries, held, own=None, keeping=None, store=None):
    rows, suffix, cap, page_len = sizes
    keys, count = cap * page_len, len(queries)
    heads = len(jobs) // count
    shapes, out_specs = [], []
    for _ in queries:
        shapes.append(jax.ShapeDtypeStruct((heads, rows, HEAD_SIZE), jnp.float32))
        shapes.append(jax.ShapeDtypeStruct((heads, STAT_ROWS, HEAD_SIZE), jnp.bfloat16))
        out_specs += [VMEM, VMEM]
    scratch = [pltpu.VMEM((2, rows, keys), jnp.float32)]
    args, aliases = [meta, *queries], {}
    if own is not None:
        args.append(own)
        scratch.append(pltpu.VMEM((2, rows, suffix), jnp.float32))
    args.append(held)
    in_specs = [SMEM] + [VMEM] * (len(args) - 1)
    if keeping:
        shapes.append(jax.ShapeDtypeStruct(held.shape, held.dtype))
        out_specs.append(HBM)
        scratch.append(pltpu.SemaphoreType.DMA)
    if store is not None:
        aliases[len(args)] = 2 * count
        args.append(store)
        in_specs.append(HBM)
    work = pl.CostEstimate(
        flops=len(jobs) * rows * keys * HEAD_SIZE * 8,
        bytes_accessed=len(jobs) * (rows * 6 + keys * 4) * HEAD_SIZE,
        transcendentals=len(jobs) * rows * keys,
    )
    out = pl.pallas_call(
        functools.partial(attend_kernel, sizes + (count,), jobs, own is not None, keeping),
        out_shape=shapes,
        in_specs=in_specs,
        out_specs=out_specs,
        scratch_shapes=scratch,
        input_output_aliases=aliases,
        compiler_params=pltpu.CompilerParams(vmem_limit_bytes=GRANT),
        cost_estimate=work,
    )(*args)
    return [(out[2 * n], out[2 * n + 1]) for n in range(count)] + list(out[2 * count:])


def hold_kernel(pages_ref, before_ref, out_ref, sem):
    copy = pltpu.make_async_copy(pages_ref, out_ref, sem)
    copy.start()
    copy.wait()


def hold(pages, before):
    return pl.pallas_call(
        hold_kernel,
        out_shape=jax.ShapeDtypeStruct(pages.shape, pages.dtype),
        in_specs=[HBM, VMEM],
        out_specs=VMEM,
        scratch_shapes=[pltpu.SemaphoreType.DMA],
        compiler_params=pltpu.CompilerParams(vmem_limit_bytes=2 * GRANT),
        cost_estimate=LIGHT,
    )(pages, before)


def place_kernel(half, column, me_ref, core_ref, near_ref, far_ref, page_ref, old_ref, out_ref, sem):
    me, core = me_ref[0], core_ref[0]
    is_near = ((me >= half) == (me % 2 == 0)) == (core % 2 == 0)
    slot = jnp.where(is_near, near_ref[0, column], far_ref[0, column])
    copy = pltpu.make_async_copy(page_ref.at[0], out_ref.at[slot], sem)
    copy.start()
    copy.wait()


def place_page(half, column, me, core, near, far, page, store):
    return pl.pallas_call(
        functools.partial(place_kernel, half, column),
        out_shape=jax.ShapeDtypeStruct(store.shape, store.dtype),
        in_specs=[SMEM] * 4 + [VMEM, HBM],
        out_specs=HBM,
        scratch_shapes=[pltpu.SemaphoreType.DMA],
        input_output_aliases={5: 0},
        compiler_params=pltpu.CompilerParams(vmem_limit_bytes=GRANT),
        cost_estimate=LIGHT,
    )(me[None], core[None], near, far, page, store)


def blend(parts):
    top = functools.reduce(jnp.maximum, [m for _, m, _ in parts])
    scales = [jnp.exp2(m - top) for _, m, _ in parts]
    acc = sum(a * f for (a, _, _), f in zip(parts, scales))
    total = sum(l * f for (_, _, l), f in zip(parts, scales))
    return acc, top, total


def pack_kernel(acc_ref, stat_ref, out_ref):
    heads, rows = acc_ref.shape[:2]
    for h in range(heads):
        out_ref[h, :rows, :] = acc_ref[h].astype(jnp.bfloat16)
        out_ref[h, rows:, :] = stat_ref[h]


def merge_kernel(in_first, first, in_ref, acc_ref, stat_ref, out_ref):
    heads, rows = out_ref.shape[0], acc_ref.shape[1]
    for h in range(heads):
        in_top, in_total = unpack_stats(in_ref[in_first + h, rows:, :])
        my_top, my_total = unpack_stats(stat_ref[first + h])
        tops, totals = [], []
        for j in range(rows // HEAD_SIZE):
            acc, top, total = blend(
                [
                    (in_ref[in_first + h, block_of(j), :].astype(jnp.float32), in_top[j], in_total[j]),
                    (acc_ref[first + h, block_of(j), :], my_top[j], my_total[j]),
                ]
            )
            out_ref[h, block_of(j), :] = acc.astype(out_ref.dtype)
            tops.append(top)
            totals.append(total)
        out_ref[h, rows:, :] = pack_stats(tops, totals)


def final_kernel(suffix, first, in_ref, acc_ref, stat_ref, *refs):
    out_ref, done, sems = refs[-3:]
    heads, rows = in_ref.shape[0], acc_ref.shape[1]
    groups = rows // suffix
    copies = []
    for h in range(heads):
        in_top, in_total = unpack_stats(in_ref[h, rows:, :])
        my_top, my_total = unpack_stats(stat_ref[h])
        for j in range(rows // HEAD_SIZE):
            acc, _, total = blend(
                [
                    (in_ref[h, block_of(j), :].astype(jnp.float32), in_top[j], in_total[j]),
                    (acc_ref[h, block_of(j), :], my_top[j], my_total[j]),
                ]
            )
            out = (acc / total).astype(jnp.bfloat16)
            for i in range(HEAD_SIZE // suffix):
                g = h * groups + j * (HEAD_SIZE // suffix) + i
                done[0, :, block_of(g)] = out[i * suffix:(i + 1) * suffix]
        width = groups * HEAD_SIZE
        copies.append(
            pltpu.make_async_copy(
                done.at[:, :, pl.ds(h * width, width)],
                out_ref.at[:, :, pl.ds((first + h) * width, width)],
                sems.at[h],
            )
        )
        copies[-1].start()
    for copy in copies:
        copy.wait()


def finish(suffix, first, like, block, part, before=None):
    heads, rows = block.shape[0], part[0].shape[1]
    args = [block, *part] + ([] if before is None else [before])
    return pl.pallas_call(
        functools.partial(final_kernel, suffix, first),
        out_shape=jax.ShapeDtypeStruct(like.shape, like.dtype),
        in_specs=[VMEM] * 3 + [HBM] * (len(args) - 3),
        out_specs=HBM,
        scratch_shapes=[
            pltpu.VMEM((1, suffix, heads * rows // suffix * HEAD_SIZE), like.dtype),
            pltpu.SemaphoreType.DMA((heads,)),
        ],
        input_output_aliases={} if before is None else {3: 0},
        compiler_params=pltpu.CompilerParams(vmem_limit_bytes=GRANT),
    )(*args)


def call(kernel, shape, *args):
    size = sum(a.size * a.dtype.itemsize for a in args)
    return pl.pallas_call(
        kernel,
        out_shape=shape,
        in_specs=[VMEM] * len(args),
        out_specs=[VMEM] * len(shape) if isinstance(shape, list) else VMEM,
        compiler_params=pltpu.CompilerParams(vmem_limit_bytes=GRANT),
        cost_estimate=pl.CostEstimate(flops=size, bytes_accessed=2 * size, transcendentals=0),
    )(*args)


def lists_kernel(cap, pages_dev, length_ref, slot_ref, table_ref, out_ref):
    maxp = table_ref.shape[1]
    table = table_ref[...]
    owner = lax.div(table, pages_dev)
    local = (table - owner * pages_dev).astype(jnp.float32)
    owner = owner.astype(jnp.float32)
    down, along = iota((maxp, maxp), 0), iota((maxp, maxp), 1)

    def turned(x):
        return jnp.sum(jnp.where(down == along, x, 0.0), 1, keepdims=True)

    before = (turned(owner) == owner) & (along < down)
    rank = jnp.sum(jnp.where(before, 1.0, 0.0), 1, keepdims=True)
    place = iota((maxp, HEAD_SIZE), 1)
    live = jnp.where(iota((maxp, HEAD_SIZE), 0) < length_ref[0], 1.0, 0.0)
    ids = jnp.where(rank == place.astype(jnp.float32), turned(local), 0.0)
    fields = jnp.where(place < cap, ids, jnp.where(place == cap, live, 0.0))
    owned = jnp.where(owner == iota((LIST_ROWS, maxp), 0).astype(jnp.float32), 1.0, 0.0)
    lists = jnp.dot(
        owned.astype(jnp.bfloat16), fields.astype(jnp.bfloat16), preferred_element_type=jnp.float32
    )
    slot = slot_ref[0].astype(jnp.float32)
    lists = jnp.where(iota(lists.shape, 1) == cap + 1, slot, lists)
    out_ref[...] = lists.astype(jnp.bfloat16)


def list_pages(cap, pages_dev, page_table, prefix_pages, new_slots):
    return pl.pallas_call(
        functools.partial(lists_kernel, cap, pages_dev),
        out_shape=jax.ShapeDtypeStruct((LIST_ROWS, HEAD_SIZE), jnp.bfloat16),
        in_specs=[SMEM, SMEM, VMEM],
        out_specs=VMEM,
        compiler_params=pltpu.CompilerParams(vmem_limit_bytes=GRANT),
    )(prefix_pages, new_slots, page_table)


def join_kernel(q_ref, lists_ref, out_ref):
    suffix, columns = q_ref.shape[1:]
    for g in range(columns // HEAD_SIZE):
        out_ref[g * suffix:(g + 1) * suffix, :] = q_ref[0, :, block_of(g)]
    out_ref[columns // HEAD_SIZE * suffix:, :] = lists_ref[...]


def queries_travel(queries, suffix_key_value, kv_pages, page_table, prefix_pages, new_slots):
    stores = lax.axis_size("store")
    cores = lax.axis_size("tensor")
    pages_dev, _, page_len, width = kv_pages.shape
    cap = page_table.shape[1] // stores
    heads = width // HEAD_SIZE
    suffix = queries.shape[1]
    rows = queries.shape[2] // width * suffix
    sizes = (rows, suffix, cap, page_len)
    half = stores // 2
    me = lax.axis_index("store")

    order = list(range(0, stores, 2)) + list(range(1, stores, 2))[::-1]
    route = [
        (order[i] * cores + core, order[(i + 1 - 2 * (core % 2)) % stores] * cores + core)
        for core in range(cores)
        for i in range(stores)
    ]

    def onward(x):
        return lax.ppermute(x, ("store", "tensor"), route)

    def listed(x, below):
        row = lax.dynamic_slice(x, (below + me, 0), (1, HEAD_SIZE))
        return row.astype(jnp.int32)

    def after(values, token):
        return lax.optimization_barrier((values, token))[0]

    def joined(x, rows_below):
        shape = jax.ShapeDtypeStruct((heads * rows + LIST_ROWS, HEAD_SIZE), queries.dtype)
        return call(join_kernel, shape, x, rows_below)

    first = onward(queries)
    mine = list_pages(cap, pages_dev, page_table, prefix_pages, new_slots)
    held = hold(kv_pages, mine)
    moving = joined(after(first, held), onward(mine))

    own_queries = None
    halves = [range(0, heads // 2), range(heads // 2, heads)]
    token = []
    lists, own = {}, []
    for step in range(1, stores):
        came = after(moving, token)
        if step < stores - 1:
            moving = onward(came)
        lists[step] = listed(came, heads * rows)
        if step == stores - 3:
            arrived = shifted(after(suffix_key_value, token), "store", half)
        jobs = [(0, h, h) for h in range(heads)]
        keeping, pages = None, pages_dev // 2
        if step == 1:
            keeping = (0, pages)
            part, store = attend(sizes, jobs, lists[step], [came], held, None, keeping)
        elif step == 2:
            keeping = (pages, pages_dev - pages)
            part, store = attend(sizes, jobs, lists[step], [came], held, None, keeping, store)
        else:
            part, = attend(sizes, jobs, lists[step], [came], held)
        if step == 1:
            blocks = [packed(part)]
        elif step < stores - 2:
            blocks = [merged(after(partial[0], part), part, 0, 0, heads)]
        else:
            blocks = []
            for n, half_heads in enumerate(halves):
                block, at = (partial[0], half_heads[0]) if len(partial) == 1 else (partial[n], 0)
                block = after(block, [part, blocks])
                blocks.append(merged(block, part, at, half_heads[0], len(half_heads)))
        partial = [onward(block) for block in blocks]
        token = blocks
        if step == stores - 2:
            token = [blocks, arrived]
        if step in (half - 1, half):
            if own_queries is None:
                own_queries = joined(after(queries, token), mine)
            jobs = [(0, n, h) for n, h in enumerate(halves[len(own)])]
            x = after(own_queries, token)
            own += attend(sizes, jobs, listed(mine, 0), [x], held, suffix_key_value[0])
            token = [blocks, own]

    quarter = stores // 4
    near, far = lists[quarter], lists[stores - quarter]
    core = lax.axis_index("tensor")
    store = place_page(half, cap + 1, me, core, near, far, arrived, after(store, token))
    attended = finish(suffix, 0, queries, after(partial[0], store), own[0])
    attended = finish(suffix, heads // 2, queries, partial[1], own[1], attended)
    return (attended, store)


def wire_of(part, heads):
    rows, columns = part[0].shape[1:]
    return jax.ShapeDtypeStruct((heads, rows + STAT_ROWS, columns), jnp.bfloat16)


def packed(part):
    return call(pack_kernel, wire_of(part, part[0].shape[0]), *part)


def merged(block, part, in_first, first, heads):
    kernel = functools.partial(merge_kernel, in_first, first)
    return call(kernel, wire_of(part, heads), block, *part)


def on_device(queries, suffix_key_value, kv_pages, page_table, prefix_pages, new_slots):
    stores = lax.axis_size("store")
    pulled = page_table.shape[1] // stores * kv_pages[0].size
    pushed = 2 * queries[0].size
    arrays = (queries, suffix_key_value, kv_pages, page_table, prefix_pages, new_slots)
    if pulled >= pushed and stores % 8 == 0 and stores <= LIST_ROWS:
        return queries_travel(*arrays)
    return pages_travel(*arrays)


def solution(mesh):
    return jax.shard_map(
        on_device,
        mesh=mesh,
        in_specs=(
            P(("groups", "store"), None, "tensor"),
            P(("groups", "store"), None, None, "tensor"),
            P(("groups", "store"), None, None, "tensor"),
            P(("groups", "store"), None),
            P(("groups", "store")),
            P(("groups", "store")),
        ),
        out_specs=(
            P(("groups", "store"), None, "tensor"),
            P(("groups", "store"), None, None, "tensor"),
        ),
        check_vma=False,
    )
```

```python
import functools

import jax
import jax.numpy as jnp
from jax import lax
from jax.experimental import pallas as pl
from jax.experimental.pallas import tpu as pltpu
from jax.sharding import PartitionSpec as P

HEAD_SIZE = 128
LOG2E = 1.4426950408889634
DEAD = -1e30
FLOOR = -1e29
STAT_ROWS = 16
LIST_ROWS = 16
GRANT = 20 * 1024 * 1024
LIGHT = pl.CostEstimate(flops=1, bytes_accessed=1, transcendentals=0)
VMEM = pl.BlockSpec(memory_space=pltpu.VMEM)
SMEM = pl.BlockSpec(memory_space=pltpu.SMEM)
HBM = pl.BlockSpec(memory_space=pltpu.HBM)


def shifted(block, axis, distance):
    devices = range(lax.axis_size(axis))
    route = [((i - distance) % len(devices), i) for i in devices]
    return lax.ppermute(block, axis, route)


def block_update(state, head_count, key_rows, value_rows, live, scale):
    top_old, total_old, acc_old = state
    scores = (
        jnp.einsum("qhgd,khd->hgqk", head_count, key_rows, preferred_element_type=jnp.float32)
        * scale
    )
    scores = jnp.where(live, scores, -1e30)
    top_new = jnp.maximum(top_old, jnp.max(scores, axis=-1))
    weights = jnp.where(live, jnp.exp(scores - top_new[..., None]), 0.0)
    factor = jnp.exp(top_old - top_new)
    total_new = total_old * factor + jnp.sum(weights, axis=-1)
    product = jnp.einsum(
        "hgqk,khd->hgqd",
        weights.astype(jnp.bfloat16),
        value_rows,
        preferred_element_type=jnp.float32,
    )
    return (top_new, total_new, acc_old * factor[..., None] + product)


def pages_travel(queries, suffix_key_value, kv_pages, page_table, prefix_pages, new_slots):
    stores = lax.axis_size("store")
    pages_dev = kv_pages.shape[0]
    maxp = page_table.shape[1]
    cap = maxp // stores
    page_len = kv_pages.shape[2]
    width = kv_pages.shape[3]
    kv_heads = width // HEAD_SIZE
    suffix = queries.shape[1]
    groups_per_head = queries.shape[2] // width
    scale = HEAD_SIZE ** (-0.5)
    length = prefix_pages[0]
    table = page_table[0]
    owners = table // pages_dev
    local_ids = table % pages_dev
    entries = jnp.arange(maxp, dtype=jnp.int32)
    same_owner = (owners[:, None] == owners[None, :]) & (entries[:, None] < entries[None, :])
    ranks = jnp.sum(same_owner.astype(jnp.int32), axis=0)
    slots = owners * cap + ranks
    placed = slots[:, None] == entries[None, :]
    slot_entry = jnp.sum(jnp.where(placed, entries[:, None], 0), axis=0)
    wanted = jnp.sum(jnp.where(placed, local_ids[:, None], 0), axis=0)
    asked = lax.all_to_all(
        wanted.reshape(stores, cap), "store", split_axis=0, concat_axis=0, tiled=True
    )
    served = kv_pages[asked.reshape(-1)].reshape(stores, cap, 2, page_len, width)
    received = lax.all_to_all(served, "store", split_axis=0, concat_axis=0, tiled=True).reshape(
        maxp, 2, page_len, width
    )
    head_count = queries[0].reshape(suffix, kv_heads, groups_per_head, HEAD_SIZE)
    own_keys = suffix_key_value[0, 0].reshape(suffix, kv_heads, HEAD_SIZE)
    own_values = suffix_key_value[0, 1].reshape(suffix, kv_heads, HEAD_SIZE)
    rows = jnp.arange(suffix, dtype=jnp.int32)
    causal = rows[None, :] <= rows[:, None]
    start_state = (
        jnp.full((kv_heads, groups_per_head, suffix), -1e30, jnp.float32),
        jnp.zeros((kv_heads, groups_per_head, suffix), jnp.float32),
        jnp.zeros((kv_heads, groups_per_head, suffix, HEAD_SIZE), jnp.float32),
    )
    state = block_update(start_state, head_count, own_keys, own_values, causal, scale)
    block_pages = min(8, maxp)
    live_pages = slot_entry < length
    trips = maxp // block_pages

    def step_block(index, carry):
        first = index * block_pages
        block = lax.dynamic_slice_in_dim(received, first, block_pages, 0)
        alive = lax.dynamic_slice_in_dim(live_pages, first, block_pages, 0)
        alive = jnp.broadcast_to(alive[:, None], (block_pages, page_len)).reshape(
            1, block_pages * page_len
        )
        block_keys = block[:, 0].reshape(block_pages * page_len, kv_heads, HEAD_SIZE)
        block_values = block[:, 1].reshape(block_pages * page_len, kv_heads, HEAD_SIZE)
        return block_update(carry, head_count, block_keys, block_values, alive, scale)

    top_final, total_final, acc_final = lax.fori_loop(0, trips, step_block, state)
    output = acc_final / total_final[..., None]
    attended = (
        output.transpose(2, 0, 1, 3)
        .reshape(1, suffix, groups_per_head * width)
        .astype(jnp.bfloat16)
    )
    arrived, arrived_slot = shifted((suffix_key_value, new_slots), "store", stores // 2)
    new_store = lax.dynamic_update_slice_in_dim(kv_pages, arrived, arrived_slot[0], 0)
    return (attended, new_store)


def dot_nt(a, b):
    return lax.dot_general(a, b, (((1,), (1,)), ((), ())), preferred_element_type=jnp.float32)


def block_of(j):
    return slice(j * HEAD_SIZE, (j + 1) * HEAD_SIZE)


def iota(shape, dim):
    return lax.broadcasted_iota(jnp.int32, shape, dim)


def pack_stats(top, total):
    diagonal = iota((HEAD_SIZE, HEAD_SIZE), 0) == iota((HEAD_SIZE, HEAD_SIZE), 1)
    row = iota((STAT_ROWS, HEAD_SIZE), 0)
    tile = jnp.zeros((STAT_ROWS, HEAD_SIZE), jnp.float32)

    def along(x):
        return jnp.sum(jnp.where(diagonal, x, 0.0), 0, keepdims=True)

    for j, (m, l) in enumerate(zip(top, total)):
        l = along(l)
        high = l.astype(jnp.bfloat16).astype(jnp.float32)
        for t, x in enumerate((along(m), high, l - high)):
            tile = jnp.where(row == 4 * t + j, x, tile)
    return tile.astype(jnp.bfloat16)


def unpack_stats(tile):
    row = iota((STAT_ROWS, 8 * HEAD_SIZE), 0)
    block = iota((STAT_ROWS, 8 * HEAD_SIZE), 1) // HEAD_SIZE
    j = block // 2
    stat = block % 2
    spread = (
        ((row == j) & (stat == 0)) | ((row == j + 4) & (stat == 1)) | ((row == j + 8) & (stat == 1))
    )
    spread = spread.astype(jnp.float32).astype(jnp.bfloat16)
    turned = tile.astype(jnp.float32).T.astype(jnp.bfloat16)
    wide = jnp.dot(turned, spread, preferred_element_type=jnp.float32)
    part = lambda b: wide[:, b * HEAD_SIZE:(b + 1) * HEAD_SIZE]
    return [part(2 * j) for j in range(4)], [part(2 * j + 1) for j in range(4)]


def attend_kernel(sizes, jobs, own, keeping, *refs):
    rows, suffix, cap, page_len, count = sizes
    refs = list(refs)
    meta = refs.pop(0)
    queries = [refs.pop(0) for _ in range(count)]
    own_kv = refs.pop(0) if own else None
    held = refs.pop(0)
    if keeping and keeping[0]:
        refs.pop(0)
    outs = [(refs.pop(0), refs.pop(0)) for _ in range(count)]
    stored = refs.pop(0) if keeping else None
    scores = refs.pop(0)
    late_scores = refs.pop(0) if own else None
    if keeping:
        span = pl.ds(*keeping)
        keep = pltpu.make_async_copy(held.at[span], stored.at[span], refs.pop(0))
        keep.start()
    factor = HEAD_SIZE ** (-0.5) * LOG2E
    keys = cap * page_len

    def stacked(n, part, h):
        return jnp.concatenate([held[meta[n, c], part, :, block_of(h)] for c in range(cap)], 0)

    def score(i):
        n, _, h = jobs[i]
        q = queries[n][h * rows:(h + 1) * rows, :]
        scores[i % 2] = dot_nt(q, stacked(n, 0, h))
        if own:
            at = iota((rows, suffix), 0) % suffix
            causal = iota((rows, suffix), 1) <= at
            late_scores[i % 2] = jnp.where(causal, dot_nt(q, own_kv[0, :, block_of(h)]), DEAD)

    def weigh(i):
        n, spot, h = jobs[i]
        live = iota((1, keys), 1) < meta[n, cap] * page_len
        s = jnp.where(live, scores[i % 2], DEAD)
        top = jnp.max(s, axis=-1, keepdims=True)
        if own:
            top = jnp.maximum(top, jnp.max(late_scores[i % 2], axis=-1, keepdims=True))
        top = jnp.maximum(top * factor, FLOOR).astype(jnp.bfloat16).astype(jnp.float32)
        p = jnp.exp2(s * factor - top).astype(jnp.bfloat16)
        v = stacked(n, 1, h)
        v = jnp.concatenate([v, jnp.ones_like(v)], 1)
        out = jnp.dot(p, v, preferred_element_type=jnp.float32)
        if own:
            p = jnp.exp2(late_scores[i % 2] * factor - top).astype(jnp.bfloat16)
            v = own_kv[1, :, block_of(h)]
            v = jnp.concatenate([v, jnp.ones_like(v)], 1)
            out = out + jnp.dot(p, v, preferred_element_type=jnp.float32)
        acc_ref, stat_ref = outs[n]
        acc_ref[spot] = out[:, :HEAD_SIZE]
        total = out[:, HEAD_SIZE:]
        top = jnp.broadcast_to(top, total.shape)
        blocks = [block_of(j) for j in range(rows // HEAD_SIZE)]
        stat_ref[spot] = pack_stats([top[j] for j in blocks], [total[j] for j in blocks])

    for i in range(len(jobs) + 1):
        if i < len(jobs):
            score(i)
        if i > 0:
            weigh(i - 1)
    if keeping:
        keep.wait()


def attend(sizes, jobs, meta, queries, held, own=None, keeping=None, store=None):
    rows, suffix, cap, page_len = sizes
    keys, count = cap * page_len, len(queries)
    heads = len(jobs) // count
    shapes, out_specs = [], []
    for _ in queries:
        shapes.append(jax.ShapeDtypeStruct((heads, rows, HEAD_SIZE), jnp.float32))
        shapes.append(jax.ShapeDtypeStruct((heads, STAT_ROWS, HEAD_SIZE), jnp.bfloat16))
        out_specs += [VMEM, VMEM]
    scratch = [pltpu.VMEM((2, rows, keys), jnp.float32)]
    args, aliases = [meta, *queries], {}
    if own is not None:
        args.append(own)
        scratch.append(pltpu.VMEM((2, rows, suffix), jnp.float32))
    args.append(held)
    in_specs = [SMEM] + [VMEM] * (len(args) - 1)
    if keeping:
        shapes.append(jax.ShapeDtypeStruct(held.shape, held.dtype))
        out_specs.append(HBM)
        scratch.append(pltpu.SemaphoreType.DMA)
    if store is not None:
        aliases[len(args)] = 2 * count
        args.append(store)
        in_specs.append(HBM)
    work = pl.CostEstimate(
        flops=len(jobs) * rows * keys * HEAD_SIZE * 8,
        bytes_accessed=len(jobs) * (rows * 6 + keys * 4) * HEAD_SIZE,
        transcendentals=len(jobs) * rows * keys,
    )
    out = pl.pallas_call(
        functools.partial(attend_kernel, sizes + (count,), jobs, own is not None, keeping),
        out_shape=shapes,
        in_specs=in_specs,
        out_specs=out_specs,
        scratch_shapes=scratch,
        input_output_aliases=aliases,
        compiler_params=pltpu.CompilerParams(vmem_limit_bytes=GRANT),
        cost_estimate=work,
    )(*args)
    return [(out[2 * n], out[2 * n + 1]) for n in range(count)] + list(out[2 * count:])


def touch_kernel(held_ref, lists_ref, out_ref):
    out_ref[...] = lists_ref[...]


def touch(held, lists):
    return pl.pallas_call(
        touch_kernel,
        out_shape=jax.ShapeDtypeStruct(lists.shape, lists.dtype),
        in_specs=[VMEM, VMEM],
        out_specs=VMEM,
        compiler_params=pltpu.CompilerParams(vmem_limit_bytes=GRANT),
        cost_estimate=LIGHT,
    )(held, lists)


def place_kernel(half, column, me_ref, core_ref, near_ref, far_ref, *refs):
    keys_ref, values_ref, old_ref, out_ref, sems = refs
    me, core = me_ref[0], core_ref[0]
    is_near = ((me >= half) == (me % 2 == 0)) == (core % 2 == 0)
    slot = jnp.where(is_near, near_ref[0, column], far_ref[0, column])
    copies = [
        pltpu.make_async_copy(piece.at[0, 0], out_ref.at[slot, n], sems.at[n])
        for n, piece in enumerate((keys_ref, values_ref))
    ]
    for copy in copies:
        copy.start()
    for copy in copies:
        copy.wait()


def place_page(half, column, me, core, near, far, pieces, store):
    return pl.pallas_call(
        functools.partial(place_kernel, half, column),
        out_shape=jax.ShapeDtypeStruct(store.shape, store.dtype),
        in_specs=[SMEM] * 4 + [VMEM, VMEM, HBM],
        out_specs=HBM,
        scratch_shapes=[pltpu.SemaphoreType.DMA((2,))],
        input_output_aliases={6: 0},
        compiler_params=pltpu.CompilerParams(vmem_limit_bytes=GRANT),
        cost_estimate=LIGHT,
    )(me[None], core[None], near, far, *pieces, store)


def blend(parts):
    top = functools.reduce(jnp.maximum, [m for _, m, _ in parts])
    scales = [jnp.exp2(m - top) for _, m, _ in parts]
    acc = sum(a * f for (a, _, _), f in zip(parts, scales))
    total = sum(l * f for (_, _, l), f in zip(parts, scales))
    return acc, top, total


def pack_kernel(acc_ref, stat_ref, out_ref):
    heads, rows = acc_ref.shape[:2]
    for h in range(heads):
        out_ref[h, :rows, :] = acc_ref[h].astype(jnp.bfloat16)
        out_ref[h, rows:, :] = stat_ref[h]


def merge_kernel(in_first, first, in_ref, acc_ref, stat_ref, out_ref):
    heads, rows = out_ref.shape[0], acc_ref.shape[1]
    for h in range(heads):
        in_top, in_total = unpack_stats(in_ref[in_first + h, rows:, :])
        my_top, my_total = unpack_stats(stat_ref[first + h])
        tops, totals = [], []
        for j in range(rows // HEAD_SIZE):
            acc, top, total = blend(
                [
                    (in_ref[in_first + h, block_of(j), :].astype(jnp.float32), in_top[j], in_total[j]),
                    (acc_ref[first + h, block_of(j), :], my_top[j], my_total[j]),
                ]
            )
            out_ref[h, block_of(j), :] = acc.astype(out_ref.dtype)
            tops.append(top)
            totals.append(total)
        out_ref[h, rows:, :] = pack_stats(tops, totals)


def final_kernel(suffix, first, in_ref, acc_ref, stat_ref, *refs):
    out_ref, done, sems = refs[-3:]
    heads, rows = in_ref.shape[0], acc_ref.shape[1]
    groups = rows // suffix
    copies = []
    for h in range(heads):
        in_top, in_total = unpack_stats(in_ref[h, rows:, :])
        my_top, my_total = unpack_stats(stat_ref[h])
        for j in range(rows // HEAD_SIZE):
            acc, _, total = blend(
                [
                    (in_ref[h, block_of(j), :].astype(jnp.float32), in_top[j], in_total[j]),
                    (acc_ref[h, block_of(j), :], my_top[j], my_total[j]),
                ]
            )
            out = (acc / total).astype(jnp.bfloat16)
            for i in range(HEAD_SIZE // suffix):
                g = h * groups + j * (HEAD_SIZE // suffix) + i
                done[0, :, block_of(g)] = out[i * suffix:(i + 1) * suffix]
        width = groups * HEAD_SIZE
        copies.append(
            pltpu.make_async_copy(
                done.at[:, :, pl.ds(h * width, width)],
                out_ref.at[:, :, pl.ds((first + h) * width, width)],
                sems.at[h],
            )
        )
        copies[-1].start()
    for copy in copies:
        copy.wait()


def finish(suffix, first, like, block, part, before=None):
    heads, rows = block.shape[0], part[0].shape[1]
    args = [block, *part] + ([] if before is None else [before])
    return pl.pallas_call(
        functools.partial(final_kernel, suffix, first),
        out_shape=jax.ShapeDtypeStruct(like.shape, like.dtype),
        in_specs=[VMEM] * 3 + [HBM] * (len(args) - 3),
        out_specs=HBM,
        scratch_shapes=[
            pltpu.VMEM((1, suffix, heads * rows // suffix * HEAD_SIZE), like.dtype),
            pltpu.SemaphoreType.DMA((heads,)),
        ],
        input_output_aliases={} if before is None else {3: 0},
        compiler_params=pltpu.CompilerParams(vmem_limit_bytes=GRANT),
    )(*args)


def call(kernel, shape, *args):
    size = sum(a.size * a.dtype.itemsize for a in args)
    return pl.pallas_call(
        kernel,
        out_shape=shape,
        in_specs=[VMEM] * len(args),
        out_specs=[VMEM] * len(shape) if isinstance(shape, list) else VMEM,
        compiler_params=pltpu.CompilerParams(vmem_limit_bytes=GRANT),
        cost_estimate=pl.CostEstimate(flops=size, bytes_accessed=2 * size, transcendentals=0),
    )(*args)


def lists_kernel(cap, pages_dev, length_ref, slot_ref, table_ref, out_ref):
    maxp = table_ref.shape[1]
    table = table_ref[...]
    owner = lax.div(table, pages_dev)
    local = (table - owner * pages_dev).astype(jnp.float32)
    owner = owner.astype(jnp.float32)
    down, along = iota((maxp, maxp), 0), iota((maxp, maxp), 1)

    def turned(x):
        return jnp.sum(jnp.where(down == along, x, 0.0), 1, keepdims=True)

    before = (turned(owner) == owner) & (along < down)
    rank = jnp.sum(jnp.where(before, 1.0, 0.0), 1, keepdims=True)
    place = iota((maxp, HEAD_SIZE), 1)
    live = jnp.where(iota((maxp, HEAD_SIZE), 0) < length_ref[0], 1.0, 0.0)
    ids = jnp.where(rank == place.astype(jnp.float32), turned(local), 0.0)
    fields = jnp.where(place < cap, ids, jnp.where(place == cap, live, 0.0))
    owned = jnp.where(owner == iota((LIST_ROWS, maxp), 0).astype(jnp.float32), 1.0, 0.0)
    lists = jnp.dot(
        owned.astype(jnp.bfloat16), fields.astype(jnp.bfloat16), preferred_element_type=jnp.float32
    )
    slot = slot_ref[0].astype(jnp.float32)
    lists = jnp.where(iota(lists.shape, 1) == cap + 1, slot, lists)
    out_ref[...] = lists.astype(jnp.bfloat16)


def list_pages(cap, pages_dev, page_table, prefix_pages, new_slots):
    return pl.pallas_call(
        functools.partial(lists_kernel, cap, pages_dev),
        out_shape=jax.ShapeDtypeStruct((LIST_ROWS, HEAD_SIZE), jnp.bfloat16),
        in_specs=[SMEM, SMEM, VMEM],
        out_specs=VMEM,
        compiler_params=pltpu.CompilerParams(vmem_limit_bytes=GRANT),
    )(prefix_pages, new_slots, page_table)


def join_kernel(q_ref, lists_ref, out_ref):
    suffix, columns = q_ref.shape[1:]
    for g in range(columns // HEAD_SIZE):
        out_ref[g * suffix:(g + 1) * suffix, :] = q_ref[0, :, block_of(g)]
    out_ref[columns // HEAD_SIZE * suffix:, :] = lists_ref[...]


def queries_travel(queries, suffix_key_value, kv_pages, page_table, prefix_pages, new_slots):
    stores = lax.axis_size("store")
    cores = lax.axis_size("tensor")
    pages_dev, _, page_len, width = kv_pages.shape
    cap = page_table.shape[1] // stores
    heads = width // HEAD_SIZE
    suffix = queries.shape[1]
    rows = queries.shape[2] // width * suffix
    sizes = (rows, suffix, cap, page_len)
    half = stores // 2
    me = lax.axis_index("store")

    order = list(range(0, stores, 2)) + list(range(1, stores, 2))[::-1]
    route = [
        (order[i] * cores + core, order[(i + 1 - 2 * (core % 2)) % stores] * cores + core)
        for core in range(cores)
        for i in range(stores)
    ]

    def onward(x):
        return lax.ppermute(x, ("store", "tensor"), route)

    def listed(x, below):
        row = lax.dynamic_slice(x, (below + me, 0), (1, HEAD_SIZE))
        return row.astype(jnp.int32)

    def after(values, token):
        return lax.optimization_barrier((values, token))[0]

    def joined(x, rows_below):
        shape = jax.ShapeDtypeStruct((heads * rows + LIST_ROWS, HEAD_SIZE), queries.dtype)
        return call(join_kernel, shape, x, rows_below)

    first = onward(queries)
    mine = list_pages(cap, pages_dev, page_table, prefix_pages, new_slots)
    their_lists = onward(mine)
    mine = touch(kv_pages, mine)
    moving = joined(after(first, mine), their_lists)

    own_queries = None
    halves = [range(0, heads // 2), range(heads // 2, heads)]
    token = []
    lists, own, arrived = {}, [], []
    travel = (half - 1, half)
    for step in range(1, stores):
        came = after(moving, token)
        if step < stores - 1:
            moving = onward(came)
        lists[step] = listed(came, heads * rows)
        if step + 1 in travel:
            piece = suffix_key_value[:, len(arrived):len(arrived) + 1]
            arrived.append(shifted(after(piece, token), "store", half))
        jobs = [(0, h, h) for h in range(heads)]
        keeping, pages = None, pages_dev // 2
        if step == 1:
            keeping = (0, pages)
            part, store = attend(sizes, jobs, lists[step], [came], kv_pages, None, keeping)
        elif step == 2:
            keeping = (pages, pages_dev - pages)
            part, store = attend(sizes, jobs, lists[step], [came], kv_pages, None, keeping, store)
        else:
            part, = attend(sizes, jobs, lists[step], [came], kv_pages)
        if step == 1:
            blocks = [packed(part)]
        elif step < stores - 2:
            blocks = [merged(after(partial[0], part), part, 0, 0, heads)]
        else:
            blocks = []
            for n, half_heads in enumerate(halves):
                block, at = (partial[0], half_heads[0]) if len(partial) == 1 else (partial[n], 0)
                block = after(block, [part, blocks])
                blocks.append(merged(block, part, at, half_heads[0], len(half_heads)))
        partial = [onward(block) for block in blocks]
        token = blocks
        if step in travel:
            token = [blocks, arrived[travel.index(step)]]
        if step in (half - 1, half):
            if own_queries is None:
                own_queries = joined(after(queries, token), mine)
            jobs = [(0, n, h) for n, h in enumerate(halves[len(own)])]
            x = after(own_queries, token)
            own += attend(sizes, jobs, listed(mine, 0), [x], kv_pages, suffix_key_value[0])
            token = [token, own]

    quarter = stores // 4
    near, far = lists[quarter], lists[stores - quarter]
    core = lax.axis_index("tensor")
    store = place_page(half, cap + 1, me, core, near, far, arrived, after(store, token))
    attended = finish(suffix, 0, queries, after(partial[0], store), own[0])
    attended = finish(suffix, heads // 2, queries, partial[1], own[1], attended)
    return (attended, store)


def wire_of(part, heads):
    rows, columns = part[0].shape[1:]
    return jax.ShapeDtypeStruct((heads, rows + STAT_ROWS, columns), jnp.bfloat16)


def packed(part):
    return call(pack_kernel, wire_of(part, part[0].shape[0]), *part)


def merged(block, part, in_first, first, heads):
    kernel = functools.partial(merge_kernel, in_first, first)
    return call(kernel, wire_of(part, heads), block, *part)


def on_device(queries, suffix_key_value, kv_pages, page_table, prefix_pages, new_slots):
    stores = lax.axis_size("store")
    pulled = page_table.shape[1] // stores * kv_pages[0].size
    pushed = 2 * queries[0].size
    arrays = (queries, suffix_key_value, kv_pages, page_table, prefix_pages, new_slots)
    if pulled >= pushed and stores % 8 == 0 and stores <= LIST_ROWS:
        return queries_travel(*arrays)
    return pages_travel(*arrays)


def solution(mesh):
    return jax.shard_map(
        on_device,
        mesh=mesh,
        in_specs=(
            P(("groups", "store"), None, "tensor"),
            P(("groups", "store"), None, None, "tensor"),
            P(("groups", "store"), None, None, "tensor"),
            P(("groups", "store"), None),
            P(("groups", "store")),
            P(("groups", "store")),
        ),
        out_specs=(
            P(("groups", "store"), None, "tensor"),
            P(("groups", "store"), None, None, "tensor"),
        ),
        check_vma=False,
    )
```

```python
import functools

import jax
import jax.numpy as jnp
from jax import lax
from jax.experimental import pallas as pl
from jax.experimental.pallas import tpu as pltpu
from jax.sharding import PartitionSpec as P

HEAD_SIZE = 128
LOG2E = 1.4426950408889634
DEAD = -1e30
FLOOR = -1e29
STAT_ROWS = 16
LIST_ROWS = 16
GRANT = 20 * 1024 * 1024
LIGHT = pl.CostEstimate(flops=1, bytes_accessed=1, transcendentals=0)
HEAVY = pl.CostEstimate(flops=1 << 33, bytes_accessed=1 << 25, transcendentals=1 << 24)
VMEM = pl.BlockSpec(memory_space=pltpu.VMEM)
SMEM = pl.BlockSpec(memory_space=pltpu.SMEM)
HBM = pl.BlockSpec(memory_space=pltpu.HBM)


def shifted(block, axis, distance):
    devices = range(lax.axis_size(axis))
    route = [((i - distance) % len(devices), i) for i in devices]
    return lax.ppermute(block, axis, route)


def block_update(state, head_count, key_rows, value_rows, live, scale):
    top_old, total_old, acc_old = state
    scores = (
        jnp.einsum("qhgd,khd->hgqk", head_count, key_rows, preferred_element_type=jnp.float32)
        * scale
    )
    scores = jnp.where(live, scores, -1e30)
    top_new = jnp.maximum(top_old, jnp.max(scores, axis=-1))
    weights = jnp.where(live, jnp.exp(scores - top_new[..., None]), 0.0)
    factor = jnp.exp(top_old - top_new)
    total_new = total_old * factor + jnp.sum(weights, axis=-1)
    product = jnp.einsum(
        "hgqk,khd->hgqd",
        weights.astype(jnp.bfloat16),
        value_rows,
        preferred_element_type=jnp.float32,
    )
    return (top_new, total_new, acc_old * factor[..., None] + product)


def pages_travel(queries, suffix_key_value, kv_pages, page_table, prefix_pages, new_slots):
    stores = lax.axis_size("store")
    pages_dev = kv_pages.shape[0]
    maxp = page_table.shape[1]
    cap = maxp // stores
    page_len = kv_pages.shape[2]
    width = kv_pages.shape[3]
    kv_heads = width // HEAD_SIZE
    suffix = queries.shape[1]
    groups_per_head = queries.shape[2] // width
    scale = HEAD_SIZE ** (-0.5)
    length = prefix_pages[0]
    table = page_table[0]
    owners = table // pages_dev
    local_ids = table % pages_dev
    entries = jnp.arange(maxp, dtype=jnp.int32)
    same_owner = (owners[:, None] == owners[None, :]) & (entries[:, None] < entries[None, :])
    ranks = jnp.sum(same_owner.astype(jnp.int32), axis=0)
    slots = owners * cap + ranks
    placed = slots[:, None] == entries[None, :]
    slot_entry = jnp.sum(jnp.where(placed, entries[:, None], 0), axis=0)
    wanted = jnp.sum(jnp.where(placed, local_ids[:, None], 0), axis=0)
    asked = lax.all_to_all(
        wanted.reshape(stores, cap), "store", split_axis=0, concat_axis=0, tiled=True
    )
    served = kv_pages[asked.reshape(-1)].reshape(stores, cap, 2, page_len, width)
    received = lax.all_to_all(served, "store", split_axis=0, concat_axis=0, tiled=True).reshape(
        maxp, 2, page_len, width
    )
    head_count = queries[0].reshape(suffix, kv_heads, groups_per_head, HEAD_SIZE)
    own_keys = suffix_key_value[0, 0].reshape(suffix, kv_heads, HEAD_SIZE)
    own_values = suffix_key_value[0, 1].reshape(suffix, kv_heads, HEAD_SIZE)
    rows = jnp.arange(suffix, dtype=jnp.int32)
    causal = rows[None, :] <= rows[:, None]
    start_state = (
        jnp.full((kv_heads, groups_per_head, suffix), -1e30, jnp.float32),
        jnp.zeros((kv_heads, groups_per_head, suffix), jnp.float32),
        jnp.zeros((kv_heads, groups_per_head, suffix, HEAD_SIZE), jnp.float32),
    )
    state = block_update(start_state, head_count, own_keys, own_values, causal, scale)
    block_pages = min(8, maxp)
    live_pages = slot_entry < length
    trips = maxp // block_pages

    def step_block(index, carry):
        first = index * block_pages
        block = lax.dynamic_slice_in_dim(received, first, block_pages, 0)
        alive = lax.dynamic_slice_in_dim(live_pages, first, block_pages, 0)
        alive = jnp.broadcast_to(alive[:, None], (block_pages, page_len)).reshape(
            1, block_pages * page_len
        )
        block_keys = block[:, 0].reshape(block_pages * page_len, kv_heads, HEAD_SIZE)
        block_values = block[:, 1].reshape(block_pages * page_len, kv_heads, HEAD_SIZE)
        return block_update(carry, head_count, block_keys, block_values, alive, scale)

    top_final, total_final, acc_final = lax.fori_loop(0, trips, step_block, state)
    output = acc_final / total_final[..., None]
    attended = (
        output.transpose(2, 0, 1, 3)
        .reshape(1, suffix, groups_per_head * width)
        .astype(jnp.bfloat16)
    )
    arrived, arrived_slot = shifted((suffix_key_value, new_slots), "store", stores // 2)
    new_store = lax.dynamic_update_slice_in_dim(kv_pages, arrived, arrived_slot[0], 0)
    return (attended, new_store)


def dot_nt(a, b):
    return lax.dot_general(a, b, (((1,), (1,)), ((), ())), preferred_element_type=jnp.float32)


def block_of(j):
    return slice(j * HEAD_SIZE, (j + 1) * HEAD_SIZE)


def iota(shape, dim):
    return lax.broadcasted_iota(jnp.int32, shape, dim)


def pack_stats(top, total):
    diagonal = iota((HEAD_SIZE, HEAD_SIZE), 0) == iota((HEAD_SIZE, HEAD_SIZE), 1)
    row = iota((STAT_ROWS, HEAD_SIZE), 0)
    tile = jnp.zeros((STAT_ROWS, HEAD_SIZE), jnp.float32)

    def along(x):
        return jnp.sum(jnp.where(diagonal, x, 0.0), 0, keepdims=True)

    for j, (m, l) in enumerate(zip(top, total)):
        l = along(l)
        high = l.astype(jnp.bfloat16).astype(jnp.float32)
        for t, x in enumerate((along(m), high, l - high)):
            tile = jnp.where(row == 4 * t + j, x, tile)
    return tile.astype(jnp.bfloat16)


def unpack_stats(tile):
    row = iota((STAT_ROWS, 8 * HEAD_SIZE), 0)
    block = iota((STAT_ROWS, 8 * HEAD_SIZE), 1) // HEAD_SIZE
    j = block // 2
    stat = block % 2
    spread = (
        ((row == j) & (stat == 0)) | ((row == j + 4) & (stat == 1)) | ((row == j + 8) & (stat == 1))
    )
    spread = spread.astype(jnp.float32).astype(jnp.bfloat16)
    turned = tile.astype(jnp.float32).T.astype(jnp.bfloat16)
    wide = jnp.dot(turned, spread, preferred_element_type=jnp.float32)
    part = lambda b: wide[:, b * HEAD_SIZE:(b + 1) * HEAD_SIZE]
    return [part(2 * j) for j in range(4)], [part(2 * j + 1) for j in range(4)]


def attend_kernel(sizes, jobs, own, keeping, *refs):
    rows, suffix, cap, page_len, count = sizes
    refs = list(refs)
    meta = refs.pop(0)
    queries = [refs.pop(0) for _ in range(count)]
    own_kv = refs.pop(0) if own else None
    held = refs.pop(0)
    if keeping and keeping[0]:
        refs.pop(0)
    outs = [(refs.pop(0), refs.pop(0)) for _ in range(count)]
    stored = refs.pop(0) if keeping else None
    scores = refs.pop(0)
    late_scores = refs.pop(0) if own else None
    if keeping:
        span = pl.ds(*keeping)
        keep = pltpu.make_async_copy(held.at[span], stored.at[span], refs.pop(0))
        keep.start()
    factor = HEAD_SIZE ** (-0.5) * LOG2E
    keys = cap * page_len

    def stacked(n, part, h):
        return jnp.concatenate([held[meta[n, c], part, :, block_of(h)] for c in range(cap)], 0)

    def score(i):
        n, _, h = jobs[i]
        q = queries[n][h * rows:(h + 1) * rows, :]
        scores[i % 2] = dot_nt(q, stacked(n, 0, h))
        if own:
            at = iota((rows, suffix), 0) % suffix
            causal = iota((rows, suffix), 1) <= at
            late_scores[i % 2] = jnp.where(causal, dot_nt(q, own_kv[0, :, block_of(h)]), DEAD)

    def weigh(i):
        n, spot, h = jobs[i]
        live = iota((1, keys), 1) < meta[n, cap] * page_len
        s = jnp.where(live, scores[i % 2], DEAD)
        top = jnp.max(s, axis=-1, keepdims=True)
        if own:
            top = jnp.maximum(top, jnp.max(late_scores[i % 2], axis=-1, keepdims=True))
        top = jnp.maximum(top * factor, FLOOR).astype(jnp.bfloat16).astype(jnp.float32)
        p = jnp.exp2(s * factor - top).astype(jnp.bfloat16)
        v = stacked(n, 1, h)
        v = jnp.concatenate([v, jnp.ones_like(v)], 1)
        out = jnp.dot(p, v, preferred_element_type=jnp.float32)
        if own:
            p = jnp.exp2(late_scores[i % 2] * factor - top).astype(jnp.bfloat16)
            v = own_kv[1, :, block_of(h)]
            v = jnp.concatenate([v, jnp.ones_like(v)], 1)
            out = out + jnp.dot(p, v, preferred_element_type=jnp.float32)
        acc_ref, stat_ref = outs[n]
        acc_ref[spot] = out[:, :HEAD_SIZE]
        total = out[:, HEAD_SIZE:]
        top = jnp.broadcast_to(top, total.shape)
        blocks = [block_of(j) for j in range(rows // HEAD_SIZE)]
        stat_ref[spot] = pack_stats([top[j] for j in blocks], [total[j] for j in blocks])

    for i in range(len(jobs) + 1):
        if i < len(jobs):
            score(i)
        if i > 0:
            weigh(i - 1)
    if keeping:
        keep.wait()


def attend(sizes, jobs, meta, queries, held, own=None, keeping=None, store=None):
    rows, suffix, cap, page_len = sizes
    keys, count = cap * page_len, len(queries)
    heads = len(jobs) // count
    shapes, out_specs = [], []
    for _ in queries:
        shapes.append(jax.ShapeDtypeStruct((heads, rows, HEAD_SIZE), jnp.float32))
        shapes.append(jax.ShapeDtypeStruct((heads, STAT_ROWS, HEAD_SIZE), jnp.bfloat16))
        out_specs += [VMEM, VMEM]
    scratch = [pltpu.VMEM((2, rows, keys), jnp.float32)]
    args, aliases = [meta, *queries], {}
    if own is not None:
        args.append(own)
        scratch.append(pltpu.VMEM((2, rows, suffix), jnp.float32))
    args.append(held)
    in_specs = [SMEM] + [VMEM] * (len(args) - 1)
    if keeping:
        shapes.append(jax.ShapeDtypeStruct(held.shape, held.dtype))
        out_specs.append(HBM)
        scratch.append(pltpu.SemaphoreType.DMA)
    if store is not None:
        aliases[len(args)] = 2 * count
        args.append(store)
        in_specs.append(HBM)
    work = pl.CostEstimate(
        flops=len(jobs) * rows * keys * HEAD_SIZE * 8,
        bytes_accessed=len(jobs) * (rows * 6 + keys * 4) * HEAD_SIZE,
        transcendentals=len(jobs) * rows * keys,
    )
    out = pl.pallas_call(
        functools.partial(attend_kernel, sizes + (count,), jobs, own is not None, keeping),
        out_shape=shapes,
        in_specs=in_specs,
        out_specs=out_specs,
        scratch_shapes=scratch,
        input_output_aliases=aliases,
        compiler_params=pltpu.CompilerParams(vmem_limit_bytes=GRANT),
        cost_estimate=work,
    )(*args)
    return [(out[2 * n], out[2 * n + 1]) for n in range(count)] + list(out[2 * count:])


def touch_kernel(held_ref, lists_ref, out_ref):
    out_ref[...] = lists_ref[...]


def touch(held, lists):
    return pl.pallas_call(
        touch_kernel,
        out_shape=jax.ShapeDtypeStruct(lists.shape, lists.dtype),
        in_specs=[VMEM, VMEM],
        out_specs=VMEM,
        compiler_params=pltpu.CompilerParams(vmem_limit_bytes=GRANT),
        cost_estimate=HEAVY,
    )(held, lists)


def place_kernel(half, column, me_ref, core_ref, near_ref, far_ref, page_ref, old_ref, out_ref, sem):
    me, core = me_ref[0], core_ref[0]
    is_near = ((me >= half) == (me % 2 == 0)) == (core % 2 == 0)
    slot = jnp.where(is_near, near_ref[0, column], far_ref[0, column])
    copy = pltpu.make_async_copy(page_ref.at[0], out_ref.at[slot], sem)
    copy.start()
    copy.wait()


def place_page(half, column, me, core, near, far, page, store):
    return pl.pallas_call(
        functools.partial(place_kernel, half, column),
        out_shape=jax.ShapeDtypeStruct(store.shape, store.dtype),
        in_specs=[SMEM] * 4 + [VMEM, HBM],
        out_specs=HBM,
        scratch_shapes=[pltpu.SemaphoreType.DMA],
        input_output_aliases={5: 0},
        compiler_params=pltpu.CompilerParams(vmem_limit_bytes=GRANT),
        cost_estimate=LIGHT,
    )(me[None], core[None], near, far, page, store)


def blend(parts):
    top = functools.reduce(jnp.maximum, [m for _, m, _ in parts])
    scales = [jnp.exp2(m - top) for _, m, _ in parts]
    acc = sum(a * f for (a, _, _), f in zip(parts, scales))
    total = sum(l * f for (_, _, l), f in zip(parts, scales))
    return acc, top, total


def pack_kernel(acc_ref, stat_ref, out_ref):
    heads, rows = acc_ref.shape[:2]
    for h in range(heads):
        out_ref[h, :rows, :] = acc_ref[h].astype(jnp.bfloat16)
        out_ref[h, rows:, :] = stat_ref[h]


def merge_kernel(in_first, first, in_ref, acc_ref, stat_ref, out_ref):
    heads, rows = out_ref.shape[0], acc_ref.shape[1]
    for h in range(heads):
        in_top, in_total = unpack_stats(in_ref[in_first + h, rows:, :])
        my_top, my_total = unpack_stats(stat_ref[first + h])
        tops, totals = [], []
        for j in range(rows // HEAD_SIZE):
            acc, top, total = blend(
                [
                    (in_ref[in_first + h, block_of(j), :].astype(jnp.float32), in_top[j], in_total[j]),
                    (acc_ref[first + h, block_of(j), :], my_top[j], my_total[j]),
                ]
            )
            out_ref[h, block_of(j), :] = acc.astype(out_ref.dtype)
            tops.append(top)
            totals.append(total)
        out_ref[h, rows:, :] = pack_stats(tops, totals)


def final_kernel(suffix, first, in_ref, acc_ref, stat_ref, *refs):
    out_ref, done, sems = refs[-3:]
    heads, rows = in_ref.shape[0], acc_ref.shape[1]
    groups = rows // suffix
    copies = []
    for h in range(heads):
        in_top, in_total = unpack_stats(in_ref[h, rows:, :])
        my_top, my_total = unpack_stats(stat_ref[h])
        for j in range(rows // HEAD_SIZE):
            acc, _, total = blend(
                [
                    (in_ref[h, block_of(j), :].astype(jnp.float32), in_top[j], in_total[j]),
                    (acc_ref[h, block_of(j), :], my_top[j], my_total[j]),
                ]
            )
            out = (acc / total).astype(jnp.bfloat16)
            for i in range(HEAD_SIZE // suffix):
                g = h * groups + j * (HEAD_SIZE // suffix) + i
                done[0, :, block_of(g)] = out[i * suffix:(i + 1) * suffix]
        width = groups * HEAD_SIZE
        copies.append(
            pltpu.make_async_copy(
                done.at[:, :, pl.ds(h * width, width)],
                out_ref.at[:, :, pl.ds((first + h) * width, width)],
                sems.at[h],
            )
        )
        copies[-1].start()
    for copy in copies:
        copy.wait()


def finish(suffix, first, like, block, part, before=None):
    heads, rows = block.shape[0], part[0].shape[1]
    args = [block, *part] + ([] if before is None else [before])
    return pl.pallas_call(
        functools.partial(final_kernel, suffix, first),
        out_shape=jax.ShapeDtypeStruct(like.shape, like.dtype),
        in_specs=[VMEM] * 3 + [HBM] * (len(args) - 3),
        out_specs=HBM,
        scratch_shapes=[
            pltpu.VMEM((1, suffix, heads * rows // suffix * HEAD_SIZE), like.dtype),
            pltpu.SemaphoreType.DMA((heads,)),
        ],
        input_output_aliases={} if before is None else {3: 0},
        compiler_params=pltpu.CompilerParams(vmem_limit_bytes=GRANT),
    )(*args)


def call(kernel, shape, *args):
    size = sum(a.size * a.dtype.itemsize for a in args)
    return pl.pallas_call(
        kernel,
        out_shape=shape,
        in_specs=[VMEM] * len(args),
        out_specs=[VMEM] * len(shape) if isinstance(shape, list) else VMEM,
        compiler_params=pltpu.CompilerParams(vmem_limit_bytes=GRANT),
        cost_estimate=pl.CostEstimate(flops=size, bytes_accessed=2 * size, transcendentals=0),
    )(*args)


def lists_kernel(cap, pages_dev, length_ref, slot_ref, table_ref, out_ref):
    maxp = table_ref.shape[1]
    table = table_ref[...]
    owner = lax.div(table, pages_dev)
    local = (table - owner * pages_dev).astype(jnp.float32)
    owner = owner.astype(jnp.float32)
    down, along = iota((maxp, maxp), 0), iota((maxp, maxp), 1)

    def turned(x):
        return jnp.sum(jnp.where(down == along, x, 0.0), 1, keepdims=True)

    before = (turned(owner) == owner) & (along < down)
    rank = jnp.sum(jnp.where(before, 1.0, 0.0), 1, keepdims=True)
    place = iota((maxp, HEAD_SIZE), 1)
    live = jnp.where(iota((maxp, HEAD_SIZE), 0) < length_ref[0], 1.0, 0.0)
    ids = jnp.where(rank == place.astype(jnp.float32), turned(local), 0.0)
    fields = jnp.where(place < cap, ids, jnp.where(place == cap, live, 0.0))
    owned = jnp.where(owner == iota((LIST_ROWS, maxp), 0).astype(jnp.float32), 1.0, 0.0)
    lists = jnp.dot(
        owned.astype(jnp.bfloat16), fields.astype(jnp.bfloat16), preferred_element_type=jnp.float32
    )
    slot = slot_ref[0].astype(jnp.float32)
    lists = jnp.where(iota(lists.shape, 1) == cap + 1, slot, lists)
    out_ref[...] = lists.astype(jnp.bfloat16)


def list_pages(cap, pages_dev, page_table, prefix_pages, new_slots):
    return pl.pallas_call(
        functools.partial(lists_kernel, cap, pages_dev),
        out_shape=jax.ShapeDtypeStruct((LIST_ROWS, HEAD_SIZE), jnp.bfloat16),
        in_specs=[SMEM, SMEM, VMEM],
        out_specs=VMEM,
        compiler_params=pltpu.CompilerParams(vmem_limit_bytes=GRANT),
    )(prefix_pages, new_slots, page_table)


def join_kernel(q_ref, lists_ref, out_ref):
    suffix, columns = q_ref.shape[1:]
    for g in range(columns // HEAD_SIZE):
        out_ref[g * suffix:(g + 1) * suffix, :] = q_ref[0, :, block_of(g)]
    out_ref[columns // HEAD_SIZE * suffix:, :] = lists_ref[...]


def queries_travel(queries, suffix_key_value, kv_pages, page_table, prefix_pages, new_slots):
    stores = lax.axis_size("store")
    cores = lax.axis_size("tensor")
    pages_dev, _, page_len, width = kv_pages.shape
    cap = page_table.shape[1] // stores
    heads = width // HEAD_SIZE
    suffix = queries.shape[1]
    rows = queries.shape[2] // width * suffix
    sizes = (rows, suffix, cap, page_len)
    half = stores // 2
    me = lax.axis_index("store")

    order = list(range(0, stores, 2)) + list(range(1, stores, 2))[::-1]
    route = [
        (order[i] * cores + core, order[(i + 1 - 2 * (core % 2)) % stores] * cores + core)
        for core in range(cores)
        for i in range(stores)
    ]

    def onward(x):
        return lax.ppermute(x, ("store", "tensor"), route)

    def listed(x, below):
        row = lax.dynamic_slice(x, (below + me, 0), (1, HEAD_SIZE))
        return row.astype(jnp.int32)

    def after(values, token):
        return lax.optimization_barrier((values, token))[0]

    def joined(x, rows_below):
        shape = jax.ShapeDtypeStruct((heads * rows + LIST_ROWS, HEAD_SIZE), queries.dtype)
        return call(join_kernel, shape, x, rows_below)

    arrived = shifted(suffix_key_value, "store", half)
    first = onward(queries)
    mine = list_pages(cap, pages_dev, page_table, prefix_pages, new_slots)
    their_lists = onward(mine)
    mine = touch(kv_pages, after(mine, arrived))
    moving = joined(after(first, mine), their_lists)

    own_queries = None
    halves = [range(0, heads // 2), range(heads // 2, heads)]
    token = []
    lists, own = {}, []
    for step in range(1, stores):
        came = after(moving, token)
        if step < stores - 1:
            moving = onward(came)
        lists[step] = listed(came, heads * rows)
        jobs = [(0, h, h) for h in range(heads)]
        keeping, pages = None, pages_dev // 2
        if step == 1:
            keeping = (0, pages)
            part, store = attend(sizes, jobs, lists[step], [came], kv_pages, None, keeping)
        elif step == 2:
            keeping = (pages, pages_dev - pages)
            part, store = attend(sizes, jobs, lists[step], [came], kv_pages, None, keeping, store)
        else:
            part, = attend(sizes, jobs, lists[step], [came], kv_pages)
        if step == 1:
            blocks = [packed(part)]
        elif step < stores - 1:
            blocks = [merged(after(partial[0], part), part, 0, 0, heads)]
        else:
            blocks = []
            for n, half_heads in enumerate(halves):
                block, at = (partial[0], half_heads[0]) if len(partial) == 1 else (partial[n], 0)
                block = after(block, [part, blocks])
                blocks.append(merged(block, part, at, half_heads[0], len(half_heads)))
        partial = [onward(block) for block in blocks]
        token = blocks
        if step in (half - 1, half):
            if own_queries is None:
                own_queries = joined(after(queries, token), mine)
            jobs = [(0, n, h) for n, h in enumerate(halves[len(own)])]
            x = after(own_queries, token)
            own += attend(sizes, jobs, listed(mine, 0), [x], kv_pages, suffix_key_value[0])
            token = [blocks, own]

    quarter = stores // 4
    near, far = lists[quarter], lists[stores - quarter]
    core = lax.axis_index("tensor")
    store = place_page(half, cap + 1, me, core, near, far, arrived, after(store, token))
    attended = finish(suffix, 0, queries, after(partial[0], store), own[0])
    attended = finish(suffix, heads // 2, queries, partial[1], own[1], attended)
    return (attended, store)


def wire_of(part, heads):
    rows, columns = part[0].shape[1:]
    return jax.ShapeDtypeStruct((heads, rows + STAT_ROWS, columns), jnp.bfloat16)


def packed(part):
    return call(pack_kernel, wire_of(part, part[0].shape[0]), *part)


def merged(block, part, in_first, first, heads):
    kernel = functools.partial(merge_kernel, in_first, first)
    return call(kernel, wire_of(part, heads), block, *part)


def on_device(queries, suffix_key_value, kv_pages, page_table, prefix_pages, new_slots):
    stores = lax.axis_size("store")
    pulled = page_table.shape[1] // stores * kv_pages[0].size
    pushed = 2 * queries[0].size
    arrays = (queries, suffix_key_value, kv_pages, page_table, prefix_pages, new_slots)
    if pulled >= pushed and stores % 8 == 0 and stores <= LIST_ROWS:
        return queries_travel(*arrays)
    return pages_travel(*arrays)


def solution(mesh):
    return jax.shard_map(
        on_device,
        mesh=mesh,
        in_specs=(
            P(("groups", "store"), None, "tensor"),
            P(("groups", "store"), None, None, "tensor"),
            P(("groups", "store"), None, None, "tensor"),
            P(("groups", "store"), None),
            P(("groups", "store")),
            P(("groups", "store")),
        ),
        out_specs=(
            P(("groups", "store"), None, "tensor"),
            P(("groups", "store"), None, None, "tensor"),
        ),
        check_vma=False,
    )
```

```python
import functools

import jax
import jax.numpy as jnp
from jax import lax
from jax.experimental import pallas as pl
from jax.experimental.pallas import tpu as pltpu
from jax.sharding import PartitionSpec as P

HEAD_SIZE = 128
LOG2E = 1.4426950408889634
DEAD = -1e30
FLOOR = -1e29
STAT_ROWS = 16
LIST_ROWS = 16
GRANT = 20 * 1024 * 1024
LIGHT = pl.CostEstimate(flops=1, bytes_accessed=1, transcendentals=0)
VMEM = pl.BlockSpec(memory_space=pltpu.VMEM)
SMEM = pl.BlockSpec(memory_space=pltpu.SMEM)
HBM = pl.BlockSpec(memory_space=pltpu.HBM)


def shifted(block, axis, distance):
    devices = range(lax.axis_size(axis))
    route = [((i - distance) % len(devices), i) for i in devices]
    return lax.ppermute(block, axis, route)


def block_update(state, head_count, key_rows, value_rows, live, scale):
    top_old, total_old, acc_old = state
    scores = (
        jnp.einsum("qhgd,khd->hgqk", head_count, key_rows, preferred_element_type=jnp.float32)
        * scale
    )
    scores = jnp.where(live, scores, -1e30)
    top_new = jnp.maximum(top_old, jnp.max(scores, axis=-1))
    weights = jnp.where(live, jnp.exp(scores - top_new[..., None]), 0.0)
    factor = jnp.exp(top_old - top_new)
    total_new = total_old * factor + jnp.sum(weights, axis=-1)
    product = jnp.einsum(
        "hgqk,khd->hgqd",
        weights.astype(jnp.bfloat16),
        value_rows,
        preferred_element_type=jnp.float32,
    )
    return (top_new, total_new, acc_old * factor[..., None] + product)


def pages_travel(queries, suffix_key_value, kv_pages, page_table, prefix_pages, new_slots):
    stores = lax.axis_size("store")
    pages_dev = kv_pages.shape[0]
    maxp = page_table.shape[1]
    cap = maxp // stores
    page_len = kv_pages.shape[2]
    width = kv_pages.shape[3]
    kv_heads = width // HEAD_SIZE
    suffix = queries.shape[1]
    groups_per_head = queries.shape[2] // width
    scale = HEAD_SIZE ** (-0.5)
    length = prefix_pages[0]
    table = page_table[0]
    owners = table // pages_dev
    local_ids = table % pages_dev
    entries = jnp.arange(maxp, dtype=jnp.int32)
    same_owner = (owners[:, None] == owners[None, :]) & (entries[:, None] < entries[None, :])
    ranks = jnp.sum(same_owner.astype(jnp.int32), axis=0)
    slots = owners * cap + ranks
    placed = slots[:, None] == entries[None, :]
    slot_entry = jnp.sum(jnp.where(placed, entries[:, None], 0), axis=0)
    wanted = jnp.sum(jnp.where(placed, local_ids[:, None], 0), axis=0)
    asked = lax.all_to_all(
        wanted.reshape(stores, cap), "store", split_axis=0, concat_axis=0, tiled=True
    )
    served = kv_pages[asked.reshape(-1)].reshape(stores, cap, 2, page_len, width)
    received = lax.all_to_all(served, "store", split_axis=0, concat_axis=0, tiled=True).reshape(
        maxp, 2, page_len, width
    )
    head_count = queries[0].reshape(suffix, kv_heads, groups_per_head, HEAD_SIZE)
    own_keys = suffix_key_value[0, 0].reshape(suffix, kv_heads, HEAD_SIZE)
    own_values = suffix_key_value[0, 1].reshape(suffix, kv_heads, HEAD_SIZE)
    rows = jnp.arange(suffix, dtype=jnp.int32)
    causal = rows[None, :] <= rows[:, None]
    start_state = (
        jnp.full((kv_heads, groups_per_head, suffix), -1e30, jnp.float32),
        jnp.zeros((kv_heads, groups_per_head, suffix), jnp.float32),
        jnp.zeros((kv_heads, groups_per_head, suffix, HEAD_SIZE), jnp.float32),
    )
    state = block_update(start_state, head_count, own_keys, own_values, causal, scale)
    block_pages = min(8, maxp)
    live_pages = slot_entry < length
    trips = maxp // block_pages

    def step_block(index, carry):
        first = index * block_pages
        block = lax.dynamic_slice_in_dim(received, first, block_pages, 0)
        alive = lax.dynamic_slice_in_dim(live_pages, first, block_pages, 0)
        alive = jnp.broadcast_to(alive[:, None], (block_pages, page_len)).reshape(
            1, block_pages * page_len
        )
        block_keys = block[:, 0].reshape(block_pages * page_len, kv_heads, HEAD_SIZE)
        block_values = block[:, 1].reshape(block_pages * page_len, kv_heads, HEAD_SIZE)
        return block_update(carry, head_count, block_keys, block_values, alive, scale)

    top_final, total_final, acc_final = lax.fori_loop(0, trips, step_block, state)
    output = acc_final / total_final[..., None]
    attended = (
        output.transpose(2, 0, 1, 3)
        .reshape(1, suffix, groups_per_head * width)
        .astype(jnp.bfloat16)
    )
    arrived, arrived_slot = shifted((suffix_key_value, new_slots), "store", stores // 2)
    new_store = lax.dynamic_update_slice_in_dim(kv_pages, arrived, arrived_slot[0], 0)
    return (attended, new_store)


def dot_nt(a, b):
    return lax.dot_general(a, b, (((1,), (1,)), ((), ())), preferred_element_type=jnp.float32)


def block_of(j):
    return slice(j * HEAD_SIZE, (j + 1) * HEAD_SIZE)


def iota(shape, dim):
    return lax.broadcasted_iota(jnp.int32, shape, dim)


def pack_stats(top, total):
    diagonal = iota((HEAD_SIZE, HEAD_SIZE), 0) == iota((HEAD_SIZE, HEAD_SIZE), 1)
    row = iota((STAT_ROWS, HEAD_SIZE), 0)
    tile = jnp.zeros((STAT_ROWS, HEAD_SIZE), jnp.float32)

    def along(x):
        return jnp.sum(jnp.where(diagonal, x, 0.0), 0, keepdims=True)

    for j, (m, l) in enumerate(zip(top, total)):
        l = along(l)
        high = l.astype(jnp.bfloat16).astype(jnp.float32)
        for t, x in enumerate((along(m), high, l - high)):
            tile = jnp.where(row == 4 * t + j, x, tile)
    return tile.astype(jnp.bfloat16)


def unpack_stats(tile):
    row = iota((STAT_ROWS, 8 * HEAD_SIZE), 0)
    block = iota((STAT_ROWS, 8 * HEAD_SIZE), 1) // HEAD_SIZE
    j = block // 2
    stat = block % 2
    spread = (
        ((row == j) & (stat == 0)) | ((row == j + 4) & (stat == 1)) | ((row == j + 8) & (stat == 1))
    )
    spread = spread.astype(jnp.float32).astype(jnp.bfloat16)
    turned = tile.astype(jnp.float32).T.astype(jnp.bfloat16)
    wide = jnp.dot(turned, spread, preferred_element_type=jnp.float32)
    part = lambda b: wide[:, b * HEAD_SIZE:(b + 1) * HEAD_SIZE]
    return [part(2 * j) for j in range(4)], [part(2 * j + 1) for j in range(4)]


def attend_kernel(sizes, jobs, own, keeping, *refs):
    rows, suffix, cap, page_len, count = sizes
    refs = list(refs)
    meta = refs.pop(0)
    queries = [refs.pop(0) for _ in range(count)]
    own_kv = refs.pop(0) if own else None
    held = refs.pop(0)
    if keeping and keeping[0]:
        refs.pop(0)
    outs = [(refs.pop(0), refs.pop(0)) for _ in range(count)]
    stored = refs.pop(0) if keeping else None
    scores = refs.pop(0)
    late_scores = refs.pop(0) if own else None
    if keeping:
        span = pl.ds(*keeping)
        keep = pltpu.make_async_copy(held.at[span], stored.at[span], refs.pop(0))
        keep.start()
    factor = HEAD_SIZE ** (-0.5) * LOG2E
    keys = cap * page_len

    def stacked(n, part, h):
        return jnp.concatenate([held[meta[n, c], part, :, block_of(h)] for c in range(cap)], 0)

    def score(i):
        n, _, h = jobs[i]
        q = queries[n][h * rows:(h + 1) * rows, :]
        scores[i % 2] = dot_nt(q, stacked(n, 0, h))
        if own:
            at = iota((rows, suffix), 0) % suffix
            causal = iota((rows, suffix), 1) <= at
            late_scores[i % 2] = jnp.where(causal, dot_nt(q, own_kv[0, :, block_of(h)]), DEAD)

    def weigh(i):
        n, spot, h = jobs[i]
        live = iota((1, keys), 1) < meta[n, cap] * page_len
        s = jnp.where(live, scores[i % 2], DEAD)
        top = jnp.max(s, axis=-1, keepdims=True)
        if own:
            top = jnp.maximum(top, jnp.max(late_scores[i % 2], axis=-1, keepdims=True))
        top = jnp.maximum(top * factor, FLOOR).astype(jnp.bfloat16).astype(jnp.float32)
        p = jnp.exp2(s * factor - top).astype(jnp.bfloat16)
        v = stacked(n, 1, h)
        v = jnp.concatenate([v, jnp.ones_like(v)], 1)
        out = jnp.dot(p, v, preferred_element_type=jnp.float32)
        if own:
            p = jnp.exp2(late_scores[i % 2] * factor - top).astype(jnp.bfloat16)
            v = own_kv[1, :, block_of(h)]
            v = jnp.concatenate([v, jnp.ones_like(v)], 1)
            out = out + jnp.dot(p, v, preferred_element_type=jnp.float32)
        acc_ref, stat_ref = outs[n]
        acc_ref[spot] = out[:, :HEAD_SIZE]
        total = out[:, HEAD_SIZE:]
        top = jnp.broadcast_to(top, total.shape)
        blocks = [block_of(j) for j in range(rows // HEAD_SIZE)]
        stat_ref[spot] = pack_stats([top[j] for j in blocks], [total[j] for j in blocks])

    for i in range(len(jobs) + 1):
        if i < len(jobs):
            score(i)
        if i > 0:
            weigh(i - 1)
    if keeping:
        keep.wait()


def attend(sizes, jobs, meta, queries, held, own=None, keeping=None, store=None, light=True):
    rows, suffix, cap, page_len = sizes
    keys, count = cap * page_len, len(queries)
    heads = len(jobs) // count
    shapes, out_specs = [], []
    for _ in queries:
        shapes.append(jax.ShapeDtypeStruct((heads, rows, HEAD_SIZE), jnp.float32))
        shapes.append(jax.ShapeDtypeStruct((heads, STAT_ROWS, HEAD_SIZE), jnp.bfloat16))
        out_specs += [VMEM, VMEM]
    scratch = [pltpu.VMEM((2, rows, keys), jnp.float32)]
    args, aliases = [meta, *queries], {}
    if own is not None:
        args.append(own)
        scratch.append(pltpu.VMEM((2, rows, suffix), jnp.float32))
    args.append(held)
    in_specs = [SMEM] + [VMEM] * (len(args) - 1)
    if keeping:
        shapes.append(jax.ShapeDtypeStruct(held.shape, held.dtype))
        out_specs.append(HBM)
        scratch.append(pltpu.SemaphoreType.DMA)
    if store is not None:
        aliases[len(args)] = 2 * count
        args.append(store)
        in_specs.append(HBM)
    work = pl.CostEstimate(
        flops=len(jobs) * rows * keys * HEAD_SIZE * 8,
        bytes_accessed=len(jobs) * (rows * 6 + keys * 4) * HEAD_SIZE,
        transcendentals=len(jobs) * rows * keys,
    )
    out = pl.pallas_call(
        functools.partial(attend_kernel, sizes + (count,), jobs, own is not None, keeping),
        out_shape=shapes,
        in_specs=in_specs,
        out_specs=out_specs,
        scratch_shapes=scratch,
        input_output_aliases=aliases,
        compiler_params=pltpu.CompilerParams(vmem_limit_bytes=2 * GRANT),
        cost_estimate=LIGHT if light else work,
    )(*args)
    return [(out[2 * n], out[2 * n + 1]) for n in range(count)] + list(out[2 * count:])


def hold_kernel(pages_ref, before_ref, out_ref, sem):
    copy = pltpu.make_async_copy(pages_ref, out_ref, sem)
    copy.start()
    copy.wait()


def hold(pages, before):
    return pl.pallas_call(
        hold_kernel,
        out_shape=jax.ShapeDtypeStruct(pages.shape, pages.dtype),
        in_specs=[HBM, VMEM],
        out_specs=VMEM,
        scratch_shapes=[pltpu.SemaphoreType.DMA],
        compiler_params=pltpu.CompilerParams(vmem_limit_bytes=2 * GRANT),
        cost_estimate=LIGHT,
    )(pages, before)


def place_kernel(half, column, me_ref, core_ref, near_ref, far_ref, page_ref, old_ref, out_ref, sem):
    me, core = me_ref[0], core_ref[0]
    is_near = ((me >= half) == (me % 2 == 0)) == (core % 2 == 0)
    slot = jnp.where(is_near, near_ref[0, column], far_ref[0, column])
    copy = pltpu.make_async_copy(page_ref.at[0], out_ref.at[slot], sem)
    copy.start()
    copy.wait()


def place_page(half, column, me, core, near, far, page, store):
    return pl.pallas_call(
        functools.partial(place_kernel, half, column),
        out_shape=jax.ShapeDtypeStruct(store.shape, store.dtype),
        in_specs=[SMEM] * 4 + [VMEM, HBM],
        out_specs=HBM,
        scratch_shapes=[pltpu.SemaphoreType.DMA],
        input_output_aliases={5: 0},
        compiler_params=pltpu.CompilerParams(vmem_limit_bytes=GRANT),
        cost_estimate=LIGHT,
    )(me[None], core[None], near, far, page, store)


def blend(parts):
    top = functools.reduce(jnp.maximum, [m for _, m, _ in parts])
    scales = [jnp.exp2(m - top) for _, m, _ in parts]
    acc = sum(a * f for (a, _, _), f in zip(parts, scales))
    total = sum(l * f for (_, _, l), f in zip(parts, scales))
    return acc, top, total


def pack_kernel(acc_ref, stat_ref, out_ref):
    heads, rows = acc_ref.shape[:2]
    for h in range(heads):
        out_ref[h, :rows, :] = acc_ref[h].astype(jnp.bfloat16)
        out_ref[h, rows:, :] = stat_ref[h]


def merge_kernel(in_first, first, in_ref, acc_ref, stat_ref, out_ref):
    heads, rows = out_ref.shape[0], acc_ref.shape[1]
    for h in range(heads):
        in_top, in_total = unpack_stats(in_ref[in_first + h, rows:, :])
        my_top, my_total = unpack_stats(stat_ref[first + h])
        tops, totals = [], []
        for j in range(rows // HEAD_SIZE):
            acc, top, total = blend(
                [
                    (in_ref[in_first + h, block_of(j), :].astype(jnp.float32), in_top[j], in_total[j]),
                    (acc_ref[first + h, block_of(j), :], my_top[j], my_total[j]),
                ]
            )
            out_ref[h, block_of(j), :] = acc.astype(out_ref.dtype)
            tops.append(top)
            totals.append(total)
        out_ref[h, rows:, :] = pack_stats(tops, totals)


def final_kernel(suffix, first, in_ref, acc_ref, stat_ref, *refs):
    out_ref, done, sems = refs[-3:]
    heads, rows = in_ref.shape[0], acc_ref.shape[1]
    groups = rows // suffix
    copies = []
    for h in range(heads):
        in_top, in_total = unpack_stats(in_ref[h, rows:, :])
        my_top, my_total = unpack_stats(stat_ref[h])
        for j in range(rows // HEAD_SIZE):
            acc, _, total = blend(
                [
                    (in_ref[h, block_of(j), :].astype(jnp.float32), in_top[j], in_total[j]),
                    (acc_ref[h, block_of(j), :], my_top[j], my_total[j]),
                ]
            )
            out = (acc / total).astype(jnp.bfloat16)
            for i in range(HEAD_SIZE // suffix):
                g = h * groups + j * (HEAD_SIZE // suffix) + i
                done[0, :, block_of(g)] = out[i * suffix:(i + 1) * suffix]
        width = groups * HEAD_SIZE
        copies.append(
            pltpu.make_async_copy(
                done.at[:, :, pl.ds(h * width, width)],
                out_ref.at[:, :, pl.ds((first + h) * width, width)],
                sems.at[h],
            )
        )
        copies[-1].start()
    for copy in copies:
        copy.wait()


def finish(suffix, first, like, block, part, before=None):
    heads, rows = block.shape[0], part[0].shape[1]
    args = [block, *part] + ([] if before is None else [before])
    return pl.pallas_call(
        functools.partial(final_kernel, suffix, first),
        out_shape=jax.ShapeDtypeStruct(like.shape, like.dtype),
        in_specs=[VMEM] * 3 + [HBM] * (len(args) - 3),
        out_specs=HBM,
        scratch_shapes=[
            pltpu.VMEM((1, suffix, heads * rows // suffix * HEAD_SIZE), like.dtype),
            pltpu.SemaphoreType.DMA((heads,)),
        ],
        input_output_aliases={} if before is None else {3: 0},
        compiler_params=pltpu.CompilerParams(vmem_limit_bytes=GRANT),
    )(*args)


def call(kernel, shape, *args):
    size = sum(a.size * a.dtype.itemsize for a in args)
    return pl.pallas_call(
        kernel,
        out_shape=shape,
        in_specs=[VMEM] * len(args),
        out_specs=[VMEM] * len(shape) if isinstance(shape, list) else VMEM,
        compiler_params=pltpu.CompilerParams(vmem_limit_bytes=GRANT),
        cost_estimate=pl.CostEstimate(flops=size, bytes_accessed=2 * size, transcendentals=0),
    )(*args)


def lists_kernel(cap, pages_dev, length_ref, slot_ref, table_ref, out_ref):
    maxp = table_ref.shape[1]
    table = table_ref[...]
    owner = lax.div(table, pages_dev)
    local = (table - owner * pages_dev).astype(jnp.float32)
    owner = owner.astype(jnp.float32)
    down, along = iota((maxp, maxp), 0), iota((maxp, maxp), 1)

    def turned(x):
        return jnp.sum(jnp.where(down == along, x, 0.0), 1, keepdims=True)

    before = (turned(owner) == owner) & (along < down)
    rank = jnp.sum(jnp.where(before, 1.0, 0.0), 1, keepdims=True)
    place = iota((maxp, HEAD_SIZE), 1)
    live = jnp.where(iota((maxp, HEAD_SIZE), 0) < length_ref[0], 1.0, 0.0)
    ids = jnp.where(rank == place.astype(jnp.float32), turned(local), 0.0)
    fields = jnp.where(place < cap, ids, jnp.where(place == cap, live, 0.0))
    owned = jnp.where(owner == iota((LIST_ROWS, maxp), 0).astype(jnp.float32), 1.0, 0.0)
    lists = jnp.dot(
        owned.astype(jnp.bfloat16), fields.astype(jnp.bfloat16), preferred_element_type=jnp.float32
    )
    slot = slot_ref[0].astype(jnp.float32)
    lists = jnp.where(iota(lists.shape, 1) == cap + 1, slot, lists)
    out_ref[...] = lists.astype(jnp.bfloat16)


def list_pages(cap, pages_dev, page_table, prefix_pages, new_slots):
    return pl.pallas_call(
        functools.partial(lists_kernel, cap, pages_dev),
        out_shape=jax.ShapeDtypeStruct((LIST_ROWS, HEAD_SIZE), jnp.bfloat16),
        in_specs=[SMEM, SMEM, VMEM],
        out_specs=VMEM,
        compiler_params=pltpu.CompilerParams(vmem_limit_bytes=GRANT),
    )(prefix_pages, new_slots, page_table)


def join_kernel(q_ref, lists_ref, out_ref):
    suffix, columns = q_ref.shape[1:]
    for g in range(columns // HEAD_SIZE):
        out_ref[g * suffix:(g + 1) * suffix, :] = q_ref[0, :, block_of(g)]
    out_ref[columns // HEAD_SIZE * suffix:, :] = lists_ref[...]


def queries_travel(queries, suffix_key_value, kv_pages, page_table, prefix_pages, new_slots):
    stores = lax.axis_size("store")
    cores = lax.axis_size("tensor")
    pages_dev, _, page_len, width = kv_pages.shape
    cap = page_table.shape[1] // stores
    heads = width // HEAD_SIZE
    suffix = queries.shape[1]
    rows = queries.shape[2] // width * suffix
    sizes = (rows, suffix, cap, page_len)
    half = stores // 2
    me = lax.axis_index("store")

    order = list(range(0, stores, 2)) + list(range(1, stores, 2))[::-1]
    route = [
        (order[i] * cores + core, order[(i + 1 - 2 * (core % 2)) % stores] * cores + core)
        for core in range(cores)
        for i in range(stores)
    ]

    def onward(x):
        return lax.ppermute(x, ("store", "tensor"), route)

    def listed(x, below):
        row = lax.dynamic_slice(x, (below + me, 0), (1, HEAD_SIZE))
        return row.astype(jnp.int32)

    def after(values, token):
        return lax.optimization_barrier((values, token))[0]

    def joined(x, rows_below):
        shape = jax.ShapeDtypeStruct((heads * rows + LIST_ROWS, HEAD_SIZE), queries.dtype)
        return call(join_kernel, shape, x, rows_below)

    first = onward(queries)
    mine = list_pages(cap, pages_dev, page_table, prefix_pages, new_slots)
    held = hold(kv_pages, mine)
    moving = joined(after(first, held), onward(mine))

    own_queries = None
    halves = [range(0, heads // 2), range(heads // 2, heads)]
    token = []
    lists, own = {}, []
    for step in range(1, stores):
        came = after(moving, token)
        if step < stores - 1:
            moving = onward(came)
        lists[step] = listed(came, heads * rows)
        if step == stores - 3:
            arrived = shifted(after(suffix_key_value, token), "store", half)
        jobs = [(0, h, h) for h in range(heads)]
        keeping, pages = None, pages_dev // 2
        if step == 1:
            keeping = (0, pages)
            part, store = attend(sizes, jobs, lists[step], [came], held, None, keeping)
        elif step == 2:
            keeping = (pages, pages_dev - pages)
            part, store = attend(sizes, jobs, lists[step], [came], held, None, keeping, store)
        else:
            light = step < half + 2
            part, = attend(sizes, jobs, lists[step], [came], held, light=light)
        if step == 1:
            blocks = [packed(part)]
        elif step < stores - 2:
            blocks = [merged(after(partial[0], part), part, 0, 0, heads)]
        else:
            blocks = []
            for n, half_heads in enumerate(halves):
                block, at = (partial[0], half_heads[0]) if len(partial) == 1 else (partial[n], 0)
                block = after(block, [part, blocks])
                blocks.append(merged(block, part, at, half_heads[0], len(half_heads)))
        partial = [onward(block) for block in blocks]
        token = blocks
        if step == stores - 2:
            token = [blocks, arrived]
        if step in (half - 1, half):
            if own_queries is None:
                own_queries = joined(after(queries, token), mine)
            jobs = [(0, n, h) for n, h in enumerate(halves[len(own)])]
            x = after(own_queries, token)
            own += attend(sizes, jobs, listed(mine, 0), [x], held, suffix_key_value[0])
            token = [blocks, own]

    quarter = stores // 4
    near, far = lists[quarter], lists[stores - quarter]
    core = lax.axis_index("tensor")
    store = place_page(half, cap + 1, me, core, near, far, arrived, after(store, token))
    attended = finish(suffix, 0, queries, after(partial[0], store), own[0])
    attended = finish(suffix, heads // 2, queries, partial[1], own[1], attended)
    return (attended, store)


def wire_of(part, heads):
    rows, columns = part[0].shape[1:]
    return jax.ShapeDtypeStruct((heads, rows + STAT_ROWS, columns), jnp.bfloat16)


def packed(part):
    return call(pack_kernel, wire_of(part, part[0].shape[0]), *part)


def merged(block, part, in_first, first, heads):
    kernel = functools.partial(merge_kernel, in_first, first)
    return call(kernel, wire_of(part, heads), block, *part)


def on_device(queries, suffix_key_value, kv_pages, page_table, prefix_pages, new_slots):
    stores = lax.axis_size("store")
    pulled = page_table.shape[1] // stores * kv_pages[0].size
    pushed = 2 * queries[0].size
    arrays = (queries, suffix_key_value, kv_pages, page_table, prefix_pages, new_slots)
    if pulled >= pushed and stores % 8 == 0 and stores <= LIST_ROWS:
        return queries_travel(*arrays)
    return pages_travel(*arrays)


def solution(mesh):
    return jax.shard_map(
        on_device,
        mesh=mesh,
        in_specs=(
            P(("groups", "store"), None, "tensor"),
            P(("groups", "store"), None, None, "tensor"),
            P(("groups", "store"), None, None, "tensor"),
            P(("groups", "store"), None),
            P(("groups", "store")),
            P(("groups", "store")),
        ),
        out_specs=(
            P(("groups", "store"), None, "tensor"),
            P(("groups", "store"), None, None, "tensor"),
        ),
        check_vma=False,
    )
```

```python
import functools

import jax
import jax.numpy as jnp
from jax import lax
from jax.experimental import pallas as pl
from jax.experimental.pallas import tpu as pltpu
from jax.sharding import PartitionSpec as P

HEAD_SIZE = 128
LOG2E = 1.4426950408889634
DEAD = -1e30
FLOOR = -1e29
STAT_ROWS = 16
LIST_ROWS = 16
GRANT = 20 * 1024 * 1024
LIGHT = pl.CostEstimate(flops=1, bytes_accessed=1, transcendentals=0)
HEAVY = pl.CostEstimate(flops=1 << 33, bytes_accessed=1 << 25, transcendentals=1 << 24)
VMEM = pl.BlockSpec(memory_space=pltpu.VMEM)
SMEM = pl.BlockSpec(memory_space=pltpu.SMEM)
HBM = pl.BlockSpec(memory_space=pltpu.HBM)


def shifted(block, axis, distance):
    devices = range(lax.axis_size(axis))
    route = [((i - distance) % len(devices), i) for i in devices]
    return lax.ppermute(block, axis, route)


def block_update(state, head_count, key_rows, value_rows, live, scale):
    top_old, total_old, acc_old = state
    scores = (
        jnp.einsum("qhgd,khd->hgqk", head_count, key_rows, preferred_element_type=jnp.float32)
        * scale
    )
    scores = jnp.where(live, scores, -1e30)
    top_new = jnp.maximum(top_old, jnp.max(scores, axis=-1))
    weights = jnp.where(live, jnp.exp(scores - top_new[..., None]), 0.0)
    factor = jnp.exp(top_old - top_new)
    total_new = total_old * factor + jnp.sum(weights, axis=-1)
    product = jnp.einsum(
        "hgqk,khd->hgqd",
        weights.astype(jnp.bfloat16),
        value_rows,
        preferred_element_type=jnp.float32,
    )
    return (top_new, total_new, acc_old * factor[..., None] + product)


def pages_travel(queries, suffix_key_value, kv_pages, page_table, prefix_pages, new_slots):
    stores = lax.axis_size("store")
    pages_dev = kv_pages.shape[0]
    maxp = page_table.shape[1]
    cap = maxp // stores
    page_len = kv_pages.shape[2]
    width = kv_pages.shape[3]
    kv_heads = width // HEAD_SIZE
    suffix = queries.shape[1]
    groups_per_head = queries.shape[2] // width
    scale = HEAD_SIZE ** (-0.5)
    length = prefix_pages[0]
    table = page_table[0]
    owners = table // pages_dev
    local_ids = table % pages_dev
    entries = jnp.arange(maxp, dtype=jnp.int32)
    same_owner = (owners[:, None] == owners[None, :]) & (entries[:, None] < entries[None, :])
    ranks = jnp.sum(same_owner.astype(jnp.int32), axis=0)
    slots = owners * cap + ranks
    placed = slots[:, None] == entries[None, :]
    slot_entry = jnp.sum(jnp.where(placed, entries[:, None], 0), axis=0)
    wanted = jnp.sum(jnp.where(placed, local_ids[:, None], 0), axis=0)
    asked = lax.all_to_all(
        wanted.reshape(stores, cap), "store", split_axis=0, concat_axis=0, tiled=True
    )
    served = kv_pages[asked.reshape(-1)].reshape(stores, cap, 2, page_len, width)
    received = lax.all_to_all(served, "store", split_axis=0, concat_axis=0, tiled=True).reshape(
        maxp, 2, page_len, width
    )
    head_count = queries[0].reshape(suffix, kv_heads, groups_per_head, HEAD_SIZE)
    own_keys = suffix_key_value[0, 0].reshape(suffix, kv_heads, HEAD_SIZE)
    own_values = suffix_key_value[0, 1].reshape(suffix, kv_heads, HEAD_SIZE)
    rows = jnp.arange(suffix, dtype=jnp.int32)
    causal = rows[None, :] <= rows[:, None]
    start_state = (
        jnp.full((kv_heads, groups_per_head, suffix), -1e30, jnp.float32),
        jnp.zeros((kv_heads, groups_per_head, suffix), jnp.float32),
        jnp.zeros((kv_heads, groups_per_head, suffix, HEAD_SIZE), jnp.float32),
    )
    state = block_update(start_state, head_count, own_keys, own_values, causal, scale)
    block_pages = min(8, maxp)
    live_pages = slot_entry < length
    trips = maxp // block_pages

    def step_block(index, carry):
        first = index * block_pages
        block = lax.dynamic_slice_in_dim(received, first, block_pages, 0)
        alive = lax.dynamic_slice_in_dim(live_pages, first, block_pages, 0)
        alive = jnp.broadcast_to(alive[:, None], (block_pages, page_len)).reshape(
            1, block_pages * page_len
        )
        block_keys = block[:, 0].reshape(block_pages * page_len, kv_heads, HEAD_SIZE)
        block_values = block[:, 1].reshape(block_pages * page_len, kv_heads, HEAD_SIZE)
        return block_update(carry, head_count, block_keys, block_values, alive, scale)

    top_final, total_final, acc_final = lax.fori_loop(0, trips, step_block, state)
    output = acc_final / total_final[..., None]
    attended = (
        output.transpose(2, 0, 1, 3)
        .reshape(1, suffix, groups_per_head * width)
        .astype(jnp.bfloat16)
    )
    arrived, arrived_slot = shifted((suffix_key_value, new_slots), "store", stores // 2)
    new_store = lax.dynamic_update_slice_in_dim(kv_pages, arrived, arrived_slot[0], 0)
    return (attended, new_store)


def dot_nt(a, b):
    return lax.dot_general(a, b, (((1,), (1,)), ((), ())), preferred_element_type=jnp.float32)


def block_of(j):
    return slice(j * HEAD_SIZE, (j + 1) * HEAD_SIZE)


def iota(shape, dim):
    return lax.broadcasted_iota(jnp.int32, shape, dim)


def pack_stats(top, total):
    diagonal = iota((HEAD_SIZE, HEAD_SIZE), 0) == iota((HEAD_SIZE, HEAD_SIZE), 1)
    row = iota((STAT_ROWS, HEAD_SIZE), 0)
    tile = jnp.zeros((STAT_ROWS, HEAD_SIZE), jnp.float32)

    def along(x):
        return jnp.sum(jnp.where(diagonal, x, 0.0), 0, keepdims=True)

    for j, (m, l) in enumerate(zip(top, total)):
        l = along(l)
        high = l.astype(jnp.bfloat16).astype(jnp.float32)
        for t, x in enumerate((along(m), high, l - high)):
            tile = jnp.where(row == 4 * t + j, x, tile)
    return tile.astype(jnp.bfloat16)


def unpack_stats(tile):
    row = iota((STAT_ROWS, 8 * HEAD_SIZE), 0)
    block = iota((STAT_ROWS, 8 * HEAD_SIZE), 1) // HEAD_SIZE
    j = block // 2
    stat = block % 2
    spread = (
        ((row == j) & (stat == 0)) | ((row == j + 4) & (stat == 1)) | ((row == j + 8) & (stat == 1))
    )
    spread = spread.astype(jnp.float32).astype(jnp.bfloat16)
    turned = tile.astype(jnp.float32).T.astype(jnp.bfloat16)
    wide = jnp.dot(turned, spread, preferred_element_type=jnp.float32)
    part = lambda b: wide[:, b * HEAD_SIZE:(b + 1) * HEAD_SIZE]
    return [part(2 * j) for j in range(4)], [part(2 * j + 1) for j in range(4)]


def attend_kernel(sizes, jobs, own, keeping, *refs):
    rows, suffix, cap, page_len, count = sizes
    refs = list(refs)
    meta = refs.pop(0)
    queries = [refs.pop(0) for _ in range(count)]
    own_kv = refs.pop(0) if own else None
    held = refs.pop(0)
    if keeping and keeping[0]:
        refs.pop(0)
    outs = [(refs.pop(0), refs.pop(0)) for _ in range(count)]
    stored = refs.pop(0) if keeping else None
    scores = refs.pop(0)
    late_scores = refs.pop(0) if own else None
    if keeping:
        span = pl.ds(*keeping)
        keep = pltpu.make_async_copy(held.at[span], stored.at[span], refs.pop(0))
        keep.start()
    factor = HEAD_SIZE ** (-0.5) * LOG2E
    keys = cap * page_len

    def stacked(n, part, h):
        return jnp.concatenate([held[meta[n, c], part, :, block_of(h)] for c in range(cap)], 0)

    def score(i):
        n, _, h = jobs[i]
        q = queries[n][h * rows:(h + 1) * rows, :]
        scores[i % 2] = dot_nt(q, stacked(n, 0, h))
        if own:
            at = iota((rows, suffix), 0) % suffix
            causal = iota((rows, suffix), 1) <= at
            late_scores[i % 2] = jnp.where(causal, dot_nt(q, own_kv[0, :, block_of(h)]), DEAD)

    def weigh(i):
        n, spot, h = jobs[i]
        live = iota((1, keys), 1) < meta[n, cap] * page_len
        s = jnp.where(live, scores[i % 2], DEAD)
        top = jnp.max(s, axis=-1, keepdims=True)
        if own:
            top = jnp.maximum(top, jnp.max(late_scores[i % 2], axis=-1, keepdims=True))
        top = jnp.maximum(top * factor, FLOOR).astype(jnp.bfloat16).astype(jnp.float32)
        p = jnp.exp2(s * factor - top).astype(jnp.bfloat16)
        v = stacked(n, 1, h)
        v = jnp.concatenate([v, jnp.ones_like(v)], 1)
        out = jnp.dot(p, v, preferred_element_type=jnp.float32)
        if own:
            p = jnp.exp2(late_scores[i % 2] * factor - top).astype(jnp.bfloat16)
            v = own_kv[1, :, block_of(h)]
            v = jnp.concatenate([v, jnp.ones_like(v)], 1)
            out = out + jnp.dot(p, v, preferred_element_type=jnp.float32)
        acc_ref, stat_ref = outs[n]
        acc_ref[spot] = out[:, :HEAD_SIZE]
        total = out[:, HEAD_SIZE:]
        top = jnp.broadcast_to(top, total.shape)
        blocks = [block_of(j) for j in range(rows // HEAD_SIZE)]
        stat_ref[spot] = pack_stats([top[j] for j in blocks], [total[j] for j in blocks])

    for i in range(len(jobs) + 1):
        if i < len(jobs):
            score(i)
        if i > 0:
            weigh(i - 1)
    if keeping:
        keep.wait()


def attend(sizes, jobs, meta, queries, held, own=None, keeping=None, store=None, cost=None):
    rows, suffix, cap, page_len = sizes
    keys, count = cap * page_len, len(queries)
    heads = len(jobs) // count
    shapes, out_specs = [], []
    for _ in queries:
        shapes.append(jax.ShapeDtypeStruct((heads, rows, HEAD_SIZE), jnp.float32))
        shapes.append(jax.ShapeDtypeStruct((heads, STAT_ROWS, HEAD_SIZE), jnp.bfloat16))
        out_specs += [VMEM, VMEM]
    scratch = [pltpu.VMEM((2, rows, keys), jnp.float32)]
    args, aliases = [meta, *queries], {}
    if own is not None:
        args.append(own)
        scratch.append(pltpu.VMEM((2, rows, suffix), jnp.float32))
    args.append(held)
    in_specs = [SMEM] + [VMEM] * (len(args) - 1)
    if keeping:
        shapes.append(jax.ShapeDtypeStruct(held.shape, held.dtype))
        out_specs.append(HBM)
        scratch.append(pltpu.SemaphoreType.DMA)
    if store is not None:
        aliases[len(args)] = 2 * count
        args.append(store)
        in_specs.append(HBM)
    work = pl.CostEstimate(
        flops=len(jobs) * rows * keys * HEAD_SIZE * 8,
        bytes_accessed=len(jobs) * (rows * 6 + keys * 4) * HEAD_SIZE,
        transcendentals=len(jobs) * rows * keys,
    )
    out = pl.pallas_call(
        functools.partial(attend_kernel, sizes + (count,), jobs, own is not None, keeping),
        out_shape=shapes,
        in_specs=in_specs,
        out_specs=out_specs,
        scratch_shapes=scratch,
        input_output_aliases=aliases,
        compiler_params=pltpu.CompilerParams(vmem_limit_bytes=GRANT),
        cost_estimate=cost or work,
    )(*args)
    return [(out[2 * n], out[2 * n + 1]) for n in range(count)] + list(out[2 * count:])


def place_kernel(half, column, me_ref, core_ref, near_ref, far_ref, page_ref, old_ref, out_ref, sem):
    me, core = me_ref[0], core_ref[0]
    is_near = ((me >= half) == (me % 2 == 0)) == (core % 2 == 0)
    slot = jnp.where(is_near, near_ref[0, column], far_ref[0, column])
    copy = pltpu.make_async_copy(page_ref.at[0], out_ref.at[slot], sem)
    copy.start()
    copy.wait()


def place_page(half, column, me, core, near, far, page, store):
    return pl.pallas_call(
        functools.partial(place_kernel, half, column),
        out_shape=jax.ShapeDtypeStruct(store.shape, store.dtype),
        in_specs=[SMEM] * 4 + [VMEM, HBM],
        out_specs=HBM,
        scratch_shapes=[pltpu.SemaphoreType.DMA],
        input_output_aliases={5: 0},
        compiler_params=pltpu.CompilerParams(vmem_limit_bytes=GRANT),
        cost_estimate=LIGHT,
    )(me[None], core[None], near, far, page, store)


def blend(parts):
    top = functools.reduce(jnp.maximum, [m for _, m, _ in parts])
    scales = [jnp.exp2(m - top) for _, m, _ in parts]
    acc = sum(a * f for (a, _, _), f in zip(parts, scales))
    total = sum(l * f for (_, _, l), f in zip(parts, scales))
    return acc, top, total


def pack_kernel(acc_ref, stat_ref, out_ref):
    heads, rows = acc_ref.shape[:2]
    for h in range(heads):
        out_ref[h, :rows, :] = acc_ref[h].astype(jnp.bfloat16)
        out_ref[h, rows:, :] = stat_ref[h]


def merge_kernel(in_first, first, in_ref, acc_ref, stat_ref, out_ref):
    heads, rows = out_ref.shape[0], acc_ref.shape[1]
    for h in range(heads):
        in_top, in_total = unpack_stats(in_ref[in_first + h, rows:, :])
        my_top, my_total = unpack_stats(stat_ref[first + h])
        tops, totals = [], []
        for j in range(rows // HEAD_SIZE):
            acc, top, total = blend(
                [
                    (in_ref[in_first + h, block_of(j), :].astype(jnp.float32), in_top[j], in_total[j]),
                    (acc_ref[first + h, block_of(j), :], my_top[j], my_total[j]),
                ]
            )
            out_ref[h, block_of(j), :] = acc.astype(out_ref.dtype)
            tops.append(top)
            totals.append(total)
        out_ref[h, rows:, :] = pack_stats(tops, totals)


def final_kernel(suffix, first, in_ref, acc_ref, stat_ref, *refs):
    out_ref, done, sems = refs[-3:]
    heads, rows = in_ref.shape[0], acc_ref.shape[1]
    groups = rows // suffix
    copies = []
    for h in range(heads):
        in_top, in_total = unpack_stats(in_ref[h, rows:, :])
        my_top, my_total = unpack_stats(stat_ref[h])
        for j in range(rows // HEAD_SIZE):
            acc, _, total = blend(
                [
                    (in_ref[h, block_of(j), :].astype(jnp.float32), in_top[j], in_total[j]),
                    (acc_ref[h, block_of(j), :], my_top[j], my_total[j]),
                ]
            )
            out = (acc / total).astype(jnp.bfloat16)
            for i in range(HEAD_SIZE // suffix):
                g = h * groups + j * (HEAD_SIZE // suffix) + i
                done[0, :, block_of(g)] = out[i * suffix:(i + 1) * suffix]
        width = groups * HEAD_SIZE
        copies.append(
            pltpu.make_async_copy(
                done.at[:, :, pl.ds(h * width, width)],
                out_ref.at[:, :, pl.ds((first + h) * width, width)],
                sems.at[h],
            )
        )
        copies[-1].start()
    for copy in copies:
        copy.wait()


def finish(suffix, first, like, block, part, before=None):
    heads, rows = block.shape[0], part[0].shape[1]
    args = [block, *part] + ([] if before is None else [before])
    return pl.pallas_call(
        functools.partial(final_kernel, suffix, first),
        out_shape=jax.ShapeDtypeStruct(like.shape, like.dtype),
        in_specs=[VMEM] * 3 + [HBM] * (len(args) - 3),
        out_specs=HBM,
        scratch_shapes=[
            pltpu.VMEM((1, suffix, heads * rows // suffix * HEAD_SIZE), like.dtype),
            pltpu.SemaphoreType.DMA((heads,)),
        ],
        input_output_aliases={} if before is None else {3: 0},
        compiler_params=pltpu.CompilerParams(vmem_limit_bytes=GRANT),
    )(*args)


def call(kernel, shape, *args):
    size = sum(a.size * a.dtype.itemsize for a in args)
    return pl.pallas_call(
        kernel,
        out_shape=shape,
        in_specs=[VMEM] * len(args),
        out_specs=[VMEM] * len(shape) if isinstance(shape, list) else VMEM,
        compiler_params=pltpu.CompilerParams(vmem_limit_bytes=GRANT),
        cost_estimate=pl.CostEstimate(flops=size, bytes_accessed=2 * size, transcendentals=0),
    )(*args)


def lists_kernel(cap, pages_dev, length_ref, slot_ref, table_ref, out_ref):
    maxp = table_ref.shape[1]
    table = table_ref[...]
    owner = lax.div(table, pages_dev)
    local = (table - owner * pages_dev).astype(jnp.float32)
    owner = owner.astype(jnp.float32)
    down, along = iota((maxp, maxp), 0), iota((maxp, maxp), 1)

    def turned(x):
        return jnp.sum(jnp.where(down == along, x, 0.0), 1, keepdims=True)

    before = (turned(owner) == owner) & (along < down)
    rank = jnp.sum(jnp.where(before, 1.0, 0.0), 1, keepdims=True)
    place = iota((maxp, HEAD_SIZE), 1)
    live = jnp.where(iota((maxp, HEAD_SIZE), 0) < length_ref[0], 1.0, 0.0)
    ids = jnp.where(rank == place.astype(jnp.float32), turned(local), 0.0)
    fields = jnp.where(place < cap, ids, jnp.where(place == cap, live, 0.0))
    owned = jnp.where(owner == iota((LIST_ROWS, maxp), 0).astype(jnp.float32), 1.0, 0.0)
    lists = jnp.dot(
        owned.astype(jnp.bfloat16), fields.astype(jnp.bfloat16), preferred_element_type=jnp.float32
    )
    slot = slot_ref[0].astype(jnp.float32)
    lists = jnp.where(iota(lists.shape, 1) == cap + 1, slot, lists)
    out_ref[...] = lists.astype(jnp.bfloat16)


def list_pages(cap, pages_dev, page_table, prefix_pages, new_slots):
    return pl.pallas_call(
        functools.partial(lists_kernel, cap, pages_dev),
        out_shape=jax.ShapeDtypeStruct((LIST_ROWS, HEAD_SIZE), jnp.bfloat16),
        in_specs=[SMEM, SMEM, VMEM],
        out_specs=VMEM,
        compiler_params=pltpu.CompilerParams(vmem_limit_bytes=GRANT),
    )(prefix_pages, new_slots, page_table)


def join_kernel(q_ref, lists_ref, out_ref):
    suffix, columns = q_ref.shape[1:]
    for g in range(columns // HEAD_SIZE):
        out_ref[g * suffix:(g + 1) * suffix, :] = q_ref[0, :, block_of(g)]
    out_ref[columns // HEAD_SIZE * suffix:, :] = lists_ref[...]


def queries_travel(queries, suffix_key_value, kv_pages, page_table, prefix_pages, new_slots):
    stores = lax.axis_size("store")
    cores = lax.axis_size("tensor")
    pages_dev, _, page_len, width = kv_pages.shape
    cap = page_table.shape[1] // stores
    heads = width // HEAD_SIZE
    suffix = queries.shape[1]
    rows = queries.shape[2] // width * suffix
    sizes = (rows, suffix, cap, page_len)
    half = stores // 2
    me = lax.axis_index("store")

    order = list(range(0, stores, 2)) + list(range(1, stores, 2))[::-1]
    route = [
        (order[i] * cores + core, order[(i + 1 - 2 * (core % 2)) % stores] * cores + core)
        for core in range(cores)
        for i in range(stores)
    ]

    def onward(x):
        return lax.ppermute(x, ("store", "tensor"), route)

    def listed(x, below):
        row = lax.dynamic_slice(x, (below + me, 0), (1, HEAD_SIZE))
        return row.astype(jnp.int32)

    def after(values, token):
        return lax.optimization_barrier((values, token))[0]

    def joined(x, rows_below):
        shape = jax.ShapeDtypeStruct((heads * rows + LIST_ROWS, HEAD_SIZE), queries.dtype)
        return call(join_kernel, shape, x, rows_below)

    first = onward(queries)
    mine = list_pages(cap, pages_dev, page_table, prefix_pages, new_slots)
    moving = joined(first, onward(mine))

    own_queries = None
    halves = [range(0, heads // 2), range(heads // 2, heads)]
    token = []
    lists, own = {}, []
    for step in range(1, stores):
        came = after(moving, token)
        if step < stores - 1:
            moving = onward(came)
        lists[step] = listed(came, heads * rows)
        if step == stores - 3:
            arrived = shifted(after(suffix_key_value, token), "store", half)
        jobs = [(0, h, h) for h in range(heads)]
        keeping, pages = None, pages_dev // 2
        if step == 1:
            keeping = (0, pages)
            part, store = attend(sizes, jobs, lists[step], [came], kv_pages, None, keeping)
        elif step == 2:
            keeping = (pages, pages_dev - pages)
            part, store = attend(sizes, jobs, lists[step], [came], kv_pages, None, keeping, store)
        else:
            cost = {stores - 2: LIGHT, stores - 1: HEAVY}.get(step)
            part, = attend(sizes, jobs, lists[step], [came], kv_pages, cost=cost)
        if step == 1:
            blocks = [packed(part)]
        elif step < stores - 2:
            blocks = [merged(after(partial[0], part), part, 0, 0, heads)]
        else:
            part = after(part, arrived) if step == stores - 1 else part
            blocks = []
            for n, half_heads in enumerate(halves):
                block, at = (partial[0], half_heads[0]) if len(partial) == 1 else (partial[n], 0)
                block = after(block, [part, blocks])
                blocks.append(merged(block, part, at, half_heads[0], len(half_heads)))
        partial = [onward(block) for block in blocks]
        token = blocks
        if step in (half - 1, half):
            if own_queries is None:
                own_queries = joined(after(queries, token), mine)
            jobs = [(0, n, h) for n, h in enumerate(halves[len(own)])]
            x = after(own_queries, token)
            own += attend(sizes, jobs, listed(mine, 0), [x], kv_pages, suffix_key_value[0])
            token = [blocks, own]

    quarter = stores // 4
    near, far = lists[quarter], lists[stores - quarter]
    core = lax.axis_index("tensor")
    store = place_page(half, cap + 1, me, core, near, far, arrived, after(store, token))
    attended = finish(suffix, 0, queries, after(partial[0], store), own[0])
    attended = finish(suffix, heads // 2, queries, partial[1], own[1], attended)
    return (attended, store)


def wire_of(part, heads):
    rows, columns = part[0].shape[1:]
    return jax.ShapeDtypeStruct((heads, rows + STAT_ROWS, columns), jnp.bfloat16)


def packed(part):
    return call(pack_kernel, wire_of(part, part[0].shape[0]), *part)


def merged(block, part, in_first, first, heads):
    kernel = functools.partial(merge_kernel, in_first, first)
    return call(kernel, wire_of(part, heads), block, *part)


def on_device(queries, suffix_key_value, kv_pages, page_table, prefix_pages, new_slots):
    stores = lax.axis_size("store")
    pulled = page_table.shape[1] // stores * kv_pages[0].size
    pushed = 2 * queries[0].size
    arrays = (queries, suffix_key_value, kv_pages, page_table, prefix_pages, new_slots)
    if pulled >= pushed and stores % 8 == 0 and stores <= LIST_ROWS:
        return queries_travel(*arrays)
    return pages_travel(*arrays)


def solution(mesh):
    return jax.shard_map(
        on_device,
        mesh=mesh,
        in_specs=(
            P(("groups", "store"), None, "tensor"),
            P(("groups", "store"), None, None, "tensor"),
            P(("groups", "store"), None, None, "tensor"),
            P(("groups", "store"), None),
            P(("groups", "store")),
            P(("groups", "store")),
        ),
        out_specs=(
            P(("groups", "store"), None, "tensor"),
            P(("groups", "store"), None, None, "tensor"),
        ),
        check_vma=False,
    )
```

```python
import functools

import jax
import jax.numpy as jnp
from jax import lax
from jax.experimental import pallas as pl
from jax.experimental.pallas import tpu as pltpu
from jax.sharding import PartitionSpec as P

HEAD_SIZE = 128
LOG2E = 1.4426950408889634
DEAD = -1e30
FLOOR = -1e29
STAT_ROWS = 16
LIST_ROWS = 16
GRANT = 20 * 1024 * 1024
LIGHT = pl.CostEstimate(flops=1, bytes_accessed=1, transcendentals=0)
HEAVY = pl.CostEstimate(flops=1 << 33, bytes_accessed=1 << 25, transcendentals=1 << 24)
VMEM = pl.BlockSpec(memory_space=pltpu.VMEM)
SMEM = pl.BlockSpec(memory_space=pltpu.SMEM)
HBM = pl.BlockSpec(memory_space=pltpu.HBM)


def shifted(block, axis, distance):
    devices = range(lax.axis_size(axis))
    route = [((i - distance) % len(devices), i) for i in devices]
    return lax.ppermute(block, axis, route)


def block_update(state, head_count, key_rows, value_rows, live, scale):
    top_old, total_old, acc_old = state
    scores = (
        jnp.einsum("qhgd,khd->hgqk", head_count, key_rows, preferred_element_type=jnp.float32)
        * scale
    )
    scores = jnp.where(live, scores, -1e30)
    top_new = jnp.maximum(top_old, jnp.max(scores, axis=-1))
    weights = jnp.where(live, jnp.exp(scores - top_new[..., None]), 0.0)
    factor = jnp.exp(top_old - top_new)
    total_new = total_old * factor + jnp.sum(weights, axis=-1)
    product = jnp.einsum(
        "hgqk,khd->hgqd",
        weights.astype(jnp.bfloat16),
        value_rows,
        preferred_element_type=jnp.float32,
    )
    return (top_new, total_new, acc_old * factor[..., None] + product)


def pages_travel(queries, suffix_key_value, kv_pages, page_table, prefix_pages, new_slots):
    stores = lax.axis_size("store")
    pages_dev = kv_pages.shape[0]
    maxp = page_table.shape[1]
    cap = maxp // stores
    page_len = kv_pages.shape[2]
    width = kv_pages.shape[3]
    kv_heads = width // HEAD_SIZE
    suffix = queries.shape[1]
    groups_per_head = queries.shape[2] // width
    scale = HEAD_SIZE ** (-0.5)
    length = prefix_pages[0]
    table = page_table[0]
    owners = table // pages_dev
    local_ids = table % pages_dev
    entries = jnp.arange(maxp, dtype=jnp.int32)
    same_owner = (owners[:, None] == owners[None, :]) & (entries[:, None] < entries[None, :])
    ranks = jnp.sum(same_owner.astype(jnp.int32), axis=0)
    slots = owners * cap + ranks
    placed = slots[:, None] == entries[None, :]
    slot_entry = jnp.sum(jnp.where(placed, entries[:, None], 0), axis=0)
    wanted = jnp.sum(jnp.where(placed, local_ids[:, None], 0), axis=0)
    asked = lax.all_to_all(
        wanted.reshape(stores, cap), "store", split_axis=0, concat_axis=0, tiled=True
    )
    served = kv_pages[asked.reshape(-1)].reshape(stores, cap, 2, page_len, width)
    received = lax.all_to_all(served, "store", split_axis=0, concat_axis=0, tiled=True).reshape(
        maxp, 2, page_len, width
    )
    head_count = queries[0].reshape(suffix, kv_heads, groups_per_head, HEAD_SIZE)
    own_keys = suffix_key_value[0, 0].reshape(suffix, kv_heads, HEAD_SIZE)
    own_values = suffix_key_value[0, 1].reshape(suffix, kv_heads, HEAD_SIZE)
    rows = jnp.arange(suffix, dtype=jnp.int32)
    causal = rows[None, :] <= rows[:, None]
    start_state = (
        jnp.full((kv_heads, groups_per_head, suffix), -1e30, jnp.float32),
        jnp.zeros((kv_heads, groups_per_head, suffix), jnp.float32),
        jnp.zeros((kv_heads, groups_per_head, suffix, HEAD_SIZE), jnp.float32),
    )
    state = block_update(start_state, head_count, own_keys, own_values, causal, scale)
    block_pages = min(8, maxp)
    live_pages = slot_entry < length
    trips = maxp // block_pages

    def step_block(index, carry):
        first = index * block_pages
        block = lax.dynamic_slice_in_dim(received, first, block_pages, 0)
        alive = lax.dynamic_slice_in_dim(live_pages, first, block_pages, 0)
        alive = jnp.broadcast_to(alive[:, None], (block_pages, page_len)).reshape(
            1, block_pages * page_len
        )
        block_keys = block[:, 0].reshape(block_pages * page_len, kv_heads, HEAD_SIZE)
        block_values = block[:, 1].reshape(block_pages * page_len, kv_heads, HEAD_SIZE)
        return block_update(carry, head_count, block_keys, block_values, alive, scale)

    top_final, total_final, acc_final = lax.fori_loop(0, trips, step_block, state)
    output = acc_final / total_final[..., None]
    attended = (
        output.transpose(2, 0, 1, 3)
        .reshape(1, suffix, groups_per_head * width)
        .astype(jnp.bfloat16)
    )
    arrived, arrived_slot = shifted((suffix_key_value, new_slots), "store", stores // 2)
    new_store = lax.dynamic_update_slice_in_dim(kv_pages, arrived, arrived_slot[0], 0)
    return (attended, new_store)


def dot_nt(a, b):
    return lax.dot_general(a, b, (((1,), (1,)), ((), ())), preferred_element_type=jnp.float32)


def block_of(j):
    return slice(j * HEAD_SIZE, (j + 1) * HEAD_SIZE)


def iota(shape, dim):
    return lax.broadcasted_iota(jnp.int32, shape, dim)


def pack_stats(top, total):
    diagonal = iota((HEAD_SIZE, HEAD_SIZE), 0) == iota((HEAD_SIZE, HEAD_SIZE), 1)
    row = iota((STAT_ROWS, HEAD_SIZE), 0)
    tile = jnp.zeros((STAT_ROWS, HEAD_SIZE), jnp.float32)

    def along(x):
        return jnp.sum(jnp.where(diagonal, x, 0.0), 0, keepdims=True)

    for j, (m, l) in enumerate(zip(top, total)):
        l = along(l)
        high = l.astype(jnp.bfloat16).astype(jnp.float32)
        for t, x in enumerate((along(m), high, l - high)):
            tile = jnp.where(row == 4 * t + j, x, tile)
    return tile.astype(jnp.bfloat16)


def unpack_stats(tile):
    row = iota((STAT_ROWS, 8 * HEAD_SIZE), 0)
    block = iota((STAT_ROWS, 8 * HEAD_SIZE), 1) // HEAD_SIZE
    j = block // 2
    stat = block % 2
    spread = (
        ((row == j) & (stat == 0)) | ((row == j + 4) & (stat == 1)) | ((row == j + 8) & (stat == 1))
    )
    spread = spread.astype(jnp.float32).astype(jnp.bfloat16)
    turned = tile.astype(jnp.float32).T.astype(jnp.bfloat16)
    wide = jnp.dot(turned, spread, preferred_element_type=jnp.float32)
    part = lambda b: wide[:, b * HEAD_SIZE:(b + 1) * HEAD_SIZE]
    return [part(2 * j) for j in range(4)], [part(2 * j + 1) for j in range(4)]


def attend_kernel(sizes, jobs, own, keeping, *refs):
    rows, suffix, cap, page_len, count = sizes
    refs = list(refs)
    meta = refs.pop(0)
    queries = [refs.pop(0) for _ in range(count)]
    own_kv = refs.pop(0) if own else None
    held = refs.pop(0)
    if keeping and keeping[0]:
        refs.pop(0)
    outs = [(refs.pop(0), refs.pop(0)) for _ in range(count)]
    stored = refs.pop(0) if keeping else None
    scores = refs.pop(0)
    late_scores = refs.pop(0) if own else None
    if keeping:
        span = pl.ds(*keeping)
        keep = pltpu.make_async_copy(held.at[span], stored.at[span], refs.pop(0))
        keep.start()
    factor = HEAD_SIZE ** (-0.5) * LOG2E
    keys = cap * page_len

    def stacked(n, part, h):
        return jnp.concatenate([held[meta[n, c], part, :, block_of(h)] for c in range(cap)], 0)

    def score(i):
        n, _, h = jobs[i]
        q = queries[n][h * rows:(h + 1) * rows, :]
        scores[i % 2] = dot_nt(q, stacked(n, 0, h))
        if own:
            at = iota((rows, suffix), 0) % suffix
            causal = iota((rows, suffix), 1) <= at
            late_scores[i % 2] = jnp.where(causal, dot_nt(q, own_kv[0, :, block_of(h)]), DEAD)

    def weigh(i):
        n, spot, h = jobs[i]
        live = iota((1, keys), 1) < meta[n, cap] * page_len
        s = jnp.where(live, scores[i % 2], DEAD)
        top = jnp.max(s, axis=-1, keepdims=True)
        if own:
            top = jnp.maximum(top, jnp.max(late_scores[i % 2], axis=-1, keepdims=True))
        top = jnp.maximum(top * factor, FLOOR).astype(jnp.bfloat16).astype(jnp.float32)
        p = jnp.exp2(s * factor - top).astype(jnp.bfloat16)
        v = stacked(n, 1, h)
        v = jnp.concatenate([v, jnp.ones_like(v)], 1)
        out = jnp.dot(p, v, preferred_element_type=jnp.float32)
        if own:
            p = jnp.exp2(late_scores[i % 2] * factor - top).astype(jnp.bfloat16)
            v = own_kv[1, :, block_of(h)]
            v = jnp.concatenate([v, jnp.ones_like(v)], 1)
            out = out + jnp.dot(p, v, preferred_element_type=jnp.float32)
        acc_ref, stat_ref = outs[n]
        acc_ref[spot] = out[:, :HEAD_SIZE]
        total = out[:, HEAD_SIZE:]
        top = jnp.broadcast_to(top, total.shape)
        blocks = [block_of(j) for j in range(rows // HEAD_SIZE)]
        stat_ref[spot] = pack_stats([top[j] for j in blocks], [total[j] for j in blocks])

    for i in range(len(jobs) + 1):
        if i < len(jobs):
            score(i)
        if i > 0:
            weigh(i - 1)
    if keeping:
        keep.wait()


def attend(sizes, jobs, meta, queries, held, own=None, keeping=None, store=None, cost=None):
    rows, suffix, cap, page_len = sizes
    keys, count = cap * page_len, len(queries)
    heads = len(jobs) // count
    shapes, out_specs = [], []
    for _ in queries:
        shapes.append(jax.ShapeDtypeStruct((heads, rows, HEAD_SIZE), jnp.float32))
        shapes.append(jax.ShapeDtypeStruct((heads, STAT_ROWS, HEAD_SIZE), jnp.bfloat16))
        out_specs += [VMEM, VMEM]
    scratch = [pltpu.VMEM((2, rows, keys), jnp.float32)]
    args, aliases = [meta, *queries], {}
    if own is not None:
        args.append(own)
        scratch.append(pltpu.VMEM((2, rows, suffix), jnp.float32))
    args.append(held)
    in_specs = [SMEM] + [VMEM] * (len(args) - 1)
    if keeping:
        shapes.append(jax.ShapeDtypeStruct(held.shape, held.dtype))
        out_specs.append(HBM)
        scratch.append(pltpu.SemaphoreType.DMA)
    if store is not None:
        aliases[len(args)] = 2 * count
        args.append(store)
        in_specs.append(HBM)
    work = pl.CostEstimate(
        flops=len(jobs) * rows * keys * HEAD_SIZE * 8,
        bytes_accessed=len(jobs) * (rows * 6 + keys * 4) * HEAD_SIZE,
        transcendentals=len(jobs) * rows * keys,
    )
    out = pl.pallas_call(
        functools.partial(attend_kernel, sizes + (count,), jobs, own is not None, keeping),
        out_shape=shapes,
        in_specs=in_specs,
        out_specs=out_specs,
        scratch_shapes=scratch,
        input_output_aliases=aliases,
        compiler_params=pltpu.CompilerParams(vmem_limit_bytes=GRANT),
        cost_estimate=cost or work,
    )(*args)
    return [(out[2 * n], out[2 * n + 1]) for n in range(count)] + list(out[2 * count:])


def touch_kernel(held_ref, lists_ref, out_ref):
    out_ref[...] = lists_ref[...]


def touch(held, lists):
    return pl.pallas_call(
        touch_kernel,
        out_shape=jax.ShapeDtypeStruct(lists.shape, lists.dtype),
        in_specs=[VMEM, VMEM],
        out_specs=VMEM,
        compiler_params=pltpu.CompilerParams(vmem_limit_bytes=GRANT),
        cost_estimate=LIGHT,
    )(held, lists)


def place_kernel(half, column, me_ref, core_ref, near_ref, far_ref, page_ref, old_ref, out_ref, sem):
    me, core = me_ref[0], core_ref[0]
    is_near = ((me >= half) == (me % 2 == 0)) == (core % 2 == 0)
    slot = jnp.where(is_near, near_ref[0, column], far_ref[0, column])
    copy = pltpu.make_async_copy(page_ref.at[0], out_ref.at[slot], sem)
    copy.start()
    copy.wait()


def place_page(half, column, me, core, near, far, page, store):
    return pl.pallas_call(
        functools.partial(place_kernel, half, column),
        out_shape=jax.ShapeDtypeStruct(store.shape, store.dtype),
        in_specs=[SMEM] * 4 + [VMEM, HBM],
        out_specs=HBM,
        scratch_shapes=[pltpu.SemaphoreType.DMA],
        input_output_aliases={5: 0},
        compiler_params=pltpu.CompilerParams(vmem_limit_bytes=GRANT),
        cost_estimate=LIGHT,
    )(me[None], core[None], near, far, page, store)


def blend(parts):
    top = functools.reduce(jnp.maximum, [m for _, m, _ in parts])
    scales = [jnp.exp2(m - top) for _, m, _ in parts]
    acc = sum(a * f for (a, _, _), f in zip(parts, scales))
    total = sum(l * f for (_, _, l), f in zip(parts, scales))
    return acc, top, total


def pack_kernel(acc_ref, stat_ref, out_ref):
    heads, rows = acc_ref.shape[:2]
    for h in range(heads):
        out_ref[h, :rows, :] = acc_ref[h].astype(jnp.bfloat16)
        out_ref[h, rows:, :] = stat_ref[h]


def merge_kernel(in_first, first, in_ref, acc_ref, stat_ref, out_ref):
    heads, rows = out_ref.shape[0], acc_ref.shape[1]
    for h in range(heads):
        in_top, in_total = unpack_stats(in_ref[in_first + h, rows:, :])
        my_top, my_total = unpack_stats(stat_ref[first + h])
        tops, totals = [], []
        for j in range(rows // HEAD_SIZE):
            acc, top, total = blend(
                [
                    (in_ref[in_first + h, block_of(j), :].astype(jnp.float32), in_top[j], in_total[j]),
                    (acc_ref[first + h, block_of(j), :], my_top[j], my_total[j]),
                ]
            )
            out_ref[h, block_of(j), :] = acc.astype(out_ref.dtype)
            tops.append(top)
            totals.append(total)
        out_ref[h, rows:, :] = pack_stats(tops, totals)


def final_kernel(suffix, first, in_ref, acc_ref, stat_ref, *refs):
    out_ref, done, sems = refs[-3:]
    heads, rows = in_ref.shape[0], acc_ref.shape[1]
    groups = rows // suffix
    copies = []
    for h in range(heads):
        in_top, in_total = unpack_stats(in_ref[h, rows:, :])
        my_top, my_total = unpack_stats(stat_ref[h])
        for j in range(rows // HEAD_SIZE):
            acc, _, total = blend(
                [
                    (in_ref[h, block_of(j), :].astype(jnp.float32), in_top[j], in_total[j]),
                    (acc_ref[h, block_of(j), :], my_top[j], my_total[j]),
                ]
            )
            out = (acc / total).astype(jnp.bfloat16)
            for i in range(HEAD_SIZE // suffix):
                g = h * groups + j * (HEAD_SIZE // suffix) + i
                done[0, :, block_of(g)] = out[i * suffix:(i + 1) * suffix]
        width = groups * HEAD_SIZE
        copies.append(
            pltpu.make_async_copy(
                done.at[:, :, pl.ds(h * width, width)],
                out_ref.at[:, :, pl.ds((first + h) * width, width)],
                sems.at[h],
            )
        )
        copies[-1].start()
    for copy in copies:
        copy.wait()


def finish(suffix, first, like, block, part, before=None):
    heads, rows = block.shape[0], part[0].shape[1]
    args = [block, *part] + ([] if before is None else [before])
    return pl.pallas_call(
        functools.partial(final_kernel, suffix, first),
        out_shape=jax.ShapeDtypeStruct(like.shape, like.dtype),
        in_specs=[VMEM] * 3 + [HBM] * (len(args) - 3),
        out_specs=HBM,
        scratch_shapes=[
            pltpu.VMEM((1, suffix, heads * rows // suffix * HEAD_SIZE), like.dtype),
            pltpu.SemaphoreType.DMA((heads,)),
        ],
        input_output_aliases={} if before is None else {3: 0},
        compiler_params=pltpu.CompilerParams(vmem_limit_bytes=GRANT),
    )(*args)


def call(kernel, shape, *args):
    size = sum(a.size * a.dtype.itemsize for a in args)
    return pl.pallas_call(
        kernel,
        out_shape=shape,
        in_specs=[VMEM] * len(args),
        out_specs=[VMEM] * len(shape) if isinstance(shape, list) else VMEM,
        compiler_params=pltpu.CompilerParams(vmem_limit_bytes=GRANT),
        cost_estimate=pl.CostEstimate(flops=size, bytes_accessed=2 * size, transcendentals=0),
    )(*args)


def lists_kernel(cap, pages_dev, length_ref, slot_ref, table_ref, out_ref):
    maxp = table_ref.shape[1]
    table = table_ref[...]
    owner = lax.div(table, pages_dev)
    local = (table - owner * pages_dev).astype(jnp.float32)
    owner = owner.astype(jnp.float32)
    down, along = iota((maxp, maxp), 0), iota((maxp, maxp), 1)

    def turned(x):
        return jnp.sum(jnp.where(down == along, x, 0.0), 1, keepdims=True)

    before = (turned(owner) == owner) & (along < down)
    rank = jnp.sum(jnp.where(before, 1.0, 0.0), 1, keepdims=True)
    place = iota((maxp, HEAD_SIZE), 1)
    live = jnp.where(iota((maxp, HEAD_SIZE), 0) < length_ref[0], 1.0, 0.0)
    ids = jnp.where(rank == place.astype(jnp.float32), turned(local), 0.0)
    fields = jnp.where(place < cap, ids, jnp.where(place == cap, live, 0.0))
    owned = jnp.where(owner == iota((LIST_ROWS, maxp), 0).astype(jnp.float32), 1.0, 0.0)
    lists = jnp.dot(
        owned.astype(jnp.bfloat16), fields.astype(jnp.bfloat16), preferred_element_type=jnp.float32
    )
    slot = slot_ref[0].astype(jnp.float32)
    lists = jnp.where(iota(lists.shape, 1) == cap + 1, slot, lists)
    out_ref[...] = lists.astype(jnp.bfloat16)


def list_pages(cap, pages_dev, page_table, prefix_pages, new_slots):
    return pl.pallas_call(
        functools.partial(lists_kernel, cap, pages_dev),
        out_shape=jax.ShapeDtypeStruct((LIST_ROWS, HEAD_SIZE), jnp.bfloat16),
        in_specs=[SMEM, SMEM, VMEM],
        out_specs=VMEM,
        compiler_params=pltpu.CompilerParams(vmem_limit_bytes=GRANT),
    )(prefix_pages, new_slots, page_table)


def join_kernel(q_ref, lists_ref, out_ref):
    suffix, columns = q_ref.shape[1:]
    for g in range(columns // HEAD_SIZE):
        out_ref[g * suffix:(g + 1) * suffix, :] = q_ref[0, :, block_of(g)]
    out_ref[columns // HEAD_SIZE * suffix:, :] = lists_ref[...]


def queries_travel(queries, suffix_key_value, kv_pages, page_table, prefix_pages, new_slots):
    stores = lax.axis_size("store")
    cores = lax.axis_size("tensor")
    pages_dev, _, page_len, width = kv_pages.shape
    cap = page_table.shape[1] // stores
    heads = width // HEAD_SIZE
    suffix = queries.shape[1]
    rows = queries.shape[2] // width * suffix
    sizes = (rows, suffix, cap, page_len)
    half = stores // 2
    me = lax.axis_index("store")

    order = list(range(0, stores, 2)) + list(range(1, stores, 2))[::-1]
    route = [
        (order[i] * cores + core, order[(i + 1 - 2 * (core % 2)) % stores] * cores + core)
        for core in range(cores)
        for i in range(stores)
    ]

    def onward(x):
        return lax.ppermute(x, ("store", "tensor"), route)

    def listed(x, below):
        row = lax.dynamic_slice(x, (below + me, 0), (1, HEAD_SIZE))
        return row.astype(jnp.int32)

    def after(values, token):
        return lax.optimization_barrier((values, token))[0]

    def joined(x, rows_below):
        shape = jax.ShapeDtypeStruct((heads * rows + LIST_ROWS, HEAD_SIZE), queries.dtype)
        return call(join_kernel, shape, x, rows_below)

    first = onward(queries)
    mine = list_pages(cap, pages_dev, page_table, prefix_pages, new_slots)
    their_lists = onward(mine)
    mine = touch(kv_pages, mine)
    moving = joined(after(first, mine), their_lists)

    own_queries = None
    halves = [range(0, heads // 2), range(heads // 2, heads)]
    token = []
    lists, own = {}, []
    for step in range(1, stores):
        came = after(moving, token)
        if step < stores - 1:
            moving = onward(came)
        lists[step] = listed(came, heads * rows)
        if step == stores - 3:
            arrived = shifted(after(suffix_key_value, token), "store", half)
        jobs = [(0, h, h) for h in range(heads)]
        keeping, pages = None, pages_dev // 2
        if step == 2:
            keeping = (0, pages)
            part, store = attend(sizes, jobs, lists[step], [came], kv_pages, None, keeping)
        elif step == 3:
            keeping = (pages, pages_dev - pages)
            part, store = attend(sizes, jobs, lists[step], [came], kv_pages, None, keeping, store)
        else:
            cost = {stores - 2: LIGHT, stores - 1: HEAVY}.get(step)
            part, = attend(sizes, jobs, lists[step], [came], kv_pages, cost=cost)
        if step == 1:
            blocks = [packed(part)]
        elif step < stores - 2:
            blocks = [merged(after(partial[0], part), part, 0, 0, heads)]
        else:
            part = after(part, arrived) if step == stores - 1 else part
            blocks = []
            for n, half_heads in enumerate(halves):
                block, at = (partial[0], half_heads[0]) if len(partial) == 1 else (partial[n], 0)
                block = after(block, [part, blocks])
                blocks.append(merged(block, part, at, half_heads[0], len(half_heads)))
        partial = [onward(block) for block in blocks]
        token = blocks
        if step in (half - 1, half):
            if own_queries is None:
                own_queries = joined(after(queries, token), mine)
            jobs = [(0, n, h) for n, h in enumerate(halves[len(own)])]
            x = after(own_queries, token)
            own += attend(sizes, jobs, listed(mine, 0), [x], kv_pages, suffix_key_value[0])
            token = [blocks, own]

    quarter = stores // 4
    near, far = lists[quarter], lists[stores - quarter]
    core = lax.axis_index("tensor")
    store = place_page(half, cap + 1, me, core, near, far, arrived, after(store, token))
    attended = finish(suffix, 0, queries, after(partial[0], store), own[0])
    attended = finish(suffix, heads // 2, queries, partial[1], own[1], attended)
    return (attended, store)


def wire_of(part, heads):
    rows, columns = part[0].shape[1:]
    return jax.ShapeDtypeStruct((heads, rows + STAT_ROWS, columns), jnp.bfloat16)


def packed(part):
    return call(pack_kernel, wire_of(part, part[0].shape[0]), *part)


def merged(block, part, in_first, first, heads):
    kernel = functools.partial(merge_kernel, in_first, first)
    return call(kernel, wire_of(part, heads), block, *part)


def on_device(queries, suffix_key_value, kv_pages, page_table, prefix_pages, new_slots):
    stores = lax.axis_size("store")
    pulled = page_table.shape[1] // stores * kv_pages[0].size
    pushed = 2 * queries[0].size
    arrays = (queries, suffix_key_value, kv_pages, page_table, prefix_pages, new_slots)
    if pulled >= pushed and stores % 8 == 0 and stores <= LIST_ROWS:
        return queries_travel(*arrays)
    return pages_travel(*arrays)


def solution(mesh):
    return jax.shard_map(
        on_device,
        mesh=mesh,
        in_specs=(
            P(("groups", "store"), None, "tensor"),
            P(("groups", "store"), None, None, "tensor"),
            P(("groups", "store"), None, None, "tensor"),
            P(("groups", "store"), None),
            P(("groups", "store")),
            P(("groups", "store")),
        ),
        out_specs=(
            P(("groups", "store"), None, "tensor"),
            P(("groups", "store"), None, None, "tensor"),
        ),
        check_vma=False,
    )
```

```python
import functools

import jax
import jax.numpy as jnp
from jax import lax
from jax.experimental import pallas as pl
from jax.experimental.pallas import tpu as pltpu
from jax.sharding import PartitionSpec as P

HEAD_SIZE = 128
LOG2E = 1.4426950408889634
DEAD = -1e30
FLOOR = -1e29
STAT_ROWS = 16
LIST_ROWS = 16
GRANT = 20 * 1024 * 1024
LIGHT = pl.CostEstimate(flops=1, bytes_accessed=1, transcendentals=0)
HEAVY = pl.CostEstimate(flops=1 << 33, bytes_accessed=1 << 25, transcendentals=1 << 24)
VMEM = pl.BlockSpec(memory_space=pltpu.VMEM)
SMEM = pl.BlockSpec(memory_space=pltpu.SMEM)
HBM = pl.BlockSpec(memory_space=pltpu.HBM)


def shifted(block, axis, distance):
    devices = range(lax.axis_size(axis))
    route = [((i - distance) % len(devices), i) for i in devices]
    return lax.ppermute(block, axis, route)


def block_update(state, head_count, key_rows, value_rows, live, scale):
    top_old, total_old, acc_old = state
    scores = (
        jnp.einsum("qhgd,khd->hgqk", head_count, key_rows, preferred_element_type=jnp.float32)
        * scale
    )
    scores = jnp.where(live, scores, -1e30)
    top_new = jnp.maximum(top_old, jnp.max(scores, axis=-1))
    weights = jnp.where(live, jnp.exp(scores - top_new[..., None]), 0.0)
    factor = jnp.exp(top_old - top_new)
    total_new = total_old * factor + jnp.sum(weights, axis=-1)
    product = jnp.einsum(
        "hgqk,khd->hgqd",
        weights.astype(jnp.bfloat16),
        value_rows,
        preferred_element_type=jnp.float32,
    )
    return (top_new, total_new, acc_old * factor[..., None] + product)


def pages_travel(queries, suffix_key_value, kv_pages, page_table, prefix_pages, new_slots):
    stores = lax.axis_size("store")
    pages_dev = kv_pages.shape[0]
    maxp = page_table.shape[1]
    cap = maxp // stores
    page_len = kv_pages.shape[2]
    width = kv_pages.shape[3]
    kv_heads = width // HEAD_SIZE
    suffix = queries.shape[1]
    groups_per_head = queries.shape[2] // width
    scale = HEAD_SIZE ** (-0.5)
    length = prefix_pages[0]
    table = page_table[0]
    owners = table // pages_dev
    local_ids = table % pages_dev
    entries = jnp.arange(maxp, dtype=jnp.int32)
    same_owner = (owners[:, None] == owners[None, :]) & (entries[:, None] < entries[None, :])
    ranks = jnp.sum(same_owner.astype(jnp.int32), axis=0)
    slots = owners * cap + ranks
    placed = slots[:, None] == entries[None, :]
    slot_entry = jnp.sum(jnp.where(placed, entries[:, None], 0), axis=0)
    wanted = jnp.sum(jnp.where(placed, local_ids[:, None], 0), axis=0)
    asked = lax.all_to_all(
        wanted.reshape(stores, cap), "store", split_axis=0, concat_axis=0, tiled=True
    )
    served = kv_pages[asked.reshape(-1)].reshape(stores, cap, 2, page_len, width)
    received = lax.all_to_all(served, "store", split_axis=0, concat_axis=0, tiled=True).reshape(
        maxp, 2, page_len, width
    )
    head_count = queries[0].reshape(suffix, kv_heads, groups_per_head, HEAD_SIZE)
    own_keys = suffix_key_value[0, 0].reshape(suffix, kv_heads, HEAD_SIZE)
    own_values = suffix_key_value[0, 1].reshape(suffix, kv_heads, HEAD_SIZE)
    rows = jnp.arange(suffix, dtype=jnp.int32)
    causal = rows[None, :] <= rows[:, None]
    start_state = (
        jnp.full((kv_heads, groups_per_head, suffix), -1e30, jnp.float32),
        jnp.zeros((kv_heads, groups_per_head, suffix), jnp.float32),
        jnp.zeros((kv_heads, groups_per_head, suffix, HEAD_SIZE), jnp.float32),
    )
    state = block_update(start_state, head_count, own_keys, own_values, causal, scale)
    block_pages = min(8, maxp)
    live_pages = slot_entry < length
    trips = maxp // block_pages

    def step_block(index, carry):
        first = index * block_pages
        block = lax.dynamic_slice_in_dim(received, first, block_pages, 0)
        alive = lax.dynamic_slice_in_dim(live_pages, first, block_pages, 0)
        alive = jnp.broadcast_to(alive[:, None], (block_pages, page_len)).reshape(
            1, block_pages * page_len
        )
        block_keys = block[:, 0].reshape(block_pages * page_len, kv_heads, HEAD_SIZE)
        block_values = block[:, 1].reshape(block_pages * page_len, kv_heads, HEAD_SIZE)
        return block_update(carry, head_count, block_keys, block_values, alive, scale)

    top_final, total_final, acc_final = lax.fori_loop(0, trips, step_block, state)
    output = acc_final / total_final[..., None]
    attended = (
        output.transpose(2, 0, 1, 3)
        .reshape(1, suffix, groups_per_head * width)
        .astype(jnp.bfloat16)
    )
    arrived, arrived_slot = shifted((suffix_key_value, new_slots), "store", stores // 2)
    new_store = lax.dynamic_update_slice_in_dim(kv_pages, arrived, arrived_slot[0], 0)
    return (attended, new_store)


def dot_nt(a, b):
    return lax.dot_general(a, b, (((1,), (1,)), ((), ())), preferred_element_type=jnp.float32)


def block_of(j):
    return slice(j * HEAD_SIZE, (j + 1) * HEAD_SIZE)


def iota(shape, dim):
    return lax.broadcasted_iota(jnp.int32, shape, dim)


def pack_stats(top, total):
    diagonal = iota((HEAD_SIZE, HEAD_SIZE), 0) == iota((HEAD_SIZE, HEAD_SIZE), 1)
    row = iota((STAT_ROWS, HEAD_SIZE), 0)
    tile = jnp.zeros((STAT_ROWS, HEAD_SIZE), jnp.float32)

    def along(x):
        return jnp.sum(jnp.where(diagonal, x, 0.0), 0, keepdims=True)

    for j, (m, l) in enumerate(zip(top, total)):
        l = along(l)
        high = l.astype(jnp.bfloat16).astype(jnp.float32)
        for t, x in enumerate((along(m), high, l - high)):
            tile = jnp.where(row == 4 * t + j, x, tile)
    return tile.astype(jnp.bfloat16)


def unpack_stats(tile):
    row = iota((STAT_ROWS, 8 * HEAD_SIZE), 0)
    block = iota((STAT_ROWS, 8 * HEAD_SIZE), 1) // HEAD_SIZE
    j = block // 2
    stat = block % 2
    spread = (
        ((row == j) & (stat == 0)) | ((row == j + 4) & (stat == 1)) | ((row == j + 8) & (stat == 1))
    )
    spread = spread.astype(jnp.float32).astype(jnp.bfloat16)
    turned = tile.astype(jnp.float32).T.astype(jnp.bfloat16)
    wide = jnp.dot(turned, spread, preferred_element_type=jnp.float32)
    part = lambda b: wide[:, b * HEAD_SIZE:(b + 1) * HEAD_SIZE]
    return [part(2 * j) for j in range(4)], [part(2 * j + 1) for j in range(4)]


def attend_kernel(sizes, jobs, own, keeping, *refs):
    rows, suffix, cap, page_len, count = sizes
    refs = list(refs)
    meta = refs.pop(0)
    queries = [refs.pop(0) for _ in range(count)]
    own_kv = refs.pop(0) if own else None
    held = refs.pop(0)
    if keeping and keeping[0]:
        refs.pop(0)
    outs = [(refs.pop(0), refs.pop(0)) for _ in range(count)]
    stored = refs.pop(0) if keeping else None
    scores = refs.pop(0)
    late_scores = refs.pop(0) if own else None
    if keeping:
        span = pl.ds(*keeping)
        keep = pltpu.make_async_copy(held.at[span], stored.at[span], refs.pop(0))
        keep.start()
    factor = HEAD_SIZE ** (-0.5) * LOG2E
    keys = cap * page_len

    def stacked(n, part, h):
        return jnp.concatenate([held[meta[n, c], part, :, block_of(h)] for c in range(cap)], 0)

    def score(i):
        n, _, h = jobs[i]
        q = queries[n][h * rows:(h + 1) * rows, :]
        scores[i % 2] = dot_nt(q, stacked(n, 0, h))
        if own:
            at = iota((rows, suffix), 0) % suffix
            causal = iota((rows, suffix), 1) <= at
            late_scores[i % 2] = jnp.where(causal, dot_nt(q, own_kv[0, :, block_of(h)]), DEAD)

    def weigh(i):
        n, spot, h = jobs[i]
        live = iota((1, keys), 1) < meta[n, cap] * page_len
        s = jnp.where(live, scores[i % 2], DEAD)
        top = jnp.max(s, axis=-1, keepdims=True)
        if own:
            top = jnp.maximum(top, jnp.max(late_scores[i % 2], axis=-1, keepdims=True))
        top = jnp.maximum(top * factor, FLOOR).astype(jnp.bfloat16).astype(jnp.float32)
        p = jnp.exp2(s * factor - top).astype(jnp.bfloat16)
        v = stacked(n, 1, h)
        v = jnp.concatenate([v, jnp.ones_like(v)], 1)
        out = jnp.dot(p, v, preferred_element_type=jnp.float32)
        if own:
            p = jnp.exp2(late_scores[i % 2] * factor - top).astype(jnp.bfloat16)
            v = own_kv[1, :, block_of(h)]
            v = jnp.concatenate([v, jnp.ones_like(v)], 1)
            out = out + jnp.dot(p, v, preferred_element_type=jnp.float32)
        acc_ref, stat_ref = outs[n]
        acc_ref[spot] = out[:, :HEAD_SIZE]
        total = out[:, HEAD_SIZE:]
        top = jnp.broadcast_to(top, total.shape)
        blocks = [block_of(j) for j in range(rows // HEAD_SIZE)]
        stat_ref[spot] = pack_stats([top[j] for j in blocks], [total[j] for j in blocks])

    for i in range(len(jobs) + 1):
        if i < len(jobs):
            score(i)
        if i > 0:
            weigh(i - 1)
    if keeping:
        keep.wait()


def attend(sizes, jobs, meta, queries, held, own=None, keeping=None, store=None, cost=None):
    rows, suffix, cap, page_len = sizes
    keys, count = cap * page_len, len(queries)
    heads = len(jobs) // count
    shapes, out_specs = [], []
    for _ in queries:
        shapes.append(jax.ShapeDtypeStruct((heads, rows, HEAD_SIZE), jnp.float32))
        shapes.append(jax.ShapeDtypeStruct((heads, STAT_ROWS, HEAD_SIZE), jnp.bfloat16))
        out_specs += [VMEM, VMEM]
    scratch = [pltpu.VMEM((2, rows, keys), jnp.float32)]
    args, aliases = [meta, *queries], {}
    if own is not None:
        args.append(own)
        scratch.append(pltpu.VMEM((2, rows, suffix), jnp.float32))
    args.append(held)
    in_specs = [SMEM] + [VMEM] * (len(args) - 1)
    if keeping:
        shapes.append(jax.ShapeDtypeStruct(held.shape, held.dtype))
        out_specs.append(HBM)
        scratch.append(pltpu.SemaphoreType.DMA)
    if store is not None:
        aliases[len(args)] = 2 * count
        args.append(store)
        in_specs.append(HBM)
    work = pl.CostEstimate(
        flops=len(jobs) * rows * keys * HEAD_SIZE * 8,
        bytes_accessed=len(jobs) * (rows * 6 + keys * 4) * HEAD_SIZE,
        transcendentals=len(jobs) * rows * keys,
    )
    out = pl.pallas_call(
        functools.partial(attend_kernel, sizes + (count,), jobs, own is not None, keeping),
        out_shape=shapes,
        in_specs=in_specs,
        out_specs=out_specs,
        scratch_shapes=scratch,
        input_output_aliases=aliases,
        compiler_params=pltpu.CompilerParams(vmem_limit_bytes=GRANT),
        cost_estimate=cost or work,
    )(*args)
    return [(out[2 * n], out[2 * n + 1]) for n in range(count)] + list(out[2 * count:])


def touch_kernel(held_ref, lists_ref, out_ref):
    out_ref[...] = lists_ref[...]


def touch(held, lists):
    return pl.pallas_call(
        touch_kernel,
        out_shape=jax.ShapeDtypeStruct(lists.shape, lists.dtype),
        in_specs=[VMEM, VMEM],
        out_specs=VMEM,
        compiler_params=pltpu.CompilerParams(vmem_limit_bytes=GRANT),
        cost_estimate=LIGHT,
    )(held, lists)


def place_kernel(half, column, me_ref, core_ref, near_ref, far_ref, page_ref, old_ref, out_ref, sem):
    me, core = me_ref[0], core_ref[0]
    is_near = ((me >= half) == (me % 2 == 0)) == (core % 2 == 0)
    slot = jnp.where(is_near, near_ref[0, column], far_ref[0, column])
    copy = pltpu.make_async_copy(page_ref.at[0], out_ref.at[slot], sem)
    copy.start()
    copy.wait()


def place_page(half, column, me, core, near, far, page, store):
    return pl.pallas_call(
        functools.partial(place_kernel, half, column),
        out_shape=jax.ShapeDtypeStruct(store.shape, store.dtype),
        in_specs=[SMEM] * 4 + [VMEM, HBM],
        out_specs=HBM,
        scratch_shapes=[pltpu.SemaphoreType.DMA],
        input_output_aliases={5: 0},
        compiler_params=pltpu.CompilerParams(vmem_limit_bytes=GRANT),
        cost_estimate=LIGHT,
    )(me[None], core[None], near, far, page, store)


def blend(parts):
    top = functools.reduce(jnp.maximum, [m for _, m, _ in parts])
    scales = [jnp.exp2(m - top) for _, m, _ in parts]
    acc = sum(a * f for (a, _, _), f in zip(parts, scales))
    total = sum(l * f for (_, _, l), f in zip(parts, scales))
    return acc, top, total


def pack_kernel(acc_ref, stat_ref, out_ref):
    heads, rows = acc_ref.shape[:2]
    for h in range(heads):
        out_ref[h, :rows, :] = acc_ref[h].astype(jnp.bfloat16)
        out_ref[h, rows:, :] = stat_ref[h]


def merge_kernel(in_first, first, in_ref, acc_ref, stat_ref, out_ref):
    heads, rows = out_ref.shape[0], acc_ref.shape[1]
    for h in range(heads):
        in_top, in_total = unpack_stats(in_ref[in_first + h, rows:, :])
        my_top, my_total = unpack_stats(stat_ref[first + h])
        tops, totals = [], []
        for j in range(rows // HEAD_SIZE):
            acc, top, total = blend(
                [
                    (in_ref[in_first + h, block_of(j), :].astype(jnp.float32), in_top[j], in_total[j]),
                    (acc_ref[first + h, block_of(j), :], my_top[j], my_total[j]),
                ]
            )
            out_ref[h, block_of(j), :] = acc.astype(out_ref.dtype)
            tops.append(top)
            totals.append(total)
        out_ref[h, rows:, :] = pack_stats(tops, totals)


def final_kernel(suffix, first, in_ref, acc_ref, stat_ref, *refs):
    out_ref, done, sems = refs[-3:]
    heads, rows = in_ref.shape[0], acc_ref.shape[1]
    groups = rows // suffix
    copies = []
    for h in range(heads):
        in_top, in_total = unpack_stats(in_ref[h, rows:, :])
        my_top, my_total = unpack_stats(stat_ref[h])
        for j in range(rows // HEAD_SIZE):
            acc, _, total = blend(
                [
                    (in_ref[h, block_of(j), :].astype(jnp.float32), in_top[j], in_total[j]),
                    (acc_ref[h, block_of(j), :], my_top[j], my_total[j]),
                ]
            )
            out = (acc / total).astype(jnp.bfloat16)
            for i in range(HEAD_SIZE // suffix):
                g = h * groups + j * (HEAD_SIZE // suffix) + i
                done[0, :, block_of(g)] = out[i * suffix:(i + 1) * suffix]
        width = groups * HEAD_SIZE
        copies.append(
            pltpu.make_async_copy(
                done.at[:, :, pl.ds(h * width, width)],
                out_ref.at[:, :, pl.ds((first + h) * width, width)],
                sems.at[h],
            )
        )
        copies[-1].start()
    for copy in copies:
        copy.wait()


def finish(suffix, first, like, block, part, before=None):
    heads, rows = block.shape[0], part[0].shape[1]
    args = [block, *part] + ([] if before is None else [before])
    return pl.pallas_call(
        functools.partial(final_kernel, suffix, first),
        out_shape=jax.ShapeDtypeStruct(like.shape, like.dtype),
        in_specs=[VMEM] * 3 + [HBM] * (len(args) - 3),
        out_specs=HBM,
        scratch_shapes=[
            pltpu.VMEM((1, suffix, heads * rows // suffix * HEAD_SIZE), like.dtype),
            pltpu.SemaphoreType.DMA((heads,)),
        ],
        input_output_aliases={} if before is None else {3: 0},
        compiler_params=pltpu.CompilerParams(vmem_limit_bytes=GRANT),
    )(*args)


def call(kernel, shape, *args):
    size = sum(a.size * a.dtype.itemsize for a in args)
    return pl.pallas_call(
        kernel,
        out_shape=shape,
        in_specs=[VMEM] * len(args),
        out_specs=[VMEM] * len(shape) if isinstance(shape, list) else VMEM,
        compiler_params=pltpu.CompilerParams(vmem_limit_bytes=GRANT),
        cost_estimate=pl.CostEstimate(flops=size, bytes_accessed=2 * size, transcendentals=0),
    )(*args)


def lists_kernel(cap, pages_dev, length_ref, slot_ref, table_ref, out_ref):
    maxp = table_ref.shape[1]
    table = table_ref[...]
    owner = lax.div(table, pages_dev)
    local = (table - owner * pages_dev).astype(jnp.float32)
    owner = owner.astype(jnp.float32)
    down, along = iota((maxp, maxp), 0), iota((maxp, maxp), 1)

    def turned(x):
        return jnp.sum(jnp.where(down == along, x, 0.0), 1, keepdims=True)

    before = (turned(owner) == owner) & (along < down)
    rank = jnp.sum(jnp.where(before, 1.0, 0.0), 1, keepdims=True)
    place = iota((maxp, HEAD_SIZE), 1)
    live = jnp.where(iota((maxp, HEAD_SIZE), 0) < length_ref[0], 1.0, 0.0)
    ids = jnp.where(rank == place.astype(jnp.float32), turned(local), 0.0)
    fields = jnp.where(place < cap, ids, jnp.where(place == cap, live, 0.0))
    owned = jnp.where(owner == iota((LIST_ROWS, maxp), 0).astype(jnp.float32), 1.0, 0.0)
    lists = jnp.dot(
        owned.astype(jnp.bfloat16), fields.astype(jnp.bfloat16), preferred_element_type=jnp.float32
    )
    slot = slot_ref[0].astype(jnp.float32)
    lists = jnp.where(iota(lists.shape, 1) == cap + 1, slot, lists)
    out_ref[...] = lists.astype(jnp.bfloat16)


def list_pages(cap, pages_dev, page_table, prefix_pages, new_slots):
    return pl.pallas_call(
        functools.partial(lists_kernel, cap, pages_dev),
        out_shape=jax.ShapeDtypeStruct((LIST_ROWS, HEAD_SIZE), jnp.bfloat16),
        in_specs=[SMEM, SMEM, VMEM],
        out_specs=VMEM,
        compiler_params=pltpu.CompilerParams(vmem_limit_bytes=GRANT),
    )(prefix_pages, new_slots, page_table)


def join_kernel(q_ref, lists_ref, out_ref):
    suffix, columns = q_ref.shape[1:]
    for g in range(columns // HEAD_SIZE):
        out_ref[g * suffix:(g + 1) * suffix, :] = q_ref[0, :, block_of(g)]
    out_ref[columns // HEAD_SIZE * suffix:, :] = lists_ref[...]


def queries_travel(queries, suffix_key_value, kv_pages, page_table, prefix_pages, new_slots):
    stores = lax.axis_size("store")
    cores = lax.axis_size("tensor")
    pages_dev, _, page_len, width = kv_pages.shape
    cap = page_table.shape[1] // stores
    heads = width // HEAD_SIZE
    suffix = queries.shape[1]
    rows = queries.shape[2] // width * suffix
    sizes = (rows, suffix, cap, page_len)
    half = stores // 2
    me = lax.axis_index("store")

    order = list(range(0, stores, 2)) + list(range(1, stores, 2))[::-1]
    route = [
        (order[i] * cores + core, order[(i + 1 - 2 * (core % 2)) % stores] * cores + core)
        for core in range(cores)
        for i in range(stores)
    ]

    def onward(x):
        return lax.ppermute(x, ("store", "tensor"), route)

    def listed(x, below):
        row = lax.dynamic_slice(x, (below + me, 0), (1, HEAD_SIZE))
        return row.astype(jnp.int32)

    def after(values, token):
        return lax.optimization_barrier((values, token))[0]

    def joined(x, rows_below):
        shape = jax.ShapeDtypeStruct((heads * rows + LIST_ROWS, HEAD_SIZE), queries.dtype)
        return call(join_kernel, shape, x, rows_below)

    first = onward(queries)
    mine = list_pages(cap, pages_dev, page_table, prefix_pages, new_slots)
    their_lists = onward(mine)
    mine = touch(kv_pages, mine)
    moving = joined(after(first, mine), their_lists)

    own_queries = None
    halves = [range(0, heads // 2), range(heads // 2, heads)]
    token = []
    lists, own = {}, []
    for step in range(1, stores):
        came = after(moving, token)
        if step < stores - 1:
            moving = onward(came)
        lists[step] = listed(came, heads * rows)
        if step == stores - 3:
            arrived = shifted(after(suffix_key_value, token), "store", half)
        jobs = [(0, h, h) for h in range(heads)]
        keeping, pages = None, pages_dev // 2
        if step == 2:
            keeping = (0, pages)
            part, store = attend(sizes, jobs, lists[step], [came], kv_pages, None, keeping)
        elif step == 3:
            keeping = (pages, pages_dev - pages)
            part, store = attend(sizes, jobs, lists[step], [came], kv_pages, None, keeping, store)
        else:
            cost = {stores - 2: LIGHT, stores - 1: HEAVY}.get(step)
            part, = attend(sizes, jobs, lists[step], [came], kv_pages, cost=cost)
        if step == 1:
            blocks = [packed(part)]
        elif step < stores - 2:
            blocks = [merged(after(partial[0], part), part, 0, 0, heads)]
        else:
            part = after(part, arrived) if step == stores - 1 else part
            blocks = []
            for n, half_heads in enumerate(halves):
                block, at = (partial[0], half_heads[0]) if len(partial) == 1 else (partial[n], 0)
                block = after(block, [part, blocks])
                blocks.append(merged(block, part, at, half_heads[0], len(half_heads)))
        partial = [onward(block) for block in blocks]
        token = blocks
        if step in (half, half + 1):
            if own_queries is None:
                own_queries = joined(after(queries, token), mine)
            jobs = [(0, n, h) for n, h in enumerate(halves[len(own)])]
            x = after(own_queries, token)
            own += attend(sizes, jobs, listed(mine, 0), [x], kv_pages, suffix_key_value[0])
            token = [blocks, own]

    quarter = stores // 4
    near, far = lists[quarter], lists[stores - quarter]
    core = lax.axis_index("tensor")
    store = place_page(half, cap + 1, me, core, near, far, arrived, after(store, token))
    attended = finish(suffix, 0, queries, after(partial[0], store), own[0])
    attended = finish(suffix, heads // 2, queries, partial[1], own[1], attended)
    return (attended, store)


def wire_of(part, heads):
    rows, columns = part[0].shape[1:]
    return jax.ShapeDtypeStruct((heads, rows + STAT_ROWS, columns), jnp.bfloat16)


def packed(part):
    return call(pack_kernel, wire_of(part, part[0].shape[0]), *part)


def merged(block, part, in_first, first, heads):
    kernel = functools.partial(merge_kernel, in_first, first)
    return call(kernel, wire_of(part, heads), block, *part)


def on_device(queries, suffix_key_value, kv_pages, page_table, prefix_pages, new_slots):
    stores = lax.axis_size("store")
    pulled = page_table.shape[1] // stores * kv_pages[0].size
    pushed = 2 * queries[0].size
    arrays = (queries, suffix_key_value, kv_pages, page_table, prefix_pages, new_slots)
    if pulled >= pushed and stores % 8 == 0 and stores <= LIST_ROWS:
        return queries_travel(*arrays)
    return pages_travel(*arrays)


def solution(mesh):
    return jax.shard_map(
        on_device,
        mesh=mesh,
        in_specs=(
            P(("groups", "store"), None, "tensor"),
            P(("groups", "store"), None, None, "tensor"),
            P(("groups", "store"), None, None, "tensor"),
            P(("groups", "store"), None),
            P(("groups", "store")),
            P(("groups", "store")),
        ),
        out_specs=(
            P(("groups", "store"), None, "tensor"),
            P(("groups", "store"), None, None, "tensor"),
        ),
        check_vma=False,
    )
```

```python
import functools

import jax
import jax.numpy as jnp
from jax import lax
from jax.experimental import pallas as pl
from jax.experimental.pallas import tpu as pltpu
from jax.sharding import PartitionSpec as P

HEAD_SIZE = 128
LOG2E = 1.4426950408889634
DEAD = -1e30
FLOOR = -1e29
STAT_ROWS = 16
LIST_ROWS = 16
GRANT = 20 * 1024 * 1024
LIGHT = pl.CostEstimate(flops=1, bytes_accessed=1, transcendentals=0)
HEAVY = pl.CostEstimate(flops=1 << 33, bytes_accessed=1 << 25, transcendentals=1 << 24)
VMEM = pl.BlockSpec(memory_space=pltpu.VMEM)
SMEM = pl.BlockSpec(memory_space=pltpu.SMEM)
HBM = pl.BlockSpec(memory_space=pltpu.HBM)


def shifted(block, axis, distance):
    devices = range(lax.axis_size(axis))
    route = [((i - distance) % len(devices), i) for i in devices]
    return lax.ppermute(block, axis, route)


def block_update(state, head_count, key_rows, value_rows, live, scale):
    top_old, total_old, acc_old = state
    scores = (
        jnp.einsum("qhgd,khd->hgqk", head_count, key_rows, preferred_element_type=jnp.float32)
        * scale
    )
    scores = jnp.where(live, scores, -1e30)
    top_new = jnp.maximum(top_old, jnp.max(scores, axis=-1))
    weights = jnp.where(live, jnp.exp(scores - top_new[..., None]), 0.0)
    factor = jnp.exp(top_old - top_new)
    total_new = total_old * factor + jnp.sum(weights, axis=-1)
    product = jnp.einsum(
        "hgqk,khd->hgqd",
        weights.astype(jnp.bfloat16),
        value_rows,
        preferred_element_type=jnp.float32,
    )
    return (top_new, total_new, acc_old * factor[..., None] + product)


def pages_travel(queries, suffix_key_value, kv_pages, page_table, prefix_pages, new_slots):
    stores = lax.axis_size("store")
    pages_dev = kv_pages.shape[0]
    maxp = page_table.shape[1]
    cap = maxp // stores
    page_len = kv_pages.shape[2]
    width = kv_pages.shape[3]
    kv_heads = width // HEAD_SIZE
    suffix = queries.shape[1]
    groups_per_head = queries.shape[2] // width
    scale = HEAD_SIZE ** (-0.5)
    length = prefix_pages[0]
    table = page_table[0]
    owners = table // pages_dev
    local_ids = table % pages_dev
    entries = jnp.arange(maxp, dtype=jnp.int32)
    same_owner = (owners[:, None] == owners[None, :]) & (entries[:, None] < entries[None, :])
    ranks = jnp.sum(same_owner.astype(jnp.int32), axis=0)
    slots = owners * cap + ranks
    placed = slots[:, None] == entries[None, :]
    slot_entry = jnp.sum(jnp.where(placed, entries[:, None], 0), axis=0)
    wanted = jnp.sum(jnp.where(placed, local_ids[:, None], 0), axis=0)
    asked = lax.all_to_all(
        wanted.reshape(stores, cap), "store", split_axis=0, concat_axis=0, tiled=True
    )
    served = kv_pages[asked.reshape(-1)].reshape(stores, cap, 2, page_len, width)
    received = lax.all_to_all(served, "store", split_axis=0, concat_axis=0, tiled=True).reshape(
        maxp, 2, page_len, width
    )
    head_count = queries[0].reshape(suffix, kv_heads, groups_per_head, HEAD_SIZE)
    own_keys = suffix_key_value[0, 0].reshape(suffix, kv_heads, HEAD_SIZE)
    own_values = suffix_key_value[0, 1].reshape(suffix, kv_heads, HEAD_SIZE)
    rows = jnp.arange(suffix, dtype=jnp.int32)
    causal = rows[None, :] <= rows[:, None]
    start_state = (
        jnp.full((kv_heads, groups_per_head, suffix), -1e30, jnp.float32),
        jnp.zeros((kv_heads, groups_per_head, suffix), jnp.float32),
        jnp.zeros((kv_heads, groups_per_head, suffix, HEAD_SIZE), jnp.float32),
    )
    state = block_update(start_state, head_count, own_keys, own_values, causal, scale)
    block_pages = min(8, maxp)
    live_pages = slot_entry < length
    trips = maxp // block_pages

    def step_block(index, carry):
        first = index * block_pages
        block = lax.dynamic_slice_in_dim(received, first, block_pages, 0)
        alive = lax.dynamic_slice_in_dim(live_pages, first, block_pages, 0)
        alive = jnp.broadcast_to(alive[:, None], (block_pages, page_len)).reshape(
            1, block_pages * page_len
        )
        block_keys = block[:, 0].reshape(block_pages * page_len, kv_heads, HEAD_SIZE)
        block_values = block[:, 1].reshape(block_pages * page_len, kv_heads, HEAD_SIZE)
        return block_update(carry, head_count, block_keys, block_values, alive, scale)

    top_final, total_final, acc_final = lax.fori_loop(0, trips, step_block, state)
    output = acc_final / total_final[..., None]
    attended = (
        output.transpose(2, 0, 1, 3)
        .reshape(1, suffix, groups_per_head * width)
        .astype(jnp.bfloat16)
    )
    arrived, arrived_slot = shifted((suffix_key_value, new_slots), "store", stores // 2)
    new_store = lax.dynamic_update_slice_in_dim(kv_pages, arrived, arrived_slot[0], 0)
    return (attended, new_store)


def dot_nt(a, b):
    return lax.dot_general(a, b, (((1,), (1,)), ((), ())), preferred_element_type=jnp.float32)


def block_of(j):
    return slice(j * HEAD_SIZE, (j + 1) * HEAD_SIZE)


def iota(shape, dim):
    return lax.broadcasted_iota(jnp.int32, shape, dim)


def pack_stats(top, total):
    diagonal = iota((HEAD_SIZE, HEAD_SIZE), 0) == iota((HEAD_SIZE, HEAD_SIZE), 1)
    row = iota((STAT_ROWS, HEAD_SIZE), 0)
    tile = jnp.zeros((STAT_ROWS, HEAD_SIZE), jnp.float32)

    def along(x):
        return jnp.sum(jnp.where(diagonal, x, 0.0), 0, keepdims=True)

    for j, (m, l) in enumerate(zip(top, total)):
        l = along(l)
        high = l.astype(jnp.bfloat16).astype(jnp.float32)
        for t, x in enumerate((along(m), high, l - high)):
            tile = jnp.where(row == 4 * t + j, x, tile)
    return tile.astype(jnp.bfloat16)


def unpack_stats(tile):
    row = iota((STAT_ROWS, 8 * HEAD_SIZE), 0)
    block = iota((STAT_ROWS, 8 * HEAD_SIZE), 1) // HEAD_SIZE
    j = block // 2
    stat = block % 2
    spread = (
        ((row == j) & (stat == 0)) | ((row == j + 4) & (stat == 1)) | ((row == j + 8) & (stat == 1))
    )
    spread = spread.astype(jnp.float32).astype(jnp.bfloat16)
    turned = tile.astype(jnp.float32).T.astype(jnp.bfloat16)
    wide = jnp.dot(turned, spread, preferred_element_type=jnp.float32)
    part = lambda b: wide[:, b * HEAD_SIZE:(b + 1) * HEAD_SIZE]
    return [part(2 * j) for j in range(4)], [part(2 * j + 1) for j in range(4)]


def attend_kernel(sizes, jobs, own, keeping, *refs):
    rows, suffix, cap, page_len, count = sizes
    refs = list(refs)
    meta = refs.pop(0)
    queries = [refs.pop(0) for _ in range(count)]
    own_kv = refs.pop(0) if own else None
    held = refs.pop(0)
    if keeping and keeping[0]:
        refs.pop(0)
    outs = [(refs.pop(0), refs.pop(0)) for _ in range(count)]
    stored = refs.pop(0) if keeping else None
    scores = refs.pop(0)
    late_scores = refs.pop(0) if own else None
    if keeping:
        span = pl.ds(*keeping)
        keep = pltpu.make_async_copy(held.at[span], stored.at[span], refs.pop(0))
        keep.start()
    factor = HEAD_SIZE ** (-0.5) * LOG2E
    keys = cap * page_len

    def stacked(n, part, h):
        return jnp.concatenate([held[meta[n, c], part, :, block_of(h)] for c in range(cap)], 0)

    def score(i):
        n, _, h = jobs[i]
        q = queries[n][h * rows:(h + 1) * rows, :]
        scores[i % 2] = dot_nt(q, stacked(n, 0, h))
        if own:
            at = iota((rows, suffix), 0) % suffix
            causal = iota((rows, suffix), 1) <= at
            late_scores[i % 2] = jnp.where(causal, dot_nt(q, own_kv[0, :, block_of(h)]), DEAD)

    def weigh(i):
        n, spot, h = jobs[i]
        live = iota((1, keys), 1) < meta[n, cap] * page_len
        s = jnp.where(live, scores[i % 2], DEAD)
        top = jnp.max(s, axis=-1, keepdims=True)
        if own:
            top = jnp.maximum(top, jnp.max(late_scores[i % 2], axis=-1, keepdims=True))
        top = jnp.maximum(top * factor, FLOOR).astype(jnp.bfloat16).astype(jnp.float32)
        p = jnp.exp2(s * factor - top).astype(jnp.bfloat16)
        v = stacked(n, 1, h)
        v = jnp.concatenate([v, jnp.ones_like(v)], 1)
        out = jnp.dot(p, v, preferred_element_type=jnp.float32)
        if own:
            p = jnp.exp2(late_scores[i % 2] * factor - top).astype(jnp.bfloat16)
            v = own_kv[1, :, block_of(h)]
            v = jnp.concatenate([v, jnp.ones_like(v)], 1)
            out = out + jnp.dot(p, v, preferred_element_type=jnp.float32)
        acc_ref, stat_ref = outs[n]
        acc_ref[spot] = out[:, :HEAD_SIZE]
        total = out[:, HEAD_SIZE:]
        top = jnp.broadcast_to(top, total.shape)
        blocks = [block_of(j) for j in range(rows // HEAD_SIZE)]
        stat_ref[spot] = pack_stats([top[j] for j in blocks], [total[j] for j in blocks])

    for i in range(len(jobs) + 1):
        if i < len(jobs):
            score(i)
        if i > 0:
            weigh(i - 1)
    if keeping:
        keep.wait()


def attend(sizes, jobs, meta, queries, held, own=None, keeping=None, store=None, cost=None):
    rows, suffix, cap, page_len = sizes
    keys, count = cap * page_len, len(queries)
    heads = len(jobs) // count
    shapes, out_specs = [], []
    for _ in queries:
        shapes.append(jax.ShapeDtypeStruct((heads, rows, HEAD_SIZE), jnp.float32))
        shapes.append(jax.ShapeDtypeStruct((heads, STAT_ROWS, HEAD_SIZE), jnp.bfloat16))
        out_specs += [VMEM, VMEM]
    scratch = [pltpu.VMEM((2, rows, keys), jnp.float32)]
    args, aliases = [meta, *queries], {}
    if own is not None:
        args.append(own)
        scratch.append(pltpu.VMEM((2, rows, suffix), jnp.float32))
    args.append(held)
    in_specs = [SMEM] + [VMEM] * (len(args) - 1)
    if keeping:
        shapes.append(jax.ShapeDtypeStruct(held.shape, held.dtype))
        out_specs.append(HBM)
        scratch.append(pltpu.SemaphoreType.DMA)
    if store is not None:
        aliases[len(args)] = 2 * count
        args.append(store)
        in_specs.append(HBM)
    work = pl.CostEstimate(
        flops=len(jobs) * rows * keys * HEAD_SIZE * 8,
        bytes_accessed=len(jobs) * (rows * 6 + keys * 4) * HEAD_SIZE,
        transcendentals=len(jobs) * rows * keys,
    )
    out = pl.pallas_call(
        functools.partial(attend_kernel, sizes + (count,), jobs, own is not None, keeping),
        out_shape=shapes,
        in_specs=in_specs,
        out_specs=out_specs,
        scratch_shapes=scratch,
        input_output_aliases=aliases,
        compiler_params=pltpu.CompilerParams(vmem_limit_bytes=GRANT),
        cost_estimate=cost or work,
    )(*args)
    return [(out[2 * n], out[2 * n + 1]) for n in range(count)] + list(out[2 * count:])


def touch_kernel(held_ref, lists_ref, out_ref):
    out_ref[...] = lists_ref[...]


def touch(held, lists):
    return pl.pallas_call(
        touch_kernel,
        out_shape=jax.ShapeDtypeStruct(lists.shape, lists.dtype),
        in_specs=[VMEM, VMEM],
        out_specs=VMEM,
        compiler_params=pltpu.CompilerParams(vmem_limit_bytes=GRANT),
        cost_estimate=LIGHT,
    )(held, lists)


def place_kernel(half, column, me_ref, core_ref, near_ref, far_ref, page_ref, old_ref, out_ref, sem):
    me, core = me_ref[0], core_ref[0]
    is_near = ((me >= half) == (me % 2 == 0)) == (core % 2 == 0)
    slot = jnp.where(is_near, near_ref[0, column], far_ref[0, column])
    copy = pltpu.make_async_copy(page_ref.at[0], out_ref.at[slot], sem)
    copy.start()
    copy.wait()


def place_page(half, column, me, core, near, far, page, store):
    return pl.pallas_call(
        functools.partial(place_kernel, half, column),
        out_shape=jax.ShapeDtypeStruct(store.shape, store.dtype),
        in_specs=[SMEM] * 4 + [VMEM, HBM],
        out_specs=HBM,
        scratch_shapes=[pltpu.SemaphoreType.DMA],
        input_output_aliases={5: 0},
        compiler_params=pltpu.CompilerParams(vmem_limit_bytes=GRANT),
        cost_estimate=LIGHT,
    )(me[None], core[None], near, far, page, store)


def blend(parts):
    top = functools.reduce(jnp.maximum, [m for _, m, _ in parts])
    scales = [jnp.exp2(m - top) for _, m, _ in parts]
    acc = sum(a * f for (a, _, _), f in zip(parts, scales))
    total = sum(l * f for (_, _, l), f in zip(parts, scales))
    return acc, top, total


def pack_kernel(acc_ref, stat_ref, out_ref):
    heads, rows = acc_ref.shape[:2]
    for h in range(heads):
        out_ref[h, :rows, :] = acc_ref[h].astype(jnp.bfloat16)
        out_ref[h, rows:, :] = stat_ref[h]


def merge_kernel(in_first, first, in_ref, acc_ref, stat_ref, out_ref):
    heads, rows = out_ref.shape[0], acc_ref.shape[1]
    for h in range(heads):
        in_top, in_total = unpack_stats(in_ref[in_first + h, rows:, :])
        my_top, my_total = unpack_stats(stat_ref[first + h])
        tops, totals = [], []
        for j in range(rows // HEAD_SIZE):
            acc, top, total = blend(
                [
                    (in_ref[in_first + h, block_of(j), :].astype(jnp.float32), in_top[j], in_total[j]),
                    (acc_ref[first + h, block_of(j), :], my_top[j], my_total[j]),
                ]
            )
            out_ref[h, block_of(j), :] = acc.astype(out_ref.dtype)
            tops.append(top)
            totals.append(total)
        out_ref[h, rows:, :] = pack_stats(tops, totals)


def final_kernel(suffix, first, in_ref, acc_ref, stat_ref, *refs):
    out_ref, done, sems = refs[-3:]
    heads, rows = in_ref.shape[0], acc_ref.shape[1]
    groups = rows // suffix
    copies = []
    for h in range(heads):
        in_top, in_total = unpack_stats(in_ref[h, rows:, :])
        my_top, my_total = unpack_stats(stat_ref[h])
        for j in range(rows // HEAD_SIZE):
            acc, _, total = blend(
                [
                    (in_ref[h, block_of(j), :].astype(jnp.float32), in_top[j], in_total[j]),
                    (acc_ref[h, block_of(j), :], my_top[j], my_total[j]),
                ]
            )
            out = (acc / total).astype(jnp.bfloat16)
            for i in range(HEAD_SIZE // suffix):
                g = h * groups + j * (HEAD_SIZE // suffix) + i
                done[0, :, block_of(g)] = out[i * suffix:(i + 1) * suffix]
        width = groups * HEAD_SIZE
        copies.append(
            pltpu.make_async_copy(
                done.at[:, :, pl.ds(h * width, width)],
                out_ref.at[:, :, pl.ds((first + h) * width, width)],
                sems.at[h],
            )
        )
        copies[-1].start()
    for copy in copies:
        copy.wait()


def finish(suffix, first, like, block, part, before=None):
    heads, rows = block.shape[0], part[0].shape[1]
    args = [block, *part] + ([] if before is None else [before])
    return pl.pallas_call(
        functools.partial(final_kernel, suffix, first),
        out_shape=jax.ShapeDtypeStruct(like.shape, like.dtype),
        in_specs=[VMEM] * 3 + [HBM] * (len(args) - 3),
        out_specs=HBM,
        scratch_shapes=[
            pltpu.VMEM((1, suffix, heads * rows // suffix * HEAD_SIZE), like.dtype),
            pltpu.SemaphoreType.DMA((heads,)),
        ],
        input_output_aliases={} if before is None else {3: 0},
        compiler_params=pltpu.CompilerParams(vmem_limit_bytes=GRANT),
    )(*args)


def call(kernel, shape, *args):
    size = sum(a.size * a.dtype.itemsize for a in args)
    return pl.pallas_call(
        kernel,
        out_shape=shape,
        in_specs=[VMEM] * len(args),
        out_specs=[VMEM] * len(shape) if isinstance(shape, list) else VMEM,
        compiler_params=pltpu.CompilerParams(vmem_limit_bytes=GRANT),
        cost_estimate=pl.CostEstimate(flops=size, bytes_accessed=2 * size, transcendentals=0),
    )(*args)


def lists_kernel(cap, pages_dev, length_ref, slot_ref, table_ref, out_ref):
    maxp = table_ref.shape[1]
    table = table_ref[...]
    owner = lax.div(table, pages_dev)
    local = (table - owner * pages_dev).astype(jnp.float32)
    owner = owner.astype(jnp.float32)
    down, along = iota((maxp, maxp), 0), iota((maxp, maxp), 1)

    def turned(x):
        return jnp.sum(jnp.where(down == along, x, 0.0), 1, keepdims=True)

    before = (turned(owner) == owner) & (along < down)
    rank = jnp.sum(jnp.where(before, 1.0, 0.0), 1, keepdims=True)
    place = iota((maxp, HEAD_SIZE), 1)
    live = jnp.where(iota((maxp, HEAD_SIZE), 0) < length_ref[0], 1.0, 0.0)
    ids = jnp.where(rank == place.astype(jnp.float32), turned(local), 0.0)
    fields = jnp.where(place < cap, ids, jnp.where(place == cap, live, 0.0))
    owned = jnp.where(owner == iota((LIST_ROWS, maxp), 0).astype(jnp.float32), 1.0, 0.0)
    lists = jnp.dot(
        owned.astype(jnp.bfloat16), fields.astype(jnp.bfloat16), preferred_element_type=jnp.float32
    )
    slot = slot_ref[0].astype(jnp.float32)
    lists = jnp.where(iota(lists.shape, 1) == cap + 1, slot, lists)
    out_ref[...] = lists.astype(jnp.bfloat16)


def list_pages(cap, pages_dev, page_table, prefix_pages, new_slots):
    return pl.pallas_call(
        functools.partial(lists_kernel, cap, pages_dev),
        out_shape=jax.ShapeDtypeStruct((LIST_ROWS, HEAD_SIZE), jnp.bfloat16),
        in_specs=[SMEM, SMEM, VMEM],
        out_specs=VMEM,
        compiler_params=pltpu.CompilerParams(vmem_limit_bytes=GRANT),
    )(prefix_pages, new_slots, page_table)


def join_kernel(q_ref, lists_ref, out_ref):
    suffix, columns = q_ref.shape[1:]
    for g in range(columns // HEAD_SIZE):
        out_ref[g * suffix:(g + 1) * suffix, :] = q_ref[0, :, block_of(g)]
    out_ref[columns // HEAD_SIZE * suffix:, :] = lists_ref[...]


def queries_travel(queries, suffix_key_value, kv_pages, page_table, prefix_pages, new_slots):
    stores = lax.axis_size("store")
    cores = lax.axis_size("tensor")
    pages_dev, _, page_len, width = kv_pages.shape
    cap = page_table.shape[1] // stores
    heads = width // HEAD_SIZE
    suffix = queries.shape[1]
    rows = queries.shape[2] // width * suffix
    sizes = (rows, suffix, cap, page_len)
    half = stores // 2
    me = lax.axis_index("store")

    order = list(range(0, stores, 2)) + list(range(1, stores, 2))[::-1]
    route = [
        (order[i] * cores + core, order[(i + 1 - 2 * (core % 2)) % stores] * cores + core)
        for core in range(cores)
        for i in range(stores)
    ]

    def onward(x):
        return lax.ppermute(x, ("store", "tensor"), route)

    def listed(x, below):
        row = lax.dynamic_slice(x, (below + me, 0), (1, HEAD_SIZE))
        return row.astype(jnp.int32)

    def after(values, token):
        return lax.optimization_barrier((values, token))[0]

    def joined(x, rows_below):
        shape = jax.ShapeDtypeStruct((heads * rows + LIST_ROWS, HEAD_SIZE), queries.dtype)
        return call(join_kernel, shape, x, rows_below)

    first = onward(queries)
    mine = list_pages(cap, pages_dev, page_table, prefix_pages, new_slots)
    their_lists = onward(mine)
    mine = touch(kv_pages, mine)
    moving = joined(after(first, mine), their_lists)

    own_queries = None
    halves = [range(0, heads // 2), range(heads // 2, heads)]
    token = []
    lists, own = {}, []
    for step in range(1, stores):
        came = after(moving, token)
        if step < stores - 1:
            moving = onward(came)
        lists[step] = listed(came, heads * rows)
        if step == stores - 3:
            arrived = shifted(after(suffix_key_value, token), "store", half)
        jobs = [(0, h, h) for h in range(heads)]
        keeping, pages = None, pages_dev // 2
        if step == 2:
            keeping = (0, pages)
            part, store = attend(sizes, jobs, lists[step], [came], kv_pages, None, keeping)
        elif step == 3:
            keeping = (pages, pages_dev - pages)
            part, store = attend(sizes, jobs, lists[step], [came], kv_pages, None, keeping, store)
        else:
            cost = {stores - 2: LIGHT, stores - 1: HEAVY}.get(step)
            part, = attend(sizes, jobs, lists[step], [came], kv_pages, cost=cost)
        if step == 1:
            blocks = [packed(part)]
        elif step < stores - 1:
            blocks = [merged(after(partial[0], part), part, 0, 0, heads)]
        else:
            part = after(part, arrived) if step == stores - 1 else part
            blocks = []
            for n, half_heads in enumerate(halves):
                block, at = (partial[0], half_heads[0]) if len(partial) == 1 else (partial[n], 0)
                block = after(block, [part, blocks])
                blocks.append(merged(block, part, at, half_heads[0], len(half_heads)))
        partial = [onward(block) for block in blocks]
        token = blocks
        if step in (half - 1, half):
            if own_queries is None:
                own_queries = joined(after(queries, token), mine)
            jobs = [(0, n, h) for n, h in enumerate(halves[len(own)])]
            x = after(own_queries, token)
            own += attend(sizes, jobs, listed(mine, 0), [x], kv_pages, suffix_key_value[0])
            token = [blocks, own]

    quarter = stores // 4
    near, far = lists[quarter], lists[stores - quarter]
    core = lax.axis_index("tensor")
    store = place_page(half, cap + 1, me, core, near, far, arrived, after(store, token))
    attended = finish(suffix, 0, queries, after(partial[0], store), own[0])
    attended = finish(suffix, heads // 2, queries, partial[1], own[1], attended)
    return (attended, store)


def wire_of(part, heads):
    rows, columns = part[0].shape[1:]
    return jax.ShapeDtypeStruct((heads, rows + STAT_ROWS, columns), jnp.bfloat16)


def packed(part):
    return call(pack_kernel, wire_of(part, part[0].shape[0]), *part)


def merged(block, part, in_first, first, heads):
    kernel = functools.partial(merge_kernel, in_first, first)
    return call(kernel, wire_of(part, heads), block, *part)


def on_device(queries, suffix_key_value, kv_pages, page_table, prefix_pages, new_slots):
    stores = lax.axis_size("store")
    pulled = page_table.shape[1] // stores * kv_pages[0].size
    pushed = 2 * queries[0].size
    arrays = (queries, suffix_key_value, kv_pages, page_table, prefix_pages, new_slots)
    if pulled >= pushed and stores % 8 == 0 and stores <= LIST_ROWS:
        return queries_travel(*arrays)
    return pages_travel(*arrays)


def solution(mesh):
    return jax.shard_map(
        on_device,
        mesh=mesh,
        in_specs=(
            P(("groups", "store"), None, "tensor"),
            P(("groups", "store"), None, None, "tensor"),
            P(("groups", "store"), None, None, "tensor"),
            P(("groups", "store"), None),
            P(("groups", "store")),
            P(("groups", "store")),
        ),
        out_specs=(
            P(("groups", "store"), None, "tensor"),
            P(("groups", "store"), None, None, "tensor"),
        ),
        check_vma=False,
    )
```

```python
import functools

import jax
import jax.numpy as jnp
from jax import lax
from jax.experimental import pallas as pl
from jax.experimental.pallas import tpu as pltpu
from jax.sharding import PartitionSpec as P

HEAD_SIZE = 128
LOG2E = 1.4426950408889634
DEAD = -1e30
FLOOR = -1e29
STAT_ROWS = 16
LIST_ROWS = 16
GRANT = 20 * 1024 * 1024
LIGHT = pl.CostEstimate(flops=1, bytes_accessed=1, transcendentals=0)
HEAVY = pl.CostEstimate(flops=1 << 33, bytes_accessed=1 << 25, transcendentals=1 << 24)
VMEM = pl.BlockSpec(memory_space=pltpu.VMEM)
SMEM = pl.BlockSpec(memory_space=pltpu.SMEM)
HBM = pl.BlockSpec(memory_space=pltpu.HBM)


def shifted(block, axis, distance):
    devices = range(lax.axis_size(axis))
    route = [((i - distance) % len(devices), i) for i in devices]
    return lax.ppermute(block, axis, route)


def block_update(state, head_count, key_rows, value_rows, live, scale):
    top_old, total_old, acc_old = state
    scores = (
        jnp.einsum("qhgd,khd->hgqk", head_count, key_rows, preferred_element_type=jnp.float32)
        * scale
    )
    scores = jnp.where(live, scores, -1e30)
    top_new = jnp.maximum(top_old, jnp.max(scores, axis=-1))
    weights = jnp.where(live, jnp.exp(scores - top_new[..., None]), 0.0)
    factor = jnp.exp(top_old - top_new)
    total_new = total_old * factor + jnp.sum(weights, axis=-1)
    product = jnp.einsum(
        "hgqk,khd->hgqd",
        weights.astype(jnp.bfloat16),
        value_rows,
        preferred_element_type=jnp.float32,
    )
    return (top_new, total_new, acc_old * factor[..., None] + product)


def pages_travel(queries, suffix_key_value, kv_pages, page_table, prefix_pages, new_slots):
    stores = lax.axis_size("store")
    pages_dev = kv_pages.shape[0]
    maxp = page_table.shape[1]
    cap = maxp // stores
    page_len = kv_pages.shape[2]
    width = kv_pages.shape[3]
    kv_heads = width // HEAD_SIZE
    suffix = queries.shape[1]
    groups_per_head = queries.shape[2] // width
    scale = HEAD_SIZE ** (-0.5)
    length = prefix_pages[0]
    table = page_table[0]
    owners = table // pages_dev
    local_ids = table % pages_dev
    entries = jnp.arange(maxp, dtype=jnp.int32)
    same_owner = (owners[:, None] == owners[None, :]) & (entries[:, None] < entries[None, :])
    ranks = jnp.sum(same_owner.astype(jnp.int32), axis=0)
    slots = owners * cap + ranks
    placed = slots[:, None] == entries[None, :]
    slot_entry = jnp.sum(jnp.where(placed, entries[:, None], 0), axis=0)
    wanted = jnp.sum(jnp.where(placed, local_ids[:, None], 0), axis=0)
    asked = lax.all_to_all(
        wanted.reshape(stores, cap), "store", split_axis=0, concat_axis=0, tiled=True
    )
    served = kv_pages[asked.reshape(-1)].reshape(stores, cap, 2, page_len, width)
    received = lax.all_to_all(served, "store", split_axis=0, concat_axis=0, tiled=True).reshape(
        maxp, 2, page_len, width
    )
    head_count = queries[0].reshape(suffix, kv_heads, groups_per_head, HEAD_SIZE)
    own_keys = suffix_key_value[0, 0].reshape(suffix, kv_heads, HEAD_SIZE)
    own_values = suffix_key_value[0, 1].reshape(suffix, kv_heads, HEAD_SIZE)
    rows = jnp.arange(suffix, dtype=jnp.int32)
    causal = rows[None, :] <= rows[:, None]
    start_state = (
        jnp.full((kv_heads, groups_per_head, suffix), -1e30, jnp.float32),
        jnp.zeros((kv_heads, groups_per_head, suffix), jnp.float32),
        jnp.zeros((kv_heads, groups_per_head, suffix, HEAD_SIZE), jnp.float32),
    )
    state = block_update(start_state, head_count, own_keys, own_values, causal, scale)
    block_pages = min(8, maxp)
    live_pages = slot_entry < length
    trips = maxp // block_pages

    def step_block(index, carry):
        first = index * block_pages
        block = lax.dynamic_slice_in_dim(received, first, block_pages, 0)
        alive = lax.dynamic_slice_in_dim(live_pages, first, block_pages, 0)
        alive = jnp.broadcast_to(alive[:, None], (block_pages, page_len)).reshape(
            1, block_pages * page_len
        )
        block_keys = block[:, 0].reshape(block_pages * page_len, kv_heads, HEAD_SIZE)
        block_values = block[:, 1].reshape(block_pages * page_len, kv_heads, HEAD_SIZE)
        return block_update(carry, head_count, block_keys, block_values, alive, scale)

    top_final, total_final, acc_final = lax.fori_loop(0, trips, step_block, state)
    output = acc_final / total_final[..., None]
    attended = (
        output.transpose(2, 0, 1, 3)
        .reshape(1, suffix, groups_per_head * width)
        .astype(jnp.bfloat16)
    )
    arrived, arrived_slot = shifted((suffix_key_value, new_slots), "store", stores // 2)
    new_store = lax.dynamic_update_slice_in_dim(kv_pages, arrived, arrived_slot[0], 0)
    return (attended, new_store)


def dot_nt(a, b):
    return lax.dot_general(a, b, (((1,), (1,)), ((), ())), preferred_element_type=jnp.float32)


def block_of(j):
    return slice(j * HEAD_SIZE, (j + 1) * HEAD_SIZE)


def iota(shape, dim):
    return lax.broadcasted_iota(jnp.int32, shape, dim)


def pack_stats(top, total):
    diagonal = iota((HEAD_SIZE, HEAD_SIZE), 0) == iota((HEAD_SIZE, HEAD_SIZE), 1)
    row = iota((STAT_ROWS, HEAD_SIZE), 0)
    tile = jnp.zeros((STAT_ROWS, HEAD_SIZE), jnp.float32)

    def along(x):
        return jnp.sum(jnp.where(diagonal, x, 0.0), 0, keepdims=True)

    for j, (m, l) in enumerate(zip(top, total)):
        l = along(l)
        high = l.astype(jnp.bfloat16).astype(jnp.float32)
        for t, x in enumerate((along(m), high, l - high)):
            tile = jnp.where(row == 4 * t + j, x, tile)
    return tile.astype(jnp.bfloat16)


def unpack_stats(tile):
    row = iota((STAT_ROWS, 8 * HEAD_SIZE), 0)
    block = iota((STAT_ROWS, 8 * HEAD_SIZE), 1) // HEAD_SIZE
    j = block // 2
    stat = block % 2
    spread = (
        ((row == j) & (stat == 0)) | ((row == j + 4) & (stat == 1)) | ((row == j + 8) & (stat == 1))
    )
    spread = spread.astype(jnp.float32).astype(jnp.bfloat16)
    turned = tile.astype(jnp.float32).T.astype(jnp.bfloat16)
    wide = jnp.dot(turned, spread, preferred_element_type=jnp.float32)
    part = lambda b: wide[:, b * HEAD_SIZE:(b + 1) * HEAD_SIZE]
    return [part(2 * j) for j in range(4)], [part(2 * j + 1) for j in range(4)]


def attend_kernel(sizes, jobs, own, keeping, *refs):
    rows, suffix, cap, page_len, count = sizes
    refs = list(refs)
    meta = refs.pop(0)
    queries = [refs.pop(0) for _ in range(count)]
    own_kv = refs.pop(0) if own else None
    held = refs.pop(0)
    if keeping and keeping[0]:
        refs.pop(0)
    outs = [(refs.pop(0), refs.pop(0)) for _ in range(count)]
    stored = refs.pop(0) if keeping else None
    scores = refs.pop(0)
    late_scores = refs.pop(0) if own else None
    if keeping:
        span = pl.ds(*keeping)
        keep = pltpu.make_async_copy(held.at[span], stored.at[span], refs.pop(0))
        keep.start()
    factor = HEAD_SIZE ** (-0.5) * LOG2E
    keys = cap * page_len

    def stacked(n, part, h):
        return jnp.concatenate([held[meta[n, c], part, :, block_of(h)] for c in range(cap)], 0)

    def score(i):
        n, _, h = jobs[i]
        q = queries[n][h * rows:(h + 1) * rows, :]
        scores[i % 2] = dot_nt(q, stacked(n, 0, h))
        if own:
            at = iota((rows, suffix), 0) % suffix
            causal = iota((rows, suffix), 1) <= at
            late_scores[i % 2] = jnp.where(causal, dot_nt(q, own_kv[0, :, block_of(h)]), DEAD)

    def weigh(i):
        n, spot, h = jobs[i]
        live = iota((1, keys), 1) < meta[n, cap] * page_len
        s = jnp.where(live, scores[i % 2], DEAD)
        top = jnp.max(s, axis=-1, keepdims=True)
        if own:
            top = jnp.maximum(top, jnp.max(late_scores[i % 2], axis=-1, keepdims=True))
        top = jnp.maximum(top * factor, FLOOR).astype(jnp.bfloat16).astype(jnp.float32)
        p = jnp.exp2(s * factor - top).astype(jnp.bfloat16)
        v = stacked(n, 1, h)
        v = jnp.concatenate([v, jnp.ones_like(v)], 1)
        out = jnp.dot(p, v, preferred_element_type=jnp.float32)
        if own:
            p = jnp.exp2(late_scores[i % 2] * factor - top).astype(jnp.bfloat16)
            v = own_kv[1, :, block_of(h)]
            v = jnp.concatenate([v, jnp.ones_like(v)], 1)
            out = out + jnp.dot(p, v, preferred_element_type=jnp.float32)
        acc_ref, stat_ref = outs[n]
        acc_ref[spot] = out[:, :HEAD_SIZE]
        total = out[:, HEAD_SIZE:]
        top = jnp.broadcast_to(top, total.shape)
        blocks = [block_of(j) for j in range(rows // HEAD_SIZE)]
        stat_ref[spot] = pack_stats([top[j] for j in blocks], [total[j] for j in blocks])

    for i in range(len(jobs) + 1):
        if i < len(jobs):
            score(i)
        if i > 0:
            weigh(i - 1)
    if keeping:
        keep.wait()


def attend(sizes, jobs, meta, queries, held, own=None, keeping=None, store=None, cost=None):
    rows, suffix, cap, page_len = sizes
    keys, count = cap * page_len, len(queries)
    heads = len(jobs) // count
    shapes, out_specs = [], []
    for _ in queries:
        shapes.append(jax.ShapeDtypeStruct((heads, rows, HEAD_SIZE), jnp.float32))
        shapes.append(jax.ShapeDtypeStruct((heads, STAT_ROWS, HEAD_SIZE), jnp.bfloat16))
        out_specs += [VMEM, VMEM]
    scratch = [pltpu.VMEM((2, rows, keys), jnp.float32)]
    args, aliases = [meta, *queries], {}
    if own is not None:
        args.append(own)
        scratch.append(pltpu.VMEM((2, rows, suffix), jnp.float32))
    args.append(held)
    in_specs = [SMEM] + [VMEM] * (len(args) - 1)
    if keeping:
        shapes.append(jax.ShapeDtypeStruct(held.shape, held.dtype))
        out_specs.append(HBM)
        scratch.append(pltpu.SemaphoreType.DMA)
    if store is not None:
        aliases[len(args)] = 2 * count
        args.append(store)
        in_specs.append(HBM)
    work = pl.CostEstimate(
        flops=len(jobs) * rows * keys * HEAD_SIZE * 8,
        bytes_accessed=len(jobs) * (rows * 6 + keys * 4) * HEAD_SIZE,
        transcendentals=len(jobs) * rows * keys,
    )
    out = pl.pallas_call(
        functools.partial(attend_kernel, sizes + (count,), jobs, own is not None, keeping),
        out_shape=shapes,
        in_specs=in_specs,
        out_specs=out_specs,
        scratch_shapes=scratch,
        input_output_aliases=aliases,
        compiler_params=pltpu.CompilerParams(vmem_limit_bytes=GRANT),
        cost_estimate=cost or work,
    )(*args)
    return [(out[2 * n], out[2 * n + 1]) for n in range(count)] + list(out[2 * count:])


def touch_kernel(held_ref, lists_ref, out_ref):
    out_ref[...] = lists_ref[...]


def touch(held, lists):
    return pl.pallas_call(
        touch_kernel,
        out_shape=jax.ShapeDtypeStruct(lists.shape, lists.dtype),
        in_specs=[VMEM, VMEM],
        out_specs=VMEM,
        compiler_params=pltpu.CompilerParams(vmem_limit_bytes=GRANT),
        cost_estimate=LIGHT,
    )(held, lists)


def place_kernel(half, column, me_ref, core_ref, near_ref, far_ref, page_ref, old_ref, out_ref, sem):
    me, core = me_ref[0], core_ref[0]
    is_near = ((me >= half) == (me % 2 == 0)) == (core % 2 == 0)
    slot = jnp.where(is_near, near_ref[0, column], far_ref[0, column])
    copy = pltpu.make_async_copy(page_ref.at[0], out_ref.at[slot], sem)
    copy.start()
    copy.wait()


def place_page(half, column, me, core, near, far, page, store):
    return pl.pallas_call(
        functools.partial(place_kernel, half, column),
        out_shape=jax.ShapeDtypeStruct(store.shape, store.dtype),
        in_specs=[SMEM] * 4 + [VMEM, HBM],
        out_specs=HBM,
        scratch_shapes=[pltpu.SemaphoreType.DMA],
        input_output_aliases={5: 0},
        compiler_params=pltpu.CompilerParams(vmem_limit_bytes=GRANT),
        cost_estimate=LIGHT,
    )(me[None], core[None], near, far, page, store)


def blend(parts):
    top = functools.reduce(jnp.maximum, [m for _, m, _ in parts])
    scales = [jnp.exp2(m - top) for _, m, _ in parts]
    acc = sum(a * f for (a, _, _), f in zip(parts, scales))
    total = sum(l * f for (_, _, l), f in zip(parts, scales))
    return acc, top, total


def pack_kernel(acc_ref, stat_ref, out_ref):
    heads, rows = acc_ref.shape[:2]
    for h in range(heads):
        out_ref[h, :rows, :] = acc_ref[h].astype(jnp.bfloat16)
        out_ref[h, rows:, :] = stat_ref[h]


def merge_kernel(in_first, first, in_ref, acc_ref, stat_ref, out_ref):
    heads, rows = out_ref.shape[0], acc_ref.shape[1]
    for h in range(heads):
        in_top, in_total = unpack_stats(in_ref[in_first + h, rows:, :])
        my_top, my_total = unpack_stats(stat_ref[first + h])
        tops, totals = [], []
        for j in range(rows // HEAD_SIZE):
            acc, top, total = blend(
                [
                    (in_ref[in_first + h, block_of(j), :].astype(jnp.float32), in_top[j], in_total[j]),
                    (acc_ref[first + h, block_of(j), :], my_top[j], my_total[j]),
                ]
            )
            out_ref[h, block_of(j), :] = acc.astype(out_ref.dtype)
            tops.append(top)
            totals.append(total)
        out_ref[h, rows:, :] = pack_stats(tops, totals)


def final_kernel(suffix, first, in_ref, acc_ref, stat_ref, *refs):
    out_ref, done, sems = refs[-3:]
    heads, rows = in_ref.shape[0], acc_ref.shape[1]
    groups = rows // suffix
    copies = []
    for h in range(heads):
        in_top, in_total = unpack_stats(in_ref[h, rows:, :])
        my_top, my_total = unpack_stats(stat_ref[h])
        for j in range(rows // HEAD_SIZE):
            acc, _, total = blend(
                [
                    (in_ref[h, block_of(j), :].astype(jnp.float32), in_top[j], in_total[j]),
                    (acc_ref[h, block_of(j), :], my_top[j], my_total[j]),
                ]
            )
            out = (acc / total).astype(jnp.bfloat16)
            for i in range(HEAD_SIZE // suffix):
                g = h * groups + j * (HEAD_SIZE // suffix) + i
                done[0, :, block_of(g)] = out[i * suffix:(i + 1) * suffix]
        width = groups * HEAD_SIZE
        copies.append(
            pltpu.make_async_copy(
                done.at[:, :, pl.ds(h * width, width)],
                out_ref.at[:, :, pl.ds((first + h) * width, width)],
                sems.at[h],
            )
        )
        copies[-1].start()
    for copy in copies:
        copy.wait()


def finish(suffix, first, like, block, part, before=None):
    heads, rows = block.shape[0], part[0].shape[1]
    args = [block, *part] + ([] if before is None else [before])
    return pl.pallas_call(
        functools.partial(final_kernel, suffix, first),
        out_shape=jax.ShapeDtypeStruct(like.shape, like.dtype),
        in_specs=[VMEM] * 3 + [HBM] * (len(args) - 3),
        out_specs=HBM,
        scratch_shapes=[
            pltpu.VMEM((1, suffix, heads * rows // suffix * HEAD_SIZE), like.dtype),
            pltpu.SemaphoreType.DMA((heads,)),
        ],
        input_output_aliases={} if before is None else {3: 0},
        compiler_params=pltpu.CompilerParams(vmem_limit_bytes=GRANT),
    )(*args)


def call(kernel, shape, *args):
    size = sum(a.size * a.dtype.itemsize for a in args)
    return pl.pallas_call(
        kernel,
        out_shape=shape,
        in_specs=[VMEM] * len(args),
        out_specs=[VMEM] * len(shape) if isinstance(shape, list) else VMEM,
        compiler_params=pltpu.CompilerParams(vmem_limit_bytes=GRANT),
        cost_estimate=pl.CostEstimate(flops=size, bytes_accessed=2 * size, transcendentals=0),
    )(*args)


def lists_kernel(cap, pages_dev, length_ref, slot_ref, table_ref, out_ref):
    maxp = table_ref.shape[1]
    table = table_ref[...]
    owner = lax.div(table, pages_dev)
    local = (table - owner * pages_dev).astype(jnp.float32)
    owner = owner.astype(jnp.float32)
    down, along = iota((maxp, maxp), 0), iota((maxp, maxp), 1)

    def turned(x):
        return jnp.sum(jnp.where(down == along, x, 0.0), 1, keepdims=True)

    before = (turned(owner) == owner) & (along < down)
    rank = jnp.sum(jnp.where(before, 1.0, 0.0), 1, keepdims=True)
    place = iota((maxp, HEAD_SIZE), 1)
    live = jnp.where(iota((maxp, HEAD_SIZE), 0) < length_ref[0], 1.0, 0.0)
    ids = jnp.where(rank == place.astype(jnp.float32), turned(local), 0.0)
    fields = jnp.where(place < cap, ids, jnp.where(place == cap, live, 0.0))
    owned = jnp.where(owner == iota((LIST_ROWS, maxp), 0).astype(jnp.float32), 1.0, 0.0)
    lists = jnp.dot(
        owned.astype(jnp.bfloat16), fields.astype(jnp.bfloat16), preferred_element_type=jnp.float32
    )
    slot = slot_ref[0].astype(jnp.float32)
    lists = jnp.where(iota(lists.shape, 1) == cap + 1, slot, lists)
    out_ref[...] = lists.astype(jnp.bfloat16)


def list_pages(cap, pages_dev, page_table, prefix_pages, new_slots):
    return pl.pallas_call(
        functools.partial(lists_kernel, cap, pages_dev),
        out_shape=jax.ShapeDtypeStruct((LIST_ROWS, HEAD_SIZE), jnp.bfloat16),
        in_specs=[SMEM, SMEM, VMEM],
        out_specs=VMEM,
        compiler_params=pltpu.CompilerParams(vmem_limit_bytes=GRANT),
    )(prefix_pages, new_slots, page_table)


def join_kernel(q_ref, lists_ref, out_ref):
    suffix, columns = q_ref.shape[1:]
    for g in range(columns // HEAD_SIZE):
        out_ref[g * suffix:(g + 1) * suffix, :] = q_ref[0, :, block_of(g)]
    out_ref[columns // HEAD_SIZE * suffix:, :] = lists_ref[...]


def queries_travel(queries, suffix_key_value, kv_pages, page_table, prefix_pages, new_slots):
    stores = lax.axis_size("store")
    cores = lax.axis_size("tensor")
    pages_dev, _, page_len, width = kv_pages.shape
    cap = page_table.shape[1] // stores
    heads = width // HEAD_SIZE
    suffix = queries.shape[1]
    rows = queries.shape[2] // width * suffix
    sizes = (rows, suffix, cap, page_len)
    half = stores // 2
    me = lax.axis_index("store")

    order = list(range(0, stores, 2)) + list(range(1, stores, 2))[::-1]
    route = [
        (order[i] * cores + core, order[(i + 1 - 2 * (core % 2)) % stores] * cores + core)
        for core in range(cores)
        for i in range(stores)
    ]

    def onward(x):
        return lax.ppermute(x, ("store", "tensor"), route)

    def listed(x, below):
        row = lax.dynamic_slice(x, (below + me, 0), (1, HEAD_SIZE))
        return row.astype(jnp.int32)

    def after(values, token):
        return lax.optimization_barrier((values, token))[0]

    def joined(x, rows_below):
        shape = jax.ShapeDtypeStruct((heads * rows + LIST_ROWS, HEAD_SIZE), queries.dtype)
        return call(join_kernel, shape, x, rows_below)

    first = onward(queries)
    mine = list_pages(cap, pages_dev, page_table, prefix_pages, new_slots)
    their_lists = onward(mine)
    mine = touch(kv_pages, mine)
    moving = joined(after(first, mine), their_lists)

    own_queries = None
    halves = [range(0, heads // 2), range(heads // 2, heads)]
    token = []
    lists, own = {}, []
    for step in range(1, stores):
        came = after(moving, token)
        if step < stores - 1:
            moving = onward(came)
        lists[step] = listed(came, heads * rows)
        if step == stores - 3:
            arrived = shifted(after(suffix_key_value, token), "store", half)
        jobs = [(0, h, h) for h in range(heads)]
        keeping, pages = None, pages_dev // 2
        if step == 2:
            keeping = (0, pages)
            part, store = attend(sizes, jobs, lists[step], [came], kv_pages, None, keeping)
        elif step == 3:
            keeping = (pages, pages_dev - pages)
            part, store = attend(sizes, jobs, lists[step], [came], kv_pages, None, keeping, store)
        else:
            cost = {stores - 2: LIGHT, stores - 1: HEAVY}.get(step)
            part, = attend(sizes, jobs, lists[step], [came], kv_pages, cost=cost)
        if step == 1:
            blocks = [packed(part)]
        elif step < stores - 3:
            blocks = [merged(after(partial[0], part), part, 0, 0, heads)]
        else:
            part = after(part, arrived) if step == stores - 1 else part
            blocks = []
            for n, half_heads in enumerate(halves):
                block, at = (partial[0], half_heads[0]) if len(partial) == 1 else (partial[n], 0)
                block = after(block, [part, blocks])
                blocks.append(merged(block, part, at, half_heads[0], len(half_heads)))
        partial = [onward(block) for block in blocks]
        token = blocks
        if step in (half - 1, half):
            if own_queries is None:
                own_queries = joined(after(queries, token), mine)
            jobs = [(0, n, h) for n, h in enumerate(halves[len(own)])]
            x = after(own_queries, token)
            own += attend(sizes, jobs, listed(mine, 0), [x], kv_pages, suffix_key_value[0])
            token = [blocks, own]

    quarter = stores // 4
    near, far = lists[quarter], lists[stores - quarter]
    core = lax.axis_index("tensor")
    store = place_page(half, cap + 1, me, core, near, far, arrived, after(store, token))
    attended = finish(suffix, 0, queries, after(partial[0], store), own[0])
    attended = finish(suffix, heads // 2, queries, partial[1], own[1], attended)
    return (attended, store)


def wire_of(part, heads):
    rows, columns = part[0].shape[1:]
    return jax.ShapeDtypeStruct((heads, rows + STAT_ROWS, columns), jnp.bfloat16)


def packed(part):
    return call(pack_kernel, wire_of(part, part[0].shape[0]), *part)


def merged(block, part, in_first, first, heads):
    kernel = functools.partial(merge_kernel, in_first, first)
    return call(kernel, wire_of(part, heads), block, *part)


def on_device(queries, suffix_key_value, kv_pages, page_table, prefix_pages, new_slots):
    stores = lax.axis_size("store")
    pulled = page_table.shape[1] // stores * kv_pages[0].size
    pushed = 2 * queries[0].size
    arrays = (queries, suffix_key_value, kv_pages, page_table, prefix_pages, new_slots)
    if pulled >= pushed and stores % 8 == 0 and stores <= LIST_ROWS:
        return queries_travel(*arrays)
    return pages_travel(*arrays)


def solution(mesh):
    return jax.shard_map(
        on_device,
        mesh=mesh,
        in_specs=(
            P(("groups", "store"), None, "tensor"),
            P(("groups", "store"), None, None, "tensor"),
            P(("groups", "store"), None, None, "tensor"),
            P(("groups", "store"), None),
            P(("groups", "store")),
            P(("groups", "store")),
        ),
        out_specs=(
            P(("groups", "store"), None, "tensor"),
            P(("groups", "store"), None, None, "tensor"),
        ),
        check_vma=False,
    )
```
